32 devices in a mesh: rep: 4 (over y, core), shard: 8 (over z, x).
Axes of the slice: x: 2, y: 2, z: 4, core: 2. Of those that a mesh axis runs over, the one named last changes fastest.
Arguments:
- tokens: bfloat16 [8192, 2048], P(('rep', 'shard')), may hold values from -6 to 6
- cotangent: bfloat16 [8192, 2048], P(('rep', 'shard')), may hold values from -6 to 6
- block_seq: int32 [64], P(('rep', 'shard')), may hold values from 0 to 63, as said below
- block_len: int32 [64], P(('rep', 'shard')), may hold values from 0 to 128, as said below
- vectors: bfloat16 [2048, 6], P('shard')
- key_bias: bfloat16 [512, 1], P('shard'), may hold values from -3 to 3
- w_qkv: bfloat16 [2048, 6144], P('shard'), may hold values from -0.125 to 0.125
- w_out: bfloat16 [2048, 2048], P('shard'), may hold values from -0.5 to 0.5
- w_gate_up: bfloat16 [2048, 11264], P('shard'), may hold values from -0.125 to 0.125
- w_down: bfloat16 [5632, 2048], P('shard'), may hold values from -0.078125 to 0.078125
Outputs:
- activations: bfloat16 [8192, 2048], P(('rep', 'shard'))
- grad_input: bfloat16 [8192, 2048], P(('rep', 'shard'))
- grad_vectors: float32 [2048, 6], P('shard')
- grad_key_bias: float32 [512, 1], P('shard')
- grad_qkv: float32 [2048, 6144], P('shard')
- grad_out: float32 [2048, 2048], P('shard')
- grad_gate_up: float32 [2048, 11264], P('shard')
- grad_down: float32 [5632, 2048], P('shard')
The draws below stay inside these ranges and needn't reach their ends.
Inputs may be any that keep to these rules, and one draw needn't show every extreme that they name: `block_seq`: never falling; equal within a sequence and different between sequences; the blocks of a sequence are consecutive and lie on one device. One sequence fills all 256 slots of some device. `block_len`: every block of a sequence but its last holds 128 tokens; a block's tokens fill its first slots; a block with 0 holds none.
All inputs are finite; a program needn't handle non-finite values.
Results may differ from the reference program's by a relative error of at most 0.017.
Values may be sent and summed in bfloat16 or wider, within the bound.
A program may use at most 512 MiB of HBM per device.

```python
import math
import jax
import jax.numpy as jnp
from jax import lax

D = 2048
HEADS = 32
ROT = 16
FF = 5632
BLOCK = 128
BLOCKS_DEV = 2
SLOTS = 256
NBLOCKS = 64
TOKENS = 8192
N_REP = 4
N_SHARD = 8


def block_layout(key):
    devices = NBLOCKS // BLOCKS_DEV
    streams = jax.random.split(key, 4)
    starts = jax.random.randint(streams[0], (devices, BLOCKS_DEV), 0, 2)
    in_use = jax.random.randint(streams[1], (devices, 1), (BLOCKS_DEV + 1) // 2, BLOCKS_DEV + 1)
    full_device = jax.random.randint(streams[2], (), 0, devices - 1)
    tail_len = jax.random.randint(streams[3], (devices, BLOCKS_DEV), 1, BLOCK + 1)
    device = jnp.arange(devices, dtype=jnp.int32)[:, None]
    position = jnp.arange(BLOCKS_DEV, dtype=jnp.int32)[None, :]
    is_full = device == full_device
    in_use = jnp.where(is_full, BLOCKS_DEV, in_use)
    active = position < in_use
    starts = jnp.where(position == 0, 1, starts)
    starts = jnp.where(is_full, jnp.where(position == 0, 1, 0), starts)
    starts = jnp.where(active, starts, 1)
    starts = jnp.where((device == devices - 1) & (position == BLOCKS_DEV - 1), 1, starts)
    leader = lax.cummax(jnp.where(starts == 1, position, 0), axis=1)
    sequence = device * BLOCKS_DEV + leader
    closing = jnp.concatenate([starts[:, 1:], jnp.ones((devices, 1), jnp.int32)], axis=1)
    length = jnp.where(closing == 1, tail_len, BLOCK)
    length = jnp.where(is_full & (position == BLOCKS_DEV - 1), BLOCK, length)
    length = jnp.where(active, length, 0)
    return (sequence.reshape(-1).astype(jnp.int32), length.reshape(-1).astype(jnp.int32))


def draw_block_seq(key, part):
    sequence, length = block_layout(key)
    return sequence


def draw_block_len(key, part):
    sequence, length = block_layout(key)
    return length


def draw_vectors(key, part):
    key = jax.random.fold_in(key, 3)
    streams = jax.random.split(key, 2)
    gains = jnp.exp(jax.random.uniform(streams[0], (D, 2), jnp.float32, -0.5, 0.5))
    shifts = jnp.clip(0.45 * jax.random.normal(streams[1], (D, 4), jnp.float32), -1.5, 1.5)
    columns = jnp.concatenate([gains[:, 0:1], shifts[:, 0:1], gains[:, 1:2], shifts[:, 1:2], shifts[:, 2:4]], axis=1)
    return columns.astype(jnp.bfloat16)


def shard_levels(own_key, dims, cuts, smallest, high):
    level = 1.0
    for axis_at, blocks in cuts:
        heights = jax.random.uniform(jax.random.fold_in(jax.random.fold_in(own_key, 6), axis_at), (blocks,), jnp.float32, smallest / len(cuts), high / len(cuts))
        level = level * jnp.repeat(jnp.exp(heights), dims[axis_at] // blocks).reshape((-1,) + (1,) * (len(dims) - 1 - axis_at))
    return level


def normal_values(own_key, dims, width, bound, shards=(), kind=jnp.bfloat16):
    loudness = shard_levels(own_key, dims, shards, -0.22, 0.18) if shards else 1.0
    result = jax.random.normal(own_key, dims, jnp.float32) * width * loudness
    return jnp.minimum(jnp.maximum(result, -bound), bound).astype(kind)


def setup_inputs(seed: int = 0) -> dict:
    streams_of = jax.random.split(jax.random.key(seed), 11)
    return {
        "tokens": normal_values(streams_of[0], (TOKENS, D), 1.0, 6.0, ((0, 32),)),
        "cotangent": normal_values(streams_of[1], (TOKENS, D), 1.0, 6.0, ((0, 32),)),
        "block_seq": draw_block_seq(jax.random.fold_in(streams_of[10], 71), 0),
        "block_len": draw_block_len(jax.random.fold_in(streams_of[10], 71), 0),
        "vectors": draw_vectors(jax.random.fold_in(streams_of[10], 71), 0),
        "key_bias": normal_values(streams_of[5], (HEADS * ROT, 1), 0.5, 3.0, ((0, 8),)),
        "w_qkv": normal_values(streams_of[6], (D, 3 * D), D ** -0.5, 0.125, ((0, 8),)),
        "w_out": normal_values(streams_of[7], (D, D), (D // 16) ** -0.5, 0.5, ((0, 8),)),
        "w_gate_up": normal_values(streams_of[8], (D, 2 * FF), D ** -0.5, 0.125, ((0, 8),)),
        "w_down": normal_values(streams_of[9], (FF, D), FF ** -0.5, 0.078125, ((0, 8),)),
    }


@jax.custom_vjp
def low(v):
    return lax.optimization_barrier(v.astype(jnp.bfloat16)).astype(jnp.float32)

@jax.custom_vjp
def low_back(v):
    return v

def low_keep(v):
    return (low(v), None)

def low_pass(kept, grad):
    return (grad,)

def back_keep(v):
    return (v, None)

def back_low(kept, grad):
    return (low(grad),)
low.defvjp(low_keep, low_pass)
low_back.defvjp(back_keep, back_low)

def slot_layout(seq_ids, lengths, block_size):
    block_count = seq_ids.shape[0]
    block_index = jnp.arange(block_count, dtype=jnp.int32)
    same_seq = seq_ids[None, :] == seq_ids[:, None]
    earlier = lax.optimization_barrier(jnp.sum(jnp.where((block_index[None, :] < block_index[:, None]) & same_seq, 1, 0), axis=1)).astype(jnp.int32)
    offset = jnp.arange(block_size, dtype=jnp.int32)[None, :]
    seq_slot = jnp.broadcast_to(seq_ids[:, None], (block_count, block_size)).reshape(-1)
    valid_rows = (offset < lengths[:, None]).reshape(-1)
    positions = (earlier[:, None] * block_size + offset).reshape(-1)
    slot_index = jnp.arange(block_count * block_size, dtype=jnp.int32)
    allowed = (seq_slot[None, :] == seq_slot[:, None]) & (slot_index[None, :] <= slot_index[:, None])
    allowed = allowed & (valid_rows[None, :] | (slot_index[None, :] == slot_index[:, None]))
    return (valid_rows, positions, allowed)

def turn_tables(positions, rotated):
    half_turn = rotated // 2
    frequencies = jnp.exp(jnp.arange(half_turn, dtype=jnp.float32) * (-2.0 * math.log(10000.0) / rotated))
    angles = positions.astype(jnp.float32)[:, None] * frequencies[None, :]
    return (jnp.cos(angles)[:, None, :], jnp.sin(angles)[:, None, :])

def rotate(values, cosine, sine_table, rotated):
    half_turn = rotated // 2
    lower_part = values[..., :half_turn]
    upper_part = values[..., half_turn:rotated]
    unturned = values[..., rotated:]
    return jnp.concatenate([lower_part * cosine - upper_part * sine_table, upper_part * cosine + lower_part * sine_table, unturned], axis=-1)

def norm_rows(values, gain, shift):
    center = values - lax.optimization_barrier(jnp.mean(values, axis=1, keepdims=True))
    inv_std = lax.rsqrt(lax.optimization_barrier(jnp.mean(center * center, axis=1, keepdims=True)) + 1e-05)
    return center * inv_std * gain + shift

def layer(tokens_f, params, allowed, cosine, sine_table):
    vectors, key_bias, w_qkv, w_out, w_gate_up, w_down = params
    slot_count, features = tokens_f.shape
    head_dim = features // HEADS
    head_shape = (slot_count, HEADS, head_dim)
    score_scale = 1.0 / math.sqrt(head_dim)
    input_one = low(norm_rows(tokens_f, vectors[:, 0], vectors[:, 1]))
    projected = low_back(jnp.dot(input_one, w_qkv, preferred_element_type=jnp.float32, precision=lax.Precision.HIGHEST))
    key_shift = jnp.concatenate([key_bias.reshape(HEADS, ROT), jnp.zeros((HEADS, head_dim - ROT), jnp.float32)], axis=1).reshape(features)
    queries = (projected[:, :features] + vectors[:, 4]).reshape(head_shape)
    keys_all = (projected[:, features:2 * features] + key_shift).reshape(head_shape)
    values_all = (projected[:, 2 * features:] + vectors[:, 5]).reshape(head_shape)
    queries = low(rotate(queries, cosine, sine_table, ROT))
    keys_all = low(rotate(keys_all, cosine, sine_table, ROT))
    values_all = low(values_all)
    scores = low_back(jnp.einsum('shd,thd->hst', queries, keys_all, precision=lax.Precision.HIGHEST) * score_scale)
    scores = jnp.where(allowed[None], scores, -1e+30)
    attn_probs = jax.nn.softmax(scores, axis=-1)
    attn_mix = jnp.einsum('hst,thd->shd', low(attn_probs), values_all, precision=lax.Precision.HIGHEST).reshape(slot_count, features)
    attn_low = low(low_back(attn_mix))
    residual = tokens_f + low_back(jnp.dot(attn_low, w_out, preferred_element_type=jnp.float32, precision=lax.Precision.HIGHEST))
    input_two = low(norm_rows(residual, vectors[:, 2], vectors[:, 3]))
    gate_up = low_back(jnp.dot(input_two, w_gate_up, preferred_element_type=jnp.float32, precision=lax.Precision.HIGHEST))
    hidden = low(jax.nn.silu(gate_up[:, :FF]) * gate_up[:, FF:])
    return residual + low_back(jnp.dot(hidden, w_down, preferred_element_type=jnp.float32, precision=lax.Precision.HIGHEST))

def reference(tokens, cotangent, block_seq, block_len, vectors, key_bias, w_qkv, w_out, w_gate_up, w_down):
    params = tuple((array.astype(jnp.float32) for array in (vectors, key_bias, w_qkv, w_out, w_gate_up, w_down)))
    groups = N_REP * N_SHARD
    inputs = (tokens.astype(jnp.float32).reshape(groups, SLOTS, D), cotangent.astype(jnp.float32).reshape(groups, SLOTS, D), block_seq.reshape(groups, BLOCKS_DEV), block_len.reshape(groups, BLOCKS_DEV))

    def accumulate(totals, pieces):
        tokens_f, cot_f, seq_ids, lengths = pieces
        valid_rows, positions, allowed = slot_layout(seq_ids, lengths, BLOCK)
        cosine, sine_table = turn_tables(positions, ROT)

        def forward(inputs_x, weights):
            return layer(inputs_x, weights, allowed, cosine, sine_table)
        outputs, backward = jax.vjp(forward, tokens_f, params)
        grad_x, grad_params = backward(cot_f * valid_rows[:, None].astype(jnp.float32))
        totals = jax.tree.map(lambda earlier_sum, later_sum: earlier_sum + later_sum, totals, grad_params)
        return (totals, (outputs.astype(jnp.bfloat16), grad_x.astype(jnp.bfloat16)))
    zero_grads = jax.tree.map(jnp.zeros_like, params)
    totals, (outputs, grad_x) = lax.scan(accumulate, zero_grads, inputs)
    return (outputs.reshape(TOKENS, D), grad_x.reshape(TOKENS, D), totals[0], totals[1], totals[2], totals[3], totals[4], totals[5])
```

```python
import math

import jax
import jax.numpy as jnp
from jax import lax
from jax.sharding import PartitionSpec as P

HEADS = 32
ROT = 16
REPS = 4
BOTH = ("rep", "shard")
F32 = jnp.float32
BF16 = jnp.bfloat16


def dot(a, b):
    return jnp.dot(a, b, preferred_element_type=F32)


def dot_rt(a, b):
    return lax.dot_general(a, b, (((1,), (1,)), ((), ())), preferred_element_type=F32)


def dot_lt(a, b):
    return lax.dot_general(a, b, (((0,), (0,)), ((), ())), preferred_element_type=F32)


def turn_tables(positions):
    half = ROT // 2
    frequencies = jnp.exp(
        jnp.arange(half, dtype=F32) * (-2.0 * math.log(10000.0) / ROT)
    )
    angles = positions.astype(F32)[:, None] * frequencies[None, :]
    return jnp.cos(angles)[:, None, :], jnp.sin(angles)[:, None, :]


def rotate(values, cosine, sine):
    half = ROT // 2
    low, high, rest = values[..., :half], values[..., half:ROT], values[..., ROT:]
    return jnp.concatenate(
        [low * cosine - high * sine, high * cosine + low * sine, rest], axis=-1
    )


def normalize(values):
    center = values - jnp.mean(values, axis=1, keepdims=True)
    inv_std = lax.rsqrt(jnp.mean(center * center, axis=1, keepdims=True) + 1e-05)
    return center * inv_std, inv_std


def norm_back(grad_norm, normal, inv_std):
    mean_grad = jnp.mean(grad_norm, axis=1, keepdims=True)
    mean_cross = jnp.mean(grad_norm * normal, axis=1, keepdims=True)
    return inv_std * (grad_norm - mean_grad - normal * mean_cross)


def core_swap(x):
    return lax.ppermute(x, "rep", [(0, 1), (1, 0), (2, 3), (3, 2)])


def y_swap(x):
    return lax.ppermute(x, "rep", [(0, 2), (1, 3), (2, 0), (3, 1)])


def rep_parts(x):
    across = y_swap(x)
    return [x, across, core_swap(x), core_swap(across)]


def rep_gather(x):
    return jnp.concatenate(rep_parts(x), axis=0)


def rep_reduce(a, w_dot, slots):
    far = core_swap(w_dot(a[2 * slots :]).astype(BF16))
    near = w_dot(a[: 2 * slots]) + far.astype(F32)
    return near[:slots] + y_swap(near[slots:].astype(BF16)).astype(F32)


def solution(mesh):
    n = mesh.shape["shard"]
    half_ring = n // 2
    order = list(range(0, n, 2)) + list(range(n - 1, 0, -2))
    place = [order.index(s) for s in range(n)]
    up_ring = [(order[i], order[(i + 1) % n]) for i in range(n)]
    down_ring = [(b, a) for a, b in up_ring]

    def forward_hop(x):
        return lax.ppermute(x, "shard", up_ring)

    def back_hop(x):
        return lax.ppermute(x, "shard", down_ring)

    def ring_ids():
        spot = jnp.array(place, jnp.int32)[lax.axis_index("shard")]
        table = jnp.array(order, jnp.int32)
        return {k: table[(spot + k) % n] for k in range(-half_ring, half_ring + 1)}

    def gather(x, ids, forward_extra, places):
        bufs = places(None, x, ids[0])
        up = down = x
        for k in range(1, half_ring + 1):
            if k < half_ring or forward_extra:
                up = forward_hop(up)
                bufs = places(bufs, up, ids[-k])
            if k < half_ring or not forward_extra:
                down = back_hop(down)
                bufs = places(bufs, down, ids[k])
        return bufs

    def put(bufs, block, at):
        if bufs is None:
            bufs = jnp.zeros((n,) + block.shape, block.dtype)
        return lax.dynamic_update_index_in_dim(bufs, block, at, 0)

    def reduce(term, ids, forward_extra, kind=BF16):
        total = term(ids[0])
        for hop, sign, extra in ((forward_hop, 1, forward_extra), (back_hop, -1, not forward_extra)):
            length = half_ring if extra else half_ring - 1
            acc = None
            for k in range(length, 0, -1):
                part = term(ids[sign * k])
                if acc is not None:
                    part = part + acc.astype(F32)
                acc = hop(part.astype(kind))
            total = total + acc.astype(F32)
        return total

    def pick_columns(w, groups, width, r):
        chosen = [
            lax.select_n(
                r,
                *[
                    w[:, (g * REPS + q) * width : (g * REPS + q + 1) * width]
                    for q in range(REPS)
                ],
            )
            for g in range(groups)
        ]
        return jnp.concatenate(chosen, axis=1)

    def by_rep(parts, y, core):
        own, across, beside, both = parts
        low0 = lax.select(core == 0, own, beside)
        low1 = lax.select(core == 0, beside, own)
        high0 = lax.select(core == 0, across, both)
        high1 = lax.select(core == 0, both, across)
        return [
            lax.select(y == 0, low0, high0),
            lax.select(y == 0, low1, high1),
            lax.select(y == 0, high0, low0),
            lax.select(y == 0, high1, low1),
        ]

    def weave(parts, groups, width):
        pieces = [
            parts[q][:, g * width : (g + 1) * width]
            for g in range(groups)
            for q in range(REPS)
        ]
        return jnp.concatenate(pieces, axis=1).astype(F32)

    def on_device(
        tokens, cotangent, block_seq, block_len, vectors, key_bias, w_qkv, w_out, w_gate_up, w_down
    ):
        slots, features = tokens.shape
        blocks = block_seq.shape[0]
        block_size = slots // blocks
        head_dim = features // HEADS
        own_heads = HEADS // REPS
        own_width = own_heads * head_dim
        all_slots = REPS * slots
        scale = 1.0 / math.sqrt(head_dim)
        rows = features // n
        hidden_units = w_gate_up.shape[1] // 2
        own_hidden = hidden_units // REPS
        down_rows = w_down.shape[0] // REPS
        out_rows = w_out.shape[0] // REPS
        regroup = out_rows < head_dim
        r = lax.axis_index("rep")
        y, core = r // 2, r % 2
        ids = ring_ids()

        def mix_out(x):
            if not regroup:
                return x
            pairs = [
                (k * n + 4 * j + q, q * n + 4 * j + k)
                for k in range(REPS)
                for j in range(n // 4)
                for q in range(REPS)
            ]
            return lax.ppermute(x, BOTH, pairs)

        small = jnp.concatenate([vectors.T.reshape(-1), key_bias.reshape(-1)])
        lanes = 3 * own_width
        small_rows = -(-small.size // lanes)
        small_rows = -(-small_rows // 16) * 16
        small = jnp.pad(small, (0, small_rows * lanes - small.size)).reshape(small_rows, lanes)
        qkv_block = jnp.concatenate([pick_columns(w_qkv, 3 * own_heads, head_dim, r), small], axis=0)

        def put_qkv(bufs, block, at):
            a, b = (None, None) if bufs is None else bufs
            return put(a, block[:rows], at), put(b, block[rows:], at)

        wq, smalls = gather(qkv_block, ids, True, put_qkv)
        wq = wq.reshape(features, lanes)
        smalls = smalls.reshape(n, -1).astype(F32)
        vec = smalls[:, : 6 * rows].reshape(n, 6, rows).transpose(1, 0, 2).reshape(6, features)
        key_full = smalls[:, 6 * rows : 6 * rows + HEADS * ROT // n].reshape(own_heads, REPS, ROT)
        key_own = lax.dynamic_index_in_dim(key_full, r, 1, keepdims=False)
        key_shift = jnp.pad(key_own, ((0, 0), (0, head_dim - ROT))).reshape(own_width)

        def own_heads_of(v):
            return lax.dynamic_index_in_dim(
                v.reshape(own_heads, REPS, head_dim), r, 1, keepdims=False
            ).reshape(own_width)

        out_block = mix_out(lax.dynamic_slice_in_dim(w_out, r * out_rows, out_rows, 0))
        wo = gather(out_block, ids, False, put).reshape(own_width, features)
        gate_block = pick_columns(w_gate_up[:, :hidden_units], n, down_rows, r)
        up_block = pick_columns(w_gate_up[:, hidden_units:], n, down_rows, r)
        wg = gather(gate_block, ids, True, put).reshape(features, own_hidden)
        wu = gather(up_block, ids, False, put).reshape(features, own_hidden)
        down_block = lax.dynamic_slice_in_dim(w_down, r * down_rows, down_rows, 0)
        wd = gather(down_block, ids, False, put).reshape(own_hidden, features)

        meta = jnp.concatenate([block_seq, block_len]).astype(F32)
        meta = jnp.pad(meta, (0, 128 - 2 * blocks)).reshape(1, 128)
        meta = jnp.concatenate(rep_parts(jnp.broadcast_to(meta, (8, 128))), axis=0)
        meta = meta.reshape(REPS, 8, 128)[:, 0, :]
        seqs = meta[:, :blocks].astype(jnp.int32)
        lens = meta[:, blocks : 2 * blocks].astype(jnp.int32)
        index = jnp.arange(blocks, dtype=jnp.int32)
        same = seqs[:, None, :] == seqs[:, :, None]
        earlier = jnp.sum(
            jnp.where((index[None, :] < index[:, None]) & same, 1, 0), axis=2
        ).astype(jnp.int32)
        offset = jnp.arange(block_size, dtype=jnp.int32)
        seq_slot = jnp.broadcast_to(seqs[:, :, None], (REPS, blocks, block_size)).reshape(REPS, slots)
        valid = (offset[None, None, :] < lens[:, :, None]).reshape(REPS, slots)
        positions = (earlier[:, :, None] * block_size + offset[None, None, :]).reshape(all_slots)
        slot_index = jnp.arange(slots, dtype=jnp.int32)
        allowed = (seq_slot[:, None, :] == seq_slot[:, :, None]) & (
            slot_index[None, :] <= slot_index[:, None]
        )[None]
        allowed = allowed & (valid[:, None, :] | (slot_index[None, :] == slot_index[:, None])[None])
        cosine, sine = turn_tables(positions)

        x_all = rep_gather(tokens)
        own_valid = (offset[None, :] < block_len[:, None]).reshape(-1)
        grad_output = cotangent.astype(F32) * own_valid[:, None].astype(F32)
        dyl = rep_gather(grad_output.astype(BF16))

        tokens_f = tokens.astype(F32)
        normal_one, inv_one = normalize(tokens_f)
        normal_all, _ = normalize(x_all.astype(F32))
        a1 = (normal_all * vec[0] + vec[1]).astype(BF16)
        projected = dot(a1, wq)
        head_shape = (all_slots, own_heads, head_dim)
        group_shape = (REPS, slots, own_heads, head_dim)
        q = rotate((projected[:, :own_width] + own_heads_of(vec[4])).reshape(head_shape), cosine, sine)
        k = rotate((projected[:, own_width : 2 * own_width] + key_shift).reshape(head_shape), cosine, sine)
        v = projected[:, 2 * own_width :] + own_heads_of(vec[5])
        q = q.astype(BF16).reshape(group_shape)
        k = k.astype(BF16).reshape(group_shape)
        v = v.astype(BF16).reshape(group_shape)
        scores = jnp.einsum("gshd,gthd->ghst", q, k, preferred_element_type=F32) * scale
        scores = jnp.where(allowed[:, None], scores, -1e30)
        exponent = jnp.exp(scores - jnp.max(scores, axis=-1, keepdims=True))
        probs = exponent / jnp.sum(exponent, axis=-1, keepdims=True)
        probs_low = probs.astype(BF16)
        attn = jnp.einsum("ghst,gthd->gshd", probs_low, v, preferred_element_type=F32)
        attn = attn.reshape(all_slots, own_width).astype(BF16)
        resid = tokens_f + rep_reduce(attn, lambda a: dot(a, wo), slots)
        normal_two, inv_two = normalize(resid)
        a2 = rep_gather((normal_two * vec[2] + vec[3]).astype(BF16))
        gate = dot(a2, wg)
        up = dot(a2, wu)
        sig = jax.nn.sigmoid(gate)
        hidden = (gate * sig * up).astype(BF16)

        def blocks_of(a):
            return a.reshape(all_slots, n, -1).transpose(1, 0, 2)

        hidden_b = blocks_of(hidden)
        grad_down = reduce(lambda i: dot_lt(hidden_b[i], dyl), ids, False)
        activations = (resid + rep_reduce(hidden, lambda a: dot(a, wd), slots)).astype(BF16)
        grad_hidden = dot_rt(dyl, wd)
        grad_gate = (grad_hidden * up * sig * (1.0 + gate * (1.0 - sig))).astype(BF16)
        grad_up = (grad_hidden * gate * sig).astype(BF16)
        a2_b = blocks_of(a2)
        grad_wg = reduce(lambda i: dot_lt(a2_b[i], grad_gate), ids, True)
        grad_wu = reduce(lambda i: dot_lt(a2_b[i], grad_up), ids, False)
        grad_gu = jnp.concatenate([grad_gate, grad_up], axis=1)
        wgu = jnp.concatenate([wg, wu], axis=1)
        grad_a2 = rep_reduce(grad_gu, lambda a: dot_rt(a, wgu), slots)
        grad_resid = grad_output + norm_back(grad_a2 * vec[2], normal_two, inv_two)
        drl = rep_gather(grad_resid.astype(BF16))
        attn_b = blocks_of(attn)
        grad_wo = reduce(lambda i: dot_lt(attn_b[i], drl), ids, False)
        d_attn = dot_rt(drl, wo).astype(BF16).reshape(group_shape)
        grad_v = jnp.einsum("ghst,gshd->gthd", probs_low, d_attn, preferred_element_type=F32)
        grad_p = jnp.einsum("gshd,gthd->ghst", d_attn, v, preferred_element_type=F32)
        delta = jnp.sum(grad_p * probs, axis=-1, keepdims=True)
        grad_s = (probs * (grad_p - delta)).astype(BF16)
        grad_q = jnp.einsum("ghst,gthd->gshd", grad_s, k, preferred_element_type=F32) * scale
        grad_k = jnp.einsum("ghst,gshd->gthd", grad_s, q, preferred_element_type=F32) * scale
        grad_q = rotate(grad_q.reshape(head_shape), cosine, -sine)
        grad_k = rotate(grad_k.reshape(head_shape), cosine, -sine)
        grad_v = grad_v.reshape(head_shape)
        key_sum = jnp.sum(grad_k[:, :, :ROT], axis=0)
        d_qkv = jnp.concatenate(
            [g.reshape(all_slots, own_width) for g in (grad_q, grad_k, grad_v)], axis=1
        ).astype(BF16)
        a1_b = blocks_of(a1)
        grad_wq = reduce(lambda i: dot_lt(a1_b[i], d_qkv), ids, True)
        grad_a1 = rep_reduce(d_qkv, lambda a: dot_rt(a, wq), slots)
        grad_input = (grad_resid + norm_back(grad_a1 * vec[0], normal_one, inv_one)).astype(BF16)

        def spread(sums):
            zero = jnp.zeros((own_heads, REPS, sums.shape[1]), F32)
            return lax.dynamic_update_index_in_dim(zero, sums, r, 1)

        vec_sums = jnp.stack(
            [
                jnp.sum(grad_a1 * normal_one, axis=0),
                jnp.sum(grad_a1, axis=0),
                jnp.sum(grad_a2 * normal_two, axis=0),
                jnp.sum(grad_a2, axis=0),
                spread(jnp.sum(grad_q, axis=0)).reshape(features),
                spread(jnp.sum(grad_v, axis=0)).reshape(features),
            ],
            axis=0,
        )
        key_rows = HEADS * ROT // n
        packed = jnp.concatenate(
            [
                vec_sums.reshape(6, n, rows).transpose(1, 0, 2).reshape(n, 6 * rows),
                spread(key_sum).reshape(n, key_rows),
            ],
            axis=1,
        )
        width = -(-packed.shape[1] // 1024) * 1024
        packed = jnp.pad(packed, ((0, 0), (0, width - packed.shape[1]))).reshape(n, width // 128, 128)
        packed = reduce(lambda i: packed[i], ids, False, F32)
        packed = packed + core_swap(packed)
        packed = (packed + y_swap(packed)).reshape(-1)
        out_vectors = packed[: 6 * rows].reshape(6, rows).T
        out_key = packed[6 * rows : 6 * rows + key_rows].reshape(key_rows, 1)

        def everywhere(g):
            return by_rep(rep_parts(g.astype(BF16)), y, core)

        out_down = jnp.concatenate(everywhere(grad_down), axis=0).astype(F32)
        out_gate_up = jnp.concatenate(
            [weave(everywhere(g), n, down_rows) for g in (grad_wg, grad_wu)], axis=1
        )
        out_qkv = weave(everywhere(grad_wq), 3 * own_heads, head_dim)
        out_out = jnp.concatenate(everywhere(mix_out(grad_wo.astype(BF16))), axis=0).astype(F32)
        return activations, grad_input, out_vectors, out_key, out_qkv, out_out, out_gate_up, out_down

    tok, row = P(BOTH, None), P("shard", None)
    return jax.shard_map(
        on_device,
        mesh=mesh,
        in_specs=(tok, tok, P(BOTH), P(BOTH)) + (row,) * 6,
        out_specs=(tok, tok) + (row,) * 6,
        check_vma=False,
    )
```

```python
import functools
import math

import jax
import jax.numpy as jnp
from jax import lax
from jax.experimental import pallas as pl
from jax.experimental.pallas import tpu as pltpu
from jax.sharding import PartitionSpec as P

HEADS = 32
ROT = 16
REPS = 4
BOTH = ("rep", "shard")
DEPTH = 2
F32 = jnp.float32
BF16 = jnp.bfloat16


def dot(a, b):
    return jnp.dot(a, b, preferred_element_type=F32)


def dot_rt(a, b):
    return lax.dot_general(a, b, (((1,), (1,)), ((), ())), preferred_element_type=F32)


def dot_lt(a, b):
    return lax.dot_general(a, b, (((0,), (0,)), ((), ())), preferred_element_type=F32)


def turn_tables(positions):
    half = ROT // 2
    frequencies = jnp.exp(
        jnp.arange(half, dtype=F32) * (-2.0 * math.log(10000.0) / ROT)
    )
    angles = positions.astype(F32)[:, None] * frequencies[None, :]
    return jnp.cos(angles)[:, None, :], jnp.sin(angles)[:, None, :]


def rotate(values, cosine, sine):
    half = ROT // 2
    low, high, rest = values[..., :half], values[..., half:ROT], values[..., ROT:]
    return jnp.concatenate(
        [low * cosine - high * sine, high * cosine + low * sine, rest], axis=-1
    )


def normalize(values):
    center = values - jnp.mean(values, axis=1, keepdims=True)
    inv_std = lax.rsqrt(jnp.mean(center * center, axis=1, keepdims=True) + 1e-05)
    return center * inv_std, inv_std


def norm_back(grad_norm, normal, inv_std):
    mean_grad = jnp.mean(grad_norm, axis=1, keepdims=True)
    mean_cross = jnp.mean(grad_norm * normal, axis=1, keepdims=True)
    return inv_std * (grad_norm - mean_grad - normal * mean_cross)


MESH = pl.DeviceIdType.MESH
NAMES = ("q", "o", "g", "u", "d")
LONG_UP = {"q": True, "o": False, "g": True, "u": False, "d": False}
VMEM_LIMIT = 64 * 1024 * 1024 - 64 * 1024


class Place:
    def __init__(self, n):
        self.n, self.half = n, n // 2
        self.r, self.s = lax.axis_index("rep"), lax.axis_index("shard")
        self.core = self.r + 1 - 2 * (self.r % 2)
        self.across = (self.r + 2) % REPS
        odd = self.s % 2
        self.spot = (1 - odd) * (self.s // 2) + odd * (n - 1 - self.s // 2)
        self.ids = {k: self.shard_at(k) for k in range(-self.half, self.half + 1)}
        self.ring = (self.ids[1], self.ids[-1])

    def shard_at(self, k):
        q = (self.spot + k + self.n) % self.n
        back = q // self.half
        return (1 - back) * 2 * q + back * (2 * self.n - 1 - 2 * q)

    def greet(self):
        barrier = pltpu.get_barrier_semaphore()
        for who in (
            (self.core, self.s),
            (self.across, self.s),
            (self.r, self.ring[0]),
            (self.r, self.ring[1]),
        ):
            pl.semaphore_signal(barrier, inc=1, device_id=who, device_id_type=MESH)
        pl.semaphore_wait(barrier, 4)


class RepLinks:
    def __init__(self, place, send, recv):
        self.place, self.send, self.recv, self.sent = place, send, recv, []

    def copy(self, i, src, dst, who):
        return pltpu.make_async_remote_copy(
            src_ref=src,
            dst_ref=dst,
            send_sem=self.send.at[i],
            recv_sem=self.recv.at[i],
            device_id=(who, self.place.s),
            device_id_type=MESH,
        )

    def start(self, i, src, dst, who):
        c = self.copy(i, src, dst, who)
        c.start()
        self.sent.append(c)
        return c

    def gather_start(self, i, own, slots):
        a = self.start(i, own, slots.at[1], self.place.across)
        b = self.start(i + 1, own, slots.at[2], self.place.core)
        return a, b

    def gather_pass(self, i, slots, copies):
        copies[0].wait_recv()
        return copies[1], self.start(i + 2, slots.at[1], slots.at[3], self.place.core)

    def finish(self):
        for c in self.sent:
            c.wait_send()


def layer_rows(x, gain, shift):
    center = x - jnp.mean(x, axis=1, keepdims=True)
    inv = lax.rsqrt(jnp.mean(center * center, axis=1, keepdims=True) + 1e-05)
    return center * inv * gain + shift


def first_half(shape):
    return lax.broadcasted_iota(jnp.int32, shape, 1) < 64


def forward_kernel(
    n,
    q_blk, o_blk, g_blk, u_blk, d_blk, tok, dyl, meta, tables,
    q_land, o_land, g_land, u_land, d_land, a1_out, q_out, k_out, v_out, p_out, attn_out,
    resid_out, a2_out, gate_out, up_out, hid_out, dyl_out,
    wq, wo, wg, wu, xs, qs, ks, vs, ps, attn, acc, csend, crecv, ysend, yrecv, resid, a2s,
    gates, ups, hid, metas, tabs, mask, small, vecs,
    ring_send, ring_recv, load_sem, rep_send, rep_recv, out_sem,
):
    here = Place(n)
    half = here.half
    blocks = dict(zip(NAMES, (q_blk, o_blk, g_blk, u_blk, d_blk)))
    lands = dict(zip(NAMES, (q_land, o_land, g_land, u_land, d_land)))
    into = {"q": wq, "o": wo, "g": wg, "u": wu}
    slots, width = tok.shape
    rows = {name: blocks[name].shape[0] for name in NAMES}
    rows["q"] = width // n
    reach = {
        (name, d): half if LONG_UP[name] == (d == 0) else half - 1 for name in NAMES for d in (0, 1)
    }

    def message(name, d, k):
        i = here.ids[(1 - k) if d == 0 else (k - 1)]
        a = NAMES.index(name)
        src = blocks[name] if k == 1 else lands[name].at[i]
        return pltpu.make_async_remote_copy(
            src_ref=src,
            dst_ref=lands[name].at[i],
            send_sem=ring_send.at[a, d, k - 1],
            recv_sem=ring_recv.at[a, d, k - 1],
            device_id=(here.r, here.ring[d]),
            device_id_type=MESH,
        )

    def load(name, k):
        i = here.ids[k]
        a = NAMES.index(name)
        src = blocks[name] if k == 0 else lands[name].at[i]
        return pltpu.make_async_copy(
            src.at[pl.ds(0, rows[name])],
            into[name].at[pl.ds(pl.multiple_of(i * rows[name], 16), rows[name])],
            load_sem.at[a, k + half],
        )

    def load_small(k):
        src = q_blk if k == 0 else q_land.at[here.ids[k]]
        return pltpu.make_async_copy(
            src.at[pl.ds(rows["q"], 16), pl.ds(0, rows["q"])],
            small.at[here.ids[k]],
            load_sem.at[5, k + half],
        )

    def keep_own(name):
        return pltpu.make_async_copy(
            blocks[name], lands[name].at[here.s], load_sem.at[6, NAMES.index(name)]
        )

    def begin(name):
        for d in (0, 1):
            message(name, d, 1).start()
        keep_own(name).start()
        if name in into:
            load(name, 0).start()
        if name == "q":
            load_small(0).start()

    def serve(name, k):
        for d in (0, 1):
            if k <= reach[name, d]:
                message(name, d, k).wait_recv()
                if k < reach[name, d]:
                    message(name, d, k + 1).start()
                if name in into:
                    load(name, -k if d == 0 else k).start()
                if name == "q":
                    load_small(-k if d == 0 else k).start()

    def came(name):
        found = [0]
        for k in range(1, half + 1):
            found += [-k] * (k <= reach[name, 0]) + [k] * (k <= reach[name, 1])
        return found

    def loaded(name):
        for k in came(name):
            load(name, k).wait()
            if name == "q":
                load_small(k).wait()

    outs = []

    def save(src, dst):
        c = pltpu.make_async_copy(src, dst, out_sem.at[len(outs)])
        c.start()
        outs.append(c)

    here.greet()
    begin("q")
    begin("o")
    rep = RepLinks(here, rep_send, rep_recv)
    own_x = pltpu.make_async_copy(tok, xs.at[pl.ds(0, slots)], load_sem.at[7, 0])
    own_x.start()
    own_m = pltpu.make_async_copy(meta, metas.at[0], load_sem.at[7, 1])
    own_m.start()
    own_d = pltpu.make_async_copy(dyl, dyl_out.at[0], load_sem.at[7, 2])
    own_d.start()

    class XSlots:
        class at:
            def __class_getitem__(cls, g):
                return xs.at[pl.ds(g * slots, slots)]

    m_sent = rep.gather_start(0, meta, metas)
    x_sent = rep.gather_start(3, tok, XSlots)
    m_end = rep.gather_pass(0, metas, m_sent)
    serve("o", 1)
    x_end = rep.gather_pass(3, XSlots, x_sent)
    serve("q", 1)
    serve("o", 2)
    d_sent = rep.gather_start(6, dyl, dyl_out)
    serve("q", 2)
    serve("o", 3)
    serve("q", 3)
    begin("g")
    serve("o", 4)
    begin("u")
    for c in m_end + x_end:
        c.wait_recv()
    x_end[1].wait_send()
    rep.sent = [c for c in rep.sent if c is not x_end[1]]
    own_x.wait()
    own_m.wait()
    serve("q", 4)
    loaded("q")
    for s in range(n):
        vecs[0:8, s * rows["q"] : (s + 1) * rows["q"]] = small[s, 0:8, :].astype(F32)
    d_end = rep.gather_pass(6, dyl_out, d_sent)

    gain_one, shift_one = vecs[0:1, :], vecs[1:2, :]

    @pl.loop(0, REPS * slots // 16)
    def _(i):
        at = pl.ds(pl.multiple_of(i * 16, 16), 16)
        xs[at, :] = layer_rows(xs[at, :].astype(F32), gain_one, shift_one).astype(BF16)

    serve("g", 1)
    serve("u", 1)
    save(xs, a1_out)

    own_width = wq.shape[1] // 3
    pairs = own_width // 128

    def lane_bias(row, t):
        w = rows["q"]
        a = vecs[row : row + 1, 2 * t * w : 2 * t * w + 128]
        return a + vecs[row : row + 1, (2 * t + 1) * w : (2 * t + 1) * w + 128]

    block = slots // 2
    line = lax.broadcasted_iota(jnp.int32, (slots, slots), 0)
    column = lax.broadcasted_iota(jnp.int32, (slots, slots), 1)

    def attend(g):
        here_rows = pl.ds(pl.multiple_of(g * slots, slots), slots)
        acc[...] = dot(xs[here_rows, :], wq[...])
        valid = metas[g, 0:1, :]
        same = metas[g, 1:2, :]
        for j in range(3):
            tabs[j, :block, :] = tables[j, :block, :]
            tabs[j, block:, :] = jnp.where(
                same[:, :128] > 0.5, tables[j, block:, :], tables[j, :block, :]
            )
        apart = (line >= block) & (column < block) & (same < 0.5)
        open_ = (column <= line) & jnp.logical_not(apart) & ((valid > 0.5) | (line == column))
        mask[...] = jnp.where(open_, 0.0, -1e30)
        for t in range(3 * pairs):
            part, tt = t // pairs, t % pairs
            tile = acc[:, t * 128 : (t + 1) * 128] + lane_bias((4, 6, 5)[part], tt)
            if part < 2:
                tile = (
                    tile * tabs[0]
                    + pltpu.roll(tile, 120, 1) * tabs[1]
                    + pltpu.roll(tile, 8, 1) * tabs[2]
                )
            (qs, ks, vs)[part][g, tt] = tile.astype(BF16)
        low = first_half((slots, 128))
        low_low = first_half((1, 128)).astype(F32).astype(BF16)
        high_low = (1.0 - first_half((1, 128)).astype(F32)).astype(BF16)
        for t in range(pairs):
            qt, kt, vt = qs[g, t], ks[g, t], vs[g, t]
            mixed = []
            for h in (0, 1):
                mine = low_low if h == 0 else high_low
                sc = dot_rt(qt * mine, kt) * (1.0 / 8.0) + mask[...]
                e = jnp.exp(sc - jnp.max(sc, axis=1, keepdims=True))
                p = (e / jnp.sum(e, axis=1, keepdims=True)).astype(BF16)
                ps[g, 2 * t + h] = p
                mixed.append(dot(p, vt))
            attn[here_rows, t * 128 : (t + 1) * 128] = jnp.where(low, mixed[0], mixed[1]).astype(BF16)

    @pl.loop(2, 4)
    def _(g):
        attend(g)

    loaded("o")
    for g in (0, 1):
        csend[g] = dot(attn[(g + 2) * slots : (g + 3) * slots, :], wo[...]).astype(BF16)
    rs_core = rep.start(9, csend, crecv, here.core)
    serve("g", 2)
    serve("u", 2)

    @pl.loop(0, 2)
    def _(g):
        attend(g)

    for c in d_end:
        c.wait_recv()
    rs_core.wait_recv()
    ysend[...] = (dot(attn[slots : 2 * slots, :], wo[...]) + crecv[1].astype(F32)).astype(BF16)
    rs_y = rep.start(10, ysend, yrecv, here.across)
    save(qs, q_out)
    save(ks, k_out)
    save(vs, v_out)
    save(ps, p_out)
    save(attn, attn_out)
    resid[...] = dot(attn[0:slots, :], wo[...]) + crecv[0].astype(F32)
    serve("g", 3)
    serve("u", 3)
    begin("d")
    rs_y.wait_recv()
    own_again = pltpu.make_async_copy(tok, crecv.at[0], load_sem.at[7, 3])
    own_again.start()
    own_again.wait()
    gain_two, shift_two = vecs[2:3, :], vecs[3:4, :]

    @pl.loop(0, slots // 16)
    def _(i):
        at = pl.ds(pl.multiple_of(i * 16, 16), 16)
        x = resid[at, :] + yrecv[at, :].astype(F32) + crecv[0, at, :].astype(F32)
        resid[at, :] = x
        a2s[0, at, :] = layer_rows(x, gain_two, shift_two).astype(BF16)

    a_sent = rep.gather_start(11, a2s.at[0], a2s)
    save(resid, resid_out)
    serve("g", 4)
    serve("u", 4)
    serve("d", 1)
    a_end = rep.gather_pass(11, a2s, a_sent)
    for c in a_end:
        c.wait_recv()
    loaded("g")
    loaded("u")
    save(a2s, a2_out)

    def feed(g):
        at = pl.ds(pl.multiple_of(g * slots, slots), slots)
        gate = dot(a2s[g], wg[...])
        gates[at, :] = gate.astype(BF16)
        up = dot(a2s[g], wu[...])
        ups[at, :] = up.astype(BF16)
        act = gate * jax.nn.sigmoid(gate) * up
        for j in range(act.shape[1] // 128):
            hid[j * 128 : (j + 1) * 128, at] = act[:, j * 128 : (j + 1) * 128].T.astype(BF16)

    @pl.loop(0, 2)
    def _(g):
        feed(g)

    serve("d", 2)

    @pl.loop(2, 4)
    def _(g):
        feed(g)

    save(gates, gate_out)
    save(ups, up_out)
    save(hid, hid_out)
    serve("d", 3)
    serve("d", 4)
    own_d.wait()
    for name in NAMES:
        keep_own(name).wait()
        for d in (0, 1):
            for k in range(1, reach[name, d] + 1):
                message(name, d, k).wait_send()
    rep.finish()
    for c in outs:
        c.wait()


def forward_call(n, blocks, tok, dyl, meta, tables):
    slots, width = tok.shape
    q, o, g, u, d = blocks
    lanes, units = q.shape[1], g.shape[1]
    own_width = lanes // 3
    all_slots = REPS * slots
    pairs = own_width // 128
    half = n // 2
    S = jax.ShapeDtypeStruct
    heads = (REPS, pairs, slots, 128)
    out_shape = [S((n,) + b.shape, BF16) for b in blocks] + [
        S((all_slots, width), BF16),
        S(heads, BF16),
        S(heads, BF16),
        S(heads, BF16),
        S((REPS, 2 * pairs, slots, slots), BF16),
        S((all_slots, own_width), BF16),
        S((slots, width), F32),
        S((REPS, slots, width), BF16),
        S((all_slots, units), BF16),
        S((all_slots, units), BF16),
        S((units, all_slots), BF16),
        S((REPS, slots, width), BF16),
    ]
    V = pltpu.VMEM
    scratch = [
        V((width, lanes), BF16),
        V((own_width, width), BF16),
        V((width, units), BF16),
        V((width, units), BF16),
        V((all_slots, width), BF16),
        V(heads, BF16),
        V(heads, BF16),
        V(heads, BF16),
        V((REPS, 2 * pairs, slots, slots), BF16),
        V((all_slots, own_width), BF16),
        V((slots, lanes), F32),
        V((2, slots, width), BF16),
        V((2, slots, width), BF16),
        V((slots, width), BF16),
        V((slots, width), BF16),
        V((slots, width), F32),
        V((REPS, slots, width), BF16),
        V((all_slots, units), BF16),
        V((all_slots, units), BF16),
        V((units, all_slots), BF16),
        V((REPS, 8, slots), F32),
        V((3, slots, 128), F32),
        V((slots, slots), F32),
        V((n, 16, width // n), BF16),
        V((8, width), F32),
        pltpu.SemaphoreType.DMA((5, 2, half)),
        pltpu.SemaphoreType.DMA((5, 2, half)),
        pltpu.SemaphoreType.DMA((8, 2 * half + 1)),
        pltpu.SemaphoreType.DMA((14,)),
        pltpu.SemaphoreType.DMA((14,)),
        pltpu.SemaphoreType.DMA((12,)),
    ]
    anywhere = pl.BlockSpec(memory_space=pltpu.HBM)
    return pl.pallas_call(
        functools.partial(forward_kernel, n),
        out_shape=out_shape,
        in_specs=[anywhere] * 8 + [pl.BlockSpec(memory_space=pltpu.VMEM)],
        out_specs=[anywhere] * len(out_shape),
        scratch_shapes=scratch,
        compiler_params=pltpu.CompilerParams(
            collective_id=1, has_side_effects=True, vmem_limit_bytes=VMEM_LIMIT
        ),
    )(*blocks, tok, dyl, meta, tables)


def core_swap(x):
    return lax.ppermute(x, "rep", [(0, 1), (1, 0), (2, 3), (3, 2)])


def y_swap(x):
    return lax.ppermute(x, "rep", [(0, 2), (1, 3), (2, 0), (3, 1)])


def rep_parts(x):
    across = y_swap(x)
    return [x, across, core_swap(x), core_swap(across)]


def rep_gather(x):
    return jnp.concatenate(rep_parts(x), axis=0)


def rep_reduce(a, w_dot, slots):
    far = core_swap(w_dot(a[2 * slots :]).astype(BF16))
    near = w_dot(a[: 2 * slots]) + far.astype(F32)
    return near[:slots] + y_swap(near[slots:].astype(BF16)).astype(F32)


def solution(mesh):
    n = mesh.shape["shard"]
    half_ring = n // 2
    order = list(range(0, n, 2)) + list(range(n - 1, 0, -2))
    place = [order.index(s) for s in range(n)]
    up_ring = [(order[i], order[(i + 1) % n]) for i in range(n)]
    down_ring = [(b, a) for a, b in up_ring]

    def hop(x, ring, sent):
        if len(sent) >= DEPTH:
            x, _ = lax.optimization_barrier((x, sent[-DEPTH]))
        x = lax.ppermute(x, "shard", ring)
        sent.append(x)
        return x

    def ring_ids():
        spot = jnp.array(place, jnp.int32)[lax.axis_index("shard")]
        table = jnp.array(order, jnp.int32)
        return {k: table[(spot + k) % n] for k in range(-half_ring, half_ring + 1)}

    def gather(x, ids, forward_extra, places, line):
        bufs = places(None, x, ids[0])
        up = down = x
        for k in range(1, half_ring + 1):
            go_up = k < half_ring or forward_extra
            go_down = k < half_ring or not forward_extra
            if go_up:
                up = hop(up, up_ring, line[0])
            if go_down:
                down = hop(down, down_ring, line[1])
            if go_up:
                bufs = places(bufs, up, ids[-k])
            if go_down:
                bufs = places(bufs, down, ids[k])
            yield
        return bufs

    def put(bufs, block, at):
        if bufs is None:
            bufs = jnp.zeros((n,) + block.shape, block.dtype)
        return lax.dynamic_update_index_in_dim(bufs, block, at, 0)

    def reduce(term, ids, forward_extra, line, kind=BF16):
        acc = {}
        for k in range(half_ring, 0, -1):
            for side, (ring, sign, extra) in enumerate(
                ((up_ring, 1, forward_extra), (down_ring, -1, not forward_extra))
            ):
                if k == half_ring and not extra:
                    continue
                part = term(ids[sign * k])
                if side in acc:
                    part = part + acc[side].astype(F32)
                acc[side] = hop(part.astype(kind), ring, line[side])
            yield
        return term(ids[0]) + acc[0].astype(F32) + acc[1].astype(F32)

    def run(chains, turns):
        done = {}
        for name in turns:
            for _ in range(n // 8):
                if name in done:
                    continue
                try:
                    next(chains[name])
                except StopIteration as stop:
                    done[name] = stop.value
        for name, chain in chains.items():
            while name not in done:
                try:
                    next(chain)
                except StopIteration as stop:
                    done[name] = stop.value
        return done

    def pick_columns(w, groups, width, r):
        chosen = [
            lax.select_n(
                r,
                *[
                    w[:, (g * REPS + q) * width : (g * REPS + q + 1) * width]
                    for q in range(REPS)
                ],
            )
            for g in range(groups)
        ]
        return jnp.concatenate(chosen, axis=1)

    def by_rep(parts, y, core):
        own, across, beside, both = parts
        low0 = lax.select(core == 0, own, beside)
        low1 = lax.select(core == 0, beside, own)
        high0 = lax.select(core == 0, across, both)
        high1 = lax.select(core == 0, both, across)
        return [
            lax.select(y == 0, low0, high0),
            lax.select(y == 0, low1, high1),
            lax.select(y == 0, high0, low0),
            lax.select(y == 0, high1, low1),
        ]

    def weave(parts, groups, width):
        pieces = [
            parts[q][:, g * width : (g + 1) * width]
            for g in range(groups)
            for q in range(REPS)
        ]
        return jnp.concatenate(pieces, axis=1).astype(F32)

    def on_device(
        tokens, cotangent, block_seq, block_len, vectors, key_bias, w_qkv, w_out, w_gate_up, w_down
    ):
        slots, features = tokens.shape
        blocks = block_seq.shape[0]
        block_size = slots // blocks
        head_dim = features // HEADS
        own_heads = HEADS // REPS
        own_width = own_heads * head_dim
        all_slots = REPS * slots
        scale = 1.0 / math.sqrt(head_dim)
        rows = features // n
        hidden_units = w_gate_up.shape[1] // 2
        own_hidden = hidden_units // REPS
        down_rows = w_down.shape[0] // REPS
        out_rows = w_out.shape[0] // REPS
        regroup = out_rows < head_dim
        r = lax.axis_index("rep")
        y, core = r // 2, r % 2
        ids = ring_ids()

        def mix_out(x):
            if not regroup:
                return x
            pairs = [
                (k * n + 4 * j + q, q * n + 4 * j + k)
                for k in range(REPS)
                for j in range(n // 4)
                for q in range(REPS)
            ]
            return lax.ppermute(x, BOTH, pairs)

        fast = blocks == 2 and down_rows % 16 == 0 and out_rows == head_dim and rows % 128 == 0
        own_valid = (
            jnp.arange(block_size, dtype=jnp.int32)[None, :] < block_len[:, None]
        ).reshape(-1)
        grad_output = cotangent.astype(F32) * own_valid[:, None].astype(F32)
        dyl_own = grad_output.astype(BF16)
        if fast:
            lanes = 3 * own_width
            side = (lax.axis_index("shard") % 2) * head_dim
            small = jnp.zeros((16, lanes), BF16)
            small = lax.dynamic_update_slice(small, vectors[:, :4].T, (0, 0))
            mine = lax.dynamic_slice_in_dim(vectors, r * head_dim, head_dim, 0)
            small = lax.dynamic_update_slice(small, mine[:, 4:6].T, (4, side))
            mine = lax.dynamic_slice_in_dim(key_bias, r * ROT, ROT, 0)
            small = lax.dynamic_update_slice(small, mine.T, (6, side))
            q_blk = jnp.concatenate([pick_columns(w_qkv, 3 * own_heads, head_dim, r), small], axis=0)
            o_blk = lax.dynamic_slice_in_dim(w_out, r * out_rows, out_rows, 0)
            g_blk = pick_columns(w_gate_up[:, :hidden_units], n, down_rows, r)
            u_blk = pick_columns(w_gate_up[:, hidden_units:], n, down_rows, r)
            d_blk = lax.dynamic_slice_in_dim(w_down, r * down_rows, down_rows, 0)
            together = jnp.broadcast_to(block_seq[0] == block_seq[1], (slots,))
            meta = jnp.stack([own_valid, together] + [together] * 6).astype(F32)
            cosine, sine = turn_tables(jnp.arange(slots, dtype=jnp.int32))
            cosine, sine = cosine[:, 0], sine[:, 0]
            rest = jnp.ones((slots, head_dim - ROT), F32)
            none = jnp.zeros((slots, ROT // 2), F32)
            tables = jnp.stack(
                [
                    jnp.concatenate([cosine, cosine, rest] * 2, axis=1),
                    jnp.concatenate([-sine, none, 0 * rest] * 2, axis=1),
                    jnp.concatenate([none, sine, 0 * rest] * 2, axis=1),
                ]
            )
            out = forward_call(n, (q_blk, o_blk, g_blk, u_blk, d_blk), tokens, dyl_own, meta, tables)
            q_land, o_land, g_land, u_land, d_land = out[:5]
            a1, qs, ks, vs, ps, attn, resid, a2, gate, up, hid, dyl_all = out[5:]
            wq = q_land[:, :rows].reshape(features, lanes)
            wo = o_land.reshape(own_width, features)
            wg = g_land.reshape(features, own_hidden)
            wu = u_land.reshape(features, own_hidden)
            wd = d_land.reshape(own_hidden, features)
            smalls = q_land[:, rows:].astype(F32)
            vec = smalls[:, :4, :rows].transpose(1, 0, 2).reshape(4, features)
            group_shape = (REPS, slots, own_heads, head_dim)
            head_shape = (all_slots, own_heads, head_dim)
            q, k, v = [t.transpose(0, 2, 1, 3).reshape(group_shape) for t in (qs, ks, vs)]
            probs_low = ps
            probs = ps.astype(F32)
            dyl = dyl_all.reshape(all_slots, features)
            a2 = a2.reshape(all_slots, features)
            tokens_f = tokens.astype(F32)
            normal_one, inv_one = normalize(tokens_f)
            normal_two, inv_two = normalize(resid)
            gate, up = gate.astype(F32), up.astype(F32)
            sig = jax.nn.sigmoid(gate)
            hidden = hid.T
            meta_all = rep_parts(meta)
            positions = jnp.concatenate([
                jnp.concatenate([jnp.arange(128), jnp.where(m[1, 0] > 0.5, 128, 0) + jnp.arange(128)]) for m in meta_all
            ])
            cosine, sine = turn_tables(positions)
        else:
            small = jnp.concatenate([vectors.T.reshape(-1), key_bias.reshape(-1)])
            lanes = 3 * own_width
            small_rows = -(-small.size // lanes)
            small_rows = -(-small_rows // 16) * 16
            small = jnp.pad(small, (0, small_rows * lanes - small.size)).reshape(small_rows, lanes)
            qkv_block = jnp.concatenate([pick_columns(w_qkv, 3 * own_heads, head_dim, r), small], axis=0)

            def put_qkv(bufs, block, at):
                a, b = (None, None) if bufs is None else bufs
                return put(a, block[:rows], at), put(b, block[rows:], at)

            out_block = mix_out(lax.dynamic_slice_in_dim(w_out, r * out_rows, out_rows, 0))
            gate_block = pick_columns(w_gate_up[:, :hidden_units], n, down_rows, r)
            up_block = pick_columns(w_gate_up[:, hidden_units:], n, down_rows, r)
            down_block = lax.dynamic_slice_in_dim(w_down, r * down_rows, down_rows, 0)
            line = ([], [])
            got = run(
                {
                    "q": gather(qkv_block, ids, True, put_qkv, line),
                    "o": gather(out_block, ids, False, put, line),
                    "g": gather(gate_block, ids, True, put, line),
                    "u": gather(up_block, ids, False, put, line),
                    "d": gather(down_block, ids, False, put, line),
                },
                "qoqoqoqoguguguguddddd",
            )
            wq, smalls = got["q"]
            wq = wq.reshape(features, lanes)
            smalls = smalls.reshape(n, -1).astype(F32)
            vec = smalls[:, : 6 * rows].reshape(n, 6, rows).transpose(1, 0, 2).reshape(6, features)
            key_full = smalls[:, 6 * rows : 6 * rows + HEADS * ROT // n].reshape(own_heads, REPS, ROT)
            key_own = lax.dynamic_index_in_dim(key_full, r, 1, keepdims=False)
            key_shift = jnp.pad(key_own, ((0, 0), (0, head_dim - ROT))).reshape(own_width)

            def own_heads_of(v):
                return lax.dynamic_index_in_dim(
                    v.reshape(own_heads, REPS, head_dim), r, 1, keepdims=False
                ).reshape(own_width)

            wo = got["o"].reshape(own_width, features)
            wg = got["g"].reshape(features, own_hidden)
            wu = got["u"].reshape(features, own_hidden)
            wd = got["d"].reshape(own_hidden, features)

            meta = jnp.concatenate([block_seq, block_len]).astype(F32)
            meta = jnp.pad(meta, (0, 128 - 2 * blocks)).reshape(1, 128)
            meta = jnp.concatenate(rep_parts(jnp.broadcast_to(meta, (8, 128))), axis=0)
            meta = meta.reshape(REPS, 8, 128)[:, 0, :]
            seqs = meta[:, :blocks].astype(jnp.int32)
            lens = meta[:, blocks : 2 * blocks].astype(jnp.int32)
            index = jnp.arange(blocks, dtype=jnp.int32)
            same = seqs[:, None, :] == seqs[:, :, None]
            earlier = jnp.sum(
                jnp.where((index[None, :] < index[:, None]) & same, 1, 0), axis=2
            ).astype(jnp.int32)
            offset = jnp.arange(block_size, dtype=jnp.int32)
            seq_slot = jnp.broadcast_to(seqs[:, :, None], (REPS, blocks, block_size)).reshape(REPS, slots)
            valid = (offset[None, None, :] < lens[:, :, None]).reshape(REPS, slots)
            positions = (earlier[:, :, None] * block_size + offset[None, None, :]).reshape(all_slots)
            slot_index = jnp.arange(slots, dtype=jnp.int32)
            allowed = (seq_slot[:, None, :] == seq_slot[:, :, None]) & (
                slot_index[None, :] <= slot_index[:, None]
            )[None]
            allowed = allowed & (valid[:, None, :] | (slot_index[None, :] == slot_index[:, None])[None])
            cosine, sine = turn_tables(positions)

            x_all = rep_gather(tokens)
            dyl = rep_gather(dyl_own)

            tokens_f = tokens.astype(F32)
            normal_one, inv_one = normalize(tokens_f)
            normal_all, _ = normalize(x_all.astype(F32))
            a1 = (normal_all * vec[0] + vec[1]).astype(BF16)
            projected = dot(a1, wq)
            head_shape = (all_slots, own_heads, head_dim)
            group_shape = (REPS, slots, own_heads, head_dim)
            q = rotate((projected[:, :own_width] + own_heads_of(vec[4])).reshape(head_shape), cosine, sine)
            k = rotate((projected[:, own_width : 2 * own_width] + key_shift).reshape(head_shape), cosine, sine)
            v = projected[:, 2 * own_width :] + own_heads_of(vec[5])
            q = q.astype(BF16).reshape(group_shape)
            k = k.astype(BF16).reshape(group_shape)
            v = v.astype(BF16).reshape(group_shape)
            scores = jnp.einsum("gshd,gthd->ghst", q, k, preferred_element_type=F32) * scale
            scores = jnp.where(allowed[:, None], scores, -1e30)
            exponent = jnp.exp(scores - jnp.max(scores, axis=-1, keepdims=True))
            probs = exponent / jnp.sum(exponent, axis=-1, keepdims=True)
            probs_low = probs.astype(BF16)
            attn = jnp.einsum("ghst,gthd->gshd", probs_low, v, preferred_element_type=F32)
            attn = attn.reshape(all_slots, own_width).astype(BF16)
            resid = tokens_f + rep_reduce(attn, lambda a: dot(a, wo), slots)
            normal_two, inv_two = normalize(resid)
            a2 = rep_gather((normal_two * vec[2] + vec[3]).astype(BF16))
            gate = dot(a2, wg)
            up = dot(a2, wu)
            sig = jax.nn.sigmoid(gate)
            hidden = (gate * sig * up).astype(BF16)

        def blocks_of(a):
            return a.reshape(all_slots, n, -1).transpose(1, 0, 2)

        hidden_b = blocks_of(hidden)
        activations = (resid + rep_reduce(hidden, lambda a: dot(a, wd), slots)).astype(BF16)
        grad_hidden = dot_rt(dyl, wd)
        grad_gate = (grad_hidden * up * sig * (1.0 + gate * (1.0 - sig))).astype(BF16)
        grad_up = (grad_hidden * gate * sig).astype(BF16)
        a2_b = blocks_of(a2)
        grad_gu = jnp.concatenate([grad_gate, grad_up], axis=1)
        wgu = jnp.concatenate([wg, wu], axis=1)
        grad_a2 = rep_reduce(grad_gu, lambda a: dot_rt(a, wgu), slots)
        grad_resid = grad_output + norm_back(grad_a2 * vec[2], normal_two, inv_two)
        drl = rep_gather(grad_resid.astype(BF16))
        attn_b = blocks_of(attn)
        d_attn = dot_rt(drl, wo).astype(BF16).reshape(group_shape)
        grad_v = jnp.einsum("ghst,gshd->gthd", probs_low, d_attn, preferred_element_type=F32)
        grad_p = jnp.einsum("gshd,gthd->ghst", d_attn, v, preferred_element_type=F32)
        delta = jnp.sum(grad_p * probs, axis=-1, keepdims=True)
        grad_s = (probs * (grad_p - delta)).astype(BF16)
        grad_q = jnp.einsum("ghst,gthd->gshd", grad_s, k, preferred_element_type=F32) * scale
        grad_k = jnp.einsum("ghst,gshd->gthd", grad_s, q, preferred_element_type=F32) * scale
        grad_q = rotate(grad_q.reshape(head_shape), cosine, -sine)
        grad_k = rotate(grad_k.reshape(head_shape), cosine, -sine)
        grad_v = grad_v.reshape(head_shape)
        key_sum = jnp.sum(grad_k[:, :, :ROT], axis=0)
        d_qkv = jnp.concatenate(
            [g.reshape(all_slots, own_width) for g in (grad_q, grad_k, grad_v)], axis=1
        ).astype(BF16)
        a1_b = blocks_of(a1)
        grad_a1 = rep_reduce(d_qkv, lambda a: dot_rt(a, wq), slots)
        grad_input = (grad_resid + norm_back(grad_a1 * vec[0], normal_one, inv_one)).astype(BF16)

        def spread(sums):
            zero = jnp.zeros((own_heads, REPS, sums.shape[1]), F32)
            return lax.dynamic_update_index_in_dim(zero, sums, r, 1)

        vec_sums = jnp.stack(
            [
                jnp.sum(grad_a1 * normal_one, axis=0),
                jnp.sum(grad_a1, axis=0),
                jnp.sum(grad_a2 * normal_two, axis=0),
                jnp.sum(grad_a2, axis=0),
                spread(jnp.sum(grad_q, axis=0)).reshape(features),
                spread(jnp.sum(grad_v, axis=0)).reshape(features),
            ],
            axis=0,
        )
        key_rows = HEADS * ROT // n
        packed = jnp.concatenate(
            [
                vec_sums.reshape(6, n, rows).transpose(1, 0, 2).reshape(n, 6 * rows),
                spread(key_sum).reshape(n, key_rows),
            ],
            axis=1,
        )
        width = -(-packed.shape[1] // 1024) * 1024
        packed = jnp.pad(packed, ((0, 0), (0, width - packed.shape[1]))).reshape(n, width // 128, 128)
        line = ([], [])
        sums = run(
            {
                "d": reduce(lambda i: dot_lt(hidden_b[i], dyl), ids, False, line),
                "g": reduce(lambda i: dot_lt(a2_b[i], grad_gate), ids, True, line),
                "u": reduce(lambda i: dot_lt(a2_b[i], grad_up), ids, False, line),
                "q": reduce(lambda i: dot_lt(a1_b[i], d_qkv), ids, True, line),
                "o": reduce(lambda i: dot_lt(attn_b[i], drl), ids, False, line),
                "s": reduce(lambda i: packed[i], ids, True, line, F32),
            },
            "dgdgdudugugugqoqoqosoqsoss",
        )
        grad_down, grad_wg, grad_wu = sums["d"], sums["g"], sums["u"]
        grad_wq, grad_wo, packed = sums["q"], sums["o"], sums["s"]
        packed = packed + core_swap(packed)
        packed = (packed + y_swap(packed)).reshape(-1)
        out_vectors = packed[: 6 * rows].reshape(6, rows).T
        out_key = packed[6 * rows : 6 * rows + key_rows].reshape(key_rows, 1)

        def everywhere(g):
            return by_rep(rep_parts(g.astype(BF16)), y, core)

        out_down = jnp.concatenate(everywhere(grad_down), axis=0).astype(F32)
        out_gate_up = jnp.concatenate(
            [weave(everywhere(g), n, down_rows) for g in (grad_wg, grad_wu)], axis=1
        )
        out_qkv = weave(everywhere(grad_wq), 3 * own_heads, head_dim)
        out_out = jnp.concatenate(everywhere(mix_out(grad_wo.astype(BF16))), axis=0).astype(F32)
        return activations, grad_input, out_vectors, out_key, out_qkv, out_out, out_gate_up, out_down

    tok, row = P(BOTH, None), P("shard", None)
    return jax.shard_map(
        on_device,
        mesh=mesh,
        in_specs=(tok, tok, P(BOTH), P(BOTH)) + (row,) * 6,
        out_specs=(tok, tok) + (row,) * 6,
        check_vma=False,
    )
```

```python
import functools
import math

import jax
import jax.numpy as jnp
from jax import lax
from jax.experimental import pallas as pl
from jax.experimental.pallas import tpu as pltpu
from jax.sharding import PartitionSpec as P

HEADS = 32
ROT = 16
REPS = 4
BOTH = ("rep", "shard")
DEPTH = 2
F32 = jnp.float32
BF16 = jnp.bfloat16


def dot(a, b):
    return jnp.dot(a, b, preferred_element_type=F32)


def dot_rt(a, b):
    return lax.dot_general(a, b, (((1,), (1,)), ((), ())), preferred_element_type=F32)


def dot_lt(a, b):
    return lax.dot_general(a, b, (((0,), (0,)), ((), ())), preferred_element_type=F32)


def turn_tables(positions):
    half = ROT // 2
    frequencies = jnp.exp(
        jnp.arange(half, dtype=F32) * (-2.0 * math.log(10000.0) / ROT)
    )
    angles = positions.astype(F32)[:, None] * frequencies[None, :]
    return jnp.cos(angles)[:, None, :], jnp.sin(angles)[:, None, :]


def rotate(values, cosine, sine):
    half = ROT // 2
    low, high, rest = values[..., :half], values[..., half:ROT], values[..., ROT:]
    return jnp.concatenate(
        [low * cosine - high * sine, high * cosine + low * sine, rest], axis=-1
    )


def normalize(values):
    center = values - jnp.mean(values, axis=1, keepdims=True)
    inv_std = lax.rsqrt(jnp.mean(center * center, axis=1, keepdims=True) + 1e-05)
    return center * inv_std, inv_std


def norm_back(grad_norm, normal, inv_std):
    mean_grad = jnp.mean(grad_norm, axis=1, keepdims=True)
    mean_cross = jnp.mean(grad_norm * normal, axis=1, keepdims=True)
    return inv_std * (grad_norm - mean_grad - normal * mean_cross)


MESH = pl.DeviceIdType.MESH
NAMES = ("q", "o", "g", "u", "d")
LONG_UP = {"q": True, "o": False, "g": True, "u": False, "d": False}
VMEM_LIMIT = 64 * 1024 * 1024 - 64 * 1024


class Place:
    def __init__(self, n):
        self.n, self.half = n, n // 2
        self.r, self.s = lax.axis_index("rep"), lax.axis_index("shard")
        self.core = self.r + 1 - 2 * (self.r % 2)
        self.across = (self.r + 2) % REPS
        odd = self.s % 2
        self.spot = (1 - odd) * (self.s // 2) + odd * (n - 1 - self.s // 2)
        self.ids = {k: self.shard_at(k) for k in range(-self.half, self.half + 1)}
        self.ring = (self.ids[1], self.ids[-1])

    def shard_at(self, k):
        q = (self.spot + k + self.n) % self.n
        back = q // self.half
        return (1 - back) * 2 * q + back * (2 * self.n - 1 - 2 * q)

    def greet(self):
        barrier = pltpu.get_barrier_semaphore()
        for who in (
            (self.core, self.s),
            (self.across, self.s),
            (self.r, self.ring[0]),
            (self.r, self.ring[1]),
        ):
            pl.semaphore_signal(barrier, inc=1, device_id=who, device_id_type=MESH)
        pl.semaphore_wait(barrier, 4)


class RepLinks:
    def __init__(self, place, send, recv):
        self.place, self.send, self.recv, self.sent = place, send, recv, []

    def copy(self, i, src, dst, who):
        return pltpu.make_async_remote_copy(
            src_ref=src,
            dst_ref=dst,
            send_sem=self.send.at[i],
            recv_sem=self.recv.at[i],
            device_id=(who, self.place.s),
            device_id_type=MESH,
        )

    def start(self, i, src, dst, who):
        c = self.copy(i, src, dst, who)
        c.start()
        self.sent.append(c)
        return c

    def gather_start(self, i, own, slots):
        a = self.start(i, own, slots.at[1], self.place.across)
        b = self.start(i + 1, own, slots.at[2], self.place.core)
        return a, b

    def gather_pass(self, i, slots, copies):
        copies[0].wait_recv()
        return copies[1], self.start(i + 2, slots.at[1], slots.at[3], self.place.core)

    def finish(self):
        for c in self.sent:
            c.wait_send()


def layer_rows(x, gain, shift):
    center = x - jnp.mean(x, axis=1, keepdims=True)
    inv = lax.rsqrt(jnp.mean(center * center, axis=1, keepdims=True) + 1e-05)
    return center * inv * gain + shift


def first_half(shape):
    return lax.broadcasted_iota(jnp.int32, shape, 1) < 64


def forward_kernel(
    n,
    q_blk, o_blk, g_blk, u_blk, d_blk, tok, dyl, meta, tables,
    q_land, o_land, g_land, u_land, d_land, a1_out, q_out, k_out, v_out, p_out, attn_out,
    resid_out, a2_out, gate_out, up_out, hid_out, dyl_out, meta_out,
    wq, wo, wg, wu, xs, qs, ks, vs, ps, attn, attn_t, acc, csend, crecv, ysend, yrecv, resid, a2s,
    gates, ups, hid, metas, tabs, mask, small, vecs,
    ring_send, ring_recv, load_sem, rep_send, rep_recv, out_sem,
):
    here = Place(n)
    half = here.half
    blocks = dict(zip(NAMES, (q_blk, o_blk, g_blk, u_blk, d_blk)))
    lands = dict(zip(NAMES, (q_land, o_land, g_land, u_land, d_land)))
    into = {"q": wq, "o": wo, "g": wg, "u": wu}
    slots, width = tok.shape
    rows = {name: blocks[name].shape[0] for name in NAMES}
    rows["q"] = width // n
    reach = {
        (name, d): half if LONG_UP[name] == (d == 0) else half - 1 for name in NAMES for d in (0, 1)
    }

    def message(name, d, k):
        i = here.ids[(1 - k) if d == 0 else (k - 1)]
        a = NAMES.index(name)
        src = blocks[name] if k == 1 else lands[name].at[i]
        return pltpu.make_async_remote_copy(
            src_ref=src,
            dst_ref=lands[name].at[i],
            send_sem=ring_send.at[a, d, k - 1],
            recv_sem=ring_recv.at[a, d, k - 1],
            device_id=(here.r, here.ring[d]),
            device_id_type=MESH,
        )

    def load(name, k):
        i = here.ids[k]
        a = NAMES.index(name)
        src = blocks[name] if k == 0 else lands[name].at[i]
        return pltpu.make_async_copy(
            src.at[pl.ds(0, rows[name])],
            into[name].at[pl.ds(pl.multiple_of(i * rows[name], 16), rows[name])],
            load_sem.at[a, k + half],
        )

    def load_small(k):
        src = q_blk if k == 0 else q_land.at[here.ids[k]]
        return pltpu.make_async_copy(
            src.at[pl.ds(rows["q"], 16), pl.ds(0, rows["q"])],
            small.at[here.ids[k]],
            load_sem.at[5, k + half],
        )

    def keep_own(name):
        return pltpu.make_async_copy(
            blocks[name], lands[name].at[here.s], load_sem.at[6, NAMES.index(name)]
        )

    def begin(name):
        for d in (0, 1):
            message(name, d, 1).start()
        keep_own(name).start()
        if name in into:
            load(name, 0).start()
        if name == "q":
            load_small(0).start()

    def serve(name, k):
        for d in (0, 1):
            if k <= reach[name, d]:
                message(name, d, k).wait_recv()
                if k < reach[name, d]:
                    message(name, d, k + 1).start()
                if name in into:
                    load(name, -k if d == 0 else k).start()
                if name == "q":
                    load_small(-k if d == 0 else k).start()

    def came(name):
        found = [0]
        for k in range(1, half + 1):
            found += [-k] * (k <= reach[name, 0]) + [k] * (k <= reach[name, 1])
        return found

    def loaded(name):
        for k in came(name):
            load(name, k).wait()
            if name == "q":
                load_small(k).wait()

    outs = []

    def save(src, dst):
        c = pltpu.make_async_copy(src, dst, out_sem.at[len(outs)])
        c.start()
        outs.append(c)

    here.greet()
    begin("q")
    begin("o")
    rep = RepLinks(here, rep_send, rep_recv)
    own_x = pltpu.make_async_copy(tok, xs.at[pl.ds(0, slots)], load_sem.at[7, 0])
    own_x.start()
    own_m = pltpu.make_async_copy(meta, metas.at[0], load_sem.at[7, 1])
    own_m.start()
    own_d = pltpu.make_async_copy(dyl, dyl_out.at[0], load_sem.at[7, 2])
    own_d.start()

    class XSlots:
        class at:
            def __class_getitem__(cls, g):
                return xs.at[pl.ds(g * slots, slots)]

    m_sent = rep.gather_start(0, meta, metas)
    x_sent = rep.gather_start(3, tok, XSlots)
    m_end = rep.gather_pass(0, metas, m_sent)
    serve("o", 1)
    x_end = rep.gather_pass(3, XSlots, x_sent)
    serve("q", 1)
    serve("o", 2)
    d_sent = rep.gather_start(6, dyl, dyl_out)
    serve("q", 2)
    serve("o", 3)
    serve("q", 3)
    begin("g")
    serve("o", 4)
    begin("u")
    for c in m_end + x_end:
        c.wait_recv()
    x_end[1].wait_send()
    rep.sent = [c for c in rep.sent if c is not x_end[1]]
    own_x.wait()
    own_m.wait()
    serve("q", 4)
    loaded("q")
    for s in range(n):
        vecs[0:8, s * rows["q"] : (s + 1) * rows["q"]] = small[s, 0:8, :].astype(F32)
    d_end = rep.gather_pass(6, dyl_out, d_sent)

    gain_one, shift_one = vecs[0:1, :], vecs[1:2, :]

    @pl.loop(0, REPS * slots // 16)
    def _(i):
        at = pl.ds(pl.multiple_of(i * 16, 16), 16)
        xs[at, :] = layer_rows(xs[at, :].astype(F32), gain_one, shift_one).astype(BF16)

    serve("g", 1)
    serve("u", 1)
    save(xs, a1_out)

    own_width = wq.shape[1] // 3
    pairs = own_width // 128

    def lane_bias(row, t):
        w = rows["q"]
        a = vecs[row : row + 1, 2 * t * w : 2 * t * w + 128]
        return a + vecs[row : row + 1, (2 * t + 1) * w : (2 * t + 1) * w + 128]

    block = slots // 2
    line = lax.broadcasted_iota(jnp.int32, (slots, slots), 0)
    column = lax.broadcasted_iota(jnp.int32, (slots, slots), 1)

    def attend(g):
        here_rows = pl.ds(pl.multiple_of(g * slots, slots), slots)
        acc[...] = dot(xs[here_rows, :], wq[...])
        valid = metas[g, 0:1, :]
        same = metas[g, 1:2, :]
        for j in range(3):
            tabs[j, :block, :] = tables[j, :block, :]
            tabs[j, block:, :] = jnp.where(
                same[:, :128] > 0.5, tables[j, block:, :], tables[j, :block, :]
            )
        apart = (line >= block) & (column < block) & (same < 0.5)
        open_ = (column <= line) & jnp.logical_not(apart) & ((valid > 0.5) | (line == column))
        mask[...] = jnp.where(open_, 0.0, -1e30)
        for t in range(3 * pairs):
            part, tt = t // pairs, t % pairs
            tile = acc[:, t * 128 : (t + 1) * 128] + lane_bias((4, 6, 5)[part], tt)
            if part < 2:
                tile = (
                    tile * tabs[0]
                    + pltpu.roll(tile, 120, 1) * tabs[1]
                    + pltpu.roll(tile, 8, 1) * tabs[2]
                )
            (qs, ks, vs)[part][g, tt] = tile.astype(BF16)
        low = first_half((slots, 128))
        low_low = first_half((1, 128)).astype(F32).astype(BF16)
        high_low = (1.0 - first_half((1, 128)).astype(F32)).astype(BF16)
        for t in range(pairs):
            qt, kt, vt = qs[g, t], ks[g, t], vs[g, t]
            mixed = []
            for h in (0, 1):
                mine = low_low if h == 0 else high_low
                sc = dot_rt(qt * mine, kt) * (1.0 / 8.0) + mask[...]
                e = jnp.exp(sc - jnp.max(sc, axis=1, keepdims=True))
                p = (e / jnp.sum(e, axis=1, keepdims=True)).astype(BF16)
                ps[g, 2 * t + h] = p
                mixed.append(dot(p, vt))
            mix = jnp.where(low, mixed[0], mixed[1])
            attn[here_rows, t * 128 : (t + 1) * 128] = mix.astype(BF16)
            attn_t[t * 128 : (t + 1) * 128, here_rows] = mix.T.astype(BF16)

    @pl.loop(2, 4)
    def _(g):
        attend(g)

    loaded("o")
    for g in (0, 1):
        csend[g] = dot(attn[(g + 2) * slots : (g + 3) * slots, :], wo[...]).astype(BF16)
    rs_core = rep.start(9, csend, crecv, here.core)
    serve("g", 2)
    serve("u", 2)

    @pl.loop(0, 2)
    def _(g):
        attend(g)

    for c in d_end:
        c.wait_recv()
    rs_core.wait_recv()
    ysend[...] = (dot(attn[slots : 2 * slots, :], wo[...]) + crecv[1].astype(F32)).astype(BF16)
    rs_y = rep.start(10, ysend, yrecv, here.across)
    save(qs, q_out)
    save(ks, k_out)
    save(vs, v_out)
    save(ps, p_out)
    save(attn_t, attn_out)
    save(metas, meta_out)
    resid[...] = dot(attn[0:slots, :], wo[...]) + crecv[0].astype(F32)
    serve("g", 3)
    serve("u", 3)
    begin("d")
    rs_y.wait_recv()
    own_again = pltpu.make_async_copy(tok, crecv.at[0], load_sem.at[7, 3])
    own_again.start()
    own_again.wait()
    gain_two, shift_two = vecs[2:3, :], vecs[3:4, :]

    @pl.loop(0, slots // 16)
    def _(i):
        at = pl.ds(pl.multiple_of(i * 16, 16), 16)
        x = resid[at, :] + yrecv[at, :].astype(F32) + crecv[0, at, :].astype(F32)
        resid[at, :] = x
        a2s[0, at, :] = layer_rows(x, gain_two, shift_two).astype(BF16)

    a_sent = rep.gather_start(11, a2s.at[0], a2s)
    save(resid, resid_out)
    serve("g", 4)
    serve("u", 4)
    serve("d", 1)
    a_end = rep.gather_pass(11, a2s, a_sent)
    for c in a_end:
        c.wait_recv()
    loaded("g")
    loaded("u")
    save(a2s, a2_out)

    def feed(g):
        at = pl.ds(pl.multiple_of(g * slots, slots), slots)
        gate = dot(a2s[g], wg[...])
        gates[at, :] = gate.astype(BF16)
        up = dot(a2s[g], wu[...])
        ups[at, :] = up.astype(BF16)
        act = gate * jax.nn.sigmoid(gate) * up
        for j in range(act.shape[1] // 128):
            hid[j * 128 : (j + 1) * 128, at] = act[:, j * 128 : (j + 1) * 128].T.astype(BF16)

    @pl.loop(0, 2)
    def _(g):
        feed(g)

    serve("d", 2)

    @pl.loop(2, 4)
    def _(g):
        feed(g)

    save(gates, gate_out)
    save(ups, up_out)
    save(hid, hid_out)
    serve("d", 3)
    serve("d", 4)
    own_d.wait()
    for name in NAMES:
        keep_own(name).wait()
        for d in (0, 1):
            for k in range(1, reach[name, d] + 1):
                message(name, d, k).wait_send()
    rep.finish()
    for c in outs:
        c.wait()


def forward_call(n, blocks, tok, dyl, meta, tables):
    slots, width = tok.shape
    q, o, g, u, d = blocks
    lanes, units = q.shape[1], g.shape[1]
    own_width = lanes // 3
    all_slots = REPS * slots
    pairs = own_width // 128
    half = n // 2
    S = jax.ShapeDtypeStruct
    heads = (REPS, pairs, slots, 128)
    out_shape = [S((n,) + b.shape, BF16) for b in blocks] + [
        S((all_slots, width), BF16),
        S(heads, BF16),
        S(heads, BF16),
        S(heads, BF16),
        S((REPS, 2 * pairs, slots, slots), BF16),
        S((own_width, all_slots), BF16),
        S((slots, width), F32),
        S((REPS, slots, width), BF16),
        S((all_slots, units), BF16),
        S((all_slots, units), BF16),
        S((units, all_slots), BF16),
        S((REPS, slots, width), BF16),
        S((REPS, 8, slots), F32),
    ]
    V = pltpu.VMEM
    scratch = [
        V((width, lanes), BF16),
        V((own_width, width), BF16),
        V((width, units), BF16),
        V((width, units), BF16),
        V((all_slots, width), BF16),
        V(heads, BF16),
        V(heads, BF16),
        V(heads, BF16),
        V((REPS, 2 * pairs, slots, slots), BF16),
        V((all_slots, own_width), BF16),
        V((own_width, all_slots), BF16),
        V((slots, lanes), F32),
        V((2, slots, width), BF16),
        V((2, slots, width), BF16),
        V((slots, width), BF16),
        V((slots, width), BF16),
        V((slots, width), F32),
        V((REPS, slots, width), BF16),
        V((all_slots, units), BF16),
        V((all_slots, units), BF16),
        V((units, all_slots), BF16),
        V((REPS, 8, slots), F32),
        V((3, slots, 128), F32),
        V((slots, slots), F32),
        V((n, 16, width // n), BF16),
        V((8, width), F32),
        pltpu.SemaphoreType.DMA((5, 2, half)),
        pltpu.SemaphoreType.DMA((5, 2, half)),
        pltpu.SemaphoreType.DMA((8, 2 * half + 1)),
        pltpu.SemaphoreType.DMA((14,)),
        pltpu.SemaphoreType.DMA((14,)),
        pltpu.SemaphoreType.DMA((12,)),
    ]
    anywhere = pl.BlockSpec(memory_space=pltpu.HBM)
    return pl.pallas_call(
        functools.partial(forward_kernel, n),
        out_shape=out_shape,
        in_specs=[anywhere] * 8 + [pl.BlockSpec(memory_space=pltpu.VMEM)],
        out_specs=[anywhere] * len(out_shape),
        scratch_shapes=scratch,
        compiler_params=pltpu.CompilerParams(
            collective_id=1, has_side_effects=True, vmem_limit_bytes=VMEM_LIMIT
        ),
    )(*blocks, tok, dyl, meta, tables)


PARTS = ("d", "g", "u", "x", "y", "o", "s")
PARTS_UP = {"d": False, "g": True, "u": False, "x": True, "y": False, "o": False, "s": True}


def norm_rows_back(x, gain, grad):
    center = x - jnp.mean(x, axis=1, keepdims=True)
    inv = lax.rsqrt(jnp.mean(center * center, axis=1, keepdims=True) + 1e-05)
    normal = center * inv
    e = grad * gain
    cross = jnp.mean(e * normal, axis=1, keepdims=True)
    return inv * (e - jnp.mean(e, axis=1, keepdims=True) - normal * cross), normal


def backward_kernel(
    n,
    q_land, o_land, g_land, u_land, d_land, a1_in, q_in, k_in, v_in, p_in, attn_in,
    resid_in, a2_in, gate_in, up_in, hid_in, dyl_in, tok, metas, tables,
    act_out, grad_out, d_sum, g_sum, u_sum, x_sum, y_sum, o_sum, s_sum,
    land_d, land_g, land_u, land_x, land_y, land_o, land_s, core_land, y_land, drl_land,
    dyl, hid, wd, gates, ups, a2, a1, wst, wo, attn_t, heads, probs, dqkv, datt, csend, crecv,
    ysend, yrecv, own, resid, stage, rstage, sstage, small, vecs, sums, headsums, tabs,
    ring_send, ring_recv, load_sem, rep_send, rep_recv, stream_sem, rstage_sem, fin_sem,
):
    here = Place(n)
    half = here.half
    slots, width = tok.shape
    rows = width // n
    units = gates.shape[1]
    lanes = dqkv.shape[1]
    own_width = lanes // 3
    pairs = own_width // 128
    lands = dict(zip(PARTS, (land_d, land_g, land_u, land_x, land_y, land_o, land_s)))
    finals = dict(zip(PARTS, (d_sum, g_sum, u_sum, x_sum, y_sum, o_sum, s_sum)))
    shape = {name: lands[name].shape[2:] for name in PARTS}
    reach = {
        (name, d): half if PARTS_UP[name] == (d == 0) else half - 1 for name in PARTS for d in (0, 1)
    }
    rep = RepLinks(here, rep_send, rep_recv)

    def fetch(src, dst, i):
        c = pltpu.make_async_copy(src, dst, load_sem.at[i])
        c.start()
        return c

    def block_of(i, size):
        return pl.ds(pl.multiple_of(i * size, 16), size)

    def lanes_of(i, size):
        return pl.ds(pl.multiple_of(i * size, 128), size)

    def term(name, i):
        if name == "d":
            return dot(hid[block_of(i, shape["d"][0]), :], dyl[...])
        if name in ("g", "u"):
            return dot_lt(a2[:, lanes_of(i, rows)], (gates if name == "g" else ups)[...])
        if name == "x":
            return dot_lt(a1[:, lanes_of(i, rows)], dqkv[:, : lanes // 2])
        if name == "y":
            return dot_lt(a1[:, lanes_of(i, rows)], dqkv[:, lanes // 2 :])
        if name == "o":
            return dot(attn_t[block_of(i, shape["o"][0]), :], dyl[...])
        return sums[i]

    def corner(ref, name):
        return ref.at[pl.ds(0, shape[name][0]), pl.ds(0, shape[name][1])]

    def message(name, d, k, src):
        a = PARTS.index(name)
        return pltpu.make_async_remote_copy(
            src_ref=src,
            dst_ref=lands[name].at[d, k - 1],
            send_sem=ring_send.at[a, d, k - 1],
            recv_sem=ring_recv.at[a, d, k - 1],
            device_id=(here.r, here.ring[d]),
            device_id_type=MESH,
        )

    def landed(name, d, k):
        message(name, d, k, lands[name].at[d, k - 1]).wait_recv()
        dst = sstage.at[2 + d] if name == "s" else corner(rstage.at[d], name)
        c = pltpu.make_async_copy(lands[name].at[d, k - 1], dst, rstage_sem.at[d])
        c.start()
        return c, dst

    flying = {}
    turn = [0, 0]

    def serve(name, k):
        got = {}
        for d in (0, 1):
            if k < reach[name, d]:
                got[d] = landed(name, d, k + 1)
        for d in (0, 1):
            if k > reach[name, d]:
                continue
            if name == "s":
                slot, key = sstage.at[d], ("s", d)
            else:
                turn[d] = 1 - turn[d]
                slot, key = corner(stage.at[d, turn[d]], name), (d, turn[d])
            part = term(name, here.ids[k if d == 0 else -k])
            if d in got:
                got[d][0].wait()
                part = part + got[d][1][...].astype(F32)
            if key in flying:
                flying.pop(key).wait_send()
            slot[...] = part.astype(slot.dtype)
            flying[key] = message(name, d, k, slot)
            flying[key].start()

    opened = {}

    def finish(name):
        got = [landed(name, d, 1) for d in (0, 1)]
        part = term(name, here.ids[0])
        for c, ref in got:
            c.wait()
            part = part + ref[...].astype(F32)
        i = PARTS.index(name)
        ref = sstage.at[4] if name == "s" else corner(rstage.at[0], name)
        ref[...] = part.astype(ref.dtype)
        c = pltpu.make_async_copy(ref, finals[name].at[0], fin_sem.at[i])
        c.start()
        c.wait()
        opened[name] = rep.gather_start(3 * i, finals[name].at[0], finals[name])

    def hand_on(name):
        opened[name] = rep.gather_pass(3 * PARTS.index(name), finals[name], opened[name])

    base = 3 * len(PARTS)

    def stream(names, body):
        def copies(s, slot):
            found = []
            for j, name in enumerate(names):
                land = {"q": q_land, "g": g_land, "u": u_land}[name]
                found.append(
                    pltpu.make_async_copy(
                        land.at[s, pl.ds(0, rows)],
                        wst.at[slot, j, :, pl.ds(0, land.shape[2])],
                        stream_sem.at[slot, j],
                    )
                )
            return found

        for c in copies(0, 0):
            c.start()

        @pl.loop(0, n)
        def _(s):
            slot = s % 2

            @pl.when(s + 1 < n)
            def _():
                for c in copies(s + 1, 1 - slot):
                    c.start()

            for c in copies(s, slot):
                c.wait()
            body(s, slot)

    def exchange_core(i, k):
        return rep.start(base + i, csend, core_land.at[k], here.core)

    def exchange_y(i, k):
        return rep.start(base + i, ysend, y_land.at[k], here.across)

    def drop_send(c):
        c.wait_send()
        rep.sent = [x for x in rep.sent if x is not c]

    here.greet()
    c_hid = fetch(hid_in, hid, 0)
    c_dyl = fetch(dyl_in, dyl, 1)
    c_wd = fetch(d_land, wd, 2)
    c_gate = fetch(gate_in, gates, 3)
    c_up = fetch(up_in, ups, 4)
    c_a2 = fetch(a2_in, a2, 5)
    c_wo = [
        fetch(o_land.at[i], wo.at[pl.ds(i * o_land.shape[1], o_land.shape[1])], 32 + i) for i in range(n)
    ]
    c_att = fetch(attn_in, attn_t, 14)
    c_a1 = fetch(a1_in, a1, 7)
    c_res = fetch(resid_in, resid, 8)
    c_small = fetch(q_land.at[:, pl.ds(rows, 16), pl.ds(0, rows)], small, 9)
    c_hid.wait()
    c_dyl.wait()
    serve("d", half)
    for c in (c_wd, c_gate, c_up):
        c.wait()

    def feed_back(g):
        at = pl.ds(pl.multiple_of(g * slots, slots), slots)
        dh = dot_rt(dyl[at, :], wd[...])
        gate, up = gates[at, :].astype(F32), ups[at, :].astype(F32)
        sig = jax.nn.sigmoid(gate)
        gates[at, :] = (dh * up * sig * (1.0 + gate * (1.0 - sig))).astype(BF16)
        ups[at, :] = (dh * gate * sig).astype(BF16)

    @pl.loop(0, 2)
    def _(g):
        feed_back(g)

    serve("d", 3)

    @pl.loop(2, 4)
    def _(g):
        feed_back(g)

    for c in [c_a2, c_a1, c_res, c_small] + c_wo:
        c.wait()
    serve("g", 4)
    serve("u", 4)
    low_rows, high_rows = pl.ds(0, 2 * slots), pl.ds(2 * slots, 2 * slots)

    def a2_product(at, slot):
        return dot_rt(gates[at, :], wst[slot, 0, :, :units]) + dot_rt(ups[at, :], wst[slot, 1, :, :units])

    def a2_far(s, slot):
        part = a2_product(high_rows, slot).astype(BF16)
        csend[0, :, lanes_of(s, rows)] = part[:slots]
        csend[1, :, lanes_of(s, rows)] = part[slots:]

    stream(("g", "u"), a2_far)
    core1 = exchange_core(0, 0)
    serve("d", 2)
    serve("g", 3)
    serve("u", 3)
    for s in range(n):
        vecs[0:8, s * rows : (s + 1) * rows] = small[s, 0:8, :].astype(F32)
    core1.wait_recv()
    fetch(core_land.at[0], crecv, 10).wait()

    def a2_near(s, slot):
        part = a2_product(low_rows, slot)
        at = lanes_of(s, rows)
        own[:, at] = part[:slots] + crecv[0, :, at].astype(F32)
        ysend[:, at] = (part[slots:] + crecv[1, :, at].astype(F32)).astype(BF16)

    stream(("g", "u"), a2_near)
    y1 = exchange_y(1, 0)
    drop_send(core1)
    serve("d", 1)
    for g in (0, 1):
        csend[g] = dot_lt(hid[:, (g + 2) * slots : (g + 3) * slots], wd[...]).astype(BF16)
    core2 = exchange_core(2, 1)
    serve("g", 2)
    serve("u", 2)
    y1.wait_recv()
    fetch(y_land.at[0], yrecv, 11).wait()
    drop_send(y1)
    gain_two = vecs[2:3, :]
    headsums[...] = jnp.zeros_like(headsums)
    vecs[8:40, :] = jnp.zeros((32, width), F32)

    @pl.loop(0, slots // 16)
    def _(i):
        at = pl.ds(pl.multiple_of(i * 16, 16), 16)
        da = own[at, :] + yrecv[at, :].astype(F32)
        back, normal = norm_rows_back(resid[at, :], gain_two, da)
        prod = da * normal
        vecs[24:32, :] += prod[:8] + prod[8:]
        vecs[32:40, :] += da[:8] + da[8:]
        dr = dyl[at, :].astype(F32) + back
        own[at, :] = dr
        ysend[at, :] = dr.astype(BF16)

    c_drl = fetch(ysend, drl_land.at[0], 12)
    c_drl.wait()
    drl_sent = rep.gather_start(base + 3, drl_land.at[0], drl_land)
    core2.wait_recv()
    fetch(core_land.at[1], crecv, 13).wait()
    ysend[...] = (dot_lt(hid[:, slots : 2 * slots], wd[...]) + crecv[1].astype(F32)).astype(BF16)
    y2 = exchange_y(6, 1)
    resid[...] = resid[...] + dot_lt(hid[:, :slots], wd[...]) + crecv[0].astype(F32)
    serve("g", 1)
    serve("u", 1)
    finish("d")
    drl_end = rep.gather_pass(base + 3, drl_land, drl_sent)
    for c in drl_end:
        c.wait_recv()
    loads = [fetch(drl_land.at[g], dyl.at[pl.ds(g * slots, slots)], 16 + g) for g in range(REPS)]
    for c in loads:
        c.wait()
    c_att.wait()
    serve("o", 4)
    hand_on("d")

    low = first_half((slots, 128))
    halves = (
        first_half((1, 128)).astype(F32).astype(BF16),
        (1.0 - first_half((1, 128)).astype(F32)).astype(BF16),
    )
    block = slots // 2

    def head_copies(g, slot):
        found = [
            pltpu.make_async_copy(ref.at[g], heads.at[slot, j], stream_sem.at[slot, 2 + j])
            for j, ref in enumerate((q_in, k_in, v_in))
        ]
        return found + [pltpu.make_async_copy(p_in.at[g], probs.at[slot], stream_sem.at[slot, 5])]

    for c in head_copies(0, 0):
        c.start()

    def turn_back(tile):
        return tile * tabs[0] - pltpu.roll(tile, 120, 1) * tabs[1] - pltpu.roll(tile, 8, 1) * tabs[2]

    def attend_back(g):
        slot = g % 2

        @pl.when(g + 1 < REPS)
        def _():
            for c in head_copies(g + 1, 1 - slot):
                c.start()

        at = pl.ds(pl.multiple_of(g * slots, slots), slots)
        datt[...] = dot_rt(dyl[at, :], wo[...]).astype(BF16)
        same = metas[g, 1:2, :128]
        for j in range(3):
            tabs[j, :block, :] = tables[j, :block, :]
            tabs[j, block:, :] = jnp.where(same > 0.5, tables[j, block:, :], tables[j, :block, :])
        for c in head_copies(g, slot):
            c.wait()
        for t in range(pairs):
            da = datt[:, t * 128 : (t + 1) * 128]
            qt, kt, vt = heads[slot, 0, t], heads[slot, 1, t], heads[slot, 2, t]
            both = []
            for h in (0, 1):
                p = probs[slot, 2 * t + h]
                pf = p.astype(F32)
                dp = dot_rt(da * halves[h], vt)
                delta = jnp.sum(dp * pf, axis=1, keepdims=True)
                ds = (pf * (dp - delta)).astype(BF16)
                both.append((dot(ds, kt), dot_lt(ds, qt), dot_lt(p, da)))
            dq, dk, dv = [jnp.where(low, a, b) for a, b in zip(*both)]
            dq, dk = turn_back(dq * (1.0 / 8.0)), turn_back(dk * (1.0 / 8.0))
            for j, value in enumerate((dq, dk, dv)):
                row = j * pairs + t
                headsums[row : row + 1, :] += jnp.sum(value, axis=0, keepdims=True)
                first = j * own_width + t * 128
                dqkv[at, first : first + 128] = value.astype(BF16)

    @pl.loop(0, 2)
    def _(g):
        attend_back(g)

    serve("o", 3)

    @pl.loop(2, 4)
    def _(g):
        attend_back(g)

    serve("x", 4)
    serve("y", 4)
    finish("g")
    finish("u")
    drop_send(core2)

    def a1_far(s, slot):
        part = dot_rt(dqkv[high_rows, :], wst[slot, 0, :, :lanes]).astype(BF16)
        csend[0, :, lanes_of(s, rows)] = part[:slots]
        csend[1, :, lanes_of(s, rows)] = part[slots:]

    stream(("q",), a1_far)
    core3 = exchange_core(7, 2)
    serve("x", 3)
    serve("y", 3)
    serve("o", 2)
    hand_on("g")
    hand_on("u")
    y2.wait_recv()
    fetch(y_land.at[1], yrecv, 20).wait()

    @pl.loop(0, slots // 16)
    def _(i):
        at = pl.ds(pl.multiple_of(i * 16, 16), 16)
        yrecv[at, :] = (resid[at, :] + yrecv[at, :].astype(F32)).astype(BF16)

    fetch(yrecv, act_out, 21).wait()
    core3.wait_recv()
    fetch(core_land.at[2], crecv, 22).wait()
    drop_send(y2)

    def a1_near(s, slot):
        part = dot_rt(dqkv[low_rows, :], wst[slot, 0, :, :lanes])
        at = lanes_of(s, rows)
        resid[:, at] = part[:slots] + crecv[0, :, at].astype(F32)
        ysend[:, at] = (part[slots:] + crecv[1, :, at].astype(F32)).astype(BF16)

    stream(("q",), a1_near)
    y3 = exchange_y(8, 2)
    fetch(tok, crecv.at[1], 23).wait()
    serve("x", 2)
    serve("y", 2)
    serve("o", 1)
    y3.wait_recv()
    fetch(y_land.at[2], yrecv, 24).wait()
    gain_one = vecs[0:1, :]

    @pl.loop(0, slots // 16)
    def _(i):
        at = pl.ds(pl.multiple_of(i * 16, 16), 16)
        da = resid[at, :] + yrecv[at, :].astype(F32)
        back, normal = norm_rows_back(crecv[1, at, :].astype(F32), gain_one, da)
        prod = da * normal
        vecs[8:16, :] += prod[:8] + prod[8:]
        vecs[16:24, :] += da[:8] + da[8:]
        yrecv[at, :] = (own[at, :] + back).astype(BF16)

    c_grad = fetch(yrecv, grad_out, 25)
    sums[...] = jnp.zeros_like(sums)
    for j in range(4):
        total = jnp.sum(vecs[8 + 8 * j : 16 + 8 * j, :], axis=0, keepdims=True)
        for s in range(n):
            sums[s, j : j + 1, :] = total[:, s * rows : (s + 1) * rows]
    for s in range(n):
        for j, part in ((4, 0), (5, 2), (6, 1)):
            row = part * pairs + s // 2
            sums[s, j : j + 1, 0:128] = headsums[row : row + 1, :] * halves[s % 2].astype(F32)
    serve("s", 4)
    serve("x", 1)
    serve("y", 1)
    serve("s", 3)
    finish("o")
    serve("s", 2)
    serve("s", 1)
    finish("x")
    finish("y")
    finish("s")
    for name in ("o", "s", "x", "y"):
        hand_on(name)
    for name in PARTS:
        for c in opened[name]:
            c.wait_recv()
    c_grad.wait()
    rep.finish()
    for c in flying.values():
        c.wait_send()


def backward_call(n, lands, kept, tok, meta, tables):
    slots, width = tok.shape
    q_land, o_land, g_land, u_land, d_land = lands
    a1, qs, ks, vs, ps, attn_t, resid, a2, gate, up, hid, dyl = kept
    all_slots, units = gate.shape
    lanes = q_land.shape[2]
    pairs = lanes // 3 // 128
    half = n // 2
    rows = width // n
    S = jax.ShapeDtypeStruct
    block = {
        "d": (d_land.shape[1], width),
        "g": (rows, units),
        "u": (rows, units),
        "x": (rows, lanes // 2),
        "y": (rows, lanes // 2),
        "o": (o_land.shape[1], width),
        "s": (8, rows),
    }
    kind = {name: F32 if name == "s" else BF16 for name in PARTS}
    out_shape = (
        [S((slots, width), BF16), S((slots, width), BF16)]
        + [S((REPS,) + block[name], kind[name]) for name in PARTS]
        + [S((2, half) + block[name], kind[name]) for name in PARTS]
        + [S((3, 2, slots, width), BF16), S((3, slots, width), BF16), S((REPS, slots, width), BF16)]
    )
    V = pltpu.VMEM
    scratch = [
        V((all_slots, width), BF16),
        V(hid.shape, BF16),
        V((units, width), BF16),
        V((all_slots, units), BF16),
        V((all_slots, units), BF16),
        V((all_slots, width), BF16),
        V((all_slots, width), BF16),
        V((2, 2, rows, lanes), BF16),
        V((lanes // 3, width), BF16),
        V((lanes // 3, all_slots), BF16),
        V((2, 3, pairs, slots, 128), BF16),
        V((2, 2 * pairs, slots, slots), BF16),
        V((all_slots, lanes), BF16),
        V((slots, lanes // 3), BF16),
        V((2, slots, width), BF16),
        V((2, slots, width), BF16),
        V((slots, width), BF16),
        V((slots, width), BF16),
        V((slots, width), F32),
        V((slots, width), F32),
        V((2, 2, rows, width), BF16),
        V((2, rows, width), BF16),
        V((5, 8, rows), F32),
        V((n, 16, rows), BF16),
        V((40, width), F32),
        V((n, 8, rows), F32),
        V((16, 128), F32),
        V((3, slots, 128), F32),
        pltpu.SemaphoreType.DMA((len(PARTS), 2, half)),
        pltpu.SemaphoreType.DMA((len(PARTS), 2, half)),
        pltpu.SemaphoreType.DMA((32 + n,)),
        pltpu.SemaphoreType.DMA((30,)),
        pltpu.SemaphoreType.DMA((30,)),
        pltpu.SemaphoreType.DMA((2, 6)),
        pltpu.SemaphoreType.DMA((2,)),
        pltpu.SemaphoreType.DMA((len(PARTS),)),
    ]
    anywhere = pl.BlockSpec(memory_space=pltpu.HBM)
    inside = pl.BlockSpec(memory_space=pltpu.VMEM)
    out = pl.pallas_call(
        functools.partial(backward_kernel, n),
        out_shape=out_shape,
        in_specs=[anywhere] * 18 + [inside] * 2,
        out_specs=[anywhere] * len(out_shape),
        scratch_shapes=scratch,
        compiler_params=pltpu.CompilerParams(
            collective_id=2, has_side_effects=True, vmem_limit_bytes=VMEM_LIMIT
        ),
    )(q_land, o_land, g_land, u_land, d_land.reshape(units, width), a1, qs, ks, vs, ps, attn_t,
      resid, a2, gate, up, hid, dyl, tok, meta, tables)
    return out[:2], dict(zip(PARTS, out[2:9]))


def core_swap(x):
    return lax.ppermute(x, "rep", [(0, 1), (1, 0), (2, 3), (3, 2)])


def y_swap(x):
    return lax.ppermute(x, "rep", [(0, 2), (1, 3), (2, 0), (3, 1)])


def rep_parts(x):
    across = y_swap(x)
    return [x, across, core_swap(x), core_swap(across)]


def rep_gather(x):
    return jnp.concatenate(rep_parts(x), axis=0)


def rep_reduce(a, w_dot, slots):
    far = core_swap(w_dot(a[2 * slots :]).astype(BF16))
    near = w_dot(a[: 2 * slots]) + far.astype(F32)
    return near[:slots] + y_swap(near[slots:].astype(BF16)).astype(F32)


def solution(mesh):
    n = mesh.shape["shard"]
    half_ring = n // 2
    order = list(range(0, n, 2)) + list(range(n - 1, 0, -2))
    place = [order.index(s) for s in range(n)]
    up_ring = [(order[i], order[(i + 1) % n]) for i in range(n)]
    down_ring = [(b, a) for a, b in up_ring]

    def hop(x, ring, sent):
        if len(sent) >= DEPTH:
            x, _ = lax.optimization_barrier((x, sent[-DEPTH]))
        x = lax.ppermute(x, "shard", ring)
        sent.append(x)
        return x

    def ring_ids():
        spot = jnp.array(place, jnp.int32)[lax.axis_index("shard")]
        table = jnp.array(order, jnp.int32)
        return {k: table[(spot + k) % n] for k in range(-half_ring, half_ring + 1)}

    def gather(x, ids, forward_extra, places, line):
        bufs = places(None, x, ids[0])
        up = down = x
        for k in range(1, half_ring + 1):
            go_up = k < half_ring or forward_extra
            go_down = k < half_ring or not forward_extra
            if go_up:
                up = hop(up, up_ring, line[0])
            if go_down:
                down = hop(down, down_ring, line[1])
            if go_up:
                bufs = places(bufs, up, ids[-k])
            if go_down:
                bufs = places(bufs, down, ids[k])
            yield
        return bufs

    def put(bufs, block, at):
        if bufs is None:
            bufs = jnp.zeros((n,) + block.shape, block.dtype)
        return lax.dynamic_update_index_in_dim(bufs, block, at, 0)

    def reduce(term, ids, forward_extra, line, kind=BF16):
        acc = {}
        for k in range(half_ring, 0, -1):
            for side, (ring, sign, extra) in enumerate(
                ((up_ring, 1, forward_extra), (down_ring, -1, not forward_extra))
            ):
                if k == half_ring and not extra:
                    continue
                part = term(ids[sign * k])
                if side in acc:
                    part = part + acc[side].astype(F32)
                acc[side] = hop(part.astype(kind), ring, line[side])
            yield
        return term(ids[0]) + acc[0].astype(F32) + acc[1].astype(F32)

    def run(chains, turns):
        done = {}
        for name in turns:
            for _ in range(n // 8):
                if name in done:
                    continue
                try:
                    next(chains[name])
                except StopIteration as stop:
                    done[name] = stop.value
        for name, chain in chains.items():
            while name not in done:
                try:
                    next(chain)
                except StopIteration as stop:
                    done[name] = stop.value
        return done

    def pick_columns(w, groups, width, r):
        chosen = [
            lax.select_n(
                r,
                *[
                    w[:, (g * REPS + q) * width : (g * REPS + q + 1) * width]
                    for q in range(REPS)
                ],
            )
            for g in range(groups)
        ]
        return jnp.concatenate(chosen, axis=1)

    def by_rep(parts, y, core):
        own, across, beside, both = parts
        low0 = lax.select(core == 0, own, beside)
        low1 = lax.select(core == 0, beside, own)
        high0 = lax.select(core == 0, across, both)
        high1 = lax.select(core == 0, both, across)
        return [
            lax.select(y == 0, low0, high0),
            lax.select(y == 0, low1, high1),
            lax.select(y == 0, high0, low0),
            lax.select(y == 0, high1, low1),
        ]

    def weave(parts, groups, width):
        pieces = [
            parts[q][:, g * width : (g + 1) * width]
            for g in range(groups)
            for q in range(REPS)
        ]
        return jnp.concatenate(pieces, axis=1).astype(F32)

    def on_device(
        tokens, cotangent, block_seq, block_len, vectors, key_bias, w_qkv, w_out, w_gate_up, w_down
    ):
        slots, features = tokens.shape
        blocks = block_seq.shape[0]
        block_size = slots // blocks
        head_dim = features // HEADS
        own_heads = HEADS // REPS
        own_width = own_heads * head_dim
        all_slots = REPS * slots
        scale = 1.0 / math.sqrt(head_dim)
        rows = features // n
        hidden_units = w_gate_up.shape[1] // 2
        own_hidden = hidden_units // REPS
        down_rows = w_down.shape[0] // REPS
        out_rows = w_out.shape[0] // REPS
        regroup = out_rows < head_dim
        r = lax.axis_index("rep")
        y, core = r // 2, r % 2
        ids = ring_ids()

        def mix_out(x):
            if not regroup:
                return x
            pairs = [
                (k * n + 4 * j + q, q * n + 4 * j + k)
                for k in range(REPS)
                for j in range(n // 4)
                for q in range(REPS)
            ]
            return lax.ppermute(x, BOTH, pairs)

        fast = blocks == 2 and down_rows % 16 == 0 and out_rows == head_dim and rows % 128 == 0
        own_valid = (
            jnp.arange(block_size, dtype=jnp.int32)[None, :] < block_len[:, None]
        ).reshape(-1)
        grad_output = cotangent.astype(F32) * own_valid[:, None].astype(F32)
        dyl_own = grad_output.astype(BF16)
        if fast:
            lanes = 3 * own_width
            side = (lax.axis_index("shard") % 2) * head_dim
            small = jnp.zeros((16, lanes), BF16)
            small = lax.dynamic_update_slice(small, vectors[:, :4].T, (0, 0))
            mine = lax.dynamic_slice_in_dim(vectors, r * head_dim, head_dim, 0)
            small = lax.dynamic_update_slice(small, mine[:, 4:6].T, (4, side))
            mine = lax.dynamic_slice_in_dim(key_bias, r * ROT, ROT, 0)
            small = lax.dynamic_update_slice(small, mine.T, (6, side))
            q_blk = jnp.concatenate([pick_columns(w_qkv, 3 * own_heads, head_dim, r), small], axis=0)
            o_blk = lax.dynamic_slice_in_dim(w_out, r * out_rows, out_rows, 0)
            g_blk = pick_columns(w_gate_up[:, :hidden_units], n, down_rows, r)
            u_blk = pick_columns(w_gate_up[:, hidden_units:], n, down_rows, r)
            d_blk = lax.dynamic_slice_in_dim(w_down, r * down_rows, down_rows, 0)
            together = jnp.broadcast_to(block_seq[0] == block_seq[1], (slots,))
            meta = jnp.stack([own_valid, together] + [together] * 6).astype(F32)
            cosine, sine = turn_tables(jnp.arange(slots, dtype=jnp.int32))
            cosine, sine = cosine[:, 0], sine[:, 0]
            rest = jnp.ones((slots, head_dim - ROT), F32)
            none = jnp.zeros((slots, ROT // 2), F32)
            tables = jnp.stack(
                [
                    jnp.concatenate([cosine, cosine, rest] * 2, axis=1),
                    jnp.concatenate([-sine, none, 0 * rest] * 2, axis=1),
                    jnp.concatenate([none, sine, 0 * rest] * 2, axis=1),
                ]
            )
            out = forward_call(n, (q_blk, o_blk, g_blk, u_blk, d_blk), tokens, dyl_own, meta, tables)
            q_land, o_land, g_land, u_land, d_land = out[:5]
            a1, qs, ks, vs, ps, attn, resid, a2, gate, up, hid, dyl_all, metas = out[5:]
            whole = (all_slots, features)
            (activations, grad_input), parts = backward_call(
                n,
                out[:5],
                (a1, qs, ks, vs, ps, attn, resid, a2.reshape(whole), gate, up, hid, dyl_all.reshape(whole)),
                tokens,
                metas,
                tables,
            )

            def in_order(x):
                return by_rep([x[0], x[1], x[2], x[3]], y, core)

            out_down = jnp.concatenate(in_order(parts["d"]), axis=0).astype(F32)
            out_out = jnp.concatenate(in_order(parts["o"]), axis=0).astype(F32)
            out_gate_up = jnp.concatenate(
                [weave(in_order(parts[name]), n, down_rows) for name in "gu"], axis=1
            )
            g_qkv = jnp.concatenate([parts["x"], parts["y"]], axis=2)
            out_qkv = weave(in_order(g_qkv), 3 * own_heads, head_dim)
            sums = parts["s"]
            norms = sums[0, :4] + sums[1, :4] + sums[2, :4] + sums[3, :4]
            mine = in_order(lax.dynamic_slice_in_dim(sums[:, 4:7], side, head_dim, 2))
            biases = jnp.concatenate([m[:2] for m in mine], axis=1)
            out_vectors = jnp.concatenate([norms, biases], axis=0).T
            out_key = jnp.concatenate([m[2, :ROT] for m in mine]).reshape(-1, 1)
            return activations, grad_input, out_vectors, out_key, out_qkv, out_out, out_gate_up, out_down
        else:
            small = jnp.concatenate([vectors.T.reshape(-1), key_bias.reshape(-1)])
            lanes = 3 * own_width
            small_rows = -(-small.size // lanes)
            small_rows = -(-small_rows // 16) * 16
            small = jnp.pad(small, (0, small_rows * lanes - small.size)).reshape(small_rows, lanes)
            qkv_block = jnp.concatenate([pick_columns(w_qkv, 3 * own_heads, head_dim, r), small], axis=0)

            def put_qkv(bufs, block, at):
                a, b = (None, None) if bufs is None else bufs
                return put(a, block[:rows], at), put(b, block[rows:], at)

            out_block = mix_out(lax.dynamic_slice_in_dim(w_out, r * out_rows, out_rows, 0))
            gate_block = pick_columns(w_gate_up[:, :hidden_units], n, down_rows, r)
            up_block = pick_columns(w_gate_up[:, hidden_units:], n, down_rows, r)
            down_block = lax.dynamic_slice_in_dim(w_down, r * down_rows, down_rows, 0)
            line = ([], [])
            got = run(
                {
                    "q": gather(qkv_block, ids, True, put_qkv, line),
                    "o": gather(out_block, ids, False, put, line),
                    "g": gather(gate_block, ids, True, put, line),
                    "u": gather(up_block, ids, False, put, line),
                    "d": gather(down_block, ids, False, put, line),
                },
                "qoqoqoqoguguguguddddd",
            )
            wq, smalls = got["q"]
            wq = wq.reshape(features, lanes)
            smalls = smalls.reshape(n, -1).astype(F32)
            vec = smalls[:, : 6 * rows].reshape(n, 6, rows).transpose(1, 0, 2).reshape(6, features)
            key_full = smalls[:, 6 * rows : 6 * rows + HEADS * ROT // n].reshape(own_heads, REPS, ROT)
            key_own = lax.dynamic_index_in_dim(key_full, r, 1, keepdims=False)
            key_shift = jnp.pad(key_own, ((0, 0), (0, head_dim - ROT))).reshape(own_width)

            def own_heads_of(v):
                return lax.dynamic_index_in_dim(
                    v.reshape(own_heads, REPS, head_dim), r, 1, keepdims=False
                ).reshape(own_width)

            wo = got["o"].reshape(own_width, features)
            wg = got["g"].reshape(features, own_hidden)
            wu = got["u"].reshape(features, own_hidden)
            wd = got["d"].reshape(own_hidden, features)

            meta = jnp.concatenate([block_seq, block_len]).astype(F32)
            meta = jnp.pad(meta, (0, 128 - 2 * blocks)).reshape(1, 128)
            meta = jnp.concatenate(rep_parts(jnp.broadcast_to(meta, (8, 128))), axis=0)
            meta = meta.reshape(REPS, 8, 128)[:, 0, :]
            seqs = meta[:, :blocks].astype(jnp.int32)
            lens = meta[:, blocks : 2 * blocks].astype(jnp.int32)
            index = jnp.arange(blocks, dtype=jnp.int32)
            same = seqs[:, None, :] == seqs[:, :, None]
            earlier = jnp.sum(
                jnp.where((index[None, :] < index[:, None]) & same, 1, 0), axis=2
            ).astype(jnp.int32)
            offset = jnp.arange(block_size, dtype=jnp.int32)
            seq_slot = jnp.broadcast_to(seqs[:, :, None], (REPS, blocks, block_size)).reshape(REPS, slots)
            valid = (offset[None, None, :] < lens[:, :, None]).reshape(REPS, slots)
            positions = (earlier[:, :, None] * block_size + offset[None, None, :]).reshape(all_slots)
            slot_index = jnp.arange(slots, dtype=jnp.int32)
            allowed = (seq_slot[:, None, :] == seq_slot[:, :, None]) & (
                slot_index[None, :] <= slot_index[:, None]
            )[None]
            allowed = allowed & (valid[:, None, :] | (slot_index[None, :] == slot_index[:, None])[None])
            cosine, sine = turn_tables(positions)

            x_all = rep_gather(tokens)
            dyl = rep_gather(dyl_own)

            tokens_f = tokens.astype(F32)
            normal_one, inv_one = normalize(tokens_f)
            normal_all, _ = normalize(x_all.astype(F32))
            a1 = (normal_all * vec[0] + vec[1]).astype(BF16)
            projected = dot(a1, wq)
            head_shape = (all_slots, own_heads, head_dim)
            group_shape = (REPS, slots, own_heads, head_dim)
            q = rotate((projected[:, :own_width] + own_heads_of(vec[4])).reshape(head_shape), cosine, sine)
            k = rotate((projected[:, own_width : 2 * own_width] + key_shift).reshape(head_shape), cosine, sine)
            v = projected[:, 2 * own_width :] + own_heads_of(vec[5])
            q = q.astype(BF16).reshape(group_shape)
            k = k.astype(BF16).reshape(group_shape)
            v = v.astype(BF16).reshape(group_shape)
            scores = jnp.einsum("gshd,gthd->ghst", q, k, preferred_element_type=F32) * scale
            scores = jnp.where(allowed[:, None], scores, -1e30)
            exponent = jnp.exp(scores - jnp.max(scores, axis=-1, keepdims=True))
            probs = exponent / jnp.sum(exponent, axis=-1, keepdims=True)
            probs_low = probs.astype(BF16)
            attn = jnp.einsum("ghst,gthd->gshd", probs_low, v, preferred_element_type=F32)
            attn = attn.reshape(all_slots, own_width).astype(BF16)
            resid = tokens_f + rep_reduce(attn, lambda a: dot(a, wo), slots)
            normal_two, inv_two = normalize(resid)
            a2 = rep_gather((normal_two * vec[2] + vec[3]).astype(BF16))
            gate = dot(a2, wg)
            up = dot(a2, wu)
            sig = jax.nn.sigmoid(gate)
            hidden = (gate * sig * up).astype(BF16)

        def blocks_of(a):
            return a.reshape(all_slots, n, -1).transpose(1, 0, 2)

        hidden_b = blocks_of(hidden)
        activations = (resid + rep_reduce(hidden, lambda a: dot(a, wd), slots)).astype(BF16)
        grad_hidden = dot_rt(dyl, wd)
        grad_gate = (grad_hidden * up * sig * (1.0 + gate * (1.0 - sig))).astype(BF16)
        grad_up = (grad_hidden * gate * sig).astype(BF16)
        a2_b = blocks_of(a2)
        grad_gu = jnp.concatenate([grad_gate, grad_up], axis=1)
        wgu = jnp.concatenate([wg, wu], axis=1)
        grad_a2 = rep_reduce(grad_gu, lambda a: dot_rt(a, wgu), slots)
        grad_resid = grad_output + norm_back(grad_a2 * vec[2], normal_two, inv_two)
        drl = rep_gather(grad_resid.astype(BF16))
        attn_b = blocks_of(attn)
        d_attn = dot_rt(drl, wo).astype(BF16).reshape(group_shape)
        grad_v = jnp.einsum("ghst,gshd->gthd", probs_low, d_attn, preferred_element_type=F32)
        grad_p = jnp.einsum("gshd,gthd->ghst", d_attn, v, preferred_element_type=F32)
        delta = jnp.sum(grad_p * probs, axis=-1, keepdims=True)
        grad_s = (probs * (grad_p - delta)).astype(BF16)
        grad_q = jnp.einsum("ghst,gthd->gshd", grad_s, k, preferred_element_type=F32) * scale
        grad_k = jnp.einsum("ghst,gshd->gthd", grad_s, q, preferred_element_type=F32) * scale
        grad_q = rotate(grad_q.reshape(head_shape), cosine, -sine)
        grad_k = rotate(grad_k.reshape(head_shape), cosine, -sine)
        grad_v = grad_v.reshape(head_shape)
        key_sum = jnp.sum(grad_k[:, :, :ROT], axis=0)
        d_qkv = jnp.concatenate(
            [g.reshape(all_slots, own_width) for g in (grad_q, grad_k, grad_v)], axis=1
        ).astype(BF16)
        a1_b = blocks_of(a1)
        grad_a1 = rep_reduce(d_qkv, lambda a: dot_rt(a, wq), slots)
        grad_input = (grad_resid + norm_back(grad_a1 * vec[0], normal_one, inv_one)).astype(BF16)

        def spread(sums):
            zero = jnp.zeros((own_heads, REPS, sums.shape[1]), F32)
            return lax.dynamic_update_index_in_dim(zero, sums, r, 1)

        vec_sums = jnp.stack(
            [
                jnp.sum(grad_a1 * normal_one, axis=0),
                jnp.sum(grad_a1, axis=0),
                jnp.sum(grad_a2 * normal_two, axis=0),
                jnp.sum(grad_a2, axis=0),
                spread(jnp.sum(grad_q, axis=0)).reshape(features),
                spread(jnp.sum(grad_v, axis=0)).reshape(features),
            ],
            axis=0,
        )
        key_rows = HEADS * ROT // n
        packed = jnp.concatenate(
            [
                vec_sums.reshape(6, n, rows).transpose(1, 0, 2).reshape(n, 6 * rows),
                spread(key_sum).reshape(n, key_rows),
            ],
            axis=1,
        )
        width = -(-packed.shape[1] // 1024) * 1024
        packed = jnp.pad(packed, ((0, 0), (0, width - packed.shape[1]))).reshape(n, width // 128, 128)
        line = ([], [])
        sums = run(
            {
                "d": reduce(lambda i: dot_lt(hidden_b[i], dyl), ids, False, line),
                "g": reduce(lambda i: dot_lt(a2_b[i], grad_gate), ids, True, line),
                "u": reduce(lambda i: dot_lt(a2_b[i], grad_up), ids, False, line),
                "q": reduce(lambda i: dot_lt(a1_b[i], d_qkv), ids, True, line),
                "o": reduce(lambda i: dot_lt(attn_b[i], drl), ids, False, line),
                "s": reduce(lambda i: packed[i], ids, True, line, F32),
            },
            "dgdgdudugugugqoqoqosoqsoss",
        )
        grad_down, grad_wg, grad_wu = sums["d"], sums["g"], sums["u"]
        grad_wq, grad_wo, packed = sums["q"], sums["o"], sums["s"]
        packed = packed + core_swap(packed)
        packed = (packed + y_swap(packed)).reshape(-1)
        out_vectors = packed[: 6 * rows].reshape(6, rows).T
        out_key = packed[6 * rows : 6 * rows + key_rows].reshape(key_rows, 1)

        def everywhere(g):
            return by_rep(rep_parts(g.astype(BF16)), y, core)

        out_down = jnp.concatenate(everywhere(grad_down), axis=0).astype(F32)
        out_gate_up = jnp.concatenate(
            [weave(everywhere(g), n, down_rows) for g in (grad_wg, grad_wu)], axis=1
        )
        out_qkv = weave(everywhere(grad_wq), 3 * own_heads, head_dim)
        out_out = jnp.concatenate(everywhere(mix_out(grad_wo.astype(BF16))), axis=0).astype(F32)
        return activations, grad_input, out_vectors, out_key, out_qkv, out_out, out_gate_up, out_down

    tok, row = P(BOTH, None), P("shard", None)
    return jax.shard_map(
        on_device,
        mesh=mesh,
        in_specs=(tok, tok, P(BOTH), P(BOTH)) + (row,) * 6,
        out_specs=(tok, tok) + (row,) * 6,
        check_vma=False,
    )
```

```python
import functools
import math

import jax
import jax.numpy as jnp
import numpy as np
from jax import lax
from jax.experimental import pallas as pl
from jax.experimental.pallas import tpu as pltpu
from jax.sharding import PartitionSpec as P

HEADS = 32
ROT = 16
REPS = 4
BOTH = ("rep", "shard")
DEPTH = 2
F32 = jnp.float32
BF16 = jnp.bfloat16


def dot(a, b):
    return jnp.dot(a, b, preferred_element_type=F32)


def dot_rt(a, b):
    return lax.dot_general(a, b, (((1,), (1,)), ((), ())), preferred_element_type=F32)


def dot_lt(a, b):
    return lax.dot_general(a, b, (((0,), (0,)), ((), ())), preferred_element_type=F32)


def turn_tables(positions):
    half = ROT // 2
    frequencies = jnp.exp(
        jnp.arange(half, dtype=F32) * (-2.0 * math.log(10000.0) / ROT)
    )
    angles = positions.astype(F32)[:, None] * frequencies[None, :]
    return jnp.cos(angles)[:, None, :], jnp.sin(angles)[:, None, :]


def rotate(values, cosine, sine):
    half = ROT // 2
    low, high, rest = values[..., :half], values[..., half:ROT], values[..., ROT:]
    return jnp.concatenate(
        [low * cosine - high * sine, high * cosine + low * sine, rest], axis=-1
    )


def normalize(values):
    center = values - jnp.mean(values, axis=1, keepdims=True)
    inv_std = lax.rsqrt(jnp.mean(center * center, axis=1, keepdims=True) + 1e-05)
    return center * inv_std, inv_std


def norm_back(grad_norm, normal, inv_std):
    mean_grad = jnp.mean(grad_norm, axis=1, keepdims=True)
    mean_cross = jnp.mean(grad_norm * normal, axis=1, keepdims=True)
    return inv_std * (grad_norm - mean_grad - normal * mean_cross)


MESH = pl.DeviceIdType.MESH
NAMES = ("q", "o", "g", "u", "d")
LONG_UP = {"q": True, "o": False, "g": True, "u": False, "d": False}
FORE_ORDER = (
    "pm", "px", "o1", "cot", "q1", "o2", "sg", "q2", "o3", "su", "q3", "o4", "pd", "q4", "ln1", "g1", "u1",
    "at2", "at3", "of", "g2", "u2", "at0", "at1", "oy", "oo", "g3", "u3", "bd", "ln2", "g4", "u4", "d1", "pa",
    "fd0", "fd1", "d2", "fd2", "fd3", "d3", "d4",
)
VMEM_LIMIT = 64 * 1024 * 1024 - 64 * 1024


class Place:
    def __init__(self, n):
        self.n, self.half = n, n // 2
        self.r, self.s = lax.axis_index("rep"), lax.axis_index("shard")
        self.core = self.r + 1 - 2 * (self.r % 2)
        self.across = (self.r + 2) % REPS
        odd = self.s % 2
        self.spot = (1 - odd) * (self.s // 2) + odd * (n - 1 - self.s // 2)
        self.ids = {k: self.shard_at(k) for k in range(-self.half, self.half + 1)}
        self.ring = (self.ids[1], self.ids[-1])

    def shard_at(self, k):
        q = (self.spot + k + self.n) % self.n
        back = q // self.half
        return (1 - back) * 2 * q + back * (2 * self.n - 1 - 2 * q)

    def greet(self):
        barrier = pltpu.get_barrier_semaphore()
        for who in (
            (self.core, self.s),
            (self.across, self.s),
            (self.r, self.ring[0]),
            (self.r, self.ring[1]),
        ):
            pl.semaphore_signal(barrier, inc=1, device_id=who, device_id_type=MESH)
        pl.semaphore_wait(barrier, 4)


class RepLinks:
    def __init__(self, place, send, recv):
        self.place, self.send, self.recv, self.sent = place, send, recv, []

    def copy(self, i, src, dst, who):
        return pltpu.make_async_remote_copy(
            src_ref=src,
            dst_ref=dst,
            send_sem=self.send.at[i],
            recv_sem=self.recv.at[i],
            device_id=(who, self.place.s),
            device_id_type=MESH,
        )

    def start(self, i, src, dst, who):
        c = self.copy(i, src, dst, who)
        c.start()
        self.sent.append(c)
        return c

    def gather_start(self, i, own, slots):
        a = self.start(i, own, slots.at[1], self.place.across)
        b = self.start(i + 1, own, slots.at[2], self.place.core)
        return a, b

    def gather_pass(self, i, slots, copies):
        copies[0].wait_recv()
        return copies[1], self.start(i + 2, slots.at[1], slots.at[3], self.place.core)

    def finish(self):
        for c in self.sent:
            c.wait_send()


def layer_rows(x, gain, shift):
    center = x - jnp.mean(x, axis=1, keepdims=True)
    inv = lax.rsqrt(jnp.mean(center * center, axis=1, keepdims=True) + 1e-05)
    return center * inv * gain + shift


def first_half(shape):
    return lax.broadcasted_iota(jnp.int32, shape, 1) < 64


def forward_kernel(
    n,
    w_qkv, w_out, w_gu, w_down, tok, cot, vt, seqs, lens, tables,
    q_land, o_land, g_land, u_land, d_land, a1_out, q_out, k_out, v_out, p_out, attn_out,
    resid_out, a2_out, gate_out, up_out, hid_out, dyl_out, meta_out,
    q_blk, g_blk, u_blk, wq, wo, wg, wu, xs, qs, ks, vs, ps, attn, attn_t, acc, csend, crecv, ysend,
    yrecv, resid, a2s, gates, ups, hid, metas, tabs, mask, small, vecs,
    ring_send, ring_recv, load_sem, rep_send, rep_recv, out_sem,
):
    here = Place(n)
    half = here.half
    lands = dict(zip(NAMES, (q_land, o_land, g_land, u_land, d_land)))
    rows = {name: lands[name].shape[1] for name in NAMES}
    slots, width = tok.shape
    rows["q"] = width // n
    blocks = {
        "q": q_blk,
        "o": w_out.at[pl.ds(pl.multiple_of(here.r * rows["o"], 16), rows["o"])],
        "g": g_blk,
        "u": u_blk,
        "d": w_down.at[pl.ds(pl.multiple_of(here.r * rows["d"], 16), rows["d"])],
    }
    into = {"q": wq, "o": wo, "g": wg, "u": wu}
    reach = {
        (name, d): half if LONG_UP[name] == (d == 0) else half - 1 for name in NAMES for d in (0, 1)
    }

    def message(name, d, k):
        i = here.ids[(1 - k) if d == 0 else (k - 1)]
        a = NAMES.index(name)
        src = blocks[name] if k == 1 else lands[name].at[i]
        return pltpu.make_async_remote_copy(
            src_ref=src,
            dst_ref=lands[name].at[i],
            send_sem=ring_send.at[a, d, k - 1],
            recv_sem=ring_recv.at[a, d, k - 1],
            device_id=(here.r, here.ring[d]),
            device_id_type=MESH,
        )

    def load(name, k):
        i = here.ids[k]
        a = NAMES.index(name)
        src = lands[name].at[i]
        return pltpu.make_async_copy(
            src.at[pl.ds(0, rows[name])],
            into[name].at[pl.ds(pl.multiple_of(i * rows[name], 16), rows[name])],
            load_sem.at[a, k + half],
        )

    def load_small(k):
        src = q_land.at[here.ids[k]]
        return pltpu.make_async_copy(
            src.at[pl.ds(rows["q"], 16), pl.ds(0, rows["q"])],
            small.at[here.ids[k]],
            load_sem.at[5, k + half],
        )

    def keep_own(name):
        return pltpu.make_async_copy(
            blocks[name], lands[name].at[here.s], load_sem.at[6, NAMES.index(name)]
        )

    def begin(name):
        for d in (0, 1):
            message(name, d, 1).start()
        keep_own(name).start()

    def serve(name, k):
        for d in (0, 1):
            if k <= reach[name, d]:
                message(name, d, k).wait_recv()
                if k < reach[name, d]:
                    message(name, d, k + 1).start()
                if name in into:
                    load(name, -k if d == 0 else k).start()
                if name == "q":
                    load_small(-k if d == 0 else k).start()

    def own_kept(name):
        keep_own(name).wait()
        if name in into:
            load(name, 0).start()
        if name == "q":
            load_small(0).start()

    def came(name):
        found = [0]
        for k in range(1, half + 1):
            found += [-k] * (k <= reach[name, 0]) + [k] * (k <= reach[name, 1])
        return found

    def loaded(name):
        for k in came(name):
            load(name, k).wait()
            if name == "q":
                load_small(k).wait()

    outs = []

    def save(src, dst):
        c = pltpu.make_async_copy(src, dst, out_sem.at[len(outs)])
        c.start()
        outs.append(c)

    def fetch(src, dst, i):
        c = pltpu.make_async_copy(src, dst, load_sem.at[7, i])
        c.start()
        return c

    def rows16(count, body):
        @pl.loop(0, count // 16)
        def _(i):
            body(pl.ds(pl.multiple_of(i * 16, 16), 16))

    own_width = wq.shape[1] // 3
    pairs = own_width // 128
    block = slots // 2
    units = g_blk.shape[1]
    rep = RepLinks(here, rep_send, rep_recv)
    held = {}
    lane = lax.broadcasted_iota(jnp.int32, (1, 128), 1)
    low = first_half((slots, 128))

    class XSlots:
        class at:
            def __class_getitem__(cls, g):
                return xs.at[pl.ds(g * slots, slots)]

    windows = []
    for t in range(3 * pairs):
        part, tt = t // pairs, t % pairs
        for h in (0, 1):
            first = part * width + (2 * tt + h) * 4 * 64
            i = len(windows)
            dst = hid.at[pl.ds(slots * (i // 8), slots), pl.ds(128 * (i % 8), 128)]
            start = pl.multiple_of(first + (here.r // 2) * 128, 128)
            c = pltpu.make_async_copy(w_qkv.at[:, pl.ds(start, 128)], dst, rep_send.at[14 + i])
            c.start()
            windows.append((c, dst))
    own_x = fetch(tok, xs.at[pl.ds(0, slots)], 0)
    own_c = fetch(cot, ysend, 1)

    long0, long1 = lens[0], lens[1]
    spot = lax.broadcasted_iota(jnp.int32, (8, slots), 1)
    end = jnp.where(spot < block, long0, long1 + block)
    row = lax.broadcasted_iota(jnp.int32, (8, slots), 0)
    together = jnp.where(seqs[0] == seqs[1], 1.0, 0.0)
    metas[0] = jnp.where(row == 0, jnp.where(spot < end, 1.0, 0.0), together)

    base = vt[...].astype(F32)
    side = (here.s % 2) * 64
    wide = rows["q"]
    head = pltpu.roll(base, (side - here.r * 64 + wide) % wide, 1)
    keys = pltpu.roll(base, (side - here.r * ROT + wide) % wide, 1)
    line = lax.broadcasted_iota(jnp.int32, (16, wide), 0)
    place = lax.broadcasted_iota(jnp.int32, (16, wide), 1)
    inside = (place >= side) & (place < side + 64)
    key_inside = (place >= side) & (place < side + ROT)
    own_small = jnp.where(
        line < 4,
        base,
        jnp.where(
            (line < 6) & inside, head, jnp.where((line == 6) & key_inside, keys, 0.0)
        ),
    )
    q_blk[wide : wide + 16, :] = jnp.zeros((16, q_blk.shape[1]), BF16)
    q_blk[wide : wide + 16, 0:wide] = own_small.astype(BF16)

    here.greet()
    begin("o")
    held["m"] = rep.gather_start(0, metas.at[0], metas)
    held["x"] = rep.gather_start(3, tok, XSlots)
    odd = (jnp.zeros((slots, 128), jnp.int32) + here.r % 2) == 1
    for t in range(3 * pairs):
        pair = []
        for h in (0, 1):
            c, ref = windows[2 * t + h]
            c.wait()
            value = ref[...].astype(F32)
            swapped = pltpu.roll(value, 64, 1)
            pair.append(jnp.where(odd, swapped, value) if h == 0 else jnp.where(odd, value, swapped))
        q_blk[0:wide, t * 128 : (t + 1) * 128] = jnp.where(low, pair[0], pair[1]).astype(BF16)
    begin("q")

    strips = []
    span = 384
    total = REPS * units
    piece = units // n
    for j in (0, 1):
        for s in range(n):
            o = s * REPS * piece + here.r * piece
            if s < half:
                off = o % 128
                a = o - off
            else:
                pad = (128 - (o + piece) % 128) % 128
                a = o + piece + pad - span
                off = span - piece - pad
            i = len(strips)
            ref = gates if j == 0 else ups
            dst = ref.at[pl.ds(slots * (s // 3), slots), pl.ds(span * (s % 3), span)]
            start = pl.multiple_of(j * total + a, 128)
            c = pltpu.make_async_copy(w_gu.at[:, pl.ds(start, span)], dst, rep_recv.at[14 + i])
            c.start()
            strips.append((c, dst, off))

    def select(j):
        for c, _, _ in strips[j * n : (j + 1) * n]:
            c.wait()
        out = (g_blk, u_blk)[j]
        for t in range(units // 128):
            whole = None
            for s in range(128 * t // piece, (128 * t + 127) // piece + 1):
                _, ref, off = strips[j * n + s]
                shift = (2 * span - (off + 128 * t - piece * s)) % span
                value = pltpu.roll(ref[...].astype(F32), shift, 1)[:, :128]
                first = s * piece - 128 * t
                whole = value if whole is None else jnp.where(lane >= first, value, whole)
            out[:, t * 128 : (t + 1) * 128] = whole.astype(BF16)

    def sel_g():
        select(0)
        begin("g")

    def sel_u():
        select(1)
        begin("u")

    def pass_m():
        held["m"] = rep.gather_pass(0, metas, held["m"])

    def pass_x():
        held["x"] = rep.gather_pass(3, XSlots, held["x"])

    def mask_cot():
        own_c.wait()
        for j in range(2):
            count = (long0, long1)[j]

            def chunk(at, j=j, count=count):
                first = lax.broadcasted_iota(jnp.int32, (16, width), 0) + at.start
                at = pl.ds(pl.multiple_of(at.start + j * block, 16), 16)
                value = ysend[at, :].astype(F32)
                ysend[at, :] = jnp.where(first < count, value, 0.0).astype(BF16)

            rows16(block, chunk)
        fetch(ysend, dyl_out.at[0], 2).wait()
        held["d"] = rep.gather_start(6, dyl_out.at[0], dyl_out)

    def pass_d():
        held["d"] = rep.gather_pass(6, dyl_out, held["d"])

    def ln1():
        for c in held["m"] + held["x"]:
            c.wait_recv()
        own_x.wait()
        mine = held["x"][1]
        mine.wait_send()
        rep.sent = [c for c in rep.sent if c is not mine]
        own_kept("q")
        loaded("q")
        for s in range(n):
            vecs[0:8, s * rows["q"] : (s + 1) * rows["q"]] = small[s, 0:8, :].astype(F32)
        gain, shift = vecs[0:1, :], vecs[1:2, :]

        def chunk(at):
            xs[at, :] = layer_rows(xs[at, :].astype(F32), gain, shift).astype(BF16)

        rows16(REPS * slots, chunk)
        save(xs, a1_out)

    def lane_bias(row, t):
        w = rows["q"]
        a = vecs[row : row + 1, 2 * t * w : 2 * t * w + 128]
        return a + vecs[row : row + 1, (2 * t + 1) * w : (2 * t + 1) * w + 128]

    def attend(g):
        line = lax.broadcasted_iota(jnp.int32, (slots, slots), 0)
        column = lax.broadcasted_iota(jnp.int32, (slots, slots), 1)
        here_rows = pl.ds(g * slots, slots)
        acc[...] = dot(xs[here_rows, :], wq[...])
        valid = metas[g, 0:1, :]
        same = metas[g, 1:2, :]
        for j in range(3):
            tabs[j, :block, :] = tables[j, :block, :]
            tabs[j, block:, :] = jnp.where(
                same[:, :128] > 0.5, tables[j, block:, :], tables[j, :block, :]
            )
        apart = (line >= block) & (column < block) & (same < 0.5)
        open_ = (column <= line) & jnp.logical_not(apart) & ((valid > 0.5) | (line == column))
        mask[...] = jnp.where(open_, 0.0, -1e30)
        for t in range(3 * pairs):
            part, tt = t // pairs, t % pairs
            tile = acc[:, t * 128 : (t + 1) * 128] + lane_bias((4, 6, 5)[part], tt)
            if part < 2:
                tile = (
                    tile * tabs[0]
                    + pltpu.roll(tile, 120, 1) * tabs[1]
                    + pltpu.roll(tile, 8, 1) * tabs[2]
                )
            (qs, ks, vs)[part][g, tt] = tile.astype(BF16)
        low_low = first_half((1, 128)).astype(F32).astype(BF16)
        high_low = (1.0 - first_half((1, 128)).astype(F32)).astype(BF16)
        for t in range(pairs):
            qt, kt, vt_ = qs[g, t], ks[g, t], vs[g, t]
            mixed = []
            for h in (0, 1):
                mine = low_low if h == 0 else high_low
                sc = dot_rt(qt * mine, kt) * (1.0 / 8.0) + mask[...]
                e = jnp.exp(sc - jnp.max(sc, axis=1, keepdims=True))
                p = (e / jnp.sum(e, axis=1, keepdims=True)).astype(BF16)
                ps[g, 2 * t + h] = p
                mixed.append(dot(p, vt_))
            mix = jnp.where(low, mixed[0], mixed[1])
            attn[here_rows, t * 128 : (t + 1) * 128] = mix.astype(BF16)
            attn_t[t * 128 : (t + 1) * 128, here_rows] = mix.T.astype(BF16)

    def out_far():
        own_kept("o")
        loaded("o")
        for g in (0, 1):
            csend[g] = dot(attn[(g + 2) * slots : (g + 3) * slots, :], wo[...]).astype(BF16)
        held["core"] = rep.start(9, csend, crecv, here.core)

    def out_y():
        held["core"].wait_recv()
        ysend[...] = (dot(attn[slots : 2 * slots, :], wo[...]) + crecv[1].astype(F32)).astype(BF16)
        held["y"] = rep.start(10, ysend, yrecv, here.across)

    def out_own():
        resid[...] = dot(attn[0:slots, :], wo[...]) + crecv[0].astype(F32)
        held["tok"] = fetch(tok, crecv.at[0], 3)
        save(qs, q_out)
        save(ks, k_out)
        save(vs, v_out)
        save(ps, p_out)
        save(attn_t, attn_out)
        save(metas, meta_out)

    def ln2():
        held["tok"].wait()
        held["y"].wait_recv()
        gain, shift = vecs[2:3, :], vecs[3:4, :]

        def chunk(at):
            x = resid[at, :] + yrecv[at, :].astype(F32) + crecv[0, at, :].astype(F32)
            resid[at, :] = x
            a2s[0, at, :] = layer_rows(x, gain, shift).astype(BF16)

        rows16(slots, chunk)
        held["a"] = rep.gather_start(11, a2s.at[0], a2s)
        save(resid, resid_out)

    def pass_a():
        held["a"] = rep.gather_pass(11, a2s, held["a"])

    def feed(g):
        if g == 0:
            own_kept("g")
            own_kept("u")
            for c in held["a"]:
                c.wait_recv()
            loaded("g")
            loaded("u")
            save(a2s, a2_out)
        at = pl.ds(g * slots, slots)
        gate = dot(a2s[g], wg[...])
        gates[at, :] = gate.astype(BF16)
        up = dot(a2s[g], wu[...])
        ups[at, :] = up.astype(BF16)
        act = gate * jax.nn.sigmoid(gate) * up
        for j in range(act.shape[1] // 128):
            hid[j * 128 : (j + 1) * 128, at] = act[:, j * 128 : (j + 1) * 128].T.astype(BF16)
        if g == REPS - 1:
            save(gates, gate_out)
            save(ups, up_out)
            save(hid, hid_out)

    steps = {
        "sg": sel_g, "su": sel_u, "bd": lambda: begin("d"), "pm": pass_m, "px": pass_x, "cot": mask_cot,
        "pd": pass_d, "ln1": ln1, "of": out_far, "oy": out_y, "oo": out_own, "ln2": ln2, "pa": pass_a,
    }
    for name in FORE_ORDER:
        if name in steps:
            steps[name]()
        elif name[:2] == "at":
            attend(int(name[2]))
        elif name[:2] == "fd":
            feed(int(name[2]))
        else:
            serve(name[0], int(name[1]))
    for c in held["d"]:
        c.wait_recv()
    keep_own("d").wait()
    for name in NAMES:
        for d in (0, 1):
            for k in range(1, reach[name, d] + 1):
                message(name, d, k).wait_send()
    rep.finish()
    for c in outs:
        c.wait()


def forward_call(n, weights, tok, cot, vt, seqs, lens, tables):
    slots, width = tok.shape
    w_qkv, w_out, w_gu, w_down = weights
    lanes, units = w_qkv.shape[1] // REPS, w_gu.shape[1] // 2 // REPS
    rows, own_width = width // n, lanes // 3
    all_slots = REPS * slots
    pairs = own_width // 128
    half = n // 2
    S = jax.ShapeDtypeStruct
    heads = (REPS, pairs, slots, 128)
    out_shape = [
        S((n, rows + 16, lanes), BF16),
        S((n, w_out.shape[0] // REPS, width), BF16),
        S((n, rows, units), BF16),
        S((n, rows, units), BF16),
        S((n, w_down.shape[0] // REPS, width), BF16),
        S((all_slots, width), BF16),
        S(heads, BF16),
        S(heads, BF16),
        S(heads, BF16),
        S((REPS, 2 * pairs, slots, slots), BF16),
        S((own_width, all_slots), BF16),
        S((slots, width), F32),
        S((REPS, slots, width), BF16),
        S((all_slots, units), BF16),
        S((all_slots, units), BF16),
        S((units, all_slots), BF16),
        S((REPS, slots, width), BF16),
        S((REPS, 8, slots), F32),
    ]
    V = pltpu.VMEM
    scratch = [
        V((rows + 16, lanes), BF16),
        V((rows, units), BF16),
        V((rows, units), BF16),
        V((width, lanes), BF16),
        V((own_width, width), BF16),
        V((width, units), BF16),
        V((width, units), BF16),
        V((all_slots, width), BF16),
        V(heads, BF16),
        V(heads, BF16),
        V(heads, BF16),
        V((REPS, 2 * pairs, slots, slots), BF16),
        V((all_slots, own_width), BF16),
        V((own_width, all_slots), BF16),
        V((slots, lanes), F32),
        V((2, slots, width), BF16),
        V((2, slots, width), BF16),
        V((slots, width), BF16),
        V((slots, width), BF16),
        V((slots, width), F32),
        V((REPS, slots, width), BF16),
        V((all_slots, units), BF16),
        V((all_slots, units), BF16),
        V((units, all_slots), BF16),
        V((REPS, 8, slots), F32),
        V((3, slots, 128), F32),
        V((slots, slots), F32),
        V((n, 16, rows), BF16),
        V((8, width), F32),
        pltpu.SemaphoreType.DMA((5, 2, half)),
        pltpu.SemaphoreType.DMA((5, 2, half)),
        pltpu.SemaphoreType.DMA((8, 2 * half + 1)),
        pltpu.SemaphoreType.DMA((14 + 6 * pairs,)),
        pltpu.SemaphoreType.DMA((14 + 2 * n,)),
        pltpu.SemaphoreType.DMA((12,)),
    ]
    anywhere = pl.BlockSpec(memory_space=pltpu.HBM)
    inside = pl.BlockSpec(memory_space=pltpu.VMEM)
    scalars = pl.BlockSpec(memory_space=pltpu.SMEM)
    return pl.pallas_call(
        functools.partial(forward_kernel, n),
        out_shape=out_shape,
        in_specs=[anywhere] * 6 + [inside, scalars, scalars, inside],
        out_specs=[anywhere] * len(out_shape),
        scratch_shapes=scratch,
        compiler_params=pltpu.CompilerParams(
            collective_id=1, has_side_effects=True, vmem_limit_bytes=VMEM_LIMIT
        ),
    )(*weights, tok, cot, vt, seqs, lens, tables)


PARTS = ("d", "g", "u", "x", "y", "o", "s")
PARTS_UP = {"d": False, "g": True, "u": False, "x": True, "y": True, "o": False, "s": True}
BACK_ORDER = (
    "d0", "dh0", "dh1", "dh2", "dh3", "g0", "d1", "u0", "far2", "near2", "mlpf", "g1", "mlpn", "d2", "u1",
    "ln2", "g2", "pass", "ey2", "ldrl", "d3", "at0", "u2", "at1", "g3", "at2", "act", "at3", "x0", "far1",
    "y0", "fd", "u3", "fg", "x1", "near1", "y1", "o0", "hd", "x2", "hg", "o1", "fu", "x3", "y2", "sums", "s0",
    "o2", "s1", "hu", "fx", "s2", "o3", "y3", "s3", "fs", "fo", "hs", "hx", "fy", "ho", "hy",
)


def norm_rows_back(x, gain, grad):
    center = x - jnp.mean(x, axis=1, keepdims=True)
    inv = lax.rsqrt(jnp.mean(center * center, axis=1, keepdims=True) + 1e-05)
    normal = center * inv
    e = grad * gain
    cross = jnp.mean(e * normal, axis=1, keepdims=True)
    return inv * (e - jnp.mean(e, axis=1, keepdims=True) - normal * cross), normal


def backward_kernel(
    n,
    q_land, o_land, g_land, u_land, d_land, a1_in, q_in, k_in, v_in, p_in, attn_in,
    resid_in, a2_in, gate_in, up_in, hid_in, dyl_in, tok, metas, tables,
    act_out, grad_out, d_sum, g_sum, u_sum, x_sum, y_sum, o_sum, s_sum,
    land_d, land_g, land_u, land_x, land_y, land_o, land_s, core_land, y_land, drl_land,
    dyl, hid, wd, gates, ups, a2, a1, wst, wo, attn_t, heads, probs, dqkv, datt, csend, crecv,
    ysend, ysend2, yrecv, own, resid, outp, stage, rstage, sstage, small, vecs, sums, headsums, tabs,
    ring_send, ring_recv, load_sem, rep_send, rep_recv, stream_sem, rstage_sem, fin_sem,
):
    here = Place(n)
    half = here.half
    slots, width = tok.shape
    rows = width // n
    units = gates.shape[1]
    lanes = dqkv.shape[1]
    own_width = lanes // 3
    pairs = own_width // 128
    lands = dict(zip(PARTS, (land_d, land_g, land_u, land_x, land_y, land_o, land_s)))
    finals = dict(zip(PARTS, (d_sum, g_sum, u_sum, x_sum, y_sum, o_sum, s_sum)))
    shape = {name: lands[name].shape[2:] for name in PARTS}
    reach = {
        (name, d): half if PARTS_UP[name] == (d == 0) else half - 1 for name in PARTS for d in (0, 1)
    }
    rep = RepLinks(here, rep_send, rep_recv)

    def fetch(src, dst, i):
        c = pltpu.make_async_copy(src, dst, load_sem.at[i])
        c.start()
        return c

    def block_of(i, size):
        return pl.ds(pl.multiple_of(i * size, 16), size)

    def lanes_of(i, size):
        return pl.ds(pl.multiple_of(i * size, 128), size)

    def term(name, i):
        if name == "d":
            return dot(hid[block_of(i, shape["d"][0]), :], dyl[...])
        if name in ("g", "u"):
            return dot_lt(a2[:, lanes_of(i, rows)], (gates if name == "g" else ups)[...])
        if name == "x":
            return dot_lt(a1[:, lanes_of(i, rows)], dqkv[:, : lanes // 2])
        if name == "y":
            return dot_lt(a1[:, lanes_of(i, rows)], dqkv[:, lanes // 2 :])
        if name == "o":
            return dot(attn_t[block_of(i, shape["o"][0]), :], wd[: dyl.shape[0], :])
        return sums[i]

    def corner(ref, name):
        return ref.at[pl.ds(0, shape[name][0]), pl.ds(0, shape[name][1])]

    def message(name, d, k, src):
        a = PARTS.index(name)
        return pltpu.make_async_remote_copy(
            src_ref=src,
            dst_ref=lands[name].at[d, k - 1],
            send_sem=ring_send.at[a, d, k - 1],
            recv_sem=ring_recv.at[a, d, k - 1],
            device_id=(here.r, here.ring[d]),
            device_id_type=MESH,
        )

    def landed(name, d, k):
        message(name, d, k, lands[name].at[d, k - 1]).wait_recv()
        dst = sstage.at[2 + d] if name == "s" else corner(rstage.at[d], name)
        c = pltpu.make_async_copy(lands[name].at[d, k - 1], dst, rstage_sem.at[d])
        c.start()
        return c, dst

    flying = {}
    turn = [0, 0]

    def serve(name, j):
        hops = {}
        for d in (0, 1):
            k = half - j if reach[name, d] == half else half - 1 - j
            if k >= 1:
                hops[d] = k
        got = {d: landed(name, d, k + 1) for d, k in hops.items() if j > 0}
        for d, k in hops.items():
            if name == "s":
                slot, key = sstage.at[d], ("s", d)
            else:
                turn[d] = 1 - turn[d]
                slot, key = corner(stage.at[d, turn[d]], name), (d, turn[d])
            part = term(name, here.ids[k if d == 0 else -k])
            if d in got:
                got[d][0].wait()
                part = part + got[d][1][...].astype(F32)
            if key in flying:
                flying.pop(key).wait_send()
            slot[...] = part.astype(slot.dtype)
            flying[key] = message(name, d, k, slot)
            flying[key].start()

    opened = {}

    def finish(name):
        got = [landed(name, d, 1) for d in (0, 1)]
        part = term(name, here.ids[0])
        for c, ref in got:
            c.wait()
            part = part + ref[...].astype(F32)
        i = PARTS.index(name)
        ref = sstage.at[4] if name == "s" else corner(rstage.at[0], name)
        ref[...] = part.astype(ref.dtype)
        c = pltpu.make_async_copy(ref, finals[name].at[0], fin_sem.at[i])
        c.start()
        c.wait()
        opened[name] = rep.gather_start(3 * i, finals[name].at[0], finals[name])

    def hand_on(name):
        opened[name] = rep.gather_pass(3 * PARTS.index(name), finals[name], opened[name])

    base = 3 * len(PARTS)

    def stream(names, body):
        def copies(s, slot):
            found = []
            for j, name in enumerate(names):
                land = {"q": q_land, "g": g_land, "u": u_land}[name]
                found.append(
                    pltpu.make_async_copy(
                        land.at[s, pl.ds(0, rows)],
                        wst.at[slot, j, :, pl.ds(0, land.shape[2])],
                        stream_sem.at[slot, j],
                    )
                )
            return found

        for c in copies(0, 0):
            c.start()

        @pl.loop(0, n)
        def _(s):
            slot = s % 2

            @pl.when(s + 1 < n)
            def _():
                for c in copies(s + 1, 1 - slot):
                    c.start()

            for c in copies(s, slot):
                c.wait()
            body(s, slot)

    def exchange_core(i, k):
        return rep.start(base + i, csend, core_land.at[k], here.core)

    def exchange_y(i, k, src):
        return rep.start(base + i, src, y_land.at[k], here.across)

    def drop_send(c):
        c.wait_send()
        rep.sent = [x for x in rep.sent if x is not c]

    here.greet()
    c_hid = fetch(hid_in, hid, 0)
    c_dyl = fetch(dyl_in, dyl, 1)
    c_wd = fetch(d_land, wd, 2)
    c_gate = fetch(gate_in, gates, 3)
    c_up = fetch(up_in, ups, 4)
    c_a2 = fetch(a2_in, a2, 5)
    c_small = fetch(q_land.at[:, pl.ds(rows, 16), pl.ds(0, rows)], small, 9)
    c_res = fetch(resid_in, resid, 8)
    out_rows = o_land.shape[1]
    c_wo = [fetch(o_land.at[i], wo.at[pl.ds(i * out_rows, out_rows)], 32 + i) for i in range(n)]
    c_att = fetch(attn_in, attn_t, 14)
    c_a1 = fetch(a1_in, a1, 7)
    c_hid.wait()
    c_dyl.wait()
    low_rows, high_rows = pl.ds(0, 2 * slots), pl.ds(2 * slots, 2 * slots)
    halves = (
        first_half((1, 128)).astype(F32).astype(BF16),
        (1.0 - first_half((1, 128)).astype(F32)).astype(BF16),
    )
    block = slots // 2
    held = {}

    def rows16(count, body):
        @pl.loop(0, count // 16)
        def _(i):
            body(pl.ds(pl.multiple_of(i * 16, 16), 16))

    def feed_back(g):
        if g == 0:
            for c in (c_wd, c_gate, c_up):
                c.wait()
        at = pl.ds(g * slots, slots)
        dh = dot_rt(dyl[at, :], wd[...])
        gate, up = gates[at, :].astype(F32), ups[at, :].astype(F32)
        sig = jax.nn.sigmoid(gate)
        gates[at, :] = (dh * up * sig * (1.0 + gate * (1.0 - sig))).astype(BF16)
        ups[at, :] = (dh * gate * sig).astype(BF16)

    def a2_product(at, slot):
        return dot_rt(gates[at, :], wst[slot, 0, :, :units]) + dot_rt(ups[at, :], wst[slot, 1, :, :units])

    def put_far(part, s):
        csend[0, :, lanes_of(s, rows)] = part[:slots]
        csend[1, :, lanes_of(s, rows)] = part[slots:]

    def far2():
        stream(("g", "u"), lambda s, slot: put_far(a2_product(high_rows, slot).astype(BF16), s))
        held["core1"] = exchange_core(0, 0)

    def put_near(part, s, ref):
        at = lanes_of(s, rows)
        ref[:, at] = part[:slots] + crecv[0, :, at].astype(F32)
        ysend[:, at] = (part[slots:] + crecv[1, :, at].astype(F32)).astype(BF16)

    def near2():
        held["core1"].wait_recv()
        fetch(core_land.at[0], crecv, 10).wait()
        stream(("g", "u"), lambda s, slot: put_near(a2_product(low_rows, slot), s, own))
        held["y1"] = exchange_y(1, 0, ysend)

    def mlpf():
        drop_send(held["core1"])
        for g in (0, 1):
            csend[g] = dot_lt(hid[:, (g + 2) * slots : (g + 3) * slots], wd[...]).astype(BF16)
        held["core2"] = exchange_core(2, 1)

    def mlpn():
        held["core2"].wait_recv()
        fetch(core_land.at[1], crecv, 13).wait()
        ysend2[...] = (dot_lt(hid[:, slots : 2 * slots], wd[...]) + crecv[1].astype(F32)).astype(BF16)
        c_res.wait()
        outp[...] = resid[...] + dot_lt(hid[:, :slots], wd[...]) + crecv[0].astype(F32)

    def ln2():
        c_small.wait()
        for s in range(n):
            vecs[0:8, s * rows : (s + 1) * rows] = small[s, 0:8, :].astype(F32)
        headsums[...] = jnp.zeros_like(headsums)
        vecs[8:40, :] = jnp.zeros((32, width), F32)
        held["y1"].wait_recv()
        fetch(y_land.at[0], yrecv, 11).wait()
        drop_send(held["y1"])
        gain = vecs[2:3, :]

        def chunk(at):
            da = own[at, :] + yrecv[at, :].astype(F32)
            back, normal = norm_rows_back(resid[at, :], gain, da)
            prod = da * normal
            vecs[24:32, :] += prod[:8] + prod[8:]
            vecs[32:40, :] += da[:8] + da[8:]
            dr = dyl[at, :].astype(F32) + back
            own[at, :] = dr
            ysend[at, :] = dr.astype(BF16)

        rows16(slots, chunk)
        fetch(ysend, drl_land.at[0], 12).wait()
        held["drl"] = rep.gather_start(base + 3, drl_land.at[0], drl_land)

    def pass_on():
        held["drl"] = rep.gather_pass(base + 3, drl_land, held["drl"])

    def ldrl():
        for c in held["drl"]:
            c.wait_recv()
        loads = [fetch(drl_land.at[g], wd.at[pl.ds(g * slots, slots)], 16 + g) for g in range(REPS)]
        for c in loads + c_wo + [c_att]:
            c.wait()

    def ey2():
        held["y2"] = exchange_y(6, 1, ysend2)

    def head_copies(g, slot):
        found = [
            pltpu.make_async_copy(ref.at[g], heads.at[slot, j], stream_sem.at[slot, 2 + j])
            for j, ref in enumerate((q_in, k_in, v_in))
        ]
        return found + [pltpu.make_async_copy(p_in.at[g], probs.at[slot], stream_sem.at[slot, 5])]

    def turn_back(tile):
        return tile * tabs[0] - pltpu.roll(tile, 120, 1) * tabs[1] - pltpu.roll(tile, 8, 1) * tabs[2]

    def attend_back(g):
        slot = g % 2
        if g == 0:
            for c in head_copies(0, 0):
                c.start()
        if g + 1 < REPS:
            for c in head_copies(g + 1, 1 - slot):
                c.start()
        at = pl.ds(g * slots, slots)
        datt[...] = dot_rt(wd[at, :], wo[...]).astype(BF16)
        same = metas[g, 1:2, :128]
        for j in range(3):
            tabs[j, :block, :] = tables[j, :block, :]
            tabs[j, block:, :] = jnp.where(same > 0.5, tables[j, block:, :], tables[j, :block, :])
        for c in head_copies(g, slot):
            c.wait()
        low = first_half((slots, 128))
        for t in range(pairs):
            da = datt[:, t * 128 : (t + 1) * 128]
            qt, kt, vt = heads[slot, 0, t], heads[slot, 1, t], heads[slot, 2, t]
            both = []
            for h in (0, 1):
                p = probs[slot, 2 * t + h]
                pf = p.astype(F32)
                dp = dot_rt(da * halves[h], vt)
                delta = jnp.sum(dp * pf, axis=1, keepdims=True)
                ds = (pf * (dp - delta)).astype(BF16)
                both.append((dot(ds, kt), dot_lt(ds, qt), dot_lt(p, da)))
            dq, dk, dv = [jnp.where(low, a, b) for a, b in zip(*both)]
            dq, dk = turn_back(dq * (1.0 / 8.0)), turn_back(dk * (1.0 / 8.0))
            for j, value in enumerate((dq, dk, dv)):
                row = j * pairs + t
                headsums[row : row + 1, :] += jnp.sum(value, axis=0, keepdims=True)
                first = j * own_width + t * 128
                dqkv[at, first : first + 128] = value.astype(BF16)

    def far1():
        drop_send(held["core2"])

        def body(s, slot):
            put_far(dot_rt(dqkv[high_rows, :], wst[slot, 0, :, :lanes]).astype(BF16), s)

        stream(("q",), body)
        held["core3"] = exchange_core(7, 2)

    def act():
        held["y2"].wait_recv()
        fetch(y_land.at[1], yrecv, 20).wait()

        def chunk(at):
            yrecv[at, :] = (outp[at, :] + yrecv[at, :].astype(F32)).astype(BF16)

        rows16(slots, chunk)
        fetch(yrecv, act_out, 21).wait()

    def near1():
        held["core3"].wait_recv()
        fetch(core_land.at[2], crecv, 22).wait()

        def body(s, slot):
            put_near(dot_rt(dqkv[low_rows, :], wst[slot, 0, :, :lanes]), s, resid)

        stream(("q",), body)
        held["y3"] = exchange_y(8, 2, ysend)
        held["tok"] = fetch(tok, crecv.at[1], 23)

    def add_up():
        held["tok"].wait()
        held["y3"].wait_recv()
        fetch(y_land.at[2], yrecv, 24).wait()
        gain = vecs[0:1, :]

        def chunk(at):
            da = resid[at, :] + yrecv[at, :].astype(F32)
            back, normal = norm_rows_back(crecv[1, at, :].astype(F32), gain, da)
            prod = da * normal
            vecs[8:16, :] += prod[:8] + prod[8:]
            vecs[16:24, :] += da[:8] + da[8:]
            yrecv[at, :] = (own[at, :] + back).astype(BF16)

        rows16(slots, chunk)
        held["grad"] = fetch(yrecv, grad_out, 25)
        sums[...] = jnp.zeros_like(sums)
        for j in range(4):
            total = jnp.sum(vecs[8 + 8 * j : 16 + 8 * j, :], axis=0, keepdims=True)
            for s in range(n):
                sums[s, j : j + 1, :] = total[:, s * rows : (s + 1) * rows]
        for s in range(n):
            for j, part in ((4, 0), (5, 2), (6, 1)):
                row = part * pairs + s // 2
                sums[s, j : j + 1, 0:128] = headsums[row : row + 1, :] * halves[s % 2].astype(F32)

    steps = {
        "far2": far2, "near2": near2, "mlpf": mlpf, "mlpn": mlpn, "ln2": ln2, "pass": pass_on,
        "ldrl": ldrl, "ey2": ey2, "far1": far1, "act": act, "near1": near1, "sums": add_up,
    }
    for name in BACK_ORDER:
        if name in steps:
            steps[name]()
        elif name[:2] == "dh":
            feed_back(int(name[2]))
        elif name[:2] == "at":
            attend_back(int(name[2]))
        elif name[0] == "f":
            finish(name[1])
        elif name[0] == "h":
            hand_on(name[1])
        else:
            if name == "g0":
                c_a2.wait()
            if name == "x0":
                c_a1.wait()
            serve(name[0], int(name[1]))
    for name in PARTS:
        for c in opened[name]:
            c.wait_recv()
    held["grad"].wait()
    rep.finish()
    for c in flying.values():
        c.wait_send()


def backward_call(n, lands, kept, tok, meta, tables):
    slots, width = tok.shape
    q_land, o_land, g_land, u_land, d_land = lands
    a1, qs, ks, vs, ps, attn_t, resid, a2, gate, up, hid, dyl = kept
    all_slots, units = gate.shape
    lanes = q_land.shape[2]
    pairs = lanes // 3 // 128
    half = n // 2
    rows = width // n
    S = jax.ShapeDtypeStruct
    block = {
        "d": (d_land.shape[1], width),
        "g": (rows, units),
        "u": (rows, units),
        "x": (rows, lanes // 2),
        "y": (rows, lanes // 2),
        "o": (o_land.shape[1], width),
        "s": (8, rows),
    }
    kind = {name: F32 if name == "s" else BF16 for name in PARTS}
    out_shape = (
        [S((slots, width), BF16), S((slots, width), BF16)]
        + [S((REPS,) + block[name], kind[name]) for name in PARTS]
        + [S((2, half) + block[name], kind[name]) for name in PARTS]
        + [S((3, 2, slots, width), BF16), S((3, slots, width), BF16), S((REPS, slots, width), BF16)]
    )
    V = pltpu.VMEM
    scratch = [
        V((all_slots, width), BF16),
        V(hid.shape, BF16),
        V((units, width), BF16),
        V((all_slots, units), BF16),
        V((all_slots, units), BF16),
        V((all_slots, width), BF16),
        V((all_slots, width), BF16),
        V((2, 2, rows, lanes), BF16),
        V((lanes // 3, width), BF16),
        V((lanes // 3, all_slots), BF16),
        V((2, 3, pairs, slots, 128), BF16),
        V((2, 2 * pairs, slots, slots), BF16),
        V((all_slots, lanes), BF16),
        V((slots, lanes // 3), BF16),
        V((2, slots, width), BF16),
        V((2, slots, width), BF16),
        V((slots, width), BF16),
        V((slots, width), BF16),
        V((slots, width), BF16),
        V((slots, width), F32),
        V((slots, width), F32),
        V((slots, width), F32),
        V((2, 2, rows, width), BF16),
        V((2, rows, width), BF16),
        V((5, 8, rows), F32),
        V((n, 16, rows), BF16),
        V((40, width), F32),
        V((n, 8, rows), F32),
        V((16, 128), F32),
        V((3, slots, 128), F32),
        pltpu.SemaphoreType.DMA((len(PARTS), 2, half)),
        pltpu.SemaphoreType.DMA((len(PARTS), 2, half)),
        pltpu.SemaphoreType.DMA((32 + n,)),
        pltpu.SemaphoreType.DMA((30,)),
        pltpu.SemaphoreType.DMA((30,)),
        pltpu.SemaphoreType.DMA((2, 6)),
        pltpu.SemaphoreType.DMA((2,)),
        pltpu.SemaphoreType.DMA((len(PARTS),)),
    ]
    anywhere = pl.BlockSpec(memory_space=pltpu.HBM)
    inside = pl.BlockSpec(memory_space=pltpu.VMEM)
    out = pl.pallas_call(
        functools.partial(backward_kernel, n),
        out_shape=out_shape,
        in_specs=[anywhere] * 18 + [inside] * 2,
        out_specs=[anywhere] * len(out_shape),
        scratch_shapes=scratch,
        compiler_params=pltpu.CompilerParams(
            collective_id=2, has_side_effects=True, vmem_limit_bytes=VMEM_LIMIT
        ),
    )(q_land, o_land, g_land, u_land, d_land.reshape(units, width), a1, qs, ks, vs, ps, attn_t,
      resid, a2, gate, up, hid, dyl, tok, meta, tables)
    return out[:2], dict(zip(PARTS, out[2:9]))


def weave_kernel(n, rel, d_in, g_in, u_in, x_in, y_in, o_in, s_in, out_qkv, out_out, out_gu, out_down, out_small):
    step = pl.program_id(0)
    count = g_in.shape[1]
    lane = lax.broadcasted_iota(jnp.int32, (count, 128), 1)
    units = g_in.shape[2]
    piece = units // n

    @pl.when(step % 2 == 0)
    def _():
        out_down[...] = d_in[0].astype(F32)
        out_out[...] = o_in[0].astype(F32)

    def tile(ref, q, a):
        return ref[rel[q], :, a * 128 : (a + 1) * 128].astype(F32)

    def join(segments):
        whole = segments[0][1]
        for low, value in segments[1:]:
            whole = jnp.where(lane >= low, value, whole)
        return whole

    for side, ref in ((0, g_in), (1, u_in)):
        for j in range(REPS * units // 128):
            segments = []
            for c in range(128 * j // piece, (128 * j + 127) // piece + 1):
                s, q = c // REPS, c % REPS
                low, high = max(0, c * piece - 128 * j), min(128, (c + 1) * piece - 128 * j)
                start = 128 * j - piece * (c - s)
                a, m = start // 128, start % 128
                if low < 128 - m:
                    value = tile(ref, q, a)
                    segments.append((low, pltpu.roll(value, 128 - m, 1) if m else value))
                if high > 128 - m:
                    segments.append((max(low, 128 - m), pltpu.roll(tile(ref, q, a + 1), 128 - m, 1)))
            first = side * REPS * units + j * 128
            out_gu[:, first : first + 128] = join(segments)
    per = x_in.shape[2] // 64
    for t in range(out_qkv.shape[1] // 128):
        group = t // 2
        ref, at = (x_in, group) if group < per else (y_in, group - per)
        values = []
        for h in (0, 1):
            value = tile(ref, 2 * (t % 2) + h, at // 2)
            values.append((64 * h, pltpu.roll(value, 64, 1) if at % 2 != h else value))
        out_qkv[:, t * 128 : (t + 1) * 128] = join(values)

    @pl.when(step == 0)
    def _():
        out_small[...] = jnp.zeros_like(out_small)
        out_small[0:4, :] = s_in[0, 0:4, :] + s_in[1, 0:4, :] + s_in[2, 0:4, :] + s_in[3, 0:4, :]
        row = lax.broadcasted_iota(jnp.int32, (1, 128), 1)
        own = []
        for q in range(REPS):
            v = s_in[rel[q], 4:7, 0:128]
            own.append(v + pltpu.roll(v, 64, 1))
        for j in (0, 1):
            for p in (0, 1):
                out_small[4 + j : 5 + j, p * 128 : (p + 1) * 128] = jnp.where(
                    row < 64, own[2 * p][j : j + 1], own[2 * p + 1][j : j + 1]
                )
        keys = own[0][2:3]
        for q in range(1, REPS):
            keys = jnp.where(row >= q * ROT, pltpu.roll(own[q][2:3], q * ROT, 1), keys)
        out_small[6:7, 0:128] = keys


def weave_call(n, rel, parts):
    d, g, u, x, y, o, s = [parts[name] for name in PARTS]
    turns = 2 * REPS
    rows = g.shape[1]
    count = rows // turns
    S = jax.ShapeDtypeStruct

    def piece(a):
        return pl.BlockSpec((REPS, count, a.shape[2]), lambda i, rel: (0, i, 0))

    def slab(a):
        return pl.BlockSpec((1,) + a.shape[1:], lambda i, rel: (rel[i // 2], 0, 0))

    def lines(width):
        return pl.BlockSpec((count, width), lambda i, rel: (i, 0))

    def stack(a):
        return pl.BlockSpec(a.shape[1:], lambda i, rel: (i // 2, 0))

    lanes, units = 2 * REPS * x.shape[2], 2 * REPS * g.shape[2]
    return pl.pallas_call(
        functools.partial(weave_kernel, n),
        out_shape=[
            S((rows, lanes), F32),
            S((REPS * o.shape[1], o.shape[2]), F32),
            S((rows, units), F32),
            S((REPS * d.shape[1], d.shape[2]), F32),
            S(s.shape[1:], F32),
        ],
        grid_spec=pltpu.PrefetchScalarGridSpec(
            num_scalar_prefetch=1,
            grid=(turns,),
            in_specs=[slab(d), piece(g), piece(u), piece(x), piece(y), slab(o)]
            + [pl.BlockSpec(s.shape, lambda i, rel: (0, 0, 0))],
            out_specs=[
                lines(lanes),
                stack(o),
                lines(units),
                stack(d),
                pl.BlockSpec(s.shape[1:], lambda i, rel: (0, 0)),
            ],
        ),
        compiler_params=pltpu.CompilerParams(vmem_limit_bytes=VMEM_LIMIT),
    )(rel, d, g, u, x, y, o, s)


def core_swap(x):
    return lax.ppermute(x, "rep", [(0, 1), (1, 0), (2, 3), (3, 2)])


def y_swap(x):
    return lax.ppermute(x, "rep", [(0, 2), (1, 3), (2, 0), (3, 1)])


def rep_parts(x):
    across = y_swap(x)
    return [x, across, core_swap(x), core_swap(across)]


def rep_gather(x):
    return jnp.concatenate(rep_parts(x), axis=0)


def rep_reduce(a, w_dot, slots):
    far = core_swap(w_dot(a[2 * slots :]).astype(BF16))
    near = w_dot(a[: 2 * slots]) + far.astype(F32)
    return near[:slots] + y_swap(near[slots:].astype(BF16)).astype(F32)


def solution(mesh):
    n = mesh.shape["shard"]
    half_ring = n // 2
    order = list(range(0, n, 2)) + list(range(n - 1, 0, -2))
    place = [order.index(s) for s in range(n)]
    up_ring = [(order[i], order[(i + 1) % n]) for i in range(n)]
    down_ring = [(b, a) for a, b in up_ring]

    def hop(x, ring, sent):
        if len(sent) >= DEPTH:
            x, _ = lax.optimization_barrier((x, sent[-DEPTH]))
        x = lax.ppermute(x, "shard", ring)
        sent.append(x)
        return x

    def ring_ids():
        spot = jnp.array(place, jnp.int32)[lax.axis_index("shard")]
        table = jnp.array(order, jnp.int32)
        return {k: table[(spot + k) % n] for k in range(-half_ring, half_ring + 1)}

    def gather(x, ids, forward_extra, places, line):
        bufs = places(None, x, ids[0])
        up = down = x
        for k in range(1, half_ring + 1):
            go_up = k < half_ring or forward_extra
            go_down = k < half_ring or not forward_extra
            if go_up:
                up = hop(up, up_ring, line[0])
            if go_down:
                down = hop(down, down_ring, line[1])
            if go_up:
                bufs = places(bufs, up, ids[-k])
            if go_down:
                bufs = places(bufs, down, ids[k])
            yield
        return bufs

    def put(bufs, block, at):
        if bufs is None:
            bufs = jnp.zeros((n,) + block.shape, block.dtype)
        return lax.dynamic_update_index_in_dim(bufs, block, at, 0)

    def reduce(term, ids, forward_extra, line, kind=BF16):
        acc = {}
        for k in range(half_ring, 0, -1):
            for side, (ring, sign, extra) in enumerate(
                ((up_ring, 1, forward_extra), (down_ring, -1, not forward_extra))
            ):
                if k == half_ring and not extra:
                    continue
                part = term(ids[sign * k])
                if side in acc:
                    part = part + acc[side].astype(F32)
                acc[side] = hop(part.astype(kind), ring, line[side])
            yield
        return term(ids[0]) + acc[0].astype(F32) + acc[1].astype(F32)

    def run(chains, turns):
        done = {}
        for name in turns:
            for _ in range(n // 8):
                if name in done:
                    continue
                try:
                    next(chains[name])
                except StopIteration as stop:
                    done[name] = stop.value
        for name, chain in chains.items():
            while name not in done:
                try:
                    next(chain)
                except StopIteration as stop:
                    done[name] = stop.value
        return done

    def pick_columns(w, groups, width, r):
        chosen = [
            lax.select_n(
                r,
                *[
                    w[:, (g * REPS + q) * width : (g * REPS + q + 1) * width]
                    for q in range(REPS)
                ],
            )
            for g in range(groups)
        ]
        return jnp.concatenate(chosen, axis=1)

    def by_rep(parts, y, core):
        own, across, beside, both = parts
        low0 = lax.select(core == 0, own, beside)
        low1 = lax.select(core == 0, beside, own)
        high0 = lax.select(core == 0, across, both)
        high1 = lax.select(core == 0, both, across)
        return [
            lax.select(y == 0, low0, high0),
            lax.select(y == 0, low1, high1),
            lax.select(y == 0, high0, low0),
            lax.select(y == 0, high1, low1),
        ]

    def weave(parts, groups, width):
        pieces = [
            parts[q][:, g * width : (g + 1) * width]
            for g in range(groups)
            for q in range(REPS)
        ]
        return jnp.concatenate(pieces, axis=1).astype(F32)

    def on_device(
        tokens, cotangent, block_seq, block_len, vectors, key_bias, w_qkv, w_out, w_gate_up, w_down
    ):
        slots, features = tokens.shape
        blocks = block_seq.shape[0]
        block_size = slots // blocks
        head_dim = features // HEADS
        own_heads = HEADS // REPS
        own_width = own_heads * head_dim
        all_slots = REPS * slots
        scale = 1.0 / math.sqrt(head_dim)
        rows = features // n
        hidden_units = w_gate_up.shape[1] // 2
        own_hidden = hidden_units // REPS
        down_rows = w_down.shape[0] // REPS
        out_rows = w_out.shape[0] // REPS
        regroup = out_rows < head_dim
        r = lax.axis_index("rep")
        y, core = r // 2, r % 2
        ids = ring_ids()

        def mix_out(x):
            if not regroup:
                return x
            pairs = [
                (k * n + 4 * j + q, q * n + 4 * j + k)
                for k in range(REPS)
                for j in range(n // 4)
                for q in range(REPS)
            ]
            return lax.ppermute(x, BOTH, pairs)

        fast = blocks == 2 and down_rows % 16 == 0 and out_rows == head_dim and rows % 128 == 0
        own_valid = (
            jnp.arange(block_size, dtype=jnp.int32)[None, :] < block_len[:, None]
        ).reshape(-1)
        grad_output = cotangent.astype(F32) * own_valid[:, None].astype(F32)
        dyl_own = grad_output.astype(BF16)
        if fast:
            vt = jnp.concatenate(
                [vectors.T, jnp.pad(key_bias.T, ((0, 0), (0, rows - key_bias.shape[0])))], axis=0
            )
            vt = jnp.pad(vt, ((0, 9), (0, 0)))
            angles = np.arange(slots, dtype=np.float32)[:, None] * np.exp(
                np.arange(ROT // 2, dtype=np.float32) * np.float32(-2.0 * math.log(10000.0) / ROT)
            ).astype(np.float32)
            cosine, sine = np.cos(angles), np.sin(angles)
            rest = np.ones((slots, head_dim - ROT), np.float32)
            none = np.zeros((slots, ROT // 2), np.float32)
            tables = np.stack(
                [
                    np.concatenate([cosine, cosine, rest] * 2, axis=1),
                    np.concatenate([-sine, none, 0 * rest] * 2, axis=1),
                    np.concatenate([none, sine, 0 * rest] * 2, axis=1),
                ]
            ).astype(np.float32)
            weights = (w_qkv, w_out, w_gate_up, w_down)
            out = forward_call(
                n, weights, tokens, cotangent, vt, block_seq, block_len, jnp.asarray(tables)
            )
            q_land, o_land, g_land, u_land, d_land = out[:5]
            a1, qs, ks, vs, ps, attn, resid, a2, gate, up, hid, dyl_all, metas = out[5:]
            whole = (all_slots, features)
            (activations, grad_input), parts = backward_call(
                n,
                out[:5],
                (a1, qs, ks, vs, ps, attn, resid, a2.reshape(whole), gate, up, hid, dyl_all.reshape(whole)),
                tokens,
                metas,
                tables,
            )

            q = jnp.arange(REPS, dtype=jnp.int32)
            rel = jnp.where(q // 2 != y, 1, 0) + jnp.where(q % 2 != core, 2, 0)
            out_qkv, out_out, out_gate_up, out_down, sums = weave_call(n, rel.astype(jnp.int32), parts)
            out_vectors = sums[:6].T
            out_key = sums[6, : HEADS * ROT // n].reshape(-1, 1)
            return activations, grad_input, out_vectors, out_key, out_qkv, out_out, out_gate_up, out_down
        else:
            small = jnp.concatenate([vectors.T.reshape(-1), key_bias.reshape(-1)])
            lanes = 3 * own_width
            small_rows = -(-small.size // lanes)
            small_rows = -(-small_rows // 16) * 16
            small = jnp.pad(small, (0, small_rows * lanes - small.size)).reshape(small_rows, lanes)
            qkv_block = jnp.concatenate([pick_columns(w_qkv, 3 * own_heads, head_dim, r), small], axis=0)

            def put_qkv(bufs, block, at):
                a, b = (None, None) if bufs is None else bufs
                return put(a, block[:rows], at), put(b, block[rows:], at)

            out_block = mix_out(lax.dynamic_slice_in_dim(w_out, r * out_rows, out_rows, 0))
            gate_block = pick_columns(w_gate_up[:, :hidden_units], n, down_rows, r)
            up_block = pick_columns(w_gate_up[:, hidden_units:], n, down_rows, r)
            down_block = lax.dynamic_slice_in_dim(w_down, r * down_rows, down_rows, 0)
            line = ([], [])
            got = run(
                {
                    "q": gather(qkv_block, ids, True, put_qkv, line),
                    "o": gather(out_block, ids, False, put, line),
                    "g": gather(gate_block, ids, True, put, line),
                    "u": gather(up_block, ids, False, put, line),
                    "d": gather(down_block, ids, False, put, line),
                },
                "qoqoqoqoguguguguddddd",
            )
            wq, smalls = got["q"]
            wq = wq.reshape(features, lanes)
            smalls = smalls.reshape(n, -1).astype(F32)
            vec = smalls[:, : 6 * rows].reshape(n, 6, rows).transpose(1, 0, 2).reshape(6, features)
            key_full = smalls[:, 6 * rows : 6 * rows + HEADS * ROT // n].reshape(own_heads, REPS, ROT)
            key_own = lax.dynamic_index_in_dim(key_full, r, 1, keepdims=False)
            key_shift = jnp.pad(key_own, ((0, 0), (0, head_dim - ROT))).reshape(own_width)

            def own_heads_of(v):
                return lax.dynamic_index_in_dim(
                    v.reshape(own_heads, REPS, head_dim), r, 1, keepdims=False
                ).reshape(own_width)

            wo = got["o"].reshape(own_width, features)
            wg = got["g"].reshape(features, own_hidden)
            wu = got["u"].reshape(features, own_hidden)
            wd = got["d"].reshape(own_hidden, features)

            meta = jnp.concatenate([block_seq, block_len]).astype(F32)
            meta = jnp.pad(meta, (0, 128 - 2 * blocks)).reshape(1, 128)
            meta = jnp.concatenate(rep_parts(jnp.broadcast_to(meta, (8, 128))), axis=0)
            meta = meta.reshape(REPS, 8, 128)[:, 0, :]
            seqs = meta[:, :blocks].astype(jnp.int32)
            lens = meta[:, blocks : 2 * blocks].astype(jnp.int32)
            index = jnp.arange(blocks, dtype=jnp.int32)
            same = seqs[:, None, :] == seqs[:, :, None]
            earlier = jnp.sum(
                jnp.where((index[None, :] < index[:, None]) & same, 1, 0), axis=2
            ).astype(jnp.int32)
            offset = jnp.arange(block_size, dtype=jnp.int32)
            seq_slot = jnp.broadcast_to(seqs[:, :, None], (REPS, blocks, block_size)).reshape(REPS, slots)
            valid = (offset[None, None, :] < lens[:, :, None]).reshape(REPS, slots)
            positions = (earlier[:, :, None] * block_size + offset[None, None, :]).reshape(all_slots)
            slot_index = jnp.arange(slots, dtype=jnp.int32)
            allowed = (seq_slot[:, None, :] == seq_slot[:, :, None]) & (
                slot_index[None, :] <= slot_index[:, None]
            )[None]
            allowed = allowed & (valid[:, None, :] | (slot_index[None, :] == slot_index[:, None])[None])
            cosine, sine = turn_tables(positions)

            x_all = rep_gather(tokens)
            dyl = rep_gather(dyl_own)

            tokens_f = tokens.astype(F32)
            normal_one, inv_one = normalize(tokens_f)
            normal_all, _ = normalize(x_all.astype(F32))
            a1 = (normal_all * vec[0] + vec[1]).astype(BF16)
            projected = dot(a1, wq)
            head_shape = (all_slots, own_heads, head_dim)
            group_shape = (REPS, slots, own_heads, head_dim)
            q = rotate((projected[:, :own_width] + own_heads_of(vec[4])).reshape(head_shape), cosine, sine)
            k = rotate((projected[:, own_width : 2 * own_width] + key_shift).reshape(head_shape), cosine, sine)
            v = projected[:, 2 * own_width :] + own_heads_of(vec[5])
            q = q.astype(BF16).reshape(group_shape)
            k = k.astype(BF16).reshape(group_shape)
            v = v.astype(BF16).reshape(group_shape)
            scores = jnp.einsum("gshd,gthd->ghst", q, k, preferred_element_type=F32) * scale
            scores = jnp.where(allowed[:, None], scores, -1e30)
            exponent = jnp.exp(scores - jnp.max(scores, axis=-1, keepdims=True))
            probs = exponent / jnp.sum(exponent, axis=-1, keepdims=True)
            probs_low = probs.astype(BF16)
            attn = jnp.einsum("ghst,gthd->gshd", probs_low, v, preferred_element_type=F32)
            attn = attn.reshape(all_slots, own_width).astype(BF16)
            resid = tokens_f + rep_reduce(attn, lambda a: dot(a, wo), slots)
            normal_two, inv_two = normalize(resid)
            a2 = rep_gather((normal_two * vec[2] + vec[3]).astype(BF16))
            gate = dot(a2, wg)
            up = dot(a2, wu)
            sig = jax.nn.sigmoid(gate)
            hidden = (gate * sig * up).astype(BF16)

        def blocks_of(a):
            return a.reshape(all_slots, n, -1).transpose(1, 0, 2)

        hidden_b = blocks_of(hidden)
        activations = (resid + rep_reduce(hidden, lambda a: dot(a, wd), slots)).astype(BF16)
        grad_hidden = dot_rt(dyl, wd)
        grad_gate = (grad_hidden * up * sig * (1.0 + gate * (1.0 - sig))).astype(BF16)
        grad_up = (grad_hidden * gate * sig).astype(BF16)
        a2_b = blocks_of(a2)
        grad_gu = jnp.concatenate([grad_gate, grad_up], axis=1)
        wgu = jnp.concatenate([wg, wu], axis=1)
        grad_a2 = rep_reduce(grad_gu, lambda a: dot_rt(a, wgu), slots)
        grad_resid = grad_output + norm_back(grad_a2 * vec[2], normal_two, inv_two)
        drl = rep_gather(grad_resid.astype(BF16))
        attn_b = blocks_of(attn)
        d_attn = dot_rt(drl, wo).astype(BF16).reshape(group_shape)
        grad_v = jnp.einsum("ghst,gshd->gthd", probs_low, d_attn, preferred_element_type=F32)
        grad_p = jnp.einsum("gshd,gthd->ghst", d_attn, v, preferred_element_type=F32)
        delta = jnp.sum(grad_p * probs, axis=-1, keepdims=True)
        grad_s = (probs * (grad_p - delta)).astype(BF16)
        grad_q = jnp.einsum("ghst,gthd->gshd", grad_s, k, preferred_element_type=F32) * scale
        grad_k = jnp.einsum("ghst,gshd->gthd", grad_s, q, preferred_element_type=F32) * scale
        grad_q = rotate(grad_q.reshape(head_shape), cosine, -sine)
        grad_k = rotate(grad_k.reshape(head_shape), cosine, -sine)
        grad_v = grad_v.reshape(head_shape)
        key_sum = jnp.sum(grad_k[:, :, :ROT], axis=0)
        d_qkv = jnp.concatenate(
            [g.reshape(all_slots, own_width) for g in (grad_q, grad_k, grad_v)], axis=1
        ).astype(BF16)
        a1_b = blocks_of(a1)
        grad_a1 = rep_reduce(d_qkv, lambda a: dot_rt(a, wq), slots)
        grad_input = (grad_resid + norm_back(grad_a1 * vec[0], normal_one, inv_one)).astype(BF16)

        def spread(sums):
            zero = jnp.zeros((own_heads, REPS, sums.shape[1]), F32)
            return lax.dynamic_update_index_in_dim(zero, sums, r, 1)

        vec_sums = jnp.stack(
            [
                jnp.sum(grad_a1 * normal_one, axis=0),
                jnp.sum(grad_a1, axis=0),
                jnp.sum(grad_a2 * normal_two, axis=0),
                jnp.sum(grad_a2, axis=0),
                spread(jnp.sum(grad_q, axis=0)).reshape(features),
                spread(jnp.sum(grad_v, axis=0)).reshape(features),
            ],
            axis=0,
        )
        key_rows = HEADS * ROT // n
        packed = jnp.concatenate(
            [
                vec_sums.reshape(6, n, rows).transpose(1, 0, 2).reshape(n, 6 * rows),
                spread(key_sum).reshape(n, key_rows),
            ],
            axis=1,
        )
        width = -(-packed.shape[1] // 1024) * 1024
        packed = jnp.pad(packed, ((0, 0), (0, width - packed.shape[1]))).reshape(n, width // 128, 128)
        line = ([], [])
        sums = run(
            {
                "d": reduce(lambda i: dot_lt(hidden_b[i], dyl), ids, False, line),
                "g": reduce(lambda i: dot_lt(a2_b[i], grad_gate), ids, True, line),
                "u": reduce(lambda i: dot_lt(a2_b[i], grad_up), ids, False, line),
                "q": reduce(lambda i: dot_lt(a1_b[i], d_qkv), ids, True, line),
                "o": reduce(lambda i: dot_lt(attn_b[i], drl), ids, False, line),
                "s": reduce(lambda i: packed[i], ids, True, line, F32),
            },
            "dgdgdudugugugqoqoqosoqsoss",
        )
        grad_down, grad_wg, grad_wu = sums["d"], sums["g"], sums["u"]
        grad_wq, grad_wo, packed = sums["q"], sums["o"], sums["s"]
        packed = packed + core_swap(packed)
        packed = (packed + y_swap(packed)).reshape(-1)
        out_vectors = packed[: 6 * rows].reshape(6, rows).T
        out_key = packed[6 * rows : 6 * rows + key_rows].reshape(key_rows, 1)

        def everywhere(g):
            return by_rep(rep_parts(g.astype(BF16)), y, core)

        out_down = jnp.concatenate(everywhere(grad_down), axis=0).astype(F32)
        out_gate_up = jnp.concatenate(
            [weave(everywhere(g), n, down_rows) for g in (grad_wg, grad_wu)], axis=1
        )
        out_qkv = weave(everywhere(grad_wq), 3 * own_heads, head_dim)
        out_out = jnp.concatenate(everywhere(mix_out(grad_wo.astype(BF16))), axis=0).astype(F32)
        return activations, grad_input, out_vectors, out_key, out_qkv, out_out, out_gate_up, out_down

    tok, row = P(BOTH, None), P("shard", None)
    return jax.shard_map(
        on_device,
        mesh=mesh,
        in_specs=(tok, tok, P(BOTH), P(BOTH)) + (row,) * 6,
        out_specs=(tok, tok) + (row,) * 6,
        check_vma=False,
    )
```

```python
import functools
import math

import jax
import jax.numpy as jnp
import numpy as np
from jax import lax
from jax.experimental import pallas as pl
from jax.experimental.pallas import tpu as pltpu
from jax.sharding import PartitionSpec as P

HEADS = 32
ROT = 16
REPS = 4
BOTH = ("rep", "shard")
DEPTH = 2
F32 = jnp.float32
BF16 = jnp.bfloat16


def dot(a, b):
    return jnp.dot(a, b, preferred_element_type=F32)


def dot_rt(a, b):
    return lax.dot_general(a, b, (((1,), (1,)), ((), ())), preferred_element_type=F32)


def dot_lt(a, b):
    return lax.dot_general(a, b, (((0,), (0,)), ((), ())), preferred_element_type=F32)


def turn_tables(positions):
    half = ROT // 2
    frequencies = jnp.exp(
        jnp.arange(half, dtype=F32) * (-2.0 * math.log(10000.0) / ROT)
    )
    angles = positions.astype(F32)[:, None] * frequencies[None, :]
    return jnp.cos(angles)[:, None, :], jnp.sin(angles)[:, None, :]


def rotate(values, cosine, sine):
    half = ROT // 2
    low, high, rest = values[..., :half], values[..., half:ROT], values[..., ROT:]
    return jnp.concatenate(
        [low * cosine - high * sine, high * cosine + low * sine, rest], axis=-1
    )


def normalize(values):
    center = values - jnp.mean(values, axis=1, keepdims=True)
    inv_std = lax.rsqrt(jnp.mean(center * center, axis=1, keepdims=True) + 1e-05)
    return center * inv_std, inv_std


def norm_back(grad_norm, normal, inv_std):
    mean_grad = jnp.mean(grad_norm, axis=1, keepdims=True)
    mean_cross = jnp.mean(grad_norm * normal, axis=1, keepdims=True)
    return inv_std * (grad_norm - mean_grad - normal * mean_cross)


MESH = pl.DeviceIdType.MESH
NAMES = ("q", "o", "g", "u", "d")
LONG_UP = {"q": True, "o": True, "g": False, "u": False, "d": True}
FORE_ORDER = (
    "o1", "q1", "o2", "su", "pm", "q2", "sg", "px", "cot", "o3", "q3", "u1", "g1", "bd", "q4", "ln1", "at2",
    "o4", "u2", "at3", "of", "at0", "g2", "at1", "oy", "d1", "u3", "oo", "g3", "ln2", "d2", "g4", "pa", "u4",
    "pd", "fd0", "d3", "fd1", "fd2", "fd3", "d4",
)
VMEM_LIMIT = 64 * 1024 * 1024 - 64 * 1024


class Place:
    def __init__(self, n):
        self.n, self.half = n, n // 2
        self.r, self.s = lax.axis_index("rep"), lax.axis_index("shard")
        self.core = self.r + 1 - 2 * (self.r % 2)
        self.across = (self.r + 2) % REPS
        odd = self.s % 2
        self.spot = (1 - odd) * (self.s // 2) + odd * (n - 1 - self.s // 2)
        self.ids = {k: self.shard_at(k) for k in range(-self.half, self.half + 1)}
        self.ring = (self.ids[1], self.ids[-1])

    def shard_at(self, k):
        q = (self.spot + k + self.n) % self.n
        back = q // self.half
        return (1 - back) * 2 * q + back * (2 * self.n - 1 - 2 * q)

    def greet(self):
        barrier = pltpu.get_barrier_semaphore()
        for who in (
            (self.core, self.s),
            (self.across, self.s),
            (self.r, self.ring[0]),
            (self.r, self.ring[1]),
        ):
            pl.semaphore_signal(barrier, inc=1, device_id=who, device_id_type=MESH)
        pl.semaphore_wait(barrier, 4)


class RepLinks:
    def __init__(self, place, send, recv):
        self.place, self.send, self.recv, self.sent = place, send, recv, []

    def copy(self, i, src, dst, who):
        return pltpu.make_async_remote_copy(
            src_ref=src,
            dst_ref=dst,
            send_sem=self.send.at[i],
            recv_sem=self.recv.at[i],
            device_id=(who, self.place.s),
            device_id_type=MESH,
        )

    def start(self, i, src, dst, who):
        c = self.copy(i, src, dst, who)
        c.start()
        self.sent.append(c)
        return c

    def gather_start(self, i, own, slots):
        a = self.start(i, own, slots.at[1], self.place.across)
        b = self.start(i + 1, own, slots.at[2], self.place.core)
        return a, b

    def gather_pass(self, i, slots, copies):
        copies[0].wait_recv()
        return copies[1], self.start(i + 2, slots.at[1], slots.at[3], self.place.core)

    def finish(self):
        for c in self.sent:
            c.wait_send()


def layer_rows(x, gain, shift):
    center = x - jnp.mean(x, axis=1, keepdims=True)
    inv = lax.rsqrt(jnp.mean(center * center, axis=1, keepdims=True) + 1e-05)
    return center * inv * gain + shift


def first_half(shape):
    return lax.broadcasted_iota(jnp.int32, shape, 1) < 64


def forward_kernel(
    n,
    w_qkv, w_out, w_gu, w_down, tok, cot, vt, seqs, lens, tables,
    q_land, o_land, g_land, u_land, d_land, a1_out, q_out, k_out, v_out, p_out, attn_out,
    resid_out, a2_out, gate_out, up_out, hid_out, dyl_out, meta_out,
    q_blk, g_blk, u_blk, wq, wo, wg, wu, xs, qs, ks, vs, ps, attn, attn_t, acc, csend, crecv, ysend,
    yrecv, resid, a2s, gates, ups, hid, metas, tabs, mask, small, vecs,
    ring_send, ring_recv, load_sem, rep_send, rep_recv, out_sem,
):
    here = Place(n)
    half = here.half
    lands = dict(zip(NAMES, (q_land, o_land, g_land, u_land, d_land)))
    rows = {name: lands[name].shape[1] for name in NAMES}
    slots, width = tok.shape
    rows["q"] = width // n
    blocks = {
        "q": q_blk,
        "o": w_out.at[pl.ds(pl.multiple_of(here.r * rows["o"], 16), rows["o"])],
        "g": g_blk,
        "u": u_blk,
        "d": w_down.at[pl.ds(pl.multiple_of(here.r * rows["d"], 16), rows["d"])],
    }
    into = {"q": wq, "o": wo, "g": wg, "u": wu}
    reach = {
        (name, d): half if LONG_UP[name] == (d == 0) else half - 1 for name in NAMES for d in (0, 1)
    }

    def message(name, d, k):
        i = here.ids[(1 - k) if d == 0 else (k - 1)]
        a = NAMES.index(name)
        src = blocks[name] if k == 1 else lands[name].at[i]
        return pltpu.make_async_remote_copy(
            src_ref=src,
            dst_ref=lands[name].at[i],
            send_sem=ring_send.at[a, d, k - 1],
            recv_sem=ring_recv.at[a, d, k - 1],
            device_id=(here.r, here.ring[d]),
            device_id_type=MESH,
        )

    def load(name, k):
        i = here.ids[k]
        a = NAMES.index(name)
        src = lands[name].at[i]
        return pltpu.make_async_copy(
            src.at[pl.ds(0, rows[name])],
            into[name].at[pl.ds(pl.multiple_of(i * rows[name], 16), rows[name])],
            load_sem.at[a, k + half],
        )

    def load_small(k):
        src = q_land.at[here.ids[k]]
        return pltpu.make_async_copy(
            src.at[pl.ds(rows["q"], 16), pl.ds(0, rows["q"])],
            small.at[here.ids[k]],
            load_sem.at[5, k + half],
        )

    def keep_own(name):
        return pltpu.make_async_copy(
            blocks[name], lands[name].at[here.s], load_sem.at[6, NAMES.index(name)]
        )

    def begin(name):
        for d in (0, 1):
            message(name, d, 1).start()
        keep_own(name).start()

    def serve(name, k):
        for d in (0, 1):
            if k <= reach[name, d]:
                message(name, d, k).wait_recv()
                if k < reach[name, d]:
                    message(name, d, k + 1).start()
                if name in into:
                    load(name, -k if d == 0 else k).start()
                if name == "q":
                    load_small(-k if d == 0 else k).start()

    def own_kept(name):
        keep_own(name).wait()
        if name in into:
            load(name, 0).start()
        if name == "q":
            load_small(0).start()

    def came(name):
        found = [0]
        for k in range(1, half + 1):
            found += [-k] * (k <= reach[name, 0]) + [k] * (k <= reach[name, 1])
        return found

    def loaded(name):
        for k in came(name):
            load(name, k).wait()
            if name == "q":
                load_small(k).wait()

    outs = []

    def save(src, dst):
        c = pltpu.make_async_copy(src, dst, out_sem.at[len(outs)])
        c.start()
        outs.append(c)

    def fetch(src, dst, i):
        c = pltpu.make_async_copy(src, dst, load_sem.at[7, i])
        c.start()
        return c

    def rows16(count, body):
        @pl.loop(0, count // 16)
        def _(i):
            body(pl.ds(pl.multiple_of(i * 16, 16), 16))

    own_width = wq.shape[1] // 3
    pairs = own_width // 128
    block = slots // 2
    units = g_blk.shape[1]
    rep = RepLinks(here, rep_send, rep_recv)
    held = {}
    lane = lax.broadcasted_iota(jnp.int32, (1, 128), 1)
    low = first_half((slots, 128))

    class XSlots:
        class at:
            def __class_getitem__(cls, g):
                return xs.at[pl.ds(g * slots, slots)]

    windows = []
    for t in range(3 * pairs):
        part, tt = t // pairs, t % pairs
        for h in (0, 1):
            first = part * width + (2 * tt + h) * 4 * 64
            i = len(windows)
            dst = hid.at[pl.ds(slots * (i // 8), slots), pl.ds(128 * (i % 8), 128)]
            start = pl.multiple_of(first + (here.r // 2) * 128, 128)
            c = pltpu.make_async_copy(w_qkv.at[:, pl.ds(start, 128)], dst, rep_send.at[14 + i])
            c.start()
            windows.append((c, dst))
    own_x = fetch(tok, xs.at[pl.ds(0, slots)], 0)
    own_c = fetch(cot, ysend, 1)

    long0, long1 = lens[0], lens[1]
    spot = lax.broadcasted_iota(jnp.int32, (8, slots), 1)
    end = jnp.where(spot < block, long0, long1 + block)
    row = lax.broadcasted_iota(jnp.int32, (8, slots), 0)
    together = jnp.where(seqs[0] == seqs[1], 1.0, 0.0)
    metas[0] = jnp.where(row == 0, jnp.where(spot < end, 1.0, 0.0), together)

    base = vt[...].astype(F32)
    side = (here.s % 2) * 64
    wide = rows["q"]
    head = pltpu.roll(base, (side - here.r * 64 + wide) % wide, 1)
    keys = pltpu.roll(base, (side - here.r * ROT + wide) % wide, 1)
    line = lax.broadcasted_iota(jnp.int32, (16, wide), 0)
    place = lax.broadcasted_iota(jnp.int32, (16, wide), 1)
    inside = (place >= side) & (place < side + 64)
    key_inside = (place >= side) & (place < side + ROT)
    own_small = jnp.where(
        line < 4,
        base,
        jnp.where(
            (line < 6) & inside, head, jnp.where((line == 6) & key_inside, keys, 0.0)
        ),
    )
    q_blk[wide : wide + 16, :] = jnp.zeros((16, q_blk.shape[1]), BF16)
    q_blk[wide : wide + 16, 0:wide] = own_small.astype(BF16)

    here.greet()
    begin("o")
    held["m"] = rep.gather_start(0, metas.at[0], metas)
    held["x"] = rep.gather_start(3, tok, XSlots)
    odd = (jnp.zeros((slots, 128), jnp.int32) + here.r % 2) == 1
    for t in range(3 * pairs):
        pair = []
        for h in (0, 1):
            c, ref = windows[2 * t + h]
            c.wait()
            value = ref[...].astype(F32)
            swapped = pltpu.roll(value, 64, 1)
            pair.append(jnp.where(odd, swapped, value) if h == 0 else jnp.where(odd, value, swapped))
        q_blk[0:wide, t * 128 : (t + 1) * 128] = jnp.where(low, pair[0], pair[1]).astype(BF16)
    begin("q")

    strips = []
    span = 384
    total = REPS * units
    piece = units // n
    for j in (0, 1):
        for s in range(n):
            o = s * REPS * piece + here.r * piece
            if s < half:
                off = o % 128
                a = o - off
            else:
                pad = (128 - (o + piece) % 128) % 128
                a = o + piece + pad - span
                off = span - piece - pad
            i = len(strips)
            ref = gates if j == 0 else ups
            dst = ref.at[pl.ds(slots * (s // 3), slots), pl.ds(span * (s % 3), span)]
            start = pl.multiple_of(j * total + a, 128)
            c = pltpu.make_async_copy(w_gu.at[:, pl.ds(start, span)], dst, rep_recv.at[14 + i])
            c.start()
            strips.append((c, dst, off))

    def select(j):
        for c, _, _ in strips[j * n : (j + 1) * n]:
            c.wait()
        out = (g_blk, u_blk)[j]
        for t in range(units // 128):
            whole = None
            for s in range(128 * t // piece, (128 * t + 127) // piece + 1):
                _, ref, off = strips[j * n + s]
                shift = (2 * span - (off + 128 * t - piece * s)) % span
                value = pltpu.roll(ref[...].astype(F32), shift, 1)[:, :128]
                first = s * piece - 128 * t
                whole = value if whole is None else jnp.where(lane >= first, value, whole)
            out[:, t * 128 : (t + 1) * 128] = whole.astype(BF16)

    def sel_g():
        select(0)
        begin("g")

    def sel_u():
        select(1)
        begin("u")

    def pass_m():
        held["m"] = rep.gather_pass(0, metas, held["m"])

    def pass_x():
        held["x"] = rep.gather_pass(3, XSlots, held["x"])

    def mask_cot():
        own_c.wait()
        for j in range(2):
            count = (long0, long1)[j]

            def chunk(at, j=j, count=count):
                first = lax.broadcasted_iota(jnp.int32, (16, width), 0) + at.start
                at = pl.ds(pl.multiple_of(at.start + j * block, 16), 16)
                value = ysend[at, :].astype(F32)
                ysend[at, :] = jnp.where(first < count, value, 0.0).astype(BF16)

            rows16(block, chunk)
        fetch(ysend, dyl_out.at[0], 2).wait()
        held["d"] = rep.gather_start(6, dyl_out.at[0], dyl_out)

    def pass_d():
        held["d"] = rep.gather_pass(6, dyl_out, held["d"])

    def ln1():
        for c in held["m"] + held["x"]:
            c.wait_recv()
        own_x.wait()
        mine = held["x"][1]
        mine.wait_send()
        rep.sent = [c for c in rep.sent if c is not mine]
        own_kept("q")
        loaded("q")
        for s in range(n):
            vecs[0:8, s * rows["q"] : (s + 1) * rows["q"]] = small[s, 0:8, :].astype(F32)
        gain, shift = vecs[0:1, :], vecs[1:2, :]

        def chunk(at):
            xs[at, :] = layer_rows(xs[at, :].astype(F32), gain, shift).astype(BF16)

        rows16(REPS * slots, chunk)
        save(xs, a1_out)

    def lane_bias(row, t):
        w = rows["q"]
        a = vecs[row : row + 1, 2 * t * w : 2 * t * w + 128]
        return a + vecs[row : row + 1, (2 * t + 1) * w : (2 * t + 1) * w + 128]

    def attend(g):
        line = lax.broadcasted_iota(jnp.int32, (slots, slots), 0)
        column = lax.broadcasted_iota(jnp.int32, (slots, slots), 1)
        here_rows = pl.ds(g * slots, slots)
        acc[...] = dot(xs[here_rows, :], wq[...])
        valid = metas[g, 0:1, :]
        same = metas[g, 1:2, :]
        for j in range(3):
            tabs[j, :block, :] = tables[j, :block, :]
            tabs[j, block:, :] = jnp.where(
                same[:, :128] > 0.5, tables[j, block:, :], tables[j, :block, :]
            )
        apart = (line >= block) & (column < block) & (same < 0.5)
        open_ = (column <= line) & jnp.logical_not(apart) & ((valid > 0.5) | (line == column))
        mask[...] = jnp.where(open_, 0.0, -1e30)
        for t in range(3 * pairs):
            part, tt = t // pairs, t % pairs
            tile = acc[:, t * 128 : (t + 1) * 128] + lane_bias((4, 6, 5)[part], tt)
            if part < 2:
                tile = (
                    tile * tabs[0]
                    + pltpu.roll(tile, 120, 1) * tabs[1]
                    + pltpu.roll(tile, 8, 1) * tabs[2]
                )
            (qs, ks, vs)[part][g, tt] = tile.astype(BF16)
        low_low = first_half((1, 128)).astype(F32).astype(BF16)
        high_low = (1.0 - first_half((1, 128)).astype(F32)).astype(BF16)
        for t in range(pairs):
            qt, kt, vt_ = qs[g, t], ks[g, t], vs[g, t]
            mixed = []
            for h in (0, 1):
                mine = low_low if h == 0 else high_low
                sc = dot_rt(qt * mine, kt) * (1.0 / 8.0) + mask[...]
                e = jnp.exp(sc - jnp.max(sc, axis=1, keepdims=True))
                p = (e / jnp.sum(e, axis=1, keepdims=True)).astype(BF16)
                ps[g, 2 * t + h] = p
                mixed.append(dot(p, vt_))
            mix = jnp.where(low, mixed[0], mixed[1])
            attn[here_rows, t * 128 : (t + 1) * 128] = mix.astype(BF16)
            attn_t[t * 128 : (t + 1) * 128, here_rows] = mix.T.astype(BF16)

    def out_far():
        own_kept("o")
        loaded("o")
        for g in (0, 1):
            csend[g] = dot(attn[(g + 2) * slots : (g + 3) * slots, :], wo[...]).astype(BF16)
        held["core"] = rep.start(9, csend, crecv, here.core)

    def out_y():
        held["core"].wait_recv()
        ysend[...] = (dot(attn[slots : 2 * slots, :], wo[...]) + crecv[1].astype(F32)).astype(BF16)
        held["y"] = rep.start(10, ysend, yrecv, here.across)

    def out_own():
        resid[...] = dot(attn[0:slots, :], wo[...]) + crecv[0].astype(F32)
        held["tok"] = fetch(tok, crecv.at[0], 3)
        save(qs, q_out)
        save(ks, k_out)
        save(vs, v_out)
        save(ps, p_out)
        save(attn_t, attn_out)
        save(metas, meta_out)

    def ln2():
        held["tok"].wait()
        held["y"].wait_recv()
        gain, shift = vecs[2:3, :], vecs[3:4, :]

        def chunk(at):
            x = resid[at, :] + yrecv[at, :].astype(F32) + crecv[0, at, :].astype(F32)
            resid[at, :] = x
            a2s[0, at, :] = layer_rows(x, gain, shift).astype(BF16)

        rows16(slots, chunk)
        held["a"] = rep.gather_start(11, a2s.at[0], a2s)
        save(resid, resid_out)

    def pass_a():
        held["a"] = rep.gather_pass(11, a2s, held["a"])

    def feed(g):
        if g == 0:
            own_kept("g")
            own_kept("u")
            for c in held["a"]:
                c.wait_recv()
            loaded("g")
            loaded("u")
            save(a2s, a2_out)
        at = pl.ds(g * slots, slots)
        gate = dot(a2s[g], wg[...])
        gates[at, :] = gate.astype(BF16)
        up = dot(a2s[g], wu[...])
        ups[at, :] = up.astype(BF16)
        act = gate * jax.nn.sigmoid(gate) * up
        for j in range(act.shape[1] // 128):
            hid[j * 128 : (j + 1) * 128, at] = act[:, j * 128 : (j + 1) * 128].T.astype(BF16)
        if g == REPS - 1:
            save(gates, gate_out)
            save(ups, up_out)
            save(hid, hid_out)

    steps = {
        "sg": sel_g, "su": sel_u, "bd": lambda: begin("d"), "pm": pass_m, "px": pass_x, "cot": mask_cot,
        "pd": pass_d, "ln1": ln1, "of": out_far, "oy": out_y, "oo": out_own, "ln2": ln2, "pa": pass_a,
    }
    for name in FORE_ORDER:
        if name in steps:
            steps[name]()
        elif name[:2] == "at":
            attend(int(name[2]))
        elif name[:2] == "fd":
            feed(int(name[2]))
        else:
            serve(name[0], int(name[1]))
    for c in held["d"]:
        c.wait_recv()
    keep_own("d").wait()
    for name in NAMES:
        for d in (0, 1):
            for k in range(1, reach[name, d] + 1):
                message(name, d, k).wait_send()
    rep.finish()
    for c in outs:
        c.wait()


def forward_call(n, weights, tok, cot, vt, seqs, lens, tables):
    slots, width = tok.shape
    w_qkv, w_out, w_gu, w_down = weights
    lanes, units = w_qkv.shape[1] // REPS, w_gu.shape[1] // 2 // REPS
    rows, own_width = width // n, lanes // 3
    all_slots = REPS * slots
    pairs = own_width // 128
    half = n // 2
    S = jax.ShapeDtypeStruct
    heads = (REPS, pairs, slots, 128)
    out_shape = [
        S((n, rows + 16, lanes), BF16),
        S((n, w_out.shape[0] // REPS, width), BF16),
        S((n, rows, units), BF16),
        S((n, rows, units), BF16),
        S((n, w_down.shape[0] // REPS, width), BF16),
        S((all_slots, width), BF16),
        S(heads, BF16),
        S(heads, BF16),
        S(heads, BF16),
        S((REPS, 2 * pairs, slots, slots), BF16),
        S((own_width, all_slots), BF16),
        S((slots, width), F32),
        S((REPS, slots, width), BF16),
        S((all_slots, units), BF16),
        S((all_slots, units), BF16),
        S((units, all_slots), BF16),
        S((REPS, slots, width), BF16),
        S((REPS, 8, slots), F32),
    ]
    V = pltpu.VMEM
    scratch = [
        V((rows + 16, lanes), BF16),
        V((rows, units), BF16),
        V((rows, units), BF16),
        V((width, lanes), BF16),
        V((own_width, width), BF16),
        V((width, units), BF16),
        V((width, units), BF16),
        V((all_slots, width), BF16),
        V(heads, BF16),
        V(heads, BF16),
        V(heads, BF16),
        V((REPS, 2 * pairs, slots, slots), BF16),
        V((all_slots, own_width), BF16),
        V((own_width, all_slots), BF16),
        V((slots, lanes), F32),
        V((2, slots, width), BF16),
        V((2, slots, width), BF16),
        V((slots, width), BF16),
        V((slots, width), BF16),
        V((slots, width), F32),
        V((REPS, slots, width), BF16),
        V((all_slots, units), BF16),
        V((all_slots, units), BF16),
        V((units, all_slots), BF16),
        V((REPS, 8, slots), F32),
        V((3, slots, 128), F32),
        V((slots, slots), F32),
        V((n, 16, rows), BF16),
        V((8, width), F32),
        pltpu.SemaphoreType.DMA((5, 2, half)),
        pltpu.SemaphoreType.DMA((5, 2, half)),
        pltpu.SemaphoreType.DMA((8, 2 * half + 1)),
        pltpu.SemaphoreType.DMA((14 + 6 * pairs,)),
        pltpu.SemaphoreType.DMA((14 + 2 * n,)),
        pltpu.SemaphoreType.DMA((12,)),
    ]
    anywhere = pl.BlockSpec(memory_space=pltpu.HBM)
    inside = pl.BlockSpec(memory_space=pltpu.VMEM)
    scalars = pl.BlockSpec(memory_space=pltpu.SMEM)
    return pl.pallas_call(
        functools.partial(forward_kernel, n),
        out_shape=out_shape,
        in_specs=[anywhere] * 6 + [inside, scalars, scalars, inside],
        out_specs=[anywhere] * len(out_shape),
        scratch_shapes=scratch,
        compiler_params=pltpu.CompilerParams(
            collective_id=1, has_side_effects=True, vmem_limit_bytes=VMEM_LIMIT
        ),
    )(*weights, tok, cot, vt, seqs, lens, tables)


PARTS = ("d", "g", "u", "x", "y", "o", "s")
PARTS_UP = {"d": False, "g": True, "u": False, "x": True, "y": True, "o": False, "s": True}
BACK_ORDER = (
    "d0", "dh0", "dh1", "dh2", "dh3", "g0", "u0", "far2", "near2", "g1", "d1", "g2", "ln2", "d2", "mlpf",
    "mlpn", "pass", "ldrl", "u1", "at0", "g3", "at1", "d3", "at2", "u2", "at3", "ey2", "y0", "fd", "far1",
    "x0", "act", "near1", "y1", "o0", "y2", "fg", "x1", "u3", "y3", "o1", "fy", "hg", "x2", "fu", "sums",
    "x3", "o2", "s0", "o3", "fx", "hy", "hd", "s1", "fo", "s2", "s3", "hu", "fs", "hx", "ho", "hs",
)


def norm_rows_back(x, gain, grad):
    center = x - jnp.mean(x, axis=1, keepdims=True)
    inv = lax.rsqrt(jnp.mean(center * center, axis=1, keepdims=True) + 1e-05)
    normal = center * inv
    e = grad * gain
    cross = jnp.mean(e * normal, axis=1, keepdims=True)
    return inv * (e - jnp.mean(e, axis=1, keepdims=True) - normal * cross), normal


def backward_kernel(
    n,
    q_land, o_land, g_land, u_land, d_land, a1_in, q_in, k_in, v_in, p_in, attn_in,
    resid_in, a2_in, gate_in, up_in, hid_in, dyl_in, tok, metas, tables,
    act_out, grad_out, d_sum, g_sum, u_sum, x_sum, y_sum, o_sum, s_sum,
    land_d, land_g, land_u, land_x, land_y, land_o, land_s, core_land, y_land, drl_land,
    dyl, hid, wd, gates, ups, a2, a1, wst, wo, attn_t, heads, probs, dqkv, datt, csend, crecv,
    ysend, ysend2, yrecv, own, resid, outp, stage, rstage, sstage, small, vecs, sums, headsums, tabs,
    ring_send, ring_recv, load_sem, rep_send, rep_recv, stream_sem, rstage_sem, fin_sem,
):
    here = Place(n)
    half = here.half
    slots, width = tok.shape
    rows = width // n
    units = gates.shape[1]
    lanes = dqkv.shape[1]
    own_width = lanes // 3
    pairs = own_width // 128
    lands = dict(zip(PARTS, (land_d, land_g, land_u, land_x, land_y, land_o, land_s)))
    finals = dict(zip(PARTS, (d_sum, g_sum, u_sum, x_sum, y_sum, o_sum, s_sum)))
    shape = {name: lands[name].shape[2:] for name in PARTS}
    reach = {
        (name, d): half if PARTS_UP[name] == (d == 0) else half - 1 for name in PARTS for d in (0, 1)
    }
    rep = RepLinks(here, rep_send, rep_recv)

    def fetch(src, dst, i):
        c = pltpu.make_async_copy(src, dst, load_sem.at[i])
        c.start()
        return c

    def block_of(i, size):
        return pl.ds(pl.multiple_of(i * size, 16), size)

    def lanes_of(i, size):
        return pl.ds(pl.multiple_of(i * size, 128), size)

    def term(name, i):
        if name == "d":
            return dot(hid[block_of(i, shape["d"][0]), :], dyl[...])
        if name in ("g", "u"):
            return dot_lt(a2[:, lanes_of(i, rows)], (gates if name == "g" else ups)[...])
        if name == "x":
            return dot_lt(a1[:, lanes_of(i, rows)], dqkv[:, : lanes // 2])
        if name == "y":
            return dot_lt(a1[:, lanes_of(i, rows)], dqkv[:, lanes // 2 :])
        if name == "o":
            return dot(attn_t[block_of(i, shape["o"][0]), :], wd[: dyl.shape[0], :])
        return sums[i]

    def corner(ref, name):
        return ref.at[pl.ds(0, shape[name][0]), pl.ds(0, shape[name][1])]

    def message(name, d, k, src):
        a = PARTS.index(name)
        return pltpu.make_async_remote_copy(
            src_ref=src,
            dst_ref=lands[name].at[d, k - 1],
            send_sem=ring_send.at[a, d, k - 1],
            recv_sem=ring_recv.at[a, d, k - 1],
            device_id=(here.r, here.ring[d]),
            device_id_type=MESH,
        )

    def landed(name, d, k):
        message(name, d, k, lands[name].at[d, k - 1]).wait_recv()
        dst = sstage.at[2 + d] if name == "s" else corner(rstage.at[d], name)
        c = pltpu.make_async_copy(lands[name].at[d, k - 1], dst, rstage_sem.at[d])
        c.start()
        return c, dst

    flying = {}
    turn = [0, 0]

    def serve(name, j):
        hops = {}
        for d in (0, 1):
            k = half - j if reach[name, d] == half else half - 1 - j
            if k >= 1:
                hops[d] = k
        got = {d: landed(name, d, k + 1) for d, k in hops.items() if j > 0}
        for d, k in hops.items():
            if name == "s":
                slot, key = sstage.at[d], ("s", d)
            else:
                turn[d] = 1 - turn[d]
                slot, key = corner(stage.at[d, turn[d]], name), (d, turn[d])
            part = term(name, here.ids[k if d == 0 else -k])
            if d in got:
                got[d][0].wait()
                part = part + got[d][1][...].astype(F32)
            if key in flying:
                flying.pop(key).wait_send()
            slot[...] = part.astype(slot.dtype)
            flying[key] = message(name, d, k, slot)
            flying[key].start()

    opened = {}

    def finish(name):
        got = [landed(name, d, 1) for d in (0, 1)]
        part = term(name, here.ids[0])
        for c, ref in got:
            c.wait()
            part = part + ref[...].astype(F32)
        i = PARTS.index(name)
        ref = sstage.at[4] if name == "s" else corner(rstage.at[0], name)
        ref[...] = part.astype(ref.dtype)
        c = pltpu.make_async_copy(ref, finals[name].at[0], fin_sem.at[i])
        c.start()
        c.wait()
        opened[name] = rep.gather_start(3 * i, finals[name].at[0], finals[name])

    def hand_on(name):
        opened[name] = rep.gather_pass(3 * PARTS.index(name), finals[name], opened[name])

    base = 3 * len(PARTS)

    def stream(names, body):
        def copies(s, slot):
            found = []
            for j, name in enumerate(names):
                land = {"q": q_land, "g": g_land, "u": u_land}[name]
                found.append(
                    pltpu.make_async_copy(
                        land.at[s, pl.ds(0, rows)],
                        wst.at[slot, j, :, pl.ds(0, land.shape[2])],
                        stream_sem.at[slot, j],
                    )
                )
            return found

        for c in copies(0, 0):
            c.start()

        @pl.loop(0, n)
        def _(s):
            slot = s % 2

            @pl.when(s + 1 < n)
            def _():
                for c in copies(s + 1, 1 - slot):
                    c.start()

            for c in copies(s, slot):
                c.wait()
            body(s, slot)

    def exchange_core(i, k):
        return rep.start(base + i, csend, core_land.at[k], here.core)

    def exchange_y(i, k, src):
        return rep.start(base + i, src, y_land.at[k], here.across)

    def drop_send(c):
        c.wait_send()
        rep.sent = [x for x in rep.sent if x is not c]

    here.greet()
    c_hid = fetch(hid_in, hid, 0)
    c_dyl = fetch(dyl_in, dyl, 1)
    c_wd = fetch(d_land, wd, 2)
    c_gate = fetch(gate_in, gates, 3)
    c_up = fetch(up_in, ups, 4)
    c_a2 = fetch(a2_in, a2, 5)
    c_small = fetch(q_land.at[:, pl.ds(rows, 16), pl.ds(0, rows)], small, 9)
    c_res = fetch(resid_in, resid, 8)
    out_rows = o_land.shape[1]
    c_wo = [fetch(o_land.at[i], wo.at[pl.ds(i * out_rows, out_rows)], 32 + i) for i in range(n)]
    c_att = fetch(attn_in, attn_t, 14)
    c_a1 = fetch(a1_in, a1, 7)
    c_hid.wait()
    c_dyl.wait()
    low_rows, high_rows = pl.ds(0, 2 * slots), pl.ds(2 * slots, 2 * slots)
    halves = (
        first_half((1, 128)).astype(F32).astype(BF16),
        (1.0 - first_half((1, 128)).astype(F32)).astype(BF16),
    )
    block = slots // 2
    held = {}
    waited = []

    def need(c):
        if not any(c is w for w in waited):
            waited.append(c)
            c.wait()

    def rows16(count, body):
        @pl.loop(0, count // 16)
        def _(i):
            body(pl.ds(pl.multiple_of(i * 16, 16), 16))

    def feed_back(g):
        if g == 0:
            for c in (c_wd, c_gate, c_up):
                c.wait()
        at = pl.ds(g * slots, slots)
        dh = dot_rt(dyl[at, :], wd[...])
        gate, up = gates[at, :].astype(F32), ups[at, :].astype(F32)
        sig = jax.nn.sigmoid(gate)
        gates[at, :] = (dh * up * sig * (1.0 + gate * (1.0 - sig))).astype(BF16)
        ups[at, :] = (dh * gate * sig).astype(BF16)

    def a2_product(at, slot):
        return dot_rt(gates[at, :], wst[slot, 0, :, :units]) + dot_rt(ups[at, :], wst[slot, 1, :, :units])

    def put_far(part, s):
        csend[0, :, lanes_of(s, rows)] = part[:slots]
        csend[1, :, lanes_of(s, rows)] = part[slots:]

    def far2():
        stream(("g", "u"), lambda s, slot: put_far(a2_product(high_rows, slot).astype(BF16), s))
        held["core1"] = exchange_core(0, 0)

    def put_near(part, s, ref):
        at = lanes_of(s, rows)
        ref[:, at] = part[:slots] + crecv[0, :, at].astype(F32)
        ysend[:, at] = (part[slots:] + crecv[1, :, at].astype(F32)).astype(BF16)

    def near2():
        held["core1"].wait_recv()
        fetch(core_land.at[0], crecv, 10).wait()
        stream(("g", "u"), lambda s, slot: put_near(a2_product(low_rows, slot), s, own))
        held["y1"] = exchange_y(1, 0, ysend)

    def mlpf():
        drop_send(held["core1"])
        for g in (0, 1):
            csend[g] = dot_lt(hid[:, (g + 2) * slots : (g + 3) * slots], wd[...]).astype(BF16)
        held["core2"] = exchange_core(2, 1)

    def mlpn():
        held["core2"].wait_recv()
        fetch(core_land.at[1], crecv, 13).wait()
        ysend2[...] = (dot_lt(hid[:, slots : 2 * slots], wd[...]) + crecv[1].astype(F32)).astype(BF16)
        need(c_res)
        outp[...] = resid[...] + dot_lt(hid[:, :slots], wd[...]) + crecv[0].astype(F32)

    def ln2():
        need(c_small)
        need(c_res)
        for s in range(n):
            vecs[0:8, s * rows : (s + 1) * rows] = small[s, 0:8, :].astype(F32)
        headsums[...] = jnp.zeros_like(headsums)
        vecs[8:40, :] = jnp.zeros((32, width), F32)
        held["y1"].wait_recv()
        fetch(y_land.at[0], yrecv, 11).wait()
        drop_send(held["y1"])
        gain = vecs[2:3, :]

        def chunk(at):
            da = own[at, :] + yrecv[at, :].astype(F32)
            back, normal = norm_rows_back(resid[at, :], gain, da)
            prod = da * normal
            vecs[24:32, :] += prod[:8] + prod[8:]
            vecs[32:40, :] += da[:8] + da[8:]
            dr = dyl[at, :].astype(F32) + back
            own[at, :] = dr
            ysend[at, :] = dr.astype(BF16)

        rows16(slots, chunk)
        fetch(ysend, drl_land.at[0], 12).wait()
        held["drl"] = rep.gather_start(base + 3, drl_land.at[0], drl_land)

    def pass_on():
        held["drl"] = rep.gather_pass(base + 3, drl_land, held["drl"])

    def ldrl():
        for c in held["drl"]:
            c.wait_recv()
        loads = [fetch(drl_land.at[g], wd.at[pl.ds(g * slots, slots)], 16 + g) for g in range(REPS)]
        for c in loads + c_wo + [c_att]:
            c.wait()

    def ey2():
        held["y2"] = exchange_y(6, 1, ysend2)

    def head_copies(g, slot):
        found = [
            pltpu.make_async_copy(ref.at[g], heads.at[slot, j], stream_sem.at[slot, 2 + j])
            for j, ref in enumerate((q_in, k_in, v_in))
        ]
        return found + [pltpu.make_async_copy(p_in.at[g], probs.at[slot], stream_sem.at[slot, 5])]

    def turn_back(tile):
        return tile * tabs[0] - pltpu.roll(tile, 120, 1) * tabs[1] - pltpu.roll(tile, 8, 1) * tabs[2]

    def attend_back(g):
        slot = g % 2
        if g == 0:
            for c in head_copies(0, 0):
                c.start()
        if g + 1 < REPS:
            for c in head_copies(g + 1, 1 - slot):
                c.start()
        at = pl.ds(g * slots, slots)
        datt[...] = dot_rt(wd[at, :], wo[...]).astype(BF16)
        same = metas[g, 1:2, :128]
        for j in range(3):
            tabs[j, :block, :] = tables[j, :block, :]
            tabs[j, block:, :] = jnp.where(same > 0.5, tables[j, block:, :], tables[j, :block, :])
        for c in head_copies(g, slot):
            c.wait()
        low = first_half((slots, 128))
        for t in range(pairs):
            da = datt[:, t * 128 : (t + 1) * 128]
            qt, kt, vt = heads[slot, 0, t], heads[slot, 1, t], heads[slot, 2, t]
            both = []
            for h in (0, 1):
                p = probs[slot, 2 * t + h]
                pf = p.astype(F32)
                dp = dot_rt(da * halves[h], vt)
                delta = jnp.sum(dp * pf, axis=1, keepdims=True)
                ds = (pf * (dp - delta)).astype(BF16)
                both.append((dot(ds, kt), dot_lt(ds, qt), dot_lt(p, da)))
            dq, dk, dv = [jnp.where(low, a, b) for a, b in zip(*both)]
            dq, dk = turn_back(dq * (1.0 / 8.0)), turn_back(dk * (1.0 / 8.0))
            for j, value in enumerate((dq, dk, dv)):
                row = j * pairs + t
                headsums[row : row + 1, :] += jnp.sum(value, axis=0, keepdims=True)
                first = j * own_width + t * 128
                dqkv[at, first : first + 128] = value.astype(BF16)

    def far1():
        drop_send(held["core2"])

        def body(s, slot):
            put_far(dot_rt(dqkv[high_rows, :], wst[slot, 0, :, :lanes]).astype(BF16), s)

        stream(("q",), body)
        held["core3"] = exchange_core(7, 2)

    def act():
        held["y2"].wait_recv()
        fetch(y_land.at[1], yrecv, 20).wait()

        def chunk(at):
            yrecv[at, :] = (outp[at, :] + yrecv[at, :].astype(F32)).astype(BF16)

        rows16(slots, chunk)
        fetch(yrecv, act_out, 21).wait()

    def near1():
        held["core3"].wait_recv()
        fetch(core_land.at[2], crecv, 22).wait()

        def body(s, slot):
            put_near(dot_rt(dqkv[low_rows, :], wst[slot, 0, :, :lanes]), s, resid)

        stream(("q",), body)
        held["y3"] = exchange_y(8, 2, ysend)
        held["tok"] = fetch(tok, crecv.at[1], 23)

    def add_up():
        held["tok"].wait()
        held["y3"].wait_recv()
        fetch(y_land.at[2], yrecv, 24).wait()
        gain = vecs[0:1, :]

        def chunk(at):
            da = resid[at, :] + yrecv[at, :].astype(F32)
            back, normal = norm_rows_back(crecv[1, at, :].astype(F32), gain, da)
            prod = da * normal
            vecs[8:16, :] += prod[:8] + prod[8:]
            vecs[16:24, :] += da[:8] + da[8:]
            yrecv[at, :] = (own[at, :] + back).astype(BF16)

        rows16(slots, chunk)
        held["grad"] = fetch(yrecv, grad_out, 25)
        sums[...] = jnp.zeros_like(sums)
        for j in range(4):
            total = jnp.sum(vecs[8 + 8 * j : 16 + 8 * j, :], axis=0, keepdims=True)
            for s in range(n):
                sums[s, j : j + 1, :] = total[:, s * rows : (s + 1) * rows]
        for s in range(n):
            for j, part in ((4, 0), (5, 2), (6, 1)):
                row = part * pairs + s // 2
                sums[s, j : j + 1, 0:128] = headsums[row : row + 1, :] * halves[s % 2].astype(F32)

    steps = {
        "far2": far2, "near2": near2, "mlpf": mlpf, "mlpn": mlpn, "ln2": ln2, "pass": pass_on,
        "ldrl": ldrl, "ey2": ey2, "far1": far1, "act": act, "near1": near1, "sums": add_up,
    }
    for name in BACK_ORDER:
        if name in steps:
            steps[name]()
        elif name[:2] == "dh":
            feed_back(int(name[2]))
        elif name[:2] == "at":
            attend_back(int(name[2]))
        elif name[0] == "f":
            finish(name[1])
        elif name[0] == "h":
            hand_on(name[1])
        else:
            if name in ("g0", "u0"):
                need(c_a2)
            if name in ("x0", "y0"):
                need(c_a1)
            serve(name[0], int(name[1]))
    for name in PARTS:
        for c in opened[name]:
            c.wait_recv()
    held["grad"].wait()
    rep.finish()
    for c in flying.values():
        c.wait_send()


def backward_call(n, lands, kept, tok, meta, tables):
    slots, width = tok.shape
    q_land, o_land, g_land, u_land, d_land = lands
    a1, qs, ks, vs, ps, attn_t, resid, a2, gate, up, hid, dyl = kept
    all_slots, units = gate.shape
    lanes = q_land.shape[2]
    pairs = lanes // 3 // 128
    half = n // 2
    rows = width // n
    S = jax.ShapeDtypeStruct
    block = {
        "d": (d_land.shape[1], width),
        "g": (rows, units),
        "u": (rows, units),
        "x": (rows, lanes // 2),
        "y": (rows, lanes // 2),
        "o": (o_land.shape[1], width),
        "s": (8, rows),
    }
    kind = {name: F32 if name == "s" else BF16 for name in PARTS}
    out_shape = (
        [S((slots, width), BF16), S((slots, width), BF16)]
        + [S((REPS,) + block[name], kind[name]) for name in PARTS]
        + [S((2, half) + block[name], kind[name]) for name in PARTS]
        + [S((3, 2, slots, width), BF16), S((3, slots, width), BF16), S((REPS, slots, width), BF16)]
    )
    V = pltpu.VMEM
    scratch = [
        V((all_slots, width), BF16),
        V(hid.shape, BF16),
        V((units, width), BF16),
        V((all_slots, units), BF16),
        V((all_slots, units), BF16),
        V((all_slots, width), BF16),
        V((all_slots, width), BF16),
        V((2, 2, rows, lanes), BF16),
        V((lanes // 3, width), BF16),
        V((lanes // 3, all_slots), BF16),
        V((2, 3, pairs, slots, 128), BF16),
        V((2, 2 * pairs, slots, slots), BF16),
        V((all_slots, lanes), BF16),
        V((slots, lanes // 3), BF16),
        V((2, slots, width), BF16),
        V((2, slots, width), BF16),
        V((slots, width), BF16),
        V((slots, width), BF16),
        V((slots, width), BF16),
        V((slots, width), F32),
        V((slots, width), F32),
        V((slots, width), F32),
        V((2, 2, rows, width), BF16),
        V((2, rows, width), BF16),
        V((5, 8, rows), F32),
        V((n, 16, rows), BF16),
        V((40, width), F32),
        V((n, 8, rows), F32),
        V((16, 128), F32),
        V((3, slots, 128), F32),
        pltpu.SemaphoreType.DMA((len(PARTS), 2, half)),
        pltpu.SemaphoreType.DMA((len(PARTS), 2, half)),
        pltpu.SemaphoreType.DMA((32 + n,)),
        pltpu.SemaphoreType.DMA((30,)),
        pltpu.SemaphoreType.DMA((30,)),
        pltpu.SemaphoreType.DMA((2, 6)),
        pltpu.SemaphoreType.DMA((2,)),
        pltpu.SemaphoreType.DMA((len(PARTS),)),
    ]
    anywhere = pl.BlockSpec(memory_space=pltpu.HBM)
    inside = pl.BlockSpec(memory_space=pltpu.VMEM)
    out = pl.pallas_call(
        functools.partial(backward_kernel, n),
        out_shape=out_shape,
        in_specs=[anywhere] * 18 + [inside] * 2,
        out_specs=[anywhere] * len(out_shape),
        scratch_shapes=scratch,
        compiler_params=pltpu.CompilerParams(
            collective_id=2, has_side_effects=True, vmem_limit_bytes=VMEM_LIMIT
        ),
    )(q_land, o_land, g_land, u_land, d_land.reshape(units, width), a1, qs, ks, vs, ps, attn_t,
      resid, a2, gate, up, hid, dyl, tok, meta, tables)
    return out[:2], dict(zip(PARTS, out[2:9]))


def weave_kernel(
    n,
    rel, d_in, g_in, u_in, x_in, y_in, o_in, s_in, act_in, grad_in,
    out_act, out_grad, out_vectors, out_key, out_qkv, out_out, out_gu, out_down,
    small,
):
    step = pl.program_id(0)
    count = g_in.shape[1]
    lane = lax.broadcasted_iota(jnp.int32, (count, 128), 1)
    units = g_in.shape[2]
    piece = units // n
    out_act[...] = act_in[...]
    out_grad[...] = grad_in[...]

    @pl.when(step % 2 == 0)
    def _():
        out_down[...] = d_in[0].astype(F32)
        out_out[...] = o_in[0].astype(F32)

    def tile(ref, q, a):
        return ref[rel[q], :, a * 128 : (a + 1) * 128].astype(F32)

    def join(segments):
        whole = segments[0][1]
        for low, value in segments[1:]:
            whole = jnp.where(lane >= low, value, whole)
        return whole

    for side, ref in ((0, g_in), (1, u_in)):
        for j in range(REPS * units // 128):
            segments = []
            for c in range(128 * j // piece, (128 * j + 127) // piece + 1):
                s, q = c // REPS, c % REPS
                low, high = max(0, c * piece - 128 * j), min(128, (c + 1) * piece - 128 * j)
                start = 128 * j - piece * (c - s)
                a, m = start // 128, start % 128
                if low < 128 - m:
                    value = tile(ref, q, a)
                    segments.append((low, pltpu.roll(value, 128 - m, 1) if m else value))
                if high > 128 - m:
                    segments.append((max(low, 128 - m), pltpu.roll(tile(ref, q, a + 1), 128 - m, 1)))
            first = side * REPS * units + j * 128
            out_gu[:, first : first + 128] = join(segments)
    per = x_in.shape[2] // 64
    for t in range(out_qkv.shape[1] // 128):
        group = t // 2
        ref, at = (x_in, group) if group < per else (y_in, group - per)
        values = []
        for h in (0, 1):
            value = tile(ref, 2 * (t % 2) + h, at // 2)
            values.append((64 * h, pltpu.roll(value, 64, 1) if at % 2 != h else value))
        out_qkv[:, t * 128 : (t + 1) * 128] = join(values)

    @pl.when(step == 0)
    def _():
        small[...] = jnp.zeros_like(small)
        small[0:4, :] = s_in[0, 0:4, :] + s_in[1, 0:4, :] + s_in[2, 0:4, :] + s_in[3, 0:4, :]
        row = lax.broadcasted_iota(jnp.int32, (1, 128), 1)
        own = []
        for q in range(REPS):
            v = s_in[rel[q], 4:7, 0:128]
            own.append(v + pltpu.roll(v, 64, 1))
        for j in (0, 1):
            for p in (0, 1):
                small[4 + j : 5 + j, p * 128 : (p + 1) * 128] = jnp.where(
                    row < 64, own[2 * p][j : j + 1], own[2 * p + 1][j : j + 1]
                )
        keys = own[0][2:3]
        for q in range(1, REPS):
            keys = jnp.where(row >= q * ROT, pltpu.roll(own[q][2:3], q * ROT, 1), keys)
        small[6:7, 0:128] = keys
        whole = small[...].T
        out_vectors[...] = whole[:, 0:6]
        out_key[...] = whole[: out_key.shape[0], 6:7]


def weave_call(n, rel, act, grad, key_rows, parts):
    d, g, u, x, y, o, s = [parts[name] for name in PARTS]
    turns = 2 * REPS
    rows = g.shape[1]
    count = rows // turns
    S = jax.ShapeDtypeStruct

    def piece(a):
        return pl.BlockSpec((REPS, count, a.shape[2]), lambda i, rel: (0, i, 0))

    def slab(a):
        return pl.BlockSpec((1,) + a.shape[1:], lambda i, rel: (rel[i // 2], 0, 0))

    def lines(width):
        return pl.BlockSpec((count, width), lambda i, rel: (i, 0))

    def stack(a):
        return pl.BlockSpec(a.shape[1:], lambda i, rel: (i // 2, 0))

    lanes, units = 2 * REPS * x.shape[2], 2 * REPS * g.shape[2]
    return pl.pallas_call(
        functools.partial(weave_kernel, n),
        out_shape=[
            S(act.shape, BF16),
            S(grad.shape, BF16),
            S((rows, 6), F32),
            S((key_rows, 1), F32),
            S((rows, lanes), F32),
            S((REPS * o.shape[1], o.shape[2]), F32),
            S((rows, units), F32),
            S((REPS * d.shape[1], d.shape[2]), F32),
        ],
        grid_spec=pltpu.PrefetchScalarGridSpec(
            num_scalar_prefetch=1,
            grid=(turns,),
            in_specs=[slab(d), piece(g), piece(u), piece(x), piece(y), slab(o)]
            + [pl.BlockSpec(s.shape, lambda i, rel: (0, 0, 0)), lines(act.shape[1]), lines(act.shape[1])],
            out_specs=[
                lines(act.shape[1]),
                lines(act.shape[1]),
                pl.BlockSpec((rows, 6), lambda i, rel: (0, 0)),
                pl.BlockSpec((key_rows, 1), lambda i, rel: (0, 0)),
                lines(lanes),
                stack(o),
                lines(units),
                stack(d),
            ],
            scratch_shapes=[pltpu.VMEM(s.shape[1:], F32)],
        ),
        compiler_params=pltpu.CompilerParams(vmem_limit_bytes=VMEM_LIMIT),
    )(rel, d, g, u, x, y, o, s, act, grad)


def core_swap(x):
    return lax.ppermute(x, "rep", [(0, 1), (1, 0), (2, 3), (3, 2)])


def y_swap(x):
    return lax.ppermute(x, "rep", [(0, 2), (1, 3), (2, 0), (3, 1)])


def rep_parts(x):
    across = y_swap(x)
    return [x, across, core_swap(x), core_swap(across)]


def rep_gather(x):
    return jnp.concatenate(rep_parts(x), axis=0)


def rep_reduce(a, w_dot, slots):
    far = core_swap(w_dot(a[2 * slots :]).astype(BF16))
    near = w_dot(a[: 2 * slots]) + far.astype(F32)
    return near[:slots] + y_swap(near[slots:].astype(BF16)).astype(F32)


def solution(mesh):
    n = mesh.shape["shard"]
    half_ring = n // 2
    order = list(range(0, n, 2)) + list(range(n - 1, 0, -2))
    place = [order.index(s) for s in range(n)]
    up_ring = [(order[i], order[(i + 1) % n]) for i in range(n)]
    down_ring = [(b, a) for a, b in up_ring]

    def hop(x, ring, sent):
        if len(sent) >= DEPTH:
            x, _ = lax.optimization_barrier((x, sent[-DEPTH]))
        x = lax.ppermute(x, "shard", ring)
        sent.append(x)
        return x

    def ring_ids():
        spot = jnp.array(place, jnp.int32)[lax.axis_index("shard")]
        table = jnp.array(order, jnp.int32)
        return {k: table[(spot + k) % n] for k in range(-half_ring, half_ring + 1)}

    def gather(x, ids, forward_extra, places, line):
        bufs = places(None, x, ids[0])
        up = down = x
        for k in range(1, half_ring + 1):
            go_up = k < half_ring or forward_extra
            go_down = k < half_ring or not forward_extra
            if go_up:
                up = hop(up, up_ring, line[0])
            if go_down:
                down = hop(down, down_ring, line[1])
            if go_up:
                bufs = places(bufs, up, ids[-k])
            if go_down:
                bufs = places(bufs, down, ids[k])
            yield
        return bufs

    def put(bufs, block, at):
        if bufs is None:
            bufs = jnp.zeros((n,) + block.shape, block.dtype)
        return lax.dynamic_update_index_in_dim(bufs, block, at, 0)

    def reduce(term, ids, forward_extra, line, kind=BF16):
        acc = {}
        for k in range(half_ring, 0, -1):
            for side, (ring, sign, extra) in enumerate(
                ((up_ring, 1, forward_extra), (down_ring, -1, not forward_extra))
            ):
                if k == half_ring and not extra:
                    continue
                part = term(ids[sign * k])
                if side in acc:
                    part = part + acc[side].astype(F32)
                acc[side] = hop(part.astype(kind), ring, line[side])
            yield
        return term(ids[0]) + acc[0].astype(F32) + acc[1].astype(F32)

    def run(chains, turns):
        done = {}
        for name in turns:
            for _ in range(n // 8):
                if name in done:
                    continue
                try:
                    next(chains[name])
                except StopIteration as stop:
                    done[name] = stop.value
        for name, chain in chains.items():
            while name not in done:
                try:
                    next(chain)
                except StopIteration as stop:
                    done[name] = stop.value
        return done

    def pick_columns(w, groups, width, r):
        chosen = [
            lax.select_n(
                r,
                *[
                    w[:, (g * REPS + q) * width : (g * REPS + q + 1) * width]
                    for q in range(REPS)
                ],
            )
            for g in range(groups)
        ]
        return jnp.concatenate(chosen, axis=1)

    def by_rep(parts, y, core):
        own, across, beside, both = parts
        low0 = lax.select(core == 0, own, beside)
        low1 = lax.select(core == 0, beside, own)
        high0 = lax.select(core == 0, across, both)
        high1 = lax.select(core == 0, both, across)
        return [
            lax.select(y == 0, low0, high0),
            lax.select(y == 0, low1, high1),
            lax.select(y == 0, high0, low0),
            lax.select(y == 0, high1, low1),
        ]

    def weave(parts, groups, width):
        pieces = [
            parts[q][:, g * width : (g + 1) * width]
            for g in range(groups)
            for q in range(REPS)
        ]
        return jnp.concatenate(pieces, axis=1).astype(F32)

    def on_device(
        tokens, cotangent, block_seq, block_len, vectors, key_bias, w_qkv, w_out, w_gate_up, w_down
    ):
        slots, features = tokens.shape
        blocks = block_seq.shape[0]
        block_size = slots // blocks
        head_dim = features // HEADS
        own_heads = HEADS // REPS
        own_width = own_heads * head_dim
        all_slots = REPS * slots
        scale = 1.0 / math.sqrt(head_dim)
        rows = features // n
        hidden_units = w_gate_up.shape[1] // 2
        own_hidden = hidden_units // REPS
        down_rows = w_down.shape[0] // REPS
        out_rows = w_out.shape[0] // REPS
        regroup = out_rows < head_dim
        r = lax.axis_index("rep")
        y, core = r // 2, r % 2
        ids = ring_ids()

        def mix_out(x):
            if not regroup:
                return x
            pairs = [
                (k * n + 4 * j + q, q * n + 4 * j + k)
                for k in range(REPS)
                for j in range(n // 4)
                for q in range(REPS)
            ]
            return lax.ppermute(x, BOTH, pairs)

        fast = blocks == 2 and down_rows % 16 == 0 and out_rows == head_dim and rows % 128 == 0
        own_valid = (
            jnp.arange(block_size, dtype=jnp.int32)[None, :] < block_len[:, None]
        ).reshape(-1)
        grad_output = cotangent.astype(F32) * own_valid[:, None].astype(F32)
        dyl_own = grad_output.astype(BF16)
        if fast:
            vt = jnp.concatenate(
                [vectors.T, jnp.pad(key_bias.T, ((0, 0), (0, rows - key_bias.shape[0])))], axis=0
            )
            vt = jnp.pad(vt, ((0, 9), (0, 0)))
            angles = np.arange(slots, dtype=np.float32)[:, None] * np.exp(
                np.arange(ROT // 2, dtype=np.float32) * np.float32(-2.0 * math.log(10000.0) / ROT)
            ).astype(np.float32)
            cosine, sine = np.cos(angles), np.sin(angles)
            rest = np.ones((slots, head_dim - ROT), np.float32)
            none = np.zeros((slots, ROT // 2), np.float32)
            tables = np.stack(
                [
                    np.concatenate([cosine, cosine, rest] * 2, axis=1),
                    np.concatenate([-sine, none, 0 * rest] * 2, axis=1),
                    np.concatenate([none, sine, 0 * rest] * 2, axis=1),
                ]
            ).astype(np.float32)
            weights = (w_qkv, w_out, w_gate_up, w_down)
            out = forward_call(
                n, weights, tokens, cotangent, vt, block_seq, block_len, jnp.asarray(tables)
            )
            q_land, o_land, g_land, u_land, d_land = out[:5]
            a1, qs, ks, vs, ps, attn, resid, a2, gate, up, hid, dyl_all, metas = out[5:]
            whole = (all_slots, features)
            (activations, grad_input), parts = backward_call(
                n,
                out[:5],
                (a1, qs, ks, vs, ps, attn, resid, a2.reshape(whole), gate, up, hid, dyl_all.reshape(whole)),
                tokens,
                metas,
                tables,
            )

            q = jnp.arange(REPS, dtype=jnp.int32)
            rel = jnp.where(q // 2 != y, 1, 0) + jnp.where(q % 2 != core, 2, 0)
            return tuple(
                weave_call(n, rel.astype(jnp.int32), activations, grad_input, key_bias.shape[0], parts)
            )
        else:
            small = jnp.concatenate([vectors.T.reshape(-1), key_bias.reshape(-1)])
            lanes = 3 * own_width
            small_rows = -(-small.size // lanes)
            small_rows = -(-small_rows // 16) * 16
            small = jnp.pad(small, (0, small_rows * lanes - small.size)).reshape(small_rows, lanes)
            qkv_block = jnp.concatenate([pick_columns(w_qkv, 3 * own_heads, head_dim, r), small], axis=0)

            def put_qkv(bufs, block, at):
                a, b = (None, None) if bufs is None else bufs
                return put(a, block[:rows], at), put(b, block[rows:], at)

            out_block = mix_out(lax.dynamic_slice_in_dim(w_out, r * out_rows, out_rows, 0))
            gate_block = pick_columns(w_gate_up[:, :hidden_units], n, down_rows, r)
            up_block = pick_columns(w_gate_up[:, hidden_units:], n, down_rows, r)
            down_block = lax.dynamic_slice_in_dim(w_down, r * down_rows, down_rows, 0)
            line = ([], [])
            got = run(
                {
                    "q": gather(qkv_block, ids, True, put_qkv, line),
                    "o": gather(out_block, ids, False, put, line),
                    "g": gather(gate_block, ids, True, put, line),
                    "u": gather(up_block, ids, False, put, line),
                    "d": gather(down_block, ids, False, put, line),
                },
                "qoqoqoqoguguguguddddd",
            )
            wq, smalls = got["q"]
            wq = wq.reshape(features, lanes)
            smalls = smalls.reshape(n, -1).astype(F32)
            vec = smalls[:, : 6 * rows].reshape(n, 6, rows).transpose(1, 0, 2).reshape(6, features)
            key_full = smalls[:, 6 * rows : 6 * rows + HEADS * ROT // n].reshape(own_heads, REPS, ROT)
            key_own = lax.dynamic_index_in_dim(key_full, r, 1, keepdims=False)
            key_shift = jnp.pad(key_own, ((0, 0), (0, head_dim - ROT))).reshape(own_width)

            def own_heads_of(v):
                return lax.dynamic_index_in_dim(
                    v.reshape(own_heads, REPS, head_dim), r, 1, keepdims=False
                ).reshape(own_width)

            wo = got["o"].reshape(own_width, features)
            wg = got["g"].reshape(features, own_hidden)
            wu = got["u"].reshape(features, own_hidden)
            wd = got["d"].reshape(own_hidden, features)

            meta = jnp.concatenate([block_seq, block_len]).astype(F32)
            meta = jnp.pad(meta, (0, 128 - 2 * blocks)).reshape(1, 128)
            meta = jnp.concatenate(rep_parts(jnp.broadcast_to(meta, (8, 128))), axis=0)
            meta = meta.reshape(REPS, 8, 128)[:, 0, :]
            seqs = meta[:, :blocks].astype(jnp.int32)
            lens = meta[:, blocks : 2 * blocks].astype(jnp.int32)
            index = jnp.arange(blocks, dtype=jnp.int32)
            same = seqs[:, None, :] == seqs[:, :, None]
            earlier = jnp.sum(
                jnp.where((index[None, :] < index[:, None]) & same, 1, 0), axis=2
            ).astype(jnp.int32)
            offset = jnp.arange(block_size, dtype=jnp.int32)
            seq_slot = jnp.broadcast_to(seqs[:, :, None], (REPS, blocks, block_size)).reshape(REPS, slots)
            valid = (offset[None, None, :] < lens[:, :, None]).reshape(REPS, slots)
            positions = (earlier[:, :, None] * block_size + offset[None, None, :]).reshape(all_slots)
            slot_index = jnp.arange(slots, dtype=jnp.int32)
            allowed = (seq_slot[:, None, :] == seq_slot[:, :, None]) & (
                slot_index[None, :] <= slot_index[:, None]
            )[None]
            allowed = allowed & (valid[:, None, :] | (slot_index[None, :] == slot_index[:, None])[None])
            cosine, sine = turn_tables(positions)

            x_all = rep_gather(tokens)
            dyl = rep_gather(dyl_own)

            tokens_f = tokens.astype(F32)
            normal_one, inv_one = normalize(tokens_f)
            normal_all, _ = normalize(x_all.astype(F32))
            a1 = (normal_all * vec[0] + vec[1]).astype(BF16)
            projected = dot(a1, wq)
            head_shape = (all_slots, own_heads, head_dim)
            group_shape = (REPS, slots, own_heads, head_dim)
            q = rotate((projected[:, :own_width] + own_heads_of(vec[4])).reshape(head_shape), cosine, sine)
            k = rotate((projected[:, own_width : 2 * own_width] + key_shift).reshape(head_shape), cosine, sine)
            v = projected[:, 2 * own_width :] + own_heads_of(vec[5])
            q = q.astype(BF16).reshape(group_shape)
            k = k.astype(BF16).reshape(group_shape)
            v = v.astype(BF16).reshape(group_shape)
            scores = jnp.einsum("gshd,gthd->ghst", q, k, preferred_element_type=F32) * scale
            scores = jnp.where(allowed[:, None], scores, -1e30)
            exponent = jnp.exp(scores - jnp.max(scores, axis=-1, keepdims=True))
            probs = exponent / jnp.sum(exponent, axis=-1, keepdims=True)
            probs_low = probs.astype(BF16)
            attn = jnp.einsum("ghst,gthd->gshd", probs_low, v, preferred_element_type=F32)
            attn = attn.reshape(all_slots, own_width).astype(BF16)
            resid = tokens_f + rep_reduce(attn, lambda a: dot(a, wo), slots)
            normal_two, inv_two = normalize(resid)
            a2 = rep_gather((normal_two * vec[2] + vec[3]).astype(BF16))
            gate = dot(a2, wg)
            up = dot(a2, wu)
            sig = jax.nn.sigmoid(gate)
            hidden = (gate * sig * up).astype(BF16)

        def blocks_of(a):
            return a.reshape(all_slots, n, -1).transpose(1, 0, 2)

        hidden_b = blocks_of(hidden)
        activations = (resid + rep_reduce(hidden, lambda a: dot(a, wd), slots)).astype(BF16)
        grad_hidden = dot_rt(dyl, wd)
        grad_gate = (grad_hidden * up * sig * (1.0 + gate * (1.0 - sig))).astype(BF16)
        grad_up = (grad_hidden * gate * sig).astype(BF16)
        a2_b = blocks_of(a2)
        grad_gu = jnp.concatenate([grad_gate, grad_up], axis=1)
        wgu = jnp.concatenate([wg, wu], axis=1)
        grad_a2 = rep_reduce(grad_gu, lambda a: dot_rt(a, wgu), slots)
        grad_resid = grad_output + norm_back(grad_a2 * vec[2], normal_two, inv_two)
        drl = rep_gather(grad_resid.astype(BF16))
        attn_b = blocks_of(attn)
        d_attn = dot_rt(drl, wo).astype(BF16).reshape(group_shape)
        grad_v = jnp.einsum("ghst,gshd->gthd", probs_low, d_attn, preferred_element_type=F32)
        grad_p = jnp.einsum("gshd,gthd->ghst", d_attn, v, preferred_element_type=F32)
        delta = jnp.sum(grad_p * probs, axis=-1, keepdims=True)
        grad_s = (probs * (grad_p - delta)).astype(BF16)
        grad_q = jnp.einsum("ghst,gthd->gshd", grad_s, k, preferred_element_type=F32) * scale
        grad_k = jnp.einsum("ghst,gshd->gthd", grad_s, q, preferred_element_type=F32) * scale
        grad_q = rotate(grad_q.reshape(head_shape), cosine, -sine)
        grad_k = rotate(grad_k.reshape(head_shape), cosine, -sine)
        grad_v = grad_v.reshape(head_shape)
        key_sum = jnp.sum(grad_k[:, :, :ROT], axis=0)
        d_qkv = jnp.concatenate(
            [g.reshape(all_slots, own_width) for g in (grad_q, grad_k, grad_v)], axis=1
        ).astype(BF16)
        a1_b = blocks_of(a1)
        grad_a1 = rep_reduce(d_qkv, lambda a: dot_rt(a, wq), slots)
        grad_input = (grad_resid + norm_back(grad_a1 * vec[0], normal_one, inv_one)).astype(BF16)

        def spread(sums):
            zero = jnp.zeros((own_heads, REPS, sums.shape[1]), F32)
            return lax.dynamic_update_index_in_dim(zero, sums, r, 1)

        vec_sums = jnp.stack(
            [
                jnp.sum(grad_a1 * normal_one, axis=0),
                jnp.sum(grad_a1, axis=0),
                jnp.sum(grad_a2 * normal_two, axis=0),
                jnp.sum(grad_a2, axis=0),
                spread(jnp.sum(grad_q, axis=0)).reshape(features),
                spread(jnp.sum(grad_v, axis=0)).reshape(features),
            ],
            axis=0,
        )
        key_rows = HEADS * ROT // n
        packed = jnp.concatenate(
            [
                vec_sums.reshape(6, n, rows).transpose(1, 0, 2).reshape(n, 6 * rows),
                spread(key_sum).reshape(n, key_rows),
            ],
            axis=1,
        )
        width = -(-packed.shape[1] // 1024) * 1024
        packed = jnp.pad(packed, ((0, 0), (0, width - packed.shape[1]))).reshape(n, width // 128, 128)
        line = ([], [])
        sums = run(
            {
                "d": reduce(lambda i: dot_lt(hidden_b[i], dyl), ids, False, line),
                "g": reduce(lambda i: dot_lt(a2_b[i], grad_gate), ids, True, line),
                "u": reduce(lambda i: dot_lt(a2_b[i], grad_up), ids, False, line),
                "q": reduce(lambda i: dot_lt(a1_b[i], d_qkv), ids, True, line),
                "o": reduce(lambda i: dot_lt(attn_b[i], drl), ids, False, line),
                "s": reduce(lambda i: packed[i], ids, True, line, F32),
            },
            "dgdgdudugugugqoqoqosoqsoss",
        )
        grad_down, grad_wg, grad_wu = sums["d"], sums["g"], sums["u"]
        grad_wq, grad_wo, packed = sums["q"], sums["o"], sums["s"]
        packed = packed + core_swap(packed)
        packed = (packed + y_swap(packed)).reshape(-1)
        out_vectors = packed[: 6 * rows].reshape(6, rows).T
        out_key = packed[6 * rows : 6 * rows + key_rows].reshape(key_rows, 1)

        def everywhere(g):
            return by_rep(rep_parts(g.astype(BF16)), y, core)

        out_down = jnp.concatenate(everywhere(grad_down), axis=0).astype(F32)
        out_gate_up = jnp.concatenate(
            [weave(everywhere(g), n, down_rows) for g in (grad_wg, grad_wu)], axis=1
        )
        out_qkv = weave(everywhere(grad_wq), 3 * own_heads, head_dim)
        out_out = jnp.concatenate(everywhere(mix_out(grad_wo.astype(BF16))), axis=0).astype(F32)
        return activations, grad_input, out_vectors, out_key, out_qkv, out_out, out_gate_up, out_down

    tok, row = P(BOTH, None), P("shard", None)
    return jax.shard_map(
        on_device,
        mesh=mesh,
        in_specs=(tok, tok, P(BOTH), P(BOTH)) + (row,) * 6,
        out_specs=(tok, tok) + (row,) * 6,
        check_vma=False,
    )
```

```python
import functools
import math

import jax
import jax.numpy as jnp
import numpy as np
from jax import lax
from jax.experimental import pallas as pl
from jax.experimental.pallas import tpu as pltpu
from jax.sharding import PartitionSpec as P

HEADS = 32
ROT = 16
REPS = 4
BOTH = ("rep", "shard")
DEPTH = 2
F32 = jnp.float32
BF16 = jnp.bfloat16


def dot(a, b):
    return jnp.dot(a, b, preferred_element_type=F32)


def dot_rt(a, b):
    return lax.dot_general(a, b, (((1,), (1,)), ((), ())), preferred_element_type=F32)


def dot_lt(a, b):
    return lax.dot_general(a, b, (((0,), (0,)), ((), ())), preferred_element_type=F32)


def turn_tables(positions):
    half = ROT // 2
    frequencies = jnp.exp(
        jnp.arange(half, dtype=F32) * (-2.0 * math.log(10000.0) / ROT)
    )
    angles = positions.astype(F32)[:, None] * frequencies[None, :]
    return jnp.cos(angles)[:, None, :], jnp.sin(angles)[:, None, :]


def rotate(values, cosine, sine):
    half = ROT // 2
    low, high, rest = values[..., :half], values[..., half:ROT], values[..., ROT:]
    return jnp.concatenate(
        [low * cosine - high * sine, high * cosine + low * sine, rest], axis=-1
    )


def normalize(values):
    center = values - jnp.mean(values, axis=1, keepdims=True)
    inv_std = lax.rsqrt(jnp.mean(center * center, axis=1, keepdims=True) + 1e-05)
    return center * inv_std, inv_std


def norm_back(grad_norm, normal, inv_std):
    mean_grad = jnp.mean(grad_norm, axis=1, keepdims=True)
    mean_cross = jnp.mean(grad_norm * normal, axis=1, keepdims=True)
    return inv_std * (grad_norm - mean_grad - normal * mean_cross)


MESH = pl.DeviceIdType.MESH
NAMES = ("q", "o", "g", "u", "d", "s")
LONG_UP = {"q": True, "o": True, "g": False, "u": False, "d": True, "s": True}
FORE_ORDER = (
    "o1", "q1", "o2", "su", "pm", "q2", "sg", "px", "cot", "o3", "q3", "u1", "g1", "bd", "q4", "ln1", "at2",
    "o4", "u2", "at3", "of", "at0", "g2", "at1", "oy", "d1", "u3", "oo", "g3", "ln2", "d2", "g4", "pa", "u4",
    "pd", "fd0", "d3", "fd1", "fd2", "fd3", "d4",
)
VMEM_LIMIT = 64 * 1024 * 1024 - 64 * 1024


class Place:
    def __init__(self, n):
        self.n, self.half = n, n // 2
        self.r, self.s = lax.axis_index("rep"), lax.axis_index("shard")
        self.core = self.r + 1 - 2 * (self.r % 2)
        self.across = (self.r + 2) % REPS
        odd = self.s % 2
        self.spot = (1 - odd) * (self.s // 2) + odd * (n - 1 - self.s // 2)
        self.ids = {k: self.shard_at(k) for k in range(-self.half, self.half + 1)}
        self.ring = (self.ids[1], self.ids[-1])

    def shard_at(self, k):
        q = (self.spot + k + self.n) % self.n
        back = q // self.half
        return (1 - back) * 2 * q + back * (2 * self.n - 1 - 2 * q)

    def greet(self):
        barrier = pltpu.get_barrier_semaphore()
        for who in (
            (self.core, self.s),
            (self.across, self.s),
            (self.r, self.ring[0]),
            (self.r, self.ring[1]),
        ):
            pl.semaphore_signal(barrier, inc=1, device_id=who, device_id_type=MESH)
        pl.semaphore_wait(barrier, 4)


class RepLinks:
    def __init__(self, place, send, recv):
        self.place, self.send, self.recv, self.sent = place, send, recv, []

    def copy(self, i, src, dst, who):
        return pltpu.make_async_remote_copy(
            src_ref=src,
            dst_ref=dst,
            send_sem=self.send.at[i],
            recv_sem=self.recv.at[i],
            device_id=(who, self.place.s),
            device_id_type=MESH,
        )

    def start(self, i, src, dst, who):
        c = self.copy(i, src, dst, who)
        c.start()
        self.sent.append(c)
        return c

    def gather_start(self, i, own, slots):
        a = self.start(i, own, slots.at[1], self.place.across)
        b = self.start(i + 1, own, slots.at[2], self.place.core)
        return a, b

    def gather_pass(self, i, slots, copies):
        copies[0].wait_recv()
        return copies[1], self.start(i + 2, slots.at[1], slots.at[3], self.place.core)

    def finish(self):
        for c in self.sent:
            c.wait_send()


def layer_rows(x, gain, shift):
    center = x - jnp.mean(x, axis=1, keepdims=True)
    inv = lax.rsqrt(jnp.mean(center * center, axis=1, keepdims=True) + 1e-05)
    return center * inv * gain + shift


def first_half(shape):
    return lax.broadcasted_iota(jnp.int32, shape, 1) < 64


def forward_kernel(
    n,
    w_qkv, w_out, w_gu, w_down, tok, cot, vt, seqs, lens, tables,
    q_land, o_land, g_land, u_land, d_land, s_land, a1_out, q_out, k_out, v_out, p_out, attn_out,
    resid_out, a2_out, gate_out, up_out, hid_out, dyl_out, meta_out,
    q_blk, s_blk, g_blk, u_blk, wq, wo, wg, wu, xs, qs, ks, vs, ps, attn, attn_t, acc, csend, crecv, ysend,
    yrecv, resid, a2s, gates, ups, hid, metas, tabs, mask, small, vecs,
    ring_send, ring_recv, load_sem, rep_send, rep_recv, out_sem,
):
    here = Place(n)
    half = here.half
    lands = dict(zip(NAMES, (q_land, o_land, g_land, u_land, d_land, s_land)))
    rows = {name: lands[name].shape[1] for name in NAMES}
    slots, width = tok.shape
    blocks = {
        "q": q_blk,
        "s": s_blk,
        "o": w_out.at[pl.ds(pl.multiple_of(here.r * rows["o"], 16), rows["o"])],
        "g": g_blk,
        "u": u_blk,
        "d": w_down.at[pl.ds(pl.multiple_of(here.r * rows["d"], 16), rows["d"])],
    }
    into = {"q": wq, "o": wo, "g": wg, "u": wu, "s": small}
    reach = {
        (name, d): half if LONG_UP[name] == (d == 0) else half - 1 for name in NAMES for d in (0, 1)
    }

    def message(name, d, k):
        i = here.ids[(1 - k) if d == 0 else (k - 1)]
        a = NAMES.index(name)
        src = blocks[name] if k == 1 else lands[name].at[i]
        return pltpu.make_async_remote_copy(
            src_ref=src,
            dst_ref=lands[name].at[i],
            send_sem=ring_send.at[a, d, k - 1],
            recv_sem=ring_recv.at[a, d, k - 1],
            device_id=(here.r, here.ring[d]),
            device_id_type=MESH,
        )

    def load(name, k):
        i = here.ids[k]
        a = NAMES.index(name)
        dst = into[name].at[pl.ds(pl.multiple_of(i * rows[name], 16), rows[name])]
        return pltpu.make_async_copy(lands[name].at[i], dst, load_sem.at[a, k + half])

    def keep_own(name):
        return pltpu.make_async_copy(
            blocks[name] if name != "d" else csend.at[0, pl.ds(0, rows["d"])],
            lands[name].at[here.s],
            load_sem.at[6, NAMES.index(name)],
        )

    def begin(name):
        for d in (0, 1):
            message(name, d, 1).start()
        if name == "d":
            held["own"] = fetch(blocks["d"], csend.at[0, pl.ds(0, rows["d"])], 4)
        else:
            keep_own(name).start()

    def serve(name, k):
        for d in (0, 1):
            if k <= reach[name, d]:
                message(name, d, k).wait_recv()
                if k < reach[name, d]:
                    message(name, d, k + 1).start()
                if name in into:
                    load(name, -k if d == 0 else k).start()

    def own_kept(name):
        keep_own(name).wait()
        load(name, 0).start()

    def came(name):
        found = [0]
        for k in range(1, half + 1):
            found += [-k] * (k <= reach[name, 0]) + [k] * (k <= reach[name, 1])
        return found

    def loaded(name):
        for k in came(name):
            load(name, k).wait()

    outs = []
    held = {}

    def save(src, dst):
        c = pltpu.make_async_copy(src, dst, out_sem.at[len(outs)])
        c.start()
        outs.append(c)

    def fetch(src, dst, i):
        c = pltpu.make_async_copy(src, dst, load_sem.at[7, i])
        c.start()
        return c

    def rows16(count, body):
        @pl.loop(0, count // 16)
        def _(i):
            body(pl.ds(pl.multiple_of(i * 16, 16), 16))

    own_width = wq.shape[1] // 3
    pairs = own_width // 128
    block = slots // 2
    units = g_blk.shape[1]
    rep = RepLinks(here, rep_send, rep_recv)
    lane = lax.broadcasted_iota(jnp.int32, (1, 128), 1)
    low = first_half((slots, 128))

    class XSlots:
        class at:
            def __class_getitem__(cls, g):
                return xs.at[pl.ds(g * slots, slots)]

    windows = []
    for t in range(3 * pairs):
        part, tt = t // pairs, t % pairs
        for h in (0, 1):
            first = part * width + (2 * tt + h) * 4 * 64
            i = len(windows)
            dst = hid.at[pl.ds(slots * (i // 8), slots), pl.ds(128 * (i % 8), 128)]
            start = pl.multiple_of(first + (here.r // 2) * 128, 128)
            c = pltpu.make_async_copy(w_qkv.at[:, pl.ds(start, 128)], dst, rep_send.at[14 + i])
            c.start()
            windows.append((c, dst))
    own_x = fetch(tok, xs.at[pl.ds(0, slots)], 0)
    own_c = fetch(cot, ysend, 1)

    long0, long1 = lens[0], lens[1]
    spot = lax.broadcasted_iota(jnp.int32, (8, slots), 1)
    end = jnp.where(spot < block, long0, long1 + block)
    row = lax.broadcasted_iota(jnp.int32, (8, slots), 0)
    together = jnp.where(seqs[0] == seqs[1], 1.0, 0.0)
    metas[0] = jnp.where(row == 0, jnp.where(spot < end, 1.0, 0.0), together)

    base = vt[...].astype(F32)
    side = (here.s % 2) * 64
    wide = rows["q"]
    head = pltpu.roll(base, (side - here.r * 64 + wide) % wide, 1)
    keys = pltpu.roll(base, (side - here.r * ROT + wide) % wide, 1)
    line = lax.broadcasted_iota(jnp.int32, (16, wide), 0)
    place = lax.broadcasted_iota(jnp.int32, (16, wide), 1)
    inside = (place >= side) & (place < side + 64)
    key_inside = (place >= side) & (place < side + ROT)
    own_small = jnp.where(
        line < 4,
        base,
        jnp.where(
            (line < 6) & inside, head, jnp.where((line == 6) & key_inside, keys, 0.0)
        ),
    )
    s_blk[...] = own_small.astype(BF16)

    here.greet()
    begin("s")
    begin("o")
    held["m"] = rep.gather_start(0, metas.at[0], metas)
    held["x"] = rep.gather_start(3, tok, XSlots)
    odd = (jnp.zeros((slots, 128), jnp.int32) + here.r % 2) == 1
    for t in range(3 * pairs):
        pair = []
        for h in (0, 1):
            c, ref = windows[2 * t + h]
            c.wait()
            value = ref[...].astype(F32)
            swapped = pltpu.roll(value, 64, 1)
            pair.append(jnp.where(odd, swapped, value) if h == 0 else jnp.where(odd, value, swapped))
        q_blk[0:wide, t * 128 : (t + 1) * 128] = jnp.where(low, pair[0], pair[1]).astype(BF16)
    begin("q")

    strips = []
    span = 384
    total = REPS * units
    piece = units // n
    for j in (0, 1):
        for s in range(n):
            o = s * REPS * piece + here.r * piece
            if s < half:
                off = o % 128
                a = o - off
            else:
                pad = (128 - (o + piece) % 128) % 128
                a = o + piece + pad - span
                off = span - piece - pad
            i = len(strips)
            ref = gates if j == 0 else ups
            dst = ref.at[pl.ds(slots * (s // 3), slots), pl.ds(span * (s % 3), span)]
            start = pl.multiple_of(j * total + a, 128)
            c = pltpu.make_async_copy(w_gu.at[:, pl.ds(start, span)], dst, rep_recv.at[14 + i])
            c.start()
            strips.append((c, dst, off))

    def select(j):
        for c, _, _ in strips[j * n : (j + 1) * n]:
            c.wait()
        out = (g_blk, u_blk)[j]
        for t in range(units // 128):
            whole = None
            for s in range(128 * t // piece, (128 * t + 127) // piece + 1):
                _, ref, off = strips[j * n + s]
                shift = (2 * span - (off + 128 * t - piece * s)) % span
                value = pltpu.roll(ref[...].astype(F32), shift, 1)[:, :128]
                first = s * piece - 128 * t
                whole = value if whole is None else jnp.where(lane >= first, value, whole)
            out[:, t * 128 : (t + 1) * 128] = whole.astype(BF16)

    def sel_g():
        select(0)
        begin("g")

    def sel_u():
        select(1)
        begin("u")

    def pass_m():
        held["m"] = rep.gather_pass(0, metas, held["m"])

    def pass_x():
        held["x"] = rep.gather_pass(3, XSlots, held["x"])

    def mask_cot():
        own_c.wait()
        for j in range(2):
            count = (long0, long1)[j]

            def chunk(at, j=j, count=count):
                first = lax.broadcasted_iota(jnp.int32, (16, width), 0) + at.start
                at = pl.ds(pl.multiple_of(at.start + j * block, 16), 16)
                value = ysend[at, :].astype(F32)
                ysend[at, :] = jnp.where(first < count, value, 0.0).astype(BF16)

            rows16(block, chunk)
        fetch(ysend, dyl_out.at[0], 2).wait()
        held["d"] = rep.gather_start(6, dyl_out.at[0], dyl_out)

    def pass_d():
        held["d"] = rep.gather_pass(6, dyl_out, held["d"])

    def ln1():
        for c in held["m"] + held["x"]:
            c.wait_recv()
        own_x.wait()
        mine = held["x"][1]
        mine.wait_send()
        rep.sent = [c for c in rep.sent if c is not mine]
        for name in "qs":
            own_kept(name)
            loaded(name)
        held["own"].wait()
        keep_own("d").start()
        for s in range(n):
            vecs[0:8, s * wide : (s + 1) * wide] = small[s * 16 : s * 16 + 8, :].astype(F32)
        gain, shift = vecs[0:1, :], vecs[1:2, :]

        def chunk(at):
            xs[at, :] = layer_rows(xs[at, :].astype(F32), gain, shift).astype(BF16)

        rows16(REPS * slots, chunk)
        save(xs, a1_out)

    def lane_bias(row, t):
        w = rows["q"]
        a = vecs[row : row + 1, 2 * t * w : 2 * t * w + 128]
        return a + vecs[row : row + 1, (2 * t + 1) * w : (2 * t + 1) * w + 128]

    def attend(g):
        line = lax.broadcasted_iota(jnp.int32, (slots, slots), 0)
        column = lax.broadcasted_iota(jnp.int32, (slots, slots), 1)
        here_rows = pl.ds(g * slots, slots)
        acc[...] = dot(xs[here_rows, :], wq[...])
        valid = metas[g, 0:1, :]
        same = metas[g, 1:2, :]
        for j in range(3):
            tabs[j, :block, :] = tables[j, :block, :]
            tabs[j, block:, :] = jnp.where(
                same[:, :128] > 0.5, tables[j, block:, :], tables[j, :block, :]
            )
        apart = (line >= block) & (column < block) & (same < 0.5)
        open_ = (column <= line) & jnp.logical_not(apart) & ((valid > 0.5) | (line == column))
        mask[...] = jnp.where(open_, 0.0, -1e30)
        for t in range(3 * pairs):
            part, tt = t // pairs, t % pairs
            tile = acc[:, t * 128 : (t + 1) * 128] + lane_bias((4, 6, 5)[part], tt)
            if part < 2:
                tile = (
                    tile * tabs[0]
                    + pltpu.roll(tile, 120, 1) * tabs[1]
                    + pltpu.roll(tile, 8, 1) * tabs[2]
                )
            (qs, ks, vs)[part][g, tt] = tile.astype(BF16)
        low_low = first_half((1, 128)).astype(F32).astype(BF16)
        high_low = (1.0 - first_half((1, 128)).astype(F32)).astype(BF16)
        for t in range(pairs):
            qt, kt, vt_ = qs[g, t], ks[g, t], vs[g, t]
            mixed = []
            for h in (0, 1):
                mine = low_low if h == 0 else high_low
                sc = dot_rt(qt * mine, kt) * (1.0 / 8.0) + mask[...]
                e = jnp.exp(sc - jnp.max(sc, axis=1, keepdims=True))
                p = (e / jnp.sum(e, axis=1, keepdims=True)).astype(BF16)
                ps[g, 2 * t + h] = p
                mixed.append(dot(p, vt_))
            mix = jnp.where(low, mixed[0], mixed[1])
            attn[here_rows, t * 128 : (t + 1) * 128] = mix.astype(BF16)
            attn_t[t * 128 : (t + 1) * 128, here_rows] = mix.T.astype(BF16)

    def out_far():
        keep_own("d").wait()
        own_kept("o")
        loaded("o")
        for g in (0, 1):
            csend[g] = dot(attn[(g + 2) * slots : (g + 3) * slots, :], wo[...]).astype(BF16)
        held["core"] = rep.start(9, csend, crecv, here.core)

    def out_y():
        held["core"].wait_recv()
        ysend[...] = (dot(attn[slots : 2 * slots, :], wo[...]) + crecv[1].astype(F32)).astype(BF16)
        held["y"] = rep.start(10, ysend, yrecv, here.across)

    def out_own():
        resid[...] = dot(attn[0:slots, :], wo[...]) + crecv[0].astype(F32)
        held["tok"] = fetch(tok, crecv.at[0], 3)
        save(qs, q_out)
        save(ks, k_out)
        save(vs, v_out)
        save(ps, p_out)
        save(attn_t, attn_out)
        save(metas, meta_out)

    def ln2():
        held["tok"].wait()
        held["y"].wait_recv()
        gain, shift = vecs[2:3, :], vecs[3:4, :]

        def chunk(at):
            x = resid[at, :] + yrecv[at, :].astype(F32) + crecv[0, at, :].astype(F32)
            resid[at, :] = x
            a2s[0, at, :] = layer_rows(x, gain, shift).astype(BF16)

        rows16(slots, chunk)
        held["a"] = rep.gather_start(11, a2s.at[0], a2s)
        save(resid, resid_out)

    def pass_a():
        held["a"] = rep.gather_pass(11, a2s, held["a"])

    def feed(g):
        if g == 0:
            own_kept("g")
            own_kept("u")
            for c in held["a"]:
                c.wait_recv()
            loaded("g")
            loaded("u")
            save(a2s, a2_out)
        at = pl.ds(g * slots, slots)
        gate = dot(a2s[g], wg[...])
        gates[at, :] = gate.astype(BF16)
        up = dot(a2s[g], wu[...])
        ups[at, :] = up.astype(BF16)
        act = gate * jax.nn.sigmoid(gate) * up
        for j in range(act.shape[1] // 128):
            hid[j * 128 : (j + 1) * 128, at] = act[:, j * 128 : (j + 1) * 128].T.astype(BF16)
        if g == REPS - 1:
            save(gates, gate_out)
            save(ups, up_out)
            save(hid, hid_out)

    steps = {
        "sg": sel_g, "su": sel_u, "bd": lambda: begin("d"), "pm": pass_m, "px": pass_x, "cot": mask_cot,
        "pd": pass_d, "ln1": ln1, "of": out_far, "oy": out_y, "oo": out_own, "ln2": ln2, "pa": pass_a,
    }
    for name in FORE_ORDER:
        if name in steps:
            steps[name]()
        elif name[:2] == "at":
            attend(int(name[2]))
        elif name[:2] == "fd":
            feed(int(name[2]))
        else:
            if name[0] == "q":
                serve("s", int(name[1]))
            serve(name[0], int(name[1]))
    for c in held["d"]:
        c.wait_recv()
    for name in NAMES:
        for d in (0, 1):
            for k in range(1, reach[name, d] + 1):
                message(name, d, k).wait_send()
    rep.finish()
    for c in outs:
        c.wait()


def forward_call(n, weights, tok, cot, vt, seqs, lens, tables):
    slots, width = tok.shape
    w_qkv, w_out, w_gu, w_down = weights
    lanes, units = w_qkv.shape[1] // REPS, w_gu.shape[1] // 2 // REPS
    rows, own_width = width // n, lanes // 3
    all_slots = REPS * slots
    pairs = own_width // 128
    half = n // 2
    S = jax.ShapeDtypeStruct
    heads = (REPS, pairs, slots, 128)
    out_shape = [
        S((n, rows, lanes), BF16),
        S((n, w_out.shape[0] // REPS, width), BF16),
        S((n, rows, units), BF16),
        S((n, rows, units), BF16),
        S((n, w_down.shape[0] // REPS, width), BF16),
        S((n, 16, rows), BF16),
        S((all_slots, width), BF16),
        S(heads, BF16),
        S(heads, BF16),
        S(heads, BF16),
        S((REPS, 2 * pairs, slots, slots), BF16),
        S((own_width, all_slots), BF16),
        S((slots, width), F32),
        S((REPS, slots, width), BF16),
        S((all_slots, units), BF16),
        S((all_slots, units), BF16),
        S((units, all_slots), BF16),
        S((REPS, slots, width), BF16),
        S((REPS, 8, slots), F32),
    ]
    V = pltpu.VMEM
    scratch = [
        V((rows, lanes), BF16),
        V((16, rows), BF16),
        V((rows, units), BF16),
        V((rows, units), BF16),
        V((width, lanes), BF16),
        V((own_width, width), BF16),
        V((width, units), BF16),
        V((width, units), BF16),
        V((all_slots, width), BF16),
        V(heads, BF16),
        V(heads, BF16),
        V(heads, BF16),
        V((REPS, 2 * pairs, slots, slots), BF16),
        V((all_slots, own_width), BF16),
        V((own_width, all_slots), BF16),
        V((slots, lanes), F32),
        V((2, slots, width), BF16),
        V((2, slots, width), BF16),
        V((slots, width), BF16),
        V((slots, width), BF16),
        V((slots, width), F32),
        V((REPS, slots, width), BF16),
        V((all_slots, units), BF16),
        V((all_slots, units), BF16),
        V((units, all_slots), BF16),
        V((REPS, 8, slots), F32),
        V((3, slots, 128), F32),
        V((slots, slots), F32),
        V((n * 16, rows), BF16),
        V((8, width), F32),
        pltpu.SemaphoreType.DMA((6, 2, half)),
        pltpu.SemaphoreType.DMA((6, 2, half)),
        pltpu.SemaphoreType.DMA((8, 2 * half + 1)),
        pltpu.SemaphoreType.DMA((14 + 6 * pairs,)),
        pltpu.SemaphoreType.DMA((14 + 2 * n,)),
        pltpu.SemaphoreType.DMA((12,)),
    ]
    anywhere = pl.BlockSpec(memory_space=pltpu.HBM)
    inside = pl.BlockSpec(memory_space=pltpu.VMEM)
    scalars = pl.BlockSpec(memory_space=pltpu.SMEM)
    return pl.pallas_call(
        functools.partial(forward_kernel, n),
        out_shape=out_shape,
        in_specs=[anywhere] * 6 + [inside, scalars, scalars, inside],
        out_specs=[anywhere] * len(out_shape),
        scratch_shapes=scratch,
        compiler_params=pltpu.CompilerParams(
            collective_id=1, has_side_effects=True, vmem_limit_bytes=VMEM_LIMIT
        ),
    )(*weights, tok, cot, vt, seqs, lens, tables)


PARTS = ("d", "g", "u", "x", "y", "o", "p", "s")
PARTS_UP = {"d": False, "g": True, "u": False, "x": True, "y": True, "o": False, "p": False, "s": False}
BACK_ORDER = (
    "d0", "dh0", "dh1", "dh2", "dh3", "g0", "far2", "u0", "d1", "near2", "u1", "g1", "ln2", "mlpf", "u2",
    "mlpn", "pass", "g2", "ldrl", "ey2", "at0", "at1", "p0", "at2", "o0", "g3", "u3", "at3", "act", "y0",
    "far1", "d2", "near1", "y1", "fu", "x0", "fg", "y2", "x1", "d3", "y3", "sums", "x2", "fy", "o1", "x3",
    "fd", "hg", "s0", "hy", "p1", "o2", "fx", "p2", "s1", "hu", "o3", "hd", "s2", "p3", "fo", "s3", "fp",
    "fs", "ho", "hx", "hp", "hs",
)


def norm_rows_back(x, gain, grad):
    center = x - jnp.mean(x, axis=1, keepdims=True)
    inv = lax.rsqrt(jnp.mean(center * center, axis=1, keepdims=True) + 1e-05)
    normal = center * inv
    e = grad * gain
    cross = jnp.mean(e * normal, axis=1, keepdims=True)
    return inv * (e - jnp.mean(e, axis=1, keepdims=True) - normal * cross), normal


def backward_kernel(
    n,
    q_land, o_land, g_land, u_land, d_land, s_land, a1_in, q_in, k_in, v_in, p_in, attn_in,
    resid_in, a2_in, gate_in, up_in, hid_in, dyl_in, tok, metas, tables,
    act_out, grad_out, d_sum, g_sum, u_sum, x_sum, y_sum, o_sum, p_sum, s_sum,
    land_d, land_g, land_u, land_x, land_y, land_o, land_p, land_s, core_land, y_land, drl_land,
    dyl, hid, wd, gates, ups, a2, a1, wst, wo, attn_t, heads, probs, dqkv, datt, csend, crecv,
    ysend, ysend2, yrecv, own, resid, outp, stage, rstage, sstage, small, vecs, sums, headsums, tabs,
    ring_send, ring_recv, load_sem, rep_send, rep_recv, stream_sem, rstage_sem, fin_sem,
):
    here = Place(n)
    half = here.half
    slots, width = tok.shape
    rows = width // n
    units = gates.shape[1]
    lanes = dqkv.shape[1]
    own_width = lanes // 3
    pairs = own_width // 128
    lands = dict(zip(PARTS, (land_d, land_g, land_u, land_x, land_y, land_o, land_p, land_s)))
    finals = dict(zip(PARTS, (d_sum, g_sum, u_sum, x_sum, y_sum, o_sum, p_sum, s_sum)))
    shape = {name: lands[name].shape[2:] for name in PARTS}
    reach = {
        (name, d): half if PARTS_UP[name] == (d == 0) else half - 1 for name in PARTS for d in (0, 1)
    }
    rep = RepLinks(here, rep_send, rep_recv)

    def fetch(src, dst, i):
        c = pltpu.make_async_copy(src, dst, load_sem.at[i])
        c.start()
        return c

    def block_of(i, size):
        return pl.ds(pl.multiple_of(i * size, 16), size)

    def lanes_of(i, size):
        return pl.ds(pl.multiple_of(i * size, 128), size)

    def term(name, i):
        if name == "d":
            return dot(hid[block_of(i, shape["d"][0]), :], dyl[...])
        if name in ("g", "u"):
            return dot_lt(a2[:, lanes_of(i, rows)], (gates if name == "g" else ups)[...])
        if name == "x":
            return dot_lt(a1[:, lanes_of(i, rows)], dqkv[:, : lanes // 2])
        if name == "y":
            return dot_lt(a1[:, lanes_of(i, rows)], dqkv[:, lanes // 2 :])
        if name in ("o", "p"):
            cut = slice(0, width // 2) if name == "o" else slice(width // 2, width)
            return dot(attn_t[block_of(i, shape["o"][0]), :], wd[: dyl.shape[0], cut])
        return sums[i]

    def corner(ref, name):
        return ref.at[pl.ds(0, shape[name][0]), pl.ds(0, shape[name][1])]

    def message(name, d, k, src):
        a = PARTS.index(name)
        return pltpu.make_async_remote_copy(
            src_ref=src,
            dst_ref=lands[name].at[d, k - 1],
            send_sem=ring_send.at[a, d, k - 1],
            recv_sem=ring_recv.at[a, d, k - 1],
            device_id=(here.r, here.ring[d]),
            device_id_type=MESH,
        )

    def landed(name, d, k):
        message(name, d, k, lands[name].at[d, k - 1]).wait_recv()
        dst = sstage.at[2 + d] if name == "s" else corner(rstage.at[d], name)
        c = pltpu.make_async_copy(lands[name].at[d, k - 1], dst, rstage_sem.at[d])
        c.start()
        return c, dst

    flying = {}
    turn = [0, 0]

    def serve(name, j):
        hops = {}
        for d in (0, 1):
            k = half - j if reach[name, d] == half else half - 1 - j
            if k >= 1:
                hops[d] = k
        got = {d: landed(name, d, k + 1) for d, k in hops.items() if j > 0}
        for d, k in hops.items():
            if name == "s":
                slot, key = sstage.at[d], ("s", d)
            else:
                turn[d] = 1 - turn[d]
                slot, key = corner(stage.at[d, turn[d]], name), (d, turn[d])
            part = term(name, here.ids[k if d == 0 else -k])
            if d in got:
                got[d][0].wait()
                part = part + got[d][1][...].astype(F32)
            if key in flying:
                flying.pop(key).wait_send()
            slot[...] = part.astype(slot.dtype)
            flying[key] = message(name, d, k, slot)
            flying[key].start()

    opened = {}

    def finish(name):
        got = [landed(name, d, 1) for d in (0, 1)]
        part = term(name, here.ids[0])
        for c, ref in got:
            c.wait()
            part = part + ref[...].astype(F32)
        i = PARTS.index(name)
        ref = sstage.at[4] if name == "s" else corner(rstage.at[0], name)
        ref[...] = part.astype(ref.dtype)
        c = pltpu.make_async_copy(ref, finals[name].at[0], fin_sem.at[i])
        c.start()
        c.wait()
        opened[name] = rep.gather_start(3 * i, finals[name].at[0], finals[name])

    def hand_on(name):
        opened[name] = rep.gather_pass(3 * PARTS.index(name), finals[name], opened[name])

    base = 3 * len(PARTS)

    def stream(names, body):
        def copies(s, slot):
            found = []
            for j, name in enumerate(names):
                land = {"q": q_land, "g": g_land, "u": u_land}[name]
                found.append(
                    pltpu.make_async_copy(
                        land.at[s, pl.ds(0, rows)],
                        wst.at[slot, j, :, pl.ds(0, land.shape[2])],
                        stream_sem.at[slot, j],
                    )
                )
            return found

        for c in copies(0, 0):
            c.start()

        @pl.loop(0, n)
        def _(s):
            slot = s % 2

            @pl.when(s + 1 < n)
            def _():
                for c in copies(s + 1, 1 - slot):
                    c.start()

            for c in copies(s, slot):
                c.wait()
            body(s, slot)

    def exchange_core(i, k):
        return rep.start(base + i, csend, core_land.at[k], here.core)

    def exchange_y(i, k, src):
        return rep.start(base + i, src, y_land.at[k], here.across)

    def drop_send(c):
        c.wait_send()
        rep.sent = [x for x in rep.sent if x is not c]

    here.greet()
    c_hid = fetch(hid_in, hid, 0)
    c_dyl = fetch(dyl_in, dyl, 1)
    c_hid.wait()
    c_dyl.wait()
    c_wd = fetch(d_land, wd, 2)
    c_gate = fetch(gate_in, gates, 3)
    c_up = fetch(up_in, ups, 4)
    c_a2 = fetch(a2_in, a2, 5)
    c_small = fetch(s_land, small, 9)
    c_res = fetch(resid_in, resid, 8)
    out_rows = o_land.shape[1]
    c_wo = [fetch(o_land.at[i], wo.at[pl.ds(i * out_rows, out_rows)], 32 + i) for i in range(n)]
    c_att = fetch(attn_in, attn_t, 14)
    c_a1 = fetch(a1_in, a1, 7)
    low_rows, high_rows = pl.ds(0, 2 * slots), pl.ds(2 * slots, 2 * slots)
    halves = (
        first_half((1, 128)).astype(F32).astype(BF16),
        (1.0 - first_half((1, 128)).astype(F32)).astype(BF16),
    )
    block = slots // 2
    held = {}
    waited = []

    def need(c):
        if not any(c is w for w in waited):
            waited.append(c)
            c.wait()

    def rows16(count, body):
        @pl.loop(0, count // 16)
        def _(i):
            body(pl.ds(pl.multiple_of(i * 16, 16), 16))

    def feed_back(g):
        if g == 0:
            for c in (c_wd, c_gate, c_up):
                c.wait()
        at = pl.ds(g * slots, slots)
        dh = dot_rt(dyl[at, :], wd[...])
        gate, up = gates[at, :].astype(F32), ups[at, :].astype(F32)
        sig = jax.nn.sigmoid(gate)
        gates[at, :] = (dh * up * sig * (1.0 + gate * (1.0 - sig))).astype(BF16)
        ups[at, :] = (dh * gate * sig).astype(BF16)

    def a2_product(at, slot):
        return dot_rt(gates[at, :], wst[slot, 0, :, :units]) + dot_rt(ups[at, :], wst[slot, 1, :, :units])

    def put_far(part, s):
        csend[0, :, lanes_of(s, rows)] = part[:slots]
        csend[1, :, lanes_of(s, rows)] = part[slots:]

    def far2():
        stream(("g", "u"), lambda s, slot: put_far(a2_product(high_rows, slot).astype(BF16), s))
        held["core1"] = exchange_core(0, 0)

    def put_near(part, s, ref):
        at = lanes_of(s, rows)
        ref[:, at] = part[:slots] + crecv[0, :, at].astype(F32)
        ysend[:, at] = (part[slots:] + crecv[1, :, at].astype(F32)).astype(BF16)

    def near2():
        held["core1"].wait_recv()
        fetch(core_land.at[0], crecv, 10).wait()
        stream(("g", "u"), lambda s, slot: put_near(a2_product(low_rows, slot), s, own))
        held["y1"] = exchange_y(1, 0, ysend)

    def mlpf():
        drop_send(held["core1"])
        for g in (0, 1):
            csend[g] = dot_lt(hid[:, (g + 2) * slots : (g + 3) * slots], wd[...]).astype(BF16)
        held["core2"] = exchange_core(2, 1)

    def mlpn():
        held["core2"].wait_recv()
        fetch(core_land.at[1], crecv, 13).wait()
        ysend2[...] = (dot_lt(hid[:, slots : 2 * slots], wd[...]) + crecv[1].astype(F32)).astype(BF16)
        need(c_res)
        outp[...] = resid[...] + dot_lt(hid[:, :slots], wd[...]) + crecv[0].astype(F32)

    def ln2():
        need(c_small)
        need(c_res)
        for s in range(n):
            vecs[0:8, s * rows : (s + 1) * rows] = small[s, 0:8, :].astype(F32)
        headsums[...] = jnp.zeros_like(headsums)
        vecs[8:40, :] = jnp.zeros((32, width), F32)
        held["y1"].wait_recv()
        fetch(y_land.at[0], yrecv, 11).wait()
        drop_send(held["y1"])
        gain = vecs[2:3, :]

        def chunk(at):
            da = own[at, :] + yrecv[at, :].astype(F32)
            back, normal = norm_rows_back(resid[at, :], gain, da)
            prod = da * normal
            vecs[24:32, :] += prod[:8] + prod[8:]
            vecs[32:40, :] += da[:8] + da[8:]
            dr = dyl[at, :].astype(F32) + back
            own[at, :] = dr
            ysend[at, :] = dr.astype(BF16)

        rows16(slots, chunk)
        fetch(ysend, drl_land.at[0], 12).wait()
        held["drl"] = rep.gather_start(base + 3, drl_land.at[0], drl_land)

    def pass_on():
        held["drl"] = rep.gather_pass(base + 3, drl_land, held["drl"])

    def ldrl():
        for c in held["drl"]:
            c.wait_recv()
        loads = [fetch(drl_land.at[g], wd.at[pl.ds(g * slots, slots)], 16 + g) for g in range(REPS)]
        for c in loads + c_wo + [c_att]:
            c.wait()

    def ey2():
        held["y2"] = exchange_y(6, 1, ysend2)

    def head_copies(g, slot):
        found = [
            pltpu.make_async_copy(ref.at[g], heads.at[slot, j], stream_sem.at[slot, 2 + j])
            for j, ref in enumerate((q_in, k_in, v_in))
        ]
        return found + [pltpu.make_async_copy(p_in.at[g], probs.at[slot], stream_sem.at[slot, 5])]

    def turn_back(tile):
        return tile * tabs[0] - pltpu.roll(tile, 120, 1) * tabs[1] - pltpu.roll(tile, 8, 1) * tabs[2]

    def attend_back(g):
        slot = g % 2
        if g == 0:
            for c in head_copies(0, 0):
                c.start()
        if g + 1 < REPS:
            for c in head_copies(g + 1, 1 - slot):
                c.start()
        at = pl.ds(g * slots, slots)
        datt[...] = dot_rt(wd[at, :], wo[...]).astype(BF16)
        same = metas[g, 1:2, :128]
        for j in range(3):
            tabs[j, :block, :] = tables[j, :block, :]
            tabs[j, block:, :] = jnp.where(same > 0.5, tables[j, block:, :], tables[j, :block, :])
        for c in head_copies(g, slot):
            c.wait()
        low = first_half((slots, 128))
        for t in range(pairs):
            da = datt[:, t * 128 : (t + 1) * 128]
            qt, kt, vt = heads[slot, 0, t], heads[slot, 1, t], heads[slot, 2, t]
            both = []
            for h in (0, 1):
                p = probs[slot, 2 * t + h]
                pf = p.astype(F32)
                dp = dot_rt(da * halves[h], vt)
                delta = jnp.sum(dp * pf, axis=1, keepdims=True)
                ds = (pf * (dp - delta)).astype(BF16)
                both.append((dot(ds, kt), dot_lt(ds, qt), dot_lt(p, da)))
            dq, dk, dv = [jnp.where(low, a, b) for a, b in zip(*both)]
            dq, dk = turn_back(dq * (1.0 / 8.0)), turn_back(dk * (1.0 / 8.0))
            for j, value in enumerate((dq, dk, dv)):
                row = j * pairs + t
                headsums[row : row + 1, :] += jnp.sum(value, axis=0, keepdims=True)
                first = j * own_width + t * 128
                dqkv[at, first : first + 128] = value.astype(BF16)

    def far1():
        drop_send(held["core2"])

        def body(s, slot):
            put_far(dot_rt(dqkv[high_rows, :], wst[slot, 0, :, :lanes]).astype(BF16), s)

        stream(("q",), body)
        held["core3"] = exchange_core(7, 2)

    def act():
        held["y2"].wait_recv()
        fetch(y_land.at[1], yrecv, 20).wait()

        def chunk(at):
            yrecv[at, :] = (outp[at, :] + yrecv[at, :].astype(F32)).astype(BF16)

        rows16(slots, chunk)
        fetch(yrecv, act_out, 21).wait()

    def near1():
        held["core3"].wait_recv()
        fetch(core_land.at[2], crecv, 22).wait()

        def body(s, slot):
            put_near(dot_rt(dqkv[low_rows, :], wst[slot, 0, :, :lanes]), s, resid)

        stream(("q",), body)
        held["y3"] = exchange_y(8, 2, ysend)
        held["tok"] = fetch(tok, crecv.at[1], 23)

    def add_up():
        held["tok"].wait()
        held["y3"].wait_recv()
        fetch(y_land.at[2], yrecv, 24).wait()
        gain = vecs[0:1, :]

        def chunk(at):
            da = resid[at, :] + yrecv[at, :].astype(F32)
            back, normal = norm_rows_back(crecv[1, at, :].astype(F32), gain, da)
            prod = da * normal
            vecs[8:16, :] += prod[:8] + prod[8:]
            vecs[16:24, :] += da[:8] + da[8:]
            yrecv[at, :] = (own[at, :] + back).astype(BF16)

        rows16(slots, chunk)
        held["grad"] = fetch(yrecv, grad_out, 25)
        sums[...] = jnp.zeros_like(sums)
        for j in range(4):
            total = jnp.sum(vecs[8 + 8 * j : 16 + 8 * j, :], axis=0, keepdims=True)
            for s in range(n):
                sums[s, j : j + 1, :] = total[:, s * rows : (s + 1) * rows]
        for s in range(n):
            for j, part in ((4, 0), (5, 2), (6, 1)):
                row = part * pairs + s // 2
                sums[s, j : j + 1, 0:128] = headsums[row : row + 1, :] * halves[s % 2].astype(F32)

    steps = {
        "far2": far2, "near2": near2, "mlpf": mlpf, "mlpn": mlpn, "ln2": ln2, "pass": pass_on,
        "ldrl": ldrl, "ey2": ey2, "far1": far1, "act": act, "near1": near1, "sums": add_up,
    }
    for name in BACK_ORDER:
        if name in steps:
            steps[name]()
        elif name[:2] == "dh":
            feed_back(int(name[2]))
        elif name[:2] == "at":
            attend_back(int(name[2]))
        elif name[0] == "f":
            finish(name[1])
        elif name[0] == "h":
            hand_on(name[1])
        else:
            if name in ("g0", "u0"):
                need(c_a2)
            if name in ("x0", "y0"):
                need(c_a1)
            serve(name[0], int(name[1]))
    for name in PARTS:
        for c in opened[name]:
            c.wait_recv()
    held["grad"].wait()
    rep.finish()
    for c in flying.values():
        c.wait_send()


def backward_call(n, lands, kept, tok, meta, tables):
    slots, width = tok.shape
    q_land, o_land, g_land, u_land, d_land, s_land = lands
    a1, qs, ks, vs, ps, attn_t, resid, a2, gate, up, hid, dyl = kept
    all_slots, units = gate.shape
    lanes = q_land.shape[2]
    pairs = lanes // 3 // 128
    half = n // 2
    rows = width // n
    S = jax.ShapeDtypeStruct
    block = {
        "d": (d_land.shape[1], width),
        "g": (rows, units),
        "u": (rows, units),
        "x": (rows, lanes // 2),
        "y": (rows, lanes // 2),
        "o": (o_land.shape[1], width // 2),
        "p": (o_land.shape[1], width // 2),
        "s": (8, rows),
    }
    kind = {name: F32 if name == "s" else BF16 for name in PARTS}
    out_shape = (
        [S((slots, width), BF16), S((slots, width), BF16)]
        + [S((REPS,) + block[name], kind[name]) for name in PARTS]
        + [S((2, half) + block[name], kind[name]) for name in PARTS]
        + [S((3, 2, slots, width), BF16), S((3, slots, width), BF16), S((REPS, slots, width), BF16)]
    )
    V = pltpu.VMEM
    scratch = [
        V((all_slots, width), BF16),
        V(hid.shape, BF16),
        V((units, width), BF16),
        V((all_slots, units), BF16),
        V((all_slots, units), BF16),
        V((all_slots, width), BF16),
        V((all_slots, width), BF16),
        V((2, 2, rows, lanes), BF16),
        V((lanes // 3, width), BF16),
        V((lanes // 3, all_slots), BF16),
        V((2, 3, pairs, slots, 128), BF16),
        V((2, 2 * pairs, slots, slots), BF16),
        V((all_slots, lanes), BF16),
        V((slots, lanes // 3), BF16),
        V((2, slots, width), BF16),
        V((2, slots, width), BF16),
        V((slots, width), BF16),
        V((slots, width), BF16),
        V((slots, width), BF16),
        V((slots, width), F32),
        V((slots, width), F32),
        V((slots, width), F32),
        V((2, 2, rows, width), BF16),
        V((2, rows, width), BF16),
        V((5, 8, rows), F32),
        V((n, 16, rows), BF16),
        V((40, width), F32),
        V((n, 8, rows), F32),
        V((16, 128), F32),
        V((3, slots, 128), F32),
        pltpu.SemaphoreType.DMA((len(PARTS), 2, half)),
        pltpu.SemaphoreType.DMA((len(PARTS), 2, half)),
        pltpu.SemaphoreType.DMA((32 + n,)),
        pltpu.SemaphoreType.DMA((3 * len(PARTS) + 9,)),
        pltpu.SemaphoreType.DMA((3 * len(PARTS) + 9,)),
        pltpu.SemaphoreType.DMA((2, 6)),
        pltpu.SemaphoreType.DMA((2,)),
        pltpu.SemaphoreType.DMA((len(PARTS),)),
    ]
    anywhere = pl.BlockSpec(memory_space=pltpu.HBM)
    inside = pl.BlockSpec(memory_space=pltpu.VMEM)
    out = pl.pallas_call(
        functools.partial(backward_kernel, n),
        out_shape=out_shape,
        in_specs=[anywhere] * 19 + [inside] * 2,
        out_specs=[anywhere] * len(out_shape),
        scratch_shapes=scratch,
        compiler_params=pltpu.CompilerParams(
            collective_id=2, has_side_effects=True, vmem_limit_bytes=VMEM_LIMIT
        ),
    )(q_land, o_land, g_land, u_land, d_land.reshape(units, width), s_land, a1, qs, ks, vs, ps, attn_t,
      resid, a2, gate, up, hid, dyl, tok, meta, tables)
    return out[:2], dict(zip(PARTS, out[2 : 2 + len(PARTS)]))


def weave_kernel(
    n,
    rel, d_in, g_in, u_in, x_in, y_in, o_in, p_in, s_in, act_in, grad_in,
    out_act, out_grad, out_vectors, out_key, out_qkv, out_out, out_gu, out_down,
    dv, gv, uv, xv, yv, ov, pv, av, qkv, outs, gu, down, small, load_sem, save_sem,
):
    turns = 2 * REPS
    count = g_in.shape[1] // turns
    lane = lax.broadcasted_iota(jnp.int32, (count, 128), 1)
    units = g_in.shape[2]
    piece = units // n
    cut = ((g_in, gv), (u_in, uv), (x_in, xv), (y_in, yv))

    def lines(c):
        return pl.ds(pl.multiple_of(c * count, 16), count)

    def load(j, c):
        src, dst = cut[j]
        return pltpu.make_async_copy(src.at[:, lines(c)], dst.at[:, lines(c)], load_sem.at[j, c])

    def load_slab(j, q):
        src, dst = ((d_in, dv), (o_in, ov), (p_in, pv))[j]
        return pltpu.make_async_copy(src.at[rel[q]], dst.at[q], load_sem.at[4 + j, q])

    def save(j, c):
        src, dst = ((gu, out_gu), (qkv, out_qkv))[j]
        return pltpu.make_async_copy(src.at[lines(c)], dst.at[lines(c)], save_sem.at[j, c])

    def save_slab(j, q):
        src, dst = ((down, out_down), (outs, out_out))[j]
        high = src.shape[0] // REPS
        at = pl.ds(q * high, high)
        return pltpu.make_async_copy(src.at[at], dst.at[at], save_sem.at[2 + j, q])

    pair = ((act_in, out_act), (grad_in, out_grad))
    through = [pltpu.make_async_copy(pair[j][0], av.at[j], load_sem.at[7, j]) for j in (0, 1)]
    onward = [pltpu.make_async_copy(av.at[j], pair[j][1], save_sem.at[4, j]) for j in (0, 1)]
    for q in range(REPS):
        load_slab(0, q).start()
    for c in range(turns):
        for j in range(4):
            load(j, c).start()
    for q in range(REPS):
        load_slab(1, q).start()
        load_slab(2, q).start()
    for c in through:
        c.start()
    for q in range(REPS):
        load_slab(0, q).wait()
        high = dv.shape[1]
        down[q * high : (q + 1) * high, :] = dv[q].astype(F32)
        save_slab(0, q).start()

    def join(segments):
        whole = segments[0][1]
        for low, value in segments[1:]:
            whole = jnp.where(lane >= low, value, whole)
        return whole

    @pl.loop(0, turns)
    def _(c):
        for j in range(4):
            load(j, c).wait()

        def tile(ref, q, a):
            return ref[rel[q], lines(c), a * 128 : (a + 1) * 128].astype(F32)

        for side, ref in ((0, gv), (1, uv)):
            for j in range(REPS * units // 128):
                segments = []
                for k in range(128 * j // piece, (128 * j + 127) // piece + 1):
                    s, q = k // REPS, k % REPS
                    low, high = max(0, k * piece - 128 * j), min(128, (k + 1) * piece - 128 * j)
                    start = 128 * j - piece * (k - s)
                    a, m = start // 128, start % 128
                    if low < 128 - m:
                        value = tile(ref, q, a)
                        segments.append((low, pltpu.roll(value, 128 - m, 1) if m else value))
                    if high > 128 - m:
                        segments.append(
                            (max(low, 128 - m), pltpu.roll(tile(ref, q, a + 1), 128 - m, 1))
                        )
                first = side * REPS * units + j * 128
                gu[lines(c), first : first + 128] = join(segments)
        save(0, c).start()
        per = x_in.shape[2] // 64
        for t in range(qkv.shape[1] // 128):
            group = t // 2
            ref, at = (xv, group) if group < per else (yv, group - per)
            values = []
            for h in (0, 1):
                value = tile(ref, 2 * (t % 2) + h, at // 2)
                values.append((64 * h, pltpu.roll(value, 64, 1) if at % 2 != h else value))
            qkv[lines(c), t * 128 : (t + 1) * 128] = join(values)
        save(1, c).start()

    for c, d in zip(through, onward):
        c.wait()
        d.start()
    for q in range(REPS):
        load_slab(1, q).wait()
        load_slab(2, q).wait()
        high, half = ov.shape[1:]
        outs[q * high : (q + 1) * high, :half] = ov[q].astype(F32)
        outs[q * high : (q + 1) * high, half:] = pv[q].astype(F32)
        save_slab(1, q).start()
    small[...] = jnp.zeros_like(small)
    small[0:4, :] = s_in[0, 0:4, :] + s_in[1, 0:4, :] + s_in[2, 0:4, :] + s_in[3, 0:4, :]
    row = lax.broadcasted_iota(jnp.int32, (1, 128), 1)
    own = []
    for q in range(REPS):
        v = s_in[rel[q], 4:7, 0:128]
        own.append(v + pltpu.roll(v, 64, 1))
    for j in (0, 1):
        for p in (0, 1):
            small[4 + j : 5 + j, p * 128 : (p + 1) * 128] = jnp.where(
                row < 64, own[2 * p][j : j + 1], own[2 * p + 1][j : j + 1]
            )
    keys = own[0][2:3]
    for q in range(1, REPS):
        keys = jnp.where(row >= q * ROT, pltpu.roll(own[q][2:3], q * ROT, 1), keys)
    out_vectors[...] = small[0:6, :]
    out_key[...] = keys[:, : out_key.shape[1]]
    for c in onward:
        c.wait()
    for q in range(REPS):
        save_slab(0, q).wait()
        save_slab(1, q).wait()
    for c in range(turns):
        save(0, c).wait()
        save(1, c).wait()


def weave_call(n, rel, act, grad, key_rows, parts):
    d, g, u, x, y, o, p, s = [parts[name] for name in PARTS]
    rows = g.shape[1]
    S = jax.ShapeDtypeStruct
    V = pltpu.VMEM
    big = [
        (rows, 2 * REPS * x.shape[2]),
        (REPS * o.shape[1], 2 * o.shape[2]),
        (rows, 2 * REPS * g.shape[2]),
        (REPS * d.shape[1], d.shape[2]),
    ]
    anywhere = pl.BlockSpec(memory_space=pltpu.HBM)
    inside = pl.BlockSpec(memory_space=pltpu.VMEM)
    out = pl.pallas_call(
        functools.partial(weave_kernel, n),
        out_shape=[S(act.shape, BF16), S(grad.shape, BF16), S((6, rows), F32), S((1, key_rows), F32)]
        + [S(shape, F32) for shape in big],
        in_specs=[pl.BlockSpec(memory_space=pltpu.SMEM)] + [anywhere] * 7 + [inside] + [anywhere] * 2,
        out_specs=[anywhere] * 2 + [inside] * 2 + [anywhere] * 4,
        scratch_shapes=[V(a.shape, BF16) for a in (d, g, u, x, y, o, p)]
        + [V((2,) + act.shape, BF16)]
        + [V(shape, F32) for shape in big]
        + [
            V(s.shape[1:], F32),
            pltpu.SemaphoreType.DMA((8, 2 * REPS)),
            pltpu.SemaphoreType.DMA((5, 2 * REPS)),
        ],
        compiler_params=pltpu.CompilerParams(vmem_limit_bytes=VMEM_LIMIT),
    )(rel, d, g, u, x, y, o, p, s, act, grad)
    return (out[0], out[1], out[2].T, out[3].reshape(key_rows, 1)) + tuple(out[4:])


def core_swap(x):
    return lax.ppermute(x, "rep", [(0, 1), (1, 0), (2, 3), (3, 2)])


def y_swap(x):
    return lax.ppermute(x, "rep", [(0, 2), (1, 3), (2, 0), (3, 1)])


def rep_parts(x):
    across = y_swap(x)
    return [x, across, core_swap(x), core_swap(across)]


def rep_gather(x):
    return jnp.concatenate(rep_parts(x), axis=0)


def rep_reduce(a, w_dot, slots):
    far = core_swap(w_dot(a[2 * slots :]).astype(BF16))
    near = w_dot(a[: 2 * slots]) + far.astype(F32)
    return near[:slots] + y_swap(near[slots:].astype(BF16)).astype(F32)


def solution(mesh):
    n = mesh.shape["shard"]
    half_ring = n // 2
    order = list(range(0, n, 2)) + list(range(n - 1, 0, -2))
    place = [order.index(s) for s in range(n)]
    up_ring = [(order[i], order[(i + 1) % n]) for i in range(n)]
    down_ring = [(b, a) for a, b in up_ring]

    def hop(x, ring, sent):
        if len(sent) >= DEPTH:
            x, _ = lax.optimization_barrier((x, sent[-DEPTH]))
        x = lax.ppermute(x, "shard", ring)
        sent.append(x)
        return x

    def ring_ids():
        spot = jnp.array(place, jnp.int32)[lax.axis_index("shard")]
        table = jnp.array(order, jnp.int32)
        return {k: table[(spot + k) % n] for k in range(-half_ring, half_ring + 1)}

    def gather(x, ids, forward_extra, places, line):
        bufs = places(None, x, ids[0])
        up = down = x
        for k in range(1, half_ring + 1):
            go_up = k < half_ring or forward_extra
            go_down = k < half_ring or not forward_extra
            if go_up:
                up = hop(up, up_ring, line[0])
            if go_down:
                down = hop(down, down_ring, line[1])
            if go_up:
                bufs = places(bufs, up, ids[-k])
            if go_down:
                bufs = places(bufs, down, ids[k])
            yield
        return bufs

    def put(bufs, block, at):
        if bufs is None:
            bufs = jnp.zeros((n,) + block.shape, block.dtype)
        return lax.dynamic_update_index_in_dim(bufs, block, at, 0)

    def reduce(term, ids, forward_extra, line, kind=BF16):
        acc = {}
        for k in range(half_ring, 0, -1):
            for side, (ring, sign, extra) in enumerate(
                ((up_ring, 1, forward_extra), (down_ring, -1, not forward_extra))
            ):
                if k == half_ring and not extra:
                    continue
                part = term(ids[sign * k])
                if side in acc:
                    part = part + acc[side].astype(F32)
                acc[side] = hop(part.astype(kind), ring, line[side])
            yield
        return term(ids[0]) + acc[0].astype(F32) + acc[1].astype(F32)

    def run(chains, turns):
        done = {}
        for name in turns:
            for _ in range(n // 8):
                if name in done:
                    continue
                try:
                    next(chains[name])
                except StopIteration as stop:
                    done[name] = stop.value
        for name, chain in chains.items():
            while name not in done:
                try:
                    next(chain)
                except StopIteration as stop:
                    done[name] = stop.value
        return done

    def pick_columns(w, groups, width, r):
        chosen = [
            lax.select_n(
                r,
                *[
                    w[:, (g * REPS + q) * width : (g * REPS + q + 1) * width]
                    for q in range(REPS)
                ],
            )
            for g in range(groups)
        ]
        return jnp.concatenate(chosen, axis=1)

    def by_rep(parts, y, core):
        own, across, beside, both = parts
        low0 = lax.select(core == 0, own, beside)
        low1 = lax.select(core == 0, beside, own)
        high0 = lax.select(core == 0, across, both)
        high1 = lax.select(core == 0, both, across)
        return [
            lax.select(y == 0, low0, high0),
            lax.select(y == 0, low1, high1),
            lax.select(y == 0, high0, low0),
            lax.select(y == 0, high1, low1),
        ]

    def weave(parts, groups, width):
        pieces = [
            parts[q][:, g * width : (g + 1) * width]
            for g in range(groups)
            for q in range(REPS)
        ]
        return jnp.concatenate(pieces, axis=1).astype(F32)

    def on_device(
        tokens, cotangent, block_seq, block_len, vectors, key_bias, w_qkv, w_out, w_gate_up, w_down
    ):
        slots, features = tokens.shape
        blocks = block_seq.shape[0]
        block_size = slots // blocks
        head_dim = features // HEADS
        own_heads = HEADS // REPS
        own_width = own_heads * head_dim
        all_slots = REPS * slots
        scale = 1.0 / math.sqrt(head_dim)
        rows = features // n
        hidden_units = w_gate_up.shape[1] // 2
        own_hidden = hidden_units // REPS
        down_rows = w_down.shape[0] // REPS
        out_rows = w_out.shape[0] // REPS
        regroup = out_rows < head_dim
        r = lax.axis_index("rep")
        y, core = r // 2, r % 2
        ids = ring_ids()

        def mix_out(x):
            if not regroup:
                return x
            pairs = [
                (k * n + 4 * j + q, q * n + 4 * j + k)
                for k in range(REPS)
                for j in range(n // 4)
                for q in range(REPS)
            ]
            return lax.ppermute(x, BOTH, pairs)

        fast = blocks == 2 and down_rows % 16 == 0 and out_rows == head_dim and rows % 128 == 0
        own_valid = (
            jnp.arange(block_size, dtype=jnp.int32)[None, :] < block_len[:, None]
        ).reshape(-1)
        grad_output = cotangent.astype(F32) * own_valid[:, None].astype(F32)
        dyl_own = grad_output.astype(BF16)
        if fast:
            vt = jnp.concatenate(
                [vectors.T, jnp.pad(key_bias.T, ((0, 0), (0, rows - key_bias.shape[0])))], axis=0
            )
            vt = jnp.pad(vt, ((0, 9), (0, 0)))
            angles = np.arange(slots, dtype=np.float32)[:, None] * np.exp(
                np.arange(ROT // 2, dtype=np.float32) * np.float32(-2.0 * math.log(10000.0) / ROT)
            ).astype(np.float32)
            cosine, sine = np.cos(angles), np.sin(angles)
            rest = np.ones((slots, head_dim - ROT), np.float32)
            none = np.zeros((slots, ROT // 2), np.float32)
            tables = np.stack(
                [
                    np.concatenate([cosine, cosine, rest] * 2, axis=1),
                    np.concatenate([-sine, none, 0 * rest] * 2, axis=1),
                    np.concatenate([none, sine, 0 * rest] * 2, axis=1),
                ]
            ).astype(np.float32)
            weights = (w_qkv, w_out, w_gate_up, w_down)
            out = forward_call(
                n, weights, tokens, cotangent, vt, block_seq, block_len, jnp.asarray(tables)
            )
            a1, qs, ks, vs, ps, attn, resid, a2, gate, up, hid, dyl_all, metas = out[6:]
            whole = (all_slots, features)
            (activations, grad_input), parts = backward_call(
                n,
                out[:6],
                (a1, qs, ks, vs, ps, attn, resid, a2.reshape(whole), gate, up, hid, dyl_all.reshape(whole)),
                tokens,
                metas,
                tables,
            )

            q = jnp.arange(REPS, dtype=jnp.int32)
            rel = jnp.where(q // 2 != y, 1, 0) + jnp.where(q % 2 != core, 2, 0)
            rel = rel.astype(jnp.int32)
            return weave_call(n, rel, activations, grad_input, key_bias.shape[0], parts)
        else:
            small = jnp.concatenate([vectors.T.reshape(-1), key_bias.reshape(-1)])
            lanes = 3 * own_width
            small_rows = -(-small.size // lanes)
            small_rows = -(-small_rows // 16) * 16
            small = jnp.pad(small, (0, small_rows * lanes - small.size)).reshape(small_rows, lanes)
            qkv_block = jnp.concatenate([pick_columns(w_qkv, 3 * own_heads, head_dim, r), small], axis=0)

            def put_qkv(bufs, block, at):
                a, b = (None, None) if bufs is None else bufs
                return put(a, block[:rows], at), put(b, block[rows:], at)

            out_block = mix_out(lax.dynamic_slice_in_dim(w_out, r * out_rows, out_rows, 0))
            gate_block = pick_columns(w_gate_up[:, :hidden_units], n, down_rows, r)
            up_block = pick_columns(w_gate_up[:, hidden_units:], n, down_rows, r)
            down_block = lax.dynamic_slice_in_dim(w_down, r * down_rows, down_rows, 0)
            line = ([], [])
            got = run(
                {
                    "q": gather(qkv_block, ids, True, put_qkv, line),
                    "o": gather(out_block, ids, False, put, line),
                    "g": gather(gate_block, ids, True, put, line),
                    "u": gather(up_block, ids, False, put, line),
                    "d": gather(down_block, ids, False, put, line),
                },
                "qoqoqoqoguguguguddddd",
            )
            wq, smalls = got["q"]
            wq = wq.reshape(features, lanes)
            smalls = smalls.reshape(n, -1).astype(F32)
            vec = smalls[:, : 6 * rows].reshape(n, 6, rows).transpose(1, 0, 2).reshape(6, features)
            key_full = smalls[:, 6 * rows : 6 * rows + HEADS * ROT // n].reshape(own_heads, REPS, ROT)
            key_own = lax.dynamic_index_in_dim(key_full, r, 1, keepdims=False)
            key_shift = jnp.pad(key_own, ((0, 0), (0, head_dim - ROT))).reshape(own_width)

            def own_heads_of(v):
                return lax.dynamic_index_in_dim(
                    v.reshape(own_heads, REPS, head_dim), r, 1, keepdims=False
                ).reshape(own_width)

            wo = got["o"].reshape(own_width, features)
            wg = got["g"].reshape(features, own_hidden)
            wu = got["u"].reshape(features, own_hidden)
            wd = got["d"].reshape(own_hidden, features)

            meta = jnp.concatenate([block_seq, block_len]).astype(F32)
            meta = jnp.pad(meta, (0, 128 - 2 * blocks)).reshape(1, 128)
            meta = jnp.concatenate(rep_parts(jnp.broadcast_to(meta, (8, 128))), axis=0)
            meta = meta.reshape(REPS, 8, 128)[:, 0, :]
            seqs = meta[:, :blocks].astype(jnp.int32)
            lens = meta[:, blocks : 2 * blocks].astype(jnp.int32)
            index = jnp.arange(blocks, dtype=jnp.int32)
            same = seqs[:, None, :] == seqs[:, :, None]
            earlier = jnp.sum(
                jnp.where((index[None, :] < index[:, None]) & same, 1, 0), axis=2
            ).astype(jnp.int32)
            offset = jnp.arange(block_size, dtype=jnp.int32)
            seq_slot = jnp.broadcast_to(seqs[:, :, None], (REPS, blocks, block_size)).reshape(REPS, slots)
            valid = (offset[None, None, :] < lens[:, :, None]).reshape(REPS, slots)
            positions = (earlier[:, :, None] * block_size + offset[None, None, :]).reshape(all_slots)
            slot_index = jnp.arange(slots, dtype=jnp.int32)
            allowed = (seq_slot[:, None, :] == seq_slot[:, :, None]) & (
                slot_index[None, :] <= slot_index[:, None]
            )[None]
            allowed = allowed & (valid[:, None, :] | (slot_index[None, :] == slot_index[:, None])[None])
            cosine, sine = turn_tables(positions)

            x_all = rep_gather(tokens)
            dyl = rep_gather(dyl_own)

            tokens_f = tokens.astype(F32)
            normal_one, inv_one = normalize(tokens_f)
            normal_all, _ = normalize(x_all.astype(F32))
            a1 = (normal_all * vec[0] + vec[1]).astype(BF16)
            projected = dot(a1, wq)
            head_shape = (all_slots, own_heads, head_dim)
            group_shape = (REPS, slots, own_heads, head_dim)
            q = rotate((projected[:, :own_width] + own_heads_of(vec[4])).reshape(head_shape), cosine, sine)
            k = rotate((projected[:, own_width : 2 * own_width] + key_shift).reshape(head_shape), cosine, sine)
            v = projected[:, 2 * own_width :] + own_heads_of(vec[5])
            q = q.astype(BF16).reshape(group_shape)
            k = k.astype(BF16).reshape(group_shape)
            v = v.astype(BF16).reshape(group_shape)
            scores = jnp.einsum("gshd,gthd->ghst", q, k, preferred_element_type=F32) * scale
            scores = jnp.where(allowed[:, None], scores, -1e30)
            exponent = jnp.exp(scores - jnp.max(scores, axis=-1, keepdims=True))
            probs = exponent / jnp.sum(exponent, axis=-1, keepdims=True)
            probs_low = probs.astype(BF16)
            attn = jnp.einsum("ghst,gthd->gshd", probs_low, v, preferred_element_type=F32)
            attn = attn.reshape(all_slots, own_width).astype(BF16)
            resid = tokens_f + rep_reduce(attn, lambda a: dot(a, wo), slots)
            normal_two, inv_two = normalize(resid)
            a2 = rep_gather((normal_two * vec[2] + vec[3]).astype(BF16))
            gate = dot(a2, wg)
            up = dot(a2, wu)
            sig = jax.nn.sigmoid(gate)
            hidden = (gate * sig * up).astype(BF16)

        def blocks_of(a):
            return a.reshape(all_slots, n, -1).transpose(1, 0, 2)

        hidden_b = blocks_of(hidden)
        activations = (resid + rep_reduce(hidden, lambda a: dot(a, wd), slots)).astype(BF16)
        grad_hidden = dot_rt(dyl, wd)
        grad_gate = (grad_hidden * up * sig * (1.0 + gate * (1.0 - sig))).astype(BF16)
        grad_up = (grad_hidden * gate * sig).astype(BF16)
        a2_b = blocks_of(a2)
        grad_gu = jnp.concatenate([grad_gate, grad_up], axis=1)
        wgu = jnp.concatenate([wg, wu], axis=1)
        grad_a2 = rep_reduce(grad_gu, lambda a: dot_rt(a, wgu), slots)
        grad_resid = grad_output + norm_back(grad_a2 * vec[2], normal_two, inv_two)
        drl = rep_gather(grad_resid.astype(BF16))
        attn_b = blocks_of(attn)
        d_attn = dot_rt(drl, wo).astype(BF16).reshape(group_shape)
        grad_v = jnp.einsum("ghst,gshd->gthd", probs_low, d_attn, preferred_element_type=F32)
        grad_p = jnp.einsum("gshd,gthd->ghst", d_attn, v, preferred_element_type=F32)
        delta = jnp.sum(grad_p * probs, axis=-1, keepdims=True)
        grad_s = (probs * (grad_p - delta)).astype(BF16)
        grad_q = jnp.einsum("ghst,gthd->gshd", grad_s, k, preferred_element_type=F32) * scale
        grad_k = jnp.einsum("ghst,gshd->gthd", grad_s, q, preferred_element_type=F32) * scale
        grad_q = rotate(grad_q.reshape(head_shape), cosine, -sine)
        grad_k = rotate(grad_k.reshape(head_shape), cosine, -sine)
        grad_v = grad_v.reshape(head_shape)
        key_sum = jnp.sum(grad_k[:, :, :ROT], axis=0)
        d_qkv = jnp.concatenate(
            [g.reshape(all_slots, own_width) for g in (grad_q, grad_k, grad_v)], axis=1
        ).astype(BF16)
        a1_b = blocks_of(a1)
        grad_a1 = rep_reduce(d_qkv, lambda a: dot_rt(a, wq), slots)
        grad_input = (grad_resid + norm_back(grad_a1 * vec[0], normal_one, inv_one)).astype(BF16)

        def spread(sums):
            zero = jnp.zeros((own_heads, REPS, sums.shape[1]), F32)
            return lax.dynamic_update_index_in_dim(zero, sums, r, 1)

        vec_sums = jnp.stack(
            [
                jnp.sum(grad_a1 * normal_one, axis=0),
                jnp.sum(grad_a1, axis=0),
                jnp.sum(grad_a2 * normal_two, axis=0),
                jnp.sum(grad_a2, axis=0),
                spread(jnp.sum(grad_q, axis=0)).reshape(features),
                spread(jnp.sum(grad_v, axis=0)).reshape(features),
            ],
            axis=0,
        )
        key_rows = HEADS * ROT // n
        packed = jnp.concatenate(
            [
                vec_sums.reshape(6, n, rows).transpose(1, 0, 2).reshape(n, 6 * rows),
                spread(key_sum).reshape(n, key_rows),
            ],
            axis=1,
        )
        width = -(-packed.shape[1] // 1024) * 1024
        packed = jnp.pad(packed, ((0, 0), (0, width - packed.shape[1]))).reshape(n, width // 128, 128)
        line = ([], [])
        sums = run(
            {
                "d": reduce(lambda i: dot_lt(hidden_b[i], dyl), ids, False, line),
                "g": reduce(lambda i: dot_lt(a2_b[i], grad_gate), ids, True, line),
                "u": reduce(lambda i: dot_lt(a2_b[i], grad_up), ids, False, line),
                "q": reduce(lambda i: dot_lt(a1_b[i], d_qkv), ids, True, line),
                "o": reduce(lambda i: dot_lt(attn_b[i], drl), ids, False, line),
                "s": reduce(lambda i: packed[i], ids, True, line, F32),
            },
            "dgdgdudugugugqoqoqosoqsoss",
        )
        grad_down, grad_wg, grad_wu = sums["d"], sums["g"], sums["u"]
        grad_wq, grad_wo, packed = sums["q"], sums["o"], sums["s"]
        packed = packed + core_swap(packed)
        packed = (packed + y_swap(packed)).reshape(-1)
        out_vectors = packed[: 6 * rows].reshape(6, rows).T
        out_key = packed[6 * rows : 6 * rows + key_rows].reshape(key_rows, 1)

        def everywhere(g):
            return by_rep(rep_parts(g.astype(BF16)), y, core)

        out_down = jnp.concatenate(everywhere(grad_down), axis=0).astype(F32)
        out_gate_up = jnp.concatenate(
            [weave(everywhere(g), n, down_rows) for g in (grad_wg, grad_wu)], axis=1
        )
        out_qkv = weave(everywhere(grad_wq), 3 * own_heads, head_dim)
        out_out = jnp.concatenate(everywhere(mix_out(grad_wo.astype(BF16))), axis=0).astype(F32)
        return activations, grad_input, out_vectors, out_key, out_qkv, out_out, out_gate_up, out_down

    tok, row = P(BOTH, None), P("shard", None)
    return jax.shard_map(
        on_device,
        mesh=mesh,
        in_specs=(tok, tok, P(BOTH), P(BOTH)) + (row,) * 6,
        out_specs=(tok, tok) + (row,) * 6,
        check_vma=False,
    )
```

```python
import functools
import math

import jax
import jax.numpy as jnp
import numpy as np
from jax import lax
from jax.experimental import pallas as pl
from jax.experimental.pallas import tpu as pltpu
from jax.sharding import PartitionSpec as P

HEADS = 32
ROT = 16
REPS = 4
BOTH = ("rep", "shard")
DEPTH = 2
F32 = jnp.float32
BF16 = jnp.bfloat16


def dot(a, b):
    return jnp.dot(a, b, preferred_element_type=F32)


def dot_rt(a, b):
    return lax.dot_general(a, b, (((1,), (1,)), ((), ())), preferred_element_type=F32)


def dot_lt(a, b):
    return lax.dot_general(a, b, (((0,), (0,)), ((), ())), preferred_element_type=F32)


def turn_tables(positions):
    half = ROT // 2
    frequencies = jnp.exp(
        jnp.arange(half, dtype=F32) * (-2.0 * math.log(10000.0) / ROT)
    )
    angles = positions.astype(F32)[:, None] * frequencies[None, :]
    return jnp.cos(angles)[:, None, :], jnp.sin(angles)[:, None, :]


def rotate(values, cosine, sine):
    half = ROT // 2
    low, high, rest = values[..., :half], values[..., half:ROT], values[..., ROT:]
    return jnp.concatenate(
        [low * cosine - high * sine, high * cosine + low * sine, rest], axis=-1
    )


def normalize(values):
    center = values - jnp.mean(values, axis=1, keepdims=True)
    inv_std = lax.rsqrt(jnp.mean(center * center, axis=1, keepdims=True) + 1e-05)
    return center * inv_std, inv_std


def norm_back(grad_norm, normal, inv_std):
    mean_grad = jnp.mean(grad_norm, axis=1, keepdims=True)
    mean_cross = jnp.mean(grad_norm * normal, axis=1, keepdims=True)
    return inv_std * (grad_norm - mean_grad - normal * mean_cross)


MESH = pl.DeviceIdType.MESH
NAMES = ("q", "o", "g", "u", "d", "s")
LONG_UP = {"q": True, "o": True, "g": False, "u": False, "d": True, "s": True}
FORE_ORDER = (
    "o1", "q1", "o2", "su", "pm", "q2", "sg", "px", "cot", "o3", "q3", "u1", "g1", "bd", "q4", "ln1", "at2",
    "o4", "u2", "at3", "of", "at0", "g2", "at1", "oy", "d1", "u3", "oo", "g3", "ln2", "d2", "g4", "pa", "u4",
    "pd", "fd0", "d3", "fd1", "fd2", "fd3", "d4",
)
VMEM_LIMIT = 64 * 1024 * 1024 - 64 * 1024


class Place:
    def __init__(self, n):
        self.n, self.half = n, n // 2
        self.r, self.s = lax.axis_index("rep"), lax.axis_index("shard")
        self.core = self.r + 1 - 2 * (self.r % 2)
        self.across = (self.r + 2) % REPS
        odd = self.s % 2
        self.spot = (1 - odd) * (self.s // 2) + odd * (n - 1 - self.s // 2)
        self.ids = {k: self.shard_at(k) for k in range(-self.half, self.half + 1)}
        self.ring = (self.ids[1], self.ids[-1])

    def shard_at(self, k):
        q = (self.spot + k + self.n) % self.n
        back = q // self.half
        return (1 - back) * 2 * q + back * (2 * self.n - 1 - 2 * q)

    def greet(self):
        barrier = pltpu.get_barrier_semaphore()
        for who in (
            (self.core, self.s),
            (self.across, self.s),
            (self.r, self.ring[0]),
            (self.r, self.ring[1]),
        ):
            pl.semaphore_signal(barrier, inc=1, device_id=who, device_id_type=MESH)
        pl.semaphore_wait(barrier, 4)


class RepLinks:
    def __init__(self, place, send, recv):
        self.place, self.send, self.recv, self.sent = place, send, recv, []

    def copy(self, i, src, dst, who):
        return pltpu.make_async_remote_copy(
            src_ref=src,
            dst_ref=dst,
            send_sem=self.send.at[i],
            recv_sem=self.recv.at[i],
            device_id=(who, self.place.s),
            device_id_type=MESH,
        )

    def start(self, i, src, dst, who):
        c = self.copy(i, src, dst, who)
        c.start()
        self.sent.append(c)
        return c

    def gather_start(self, i, own, slots):
        a = self.start(i, own, slots.at[1], self.place.across)
        b = self.start(i + 1, own, slots.at[2], self.place.core)
        return a, b

    def gather_pass(self, i, slots, copies):
        copies[0].wait_recv()
        return copies[1], self.start(i + 2, slots.at[1], slots.at[3], self.place.core)

    def finish(self):
        for c in self.sent:
            c.wait_send()


def layer_rows(x, gain, shift):
    center = x - jnp.mean(x, axis=1, keepdims=True)
    inv = lax.rsqrt(jnp.mean(center * center, axis=1, keepdims=True) + 1e-05)
    return center * inv * gain + shift


def first_half(shape):
    return lax.broadcasted_iota(jnp.int32, shape, 1) < 64


def forward_kernel(
    n,
    w_qkv, w_out, w_gu, w_down, tok, cot, vectors, key_bias, seqs, lens, tables,
    q_land, o_land, g_land, u_land, d_land, s_land, a1_out, q_out, k_out, v_out, p_out, attn_out,
    resid_out, a2_out, gate_out, up_out, hid_out, dyl_out, meta_out,
    q_blk, s_blk, base, g_blk, u_blk, wq, wo, wg, wu, xs, qs, ks, vs, ps, attn, attn_t, acc, csend, crecv, ysend,
    yrecv, resid, a2s, gates, ups, hid, metas, tabs, mask, small, vecs,
    ring_send, ring_recv, load_sem, rep_send, rep_recv, out_sem,
):
    here = Place(n)
    half = here.half
    lands = dict(zip(NAMES, (q_land, o_land, g_land, u_land, d_land, s_land)))
    rows = {name: lands[name].shape[1] for name in NAMES}
    slots, width = tok.shape
    blocks = {
        "q": q_blk,
        "s": s_blk,
        "o": w_out.at[pl.ds(pl.multiple_of(here.r * rows["o"], 16), rows["o"])],
        "g": g_blk,
        "u": u_blk,
        "d": w_down.at[pl.ds(pl.multiple_of(here.r * rows["d"], 16), rows["d"])],
    }
    into = {"q": wq, "o": wo, "g": wg, "u": wu, "s": small}
    reach = {
        (name, d): half if LONG_UP[name] == (d == 0) else half - 1 for name in NAMES for d in (0, 1)
    }

    def message(name, d, k):
        i = here.ids[(1 - k) if d == 0 else (k - 1)]
        a = NAMES.index(name)
        src = blocks[name] if k == 1 else lands[name].at[i]
        return pltpu.make_async_remote_copy(
            src_ref=src,
            dst_ref=lands[name].at[i],
            send_sem=ring_send.at[a, d, k - 1],
            recv_sem=ring_recv.at[a, d, k - 1],
            device_id=(here.r, here.ring[d]),
            device_id_type=MESH,
        )

    def load(name, k):
        i = here.ids[k]
        a = NAMES.index(name)
        dst = into[name].at[pl.ds(pl.multiple_of(i * rows[name], 16), rows[name])]
        return pltpu.make_async_copy(lands[name].at[i], dst, load_sem.at[a, k + half])

    def keep_own(name):
        return pltpu.make_async_copy(
            blocks[name] if name != "d" else csend.at[0, pl.ds(0, rows["d"])],
            lands[name].at[here.s],
            load_sem.at[6, NAMES.index(name)],
        )

    def begin(name):
        for d in (0, 1):
            message(name, d, 1).start()
        if name == "d":
            held["own"] = fetch(blocks["d"], csend.at[0, pl.ds(0, rows["d"])], 4)
        else:
            keep_own(name).start()

    def serve(name, k):
        for d in (0, 1):
            if k <= reach[name, d]:
                message(name, d, k).wait_recv()
                if k < reach[name, d]:
                    message(name, d, k + 1).start()
                if name in into:
                    load(name, -k if d == 0 else k).start()

    def own_kept(name):
        keep_own(name).wait()
        load(name, 0).start()

    def came(name):
        found = [0]
        for k in range(1, half + 1):
            found += [-k] * (k <= reach[name, 0]) + [k] * (k <= reach[name, 1])
        return found

    def loaded(name):
        for k in came(name):
            load(name, k).wait()

    outs = []
    held = {}

    def save(src, dst):
        c = pltpu.make_async_copy(src, dst, out_sem.at[len(outs)])
        c.start()
        outs.append(c)

    def fetch(src, dst, i):
        c = pltpu.make_async_copy(src, dst, load_sem.at[7, i])
        c.start()
        return c

    def rows16(count, body):
        @pl.loop(0, count // 16)
        def _(i):
            body(pl.ds(pl.multiple_of(i * 16, 16), 16))

    own_width = wq.shape[1] // 3
    pairs = own_width // 128
    block = slots // 2
    units = g_blk.shape[1]
    rep = RepLinks(here, rep_send, rep_recv)
    lane = lax.broadcasted_iota(jnp.int32, (1, 128), 1)
    low = first_half((slots, 128))

    class XSlots:
        class at:
            def __class_getitem__(cls, g):
                return xs.at[pl.ds(g * slots, slots)]

    windows = []
    for t in range(3 * pairs):
        part, tt = t // pairs, t % pairs
        for h in (0, 1):
            first = part * width + (2 * tt + h) * 4 * 64
            i = len(windows)
            dst = hid.at[pl.ds(slots * (i // 8), slots), pl.ds(128 * (i % 8), 128)]
            start = pl.multiple_of(first + (here.r // 2) * 128, 128)
            c = pltpu.make_async_copy(w_qkv.at[:, pl.ds(start, 128)], dst, rep_send.at[14 + i])
            c.start()
            windows.append((c, dst))
    own_x = fetch(tok, xs.at[pl.ds(0, slots)], 0)
    own_c = fetch(cot, ysend, 1)

    long0, long1 = lens[0], lens[1]
    spot = lax.broadcasted_iota(jnp.int32, (8, slots), 1)
    end = jnp.where(spot < block, long0, long1 + block)
    row = lax.broadcasted_iota(jnp.int32, (8, slots), 0)
    together = jnp.where(seqs[0] == seqs[1], 1.0, 0.0)
    metas[0] = jnp.where(row == 0, jnp.where(spot < end, 1.0, 0.0), together)

    side = (here.s % 2) * 64
    wide = rows["q"]
    base[...] = jnp.zeros_like(base)
    base[0:6, :] = vectors[...].astype(F32)
    base[6:7, 0 : key_bias.shape[1]] = key_bias[...].astype(F32)
    whole = base[...]
    head = pltpu.roll(whole, (side - here.r * 64 + wide) % wide, 1)
    keys = pltpu.roll(whole, (side - here.r * ROT + wide) % wide, 1)
    line = lax.broadcasted_iota(jnp.int32, (16, wide), 0)
    place = lax.broadcasted_iota(jnp.int32, (16, wide), 1)
    inside = (place >= side) & (place < side + 64)
    key_inside = (place >= side) & (place < side + ROT)
    own_small = jnp.where(
        line < 4,
        whole,
        jnp.where(
            (line < 6) & inside, head, jnp.where((line == 6) & key_inside, keys, 0.0)
        ),
    )
    s_blk[...] = own_small.astype(BF16)

    here.greet()
    begin("s")
    begin("o")
    held["m"] = rep.gather_start(0, metas.at[0], metas)
    held["x"] = rep.gather_start(3, tok, XSlots)
    odd = (jnp.zeros((slots, 128), jnp.int32) + here.r % 2) == 1
    for t in range(3 * pairs):
        pair = []
        for h in (0, 1):
            c, ref = windows[2 * t + h]
            c.wait()
            value = ref[...].astype(F32)
            swapped = pltpu.roll(value, 64, 1)
            pair.append(jnp.where(odd, swapped, value) if h == 0 else jnp.where(odd, value, swapped))
        q_blk[0:wide, t * 128 : (t + 1) * 128] = jnp.where(low, pair[0], pair[1]).astype(BF16)
    begin("q")

    strips = []
    span = 384
    total = REPS * units
    piece = units // n
    for j in (0, 1):
        for s in range(n):
            o = s * REPS * piece + here.r * piece
            if s < half:
                off = o % 128
                a = o - off
            else:
                pad = (128 - (o + piece) % 128) % 128
                a = o + piece + pad - span
                off = span - piece - pad
            i = len(strips)
            ref = gates if j == 0 else ups
            dst = ref.at[pl.ds(slots * (s // 3), slots), pl.ds(span * (s % 3), span)]
            start = pl.multiple_of(j * total + a, 128)
            c = pltpu.make_async_copy(w_gu.at[:, pl.ds(start, span)], dst, rep_recv.at[14 + i])
            c.start()
            strips.append((c, dst, off))

    def select(j):
        for c, _, _ in strips[j * n : (j + 1) * n]:
            c.wait()
        out = (g_blk, u_blk)[j]
        for t in range(units // 128):
            whole = None
            for s in range(128 * t // piece, (128 * t + 127) // piece + 1):
                _, ref, off = strips[j * n + s]
                shift = (2 * span - (off + 128 * t - piece * s)) % span
                value = pltpu.roll(ref[...].astype(F32), shift, 1)[:, :128]
                first = s * piece - 128 * t
                whole = value if whole is None else jnp.where(lane >= first, value, whole)
            out[:, t * 128 : (t + 1) * 128] = whole.astype(BF16)

    def sel_g():
        select(0)
        begin("g")

    def sel_u():
        select(1)
        begin("u")

    def pass_m():
        held["m"] = rep.gather_pass(0, metas, held["m"])

    def pass_x():
        held["x"] = rep.gather_pass(3, XSlots, held["x"])

    def mask_cot():
        own_c.wait()
        for j in range(2):
            count = (long0, long1)[j]

            def chunk(at, j=j, count=count):
                first = lax.broadcasted_iota(jnp.int32, (16, width), 0) + at.start
                at = pl.ds(pl.multiple_of(at.start + j * block, 16), 16)
                value = ysend[at, :].astype(F32)
                ysend[at, :] = jnp.where(first < count, value, 0.0).astype(BF16)

            rows16(block, chunk)
        fetch(ysend, dyl_out.at[0], 2).wait()
        held["d"] = rep.gather_start(6, dyl_out.at[0], dyl_out)

    def pass_d():
        held["d"] = rep.gather_pass(6, dyl_out, held["d"])

    def ln1():
        for c in held["m"] + held["x"]:
            c.wait_recv()
        own_x.wait()
        mine = held["x"][1]
        mine.wait_send()
        rep.sent = [c for c in rep.sent if c is not mine]
        for name in "qs":
            own_kept(name)
            loaded(name)
        held["own"].wait()
        keep_own("d").start()
        for s in range(n):
            vecs[0:8, s * wide : (s + 1) * wide] = small[s * 16 : s * 16 + 8, :].astype(F32)
        gain, shift = vecs[0:1, :], vecs[1:2, :]

        def chunk(at):
            xs[at, :] = layer_rows(xs[at, :].astype(F32), gain, shift).astype(BF16)

        rows16(REPS * slots, chunk)
        save(xs, a1_out)

    def lane_bias(row, t):
        w = rows["q"]
        a = vecs[row : row + 1, 2 * t * w : 2 * t * w + 128]
        return a + vecs[row : row + 1, (2 * t + 1) * w : (2 * t + 1) * w + 128]

    def attend(g):
        line = lax.broadcasted_iota(jnp.int32, (slots, slots), 0)
        column = lax.broadcasted_iota(jnp.int32, (slots, slots), 1)
        here_rows = pl.ds(g * slots, slots)
        acc[...] = dot(xs[here_rows, :], wq[...])
        valid = metas[g, 0:1, :]
        same = metas[g, 1:2, :]
        for j in range(3):
            tabs[j, :block, :] = tables[j, :block, :]
            tabs[j, block:, :] = jnp.where(
                same[:, :128] > 0.5, tables[j, block:, :], tables[j, :block, :]
            )
        apart = (line >= block) & (column < block) & (same < 0.5)
        open_ = (column <= line) & jnp.logical_not(apart) & ((valid > 0.5) | (line == column))
        mask[...] = jnp.where(open_, 0.0, -1e30)
        for t in range(3 * pairs):
            part, tt = t // pairs, t % pairs
            tile = acc[:, t * 128 : (t + 1) * 128] + lane_bias((4, 6, 5)[part], tt)
            if part < 2:
                tile = (
                    tile * tabs[0]
                    + pltpu.roll(tile, 120, 1) * tabs[1]
                    + pltpu.roll(tile, 8, 1) * tabs[2]
                )
            (qs, ks, vs)[part][g, tt] = tile.astype(BF16)
        low_low = first_half((1, 128)).astype(F32).astype(BF16)
        high_low = (1.0 - first_half((1, 128)).astype(F32)).astype(BF16)
        for t in range(pairs):
            qt, kt, vt_ = qs[g, t], ks[g, t], vs[g, t]
            mixed = []
            for h in (0, 1):
                mine = low_low if h == 0 else high_low
                sc = dot_rt(qt * mine, kt) * (1.0 / 8.0) + mask[...]
                e = jnp.exp(sc - jnp.max(sc, axis=1, keepdims=True))
                p = (e / jnp.sum(e, axis=1, keepdims=True)).astype(BF16)
                ps[g, 2 * t + h] = p
                mixed.append(dot(p, vt_))
            mix = jnp.where(low, mixed[0], mixed[1])
            attn[here_rows, t * 128 : (t + 1) * 128] = mix.astype(BF16)
            attn_t[t * 128 : (t + 1) * 128, here_rows] = mix.T.astype(BF16)

    def out_far():
        keep_own("d").wait()
        own_kept("o")
        loaded("o")
        for g in (0, 1):
            csend[g] = dot(attn[(g + 2) * slots : (g + 3) * slots, :], wo[...]).astype(BF16)
        held["core"] = rep.start(9, csend, crecv, here.core)

    def out_y():
        held["core"].wait_recv()
        ysend[...] = (dot(attn[slots : 2 * slots, :], wo[...]) + crecv[1].astype(F32)).astype(BF16)
        held["y"] = rep.start(10, ysend, yrecv, here.across)

    def out_own():
        resid[...] = dot(attn[0:slots, :], wo[...]) + crecv[0].astype(F32)
        held["tok"] = fetch(tok, crecv.at[0], 3)
        save(qs, q_out)
        save(ks, k_out)
        save(vs, v_out)
        save(ps, p_out)
        save(attn_t, attn_out)
        save(metas, meta_out)

    def ln2():
        held["tok"].wait()
        held["y"].wait_recv()
        gain, shift = vecs[2:3, :], vecs[3:4, :]

        def chunk(at):
            x = resid[at, :] + yrecv[at, :].astype(F32) + crecv[0, at, :].astype(F32)
            resid[at, :] = x
            a2s[0, at, :] = layer_rows(x, gain, shift).astype(BF16)

        rows16(slots, chunk)
        held["a"] = rep.gather_start(11, a2s.at[0], a2s)
        save(resid, resid_out)

    def pass_a():
        held["a"] = rep.gather_pass(11, a2s, held["a"])

    def feed(g):
        if g == 0:
            own_kept("g")
            own_kept("u")
            for c in held["a"]:
                c.wait_recv()
            loaded("g")
            loaded("u")
            save(a2s, a2_out)
        at = pl.ds(g * slots, slots)
        gate = dot(a2s[g], wg[...])
        gates[at, :] = gate.astype(BF16)
        up = dot(a2s[g], wu[...])
        ups[at, :] = up.astype(BF16)
        act = gate * jax.nn.sigmoid(gate) * up
        for j in range(act.shape[1] // 128):
            hid[j * 128 : (j + 1) * 128, at] = act[:, j * 128 : (j + 1) * 128].T.astype(BF16)
        if g == REPS - 1:
            save(gates, gate_out)
            save(ups, up_out)
            save(hid, hid_out)

    steps = {
        "sg": sel_g, "su": sel_u, "bd": lambda: begin("d"), "pm": pass_m, "px": pass_x, "cot": mask_cot,
        "pd": pass_d, "ln1": ln1, "of": out_far, "oy": out_y, "oo": out_own, "ln2": ln2, "pa": pass_a,
    }
    for name in FORE_ORDER:
        if name in steps:
            steps[name]()
        elif name[:2] == "at":
            attend(int(name[2]))
        elif name[:2] == "fd":
            feed(int(name[2]))
        else:
            if name[0] == "q":
                serve("s", int(name[1]))
            serve(name[0], int(name[1]))
    for c in held["d"]:
        c.wait_recv()
    for name in NAMES:
        for d in (0, 1):
            for k in range(1, reach[name, d] + 1):
                message(name, d, k).wait_send()
    rep.finish()
    for c in outs:
        c.wait()


def forward_call(n, weights, tok, cot, vectors, key_bias, seqs, lens, tables):
    slots, width = tok.shape
    w_qkv, w_out, w_gu, w_down = weights
    lanes, units = w_qkv.shape[1] // REPS, w_gu.shape[1] // 2 // REPS
    rows, own_width = width // n, lanes // 3
    all_slots = REPS * slots
    pairs = own_width // 128
    half = n // 2
    S = jax.ShapeDtypeStruct
    heads = (REPS, pairs, slots, 128)
    out_shape = [
        S((n, rows, lanes), BF16),
        S((n, w_out.shape[0] // REPS, width), BF16),
        S((n, rows, units), BF16),
        S((n, rows, units), BF16),
        S((n, w_down.shape[0] // REPS, width), BF16),
        S((n, 16, rows), BF16),
        S((all_slots, width), BF16),
        S(heads, BF16),
        S(heads, BF16),
        S(heads, BF16),
        S((REPS, 2 * pairs, slots, slots), BF16),
        S((own_width, all_slots), BF16),
        S((slots, width), F32),
        S((REPS, slots, width), BF16),
        S((all_slots, units), BF16),
        S((all_slots, units), BF16),
        S((units, all_slots), BF16),
        S((REPS, slots, width), BF16),
        S((REPS, 8, slots), F32),
    ]
    V = pltpu.VMEM
    scratch = [
        V((rows, lanes), BF16),
        V((16, rows), BF16),
        V((16, rows), F32),
        V((rows, units), BF16),
        V((rows, units), BF16),
        V((width, lanes), BF16),
        V((own_width, width), BF16),
        V((width, units), BF16),
        V((width, units), BF16),
        V((all_slots, width), BF16),
        V(heads, BF16),
        V(heads, BF16),
        V(heads, BF16),
        V((REPS, 2 * pairs, slots, slots), BF16),
        V((all_slots, own_width), BF16),
        V((own_width, all_slots), BF16),
        V((slots, lanes), F32),
        V((2, slots, width), BF16),
        V((2, slots, width), BF16),
        V((slots, width), BF16),
        V((slots, width), BF16),
        V((slots, width), F32),
        V((REPS, slots, width), BF16),
        V((all_slots, units), BF16),
        V((all_slots, units), BF16),
        V((units, all_slots), BF16),
        V((REPS, 8, slots), F32),
        V((3, slots, 128), F32),
        V((slots, slots), F32),
        V((n * 16, rows), BF16),
        V((8, width), F32),
        pltpu.SemaphoreType.DMA((6, 2, half)),
        pltpu.SemaphoreType.DMA((6, 2, half)),
        pltpu.SemaphoreType.DMA((8, 2 * half + 1)),
        pltpu.SemaphoreType.DMA((14 + 6 * pairs,)),
        pltpu.SemaphoreType.DMA((14 + 2 * n,)),
        pltpu.SemaphoreType.DMA((12,)),
    ]
    anywhere = pl.BlockSpec(memory_space=pltpu.HBM)
    inside = pl.BlockSpec(memory_space=pltpu.VMEM)
    scalars = pl.BlockSpec(memory_space=pltpu.SMEM)
    return pl.pallas_call(
        functools.partial(forward_kernel, n),
        out_shape=out_shape,
        in_specs=[anywhere] * 6 + [inside, inside, scalars, scalars, inside],
        out_specs=[anywhere] * len(out_shape),
        scratch_shapes=scratch,
        compiler_params=pltpu.CompilerParams(
            collective_id=1, has_side_effects=True, vmem_limit_bytes=VMEM_LIMIT
        ),
    )(*weights, tok, cot, vectors, key_bias, seqs, lens, tables)


PARTS = ("d", "g", "u", "x", "y", "o", "p", "s")
PARTS_UP = {"d": False, "g": True, "u": False, "x": True, "y": True, "o": False, "p": False, "s": False}
BACK_ORDER = (
    "d0", "dh0", "dh1", "dh2", "dh3", "g0", "far2", "d1", "near2", "g1", "u0", "ln2", "d2", "mlpf", "g2",
    "mlpn", "pass", "ldrl", "u1", "at0", "g3", "ey2", "at1", "d3", "at2", "at3", "y0", "u2", "fd", "y1",
    "act", "far1", "x0", "near1", "y2", "x1", "fg", "u3", "y3", "x2", "sums", "fy", "p0", "s0", "x3", "fu",
    "hy", "o0", "p1", "fx", "hd", "o1", "s1", "p2", "o2", "s2", "p3", "hg", "hu", "s3", "o3", "fp", "fs",
    "fo", "hs", "hx", "hp", "ho",
)


def norm_rows_back(x, gain, grad):
    center = x - jnp.mean(x, axis=1, keepdims=True)
    inv = lax.rsqrt(jnp.mean(center * center, axis=1, keepdims=True) + 1e-05)
    normal = center * inv
    e = grad * gain
    cross = jnp.mean(e * normal, axis=1, keepdims=True)
    return inv * (e - jnp.mean(e, axis=1, keepdims=True) - normal * cross), normal


def backward_kernel(
    n,
    q_land, o_land, g_land, u_land, d_land, s_land, a1_in, q_in, k_in, v_in, p_in, attn_in,
    resid_in, a2_in, gate_in, up_in, hid_in, dyl_in, tok, metas, tables,
    act_out, grad_out, d_sum, g_sum, u_sum, x_sum, y_sum, o_sum, p_sum, s_sum,
    land_d, land_g, land_u, land_x, land_y, land_o, land_p, land_s, core_land, y_land, drl_land,
    dyl, hid, wd, gates, ups, a2, a1, wst, wo, attn_t, heads, probs, dqkv, datt, csend, crecv,
    ysend, ysend2, yrecv, own, resid, outp, stage, rstage, sstage, small, vecs, sums, headsums, tabs,
    ring_send, ring_recv, load_sem, rep_send, rep_recv, stream_sem, rstage_sem, fin_sem,
):
    here = Place(n)
    half = here.half
    slots, width = tok.shape
    rows = width // n
    units = gates.shape[1]
    lanes = dqkv.shape[1]
    own_width = lanes // 3
    pairs = own_width // 128
    lands = dict(zip(PARTS, (land_d, land_g, land_u, land_x, land_y, land_o, land_p, land_s)))
    finals = dict(zip(PARTS, (d_sum, g_sum, u_sum, x_sum, y_sum, o_sum, p_sum, s_sum)))
    shape = {name: lands[name].shape[2:] for name in PARTS}
    reach = {
        (name, d): half if PARTS_UP[name] == (d == 0) else half - 1 for name in PARTS for d in (0, 1)
    }
    rep = RepLinks(here, rep_send, rep_recv)

    def fetch(src, dst, i):
        c = pltpu.make_async_copy(src, dst, load_sem.at[i])
        c.start()
        return c

    def block_of(i, size):
        return pl.ds(pl.multiple_of(i * size, 16), size)

    def lanes_of(i, size):
        return pl.ds(pl.multiple_of(i * size, 128), size)

    def term(name, i):
        if name == "d":
            return dot(hid[block_of(i, shape["d"][0]), :], dyl[...])
        if name in ("g", "u"):
            return dot_lt(a2[:, lanes_of(i, rows)], (gates if name == "g" else ups)[...])
        if name == "x":
            return dot_lt(a1[:, lanes_of(i, rows)], dqkv[:, : lanes // 2])
        if name == "y":
            return dot_lt(a1[:, lanes_of(i, rows)], dqkv[:, lanes // 2 :])
        if name in ("o", "p"):
            cut = slice(0, width // 2) if name == "o" else slice(width // 2, width)
            return dot(attn_t[block_of(i, shape["o"][0]), :], wd[: dyl.shape[0], cut])
        return sums[i]

    def corner(ref, name):
        return ref.at[pl.ds(0, shape[name][0]), pl.ds(0, shape[name][1])]

    def message(name, d, k, src):
        a = PARTS.index(name)
        return pltpu.make_async_remote_copy(
            src_ref=src,
            dst_ref=lands[name].at[d, k - 1],
            send_sem=ring_send.at[a, d, k - 1],
            recv_sem=ring_recv.at[a, d, k - 1],
            device_id=(here.r, here.ring[d]),
            device_id_type=MESH,
        )

    def landed(name, d, k):
        message(name, d, k, lands[name].at[d, k - 1]).wait_recv()
        dst = sstage.at[2 + d] if name == "s" else corner(rstage.at[d], name)
        c = pltpu.make_async_copy(lands[name].at[d, k - 1], dst, rstage_sem.at[d])
        c.start()
        return c, dst

    flying = {}
    turn = [0, 0]

    def serve(name, j):
        hops = {}
        for d in (0, 1):
            k = half - j if reach[name, d] == half else half - 1 - j
            if k >= 1:
                hops[d] = k
        got = {d: landed(name, d, k + 1) for d, k in hops.items() if j > 0}
        for d, k in hops.items():
            if name == "s":
                slot, key = sstage.at[d], ("s", d)
            else:
                turn[d] = 1 - turn[d]
                slot, key = corner(stage.at[d, turn[d]], name), (d, turn[d])
            part = term(name, here.ids[k if d == 0 else -k])
            if d in got:
                got[d][0].wait()
                part = part + got[d][1][...].astype(F32)
            if key in flying:
                flying.pop(key).wait_send()
            slot[...] = part.astype(slot.dtype)
            flying[key] = message(name, d, k, slot)
            flying[key].start()

    opened = {}
    kept = []

    def finish(name):
        got = [landed(name, d, 1) for d in (0, 1)]
        part = term(name, here.ids[0])
        for c, ref in got:
            c.wait()
            part = part + ref[...].astype(F32)
        i = PARTS.index(name)
        late = {"s": sstage.at[4]}
        ref = late.get(name, corner(rstage.at[0], name))
        ref[...] = part.astype(ref.dtype)
        c = pltpu.make_async_copy(ref, finals[name].at[0], fin_sem.at[i])
        c.start()
        if name in late:
            opened[name] = rep.gather_start(3 * i, ref, finals[name])
            kept.append(c)
        else:
            c.wait()
            opened[name] = rep.gather_start(3 * i, finals[name].at[0], finals[name])

    def hand_on(name):
        opened[name] = rep.gather_pass(3 * PARTS.index(name), finals[name], opened[name])

    base = 3 * len(PARTS)

    def stream(names, body):
        def copies(s, slot):
            found = []
            for j, name in enumerate(names):
                land = {"q": q_land, "g": g_land, "u": u_land}[name]
                found.append(
                    pltpu.make_async_copy(
                        land.at[s, pl.ds(0, rows)],
                        wst.at[slot, j, :, pl.ds(0, land.shape[2])],
                        stream_sem.at[slot, j],
                    )
                )
            return found

        for c in copies(0, 0):
            c.start()

        @pl.loop(0, n)
        def _(s):
            slot = s % 2

            @pl.when(s + 1 < n)
            def _():
                for c in copies(s + 1, 1 - slot):
                    c.start()

            for c in copies(s, slot):
                c.wait()
            body(s, slot)

    def exchange_core(i, k):
        return rep.start(base + i, csend, core_land.at[k], here.core)

    def exchange_y(i, k, src):
        return rep.start(base + i, src, y_land.at[k], here.across)

    def drop_send(c):
        c.wait_send()
        rep.sent = [x for x in rep.sent if x is not c]

    here.greet()
    c_hid = fetch(hid_in, hid, 0)
    c_dyl = fetch(dyl_in, dyl, 1)
    c_hid.wait()
    c_dyl.wait()
    c_wd = fetch(d_land, wd, 2)
    c_gate = fetch(gate_in, gates, 3)
    c_up = fetch(up_in, ups, 4)
    c_a2 = fetch(a2_in, a2, 5)
    c_small = fetch(s_land, small, 9)
    c_res = fetch(resid_in, resid, 8)
    out_rows = o_land.shape[1]
    c_wo = [fetch(o_land.at[i], wo.at[pl.ds(i * out_rows, out_rows)], 32 + i) for i in range(n)]
    c_att = fetch(attn_in, attn_t, 14)
    c_a1 = fetch(a1_in, a1, 7)
    low_rows, high_rows = pl.ds(0, 2 * slots), pl.ds(2 * slots, 2 * slots)
    halves = (
        first_half((1, 128)).astype(F32).astype(BF16),
        (1.0 - first_half((1, 128)).astype(F32)).astype(BF16),
    )
    block = slots // 2
    held = {}
    waited = []

    def need(c):
        if not any(c is w for w in waited):
            waited.append(c)
            c.wait()

    def rows16(count, body):
        @pl.loop(0, count // 16)
        def _(i):
            body(pl.ds(pl.multiple_of(i * 16, 16), 16))

    def feed_back(g):
        if g == 0:
            for c in (c_wd, c_gate, c_up):
                c.wait()
        at = pl.ds(g * slots, slots)
        dh = dot_rt(dyl[at, :], wd[...])
        gate, up = gates[at, :].astype(F32), ups[at, :].astype(F32)
        sig = jax.nn.sigmoid(gate)
        gates[at, :] = (dh * up * sig * (1.0 + gate * (1.0 - sig))).astype(BF16)
        ups[at, :] = (dh * gate * sig).astype(BF16)

    def a2_product(at, slot):
        return dot_rt(gates[at, :], wst[slot, 0, :, :units]) + dot_rt(ups[at, :], wst[slot, 1, :, :units])

    def put_far(part, s):
        csend[0, :, lanes_of(s, rows)] = part[:slots]
        csend[1, :, lanes_of(s, rows)] = part[slots:]

    def far2():
        stream(("g", "u"), lambda s, slot: put_far(a2_product(high_rows, slot).astype(BF16), s))
        held["core1"] = exchange_core(0, 0)

    def put_near(part, s, ref):
        at = lanes_of(s, rows)
        ref[:, at] = part[:slots] + crecv[0, :, at].astype(F32)
        ysend[:, at] = (part[slots:] + crecv[1, :, at].astype(F32)).astype(BF16)

    def near2():
        held["core1"].wait_recv()
        fetch(core_land.at[0], crecv, 10).wait()
        stream(("g", "u"), lambda s, slot: put_near(a2_product(low_rows, slot), s, own))
        held["y1"] = exchange_y(1, 0, ysend)

    def mlpf():
        drop_send(held["core1"])
        for g in (0, 1):
            csend[g] = dot_lt(hid[:, (g + 2) * slots : (g + 3) * slots], wd[...]).astype(BF16)
        held["core2"] = exchange_core(2, 1)

    def mlpn():
        held["core2"].wait_recv()
        fetch(core_land.at[1], crecv, 13).wait()
        ysend2[...] = (dot_lt(hid[:, slots : 2 * slots], wd[...]) + crecv[1].astype(F32)).astype(BF16)
        need(c_res)
        outp[...] = resid[...] + dot_lt(hid[:, :slots], wd[...]) + crecv[0].astype(F32)

    def ln2():
        need(c_small)
        need(c_res)
        for s in range(n):
            vecs[0:8, s * rows : (s + 1) * rows] = small[s, 0:8, :].astype(F32)
        headsums[...] = jnp.zeros_like(headsums)
        vecs[8:40, :] = jnp.zeros((32, width), F32)
        held["y1"].wait_recv()
        fetch(y_land.at[0], yrecv, 11).wait()
        drop_send(held["y1"])
        gain = vecs[2:3, :]

        def chunk(at):
            da = own[at, :] + yrecv[at, :].astype(F32)
            back, normal = norm_rows_back(resid[at, :], gain, da)
            prod = da * normal
            vecs[24:32, :] += prod[:8] + prod[8:]
            vecs[32:40, :] += da[:8] + da[8:]
            dr = dyl[at, :].astype(F32) + back
            own[at, :] = dr
            ysend[at, :] = dr.astype(BF16)

        rows16(slots, chunk)
        fetch(ysend, drl_land.at[0], 12).wait()
        held["drl"] = rep.gather_start(base + 3, drl_land.at[0], drl_land)

    def pass_on():
        held["drl"] = rep.gather_pass(base + 3, drl_land, held["drl"])

    def ldrl():
        for c in held["drl"]:
            c.wait_recv()
        loads = [fetch(drl_land.at[g], wd.at[pl.ds(g * slots, slots)], 16 + g) for g in range(REPS)]
        for c in loads + c_wo + [c_att]:
            c.wait()

    def ey2():
        held["y2"] = exchange_y(6, 1, ysend2)

    def head_copies(g, slot):
        found = [
            pltpu.make_async_copy(ref.at[g], heads.at[slot, j], stream_sem.at[slot, 2 + j])
            for j, ref in enumerate((q_in, k_in, v_in))
        ]
        return found + [pltpu.make_async_copy(p_in.at[g], probs.at[slot], stream_sem.at[slot, 5])]

    def turn_back(tile):
        return tile * tabs[0] - pltpu.roll(tile, 120, 1) * tabs[1] - pltpu.roll(tile, 8, 1) * tabs[2]

    def attend_back(g):
        slot = g % 2
        if g == 0:
            for c in head_copies(0, 0):
                c.start()
        if g + 1 < REPS:
            for c in head_copies(g + 1, 1 - slot):
                c.start()
        at = pl.ds(g * slots, slots)
        datt[...] = dot_rt(wd[at, :], wo[...]).astype(BF16)
        same = metas[g, 1:2, :128]
        for j in range(3):
            tabs[j, :block, :] = tables[j, :block, :]
            tabs[j, block:, :] = jnp.where(same > 0.5, tables[j, block:, :], tables[j, :block, :])
        for c in head_copies(g, slot):
            c.wait()
        low = first_half((slots, 128))
        for t in range(pairs):
            da = datt[:, t * 128 : (t + 1) * 128]
            qt, kt, vt = heads[slot, 0, t], heads[slot, 1, t], heads[slot, 2, t]
            both = []
            for h in (0, 1):
                p = probs[slot, 2 * t + h]
                pf = p.astype(F32)
                dp = dot_rt(da * halves[h], vt)
                delta = jnp.sum(dp * pf, axis=1, keepdims=True)
                ds = (pf * (dp - delta)).astype(BF16)
                both.append((dot(ds, kt), dot_lt(ds, qt), dot_lt(p, da)))
            dq, dk, dv = [jnp.where(low, a, b) for a, b in zip(*both)]
            dq, dk = turn_back(dq * (1.0 / 8.0)), turn_back(dk * (1.0 / 8.0))
            for j, value in enumerate((dq, dk, dv)):
                row = j * pairs + t
                headsums[row : row + 1, :] += jnp.sum(value, axis=0, keepdims=True)
                first = j * own_width + t * 128
                dqkv[at, first : first + 128] = value.astype(BF16)

    def far1():
        drop_send(held["core2"])

        def body(s, slot):
            put_far(dot_rt(dqkv[high_rows, :], wst[slot, 0, :, :lanes]).astype(BF16), s)

        stream(("q",), body)
        held["core3"] = exchange_core(7, 2)

    def act():
        held["y2"].wait_recv()
        fetch(y_land.at[1], yrecv, 20).wait()

        def chunk(at):
            yrecv[at, :] = (outp[at, :] + yrecv[at, :].astype(F32)).astype(BF16)

        rows16(slots, chunk)
        fetch(yrecv, act_out, 21).wait()

    def near1():
        held["core3"].wait_recv()
        fetch(core_land.at[2], crecv, 22).wait()

        def body(s, slot):
            put_near(dot_rt(dqkv[low_rows, :], wst[slot, 0, :, :lanes]), s, resid)

        stream(("q",), body)
        held["y3"] = exchange_y(8, 2, ysend)
        held["tok"] = fetch(tok, crecv.at[1], 23)

    def add_up():
        held["tok"].wait()
        held["y3"].wait_recv()
        fetch(y_land.at[2], yrecv, 24).wait()
        gain = vecs[0:1, :]

        def chunk(at):
            da = resid[at, :] + yrecv[at, :].astype(F32)
            back, normal = norm_rows_back(crecv[1, at, :].astype(F32), gain, da)
            prod = da * normal
            vecs[8:16, :] += prod[:8] + prod[8:]
            vecs[16:24, :] += da[:8] + da[8:]
            yrecv[at, :] = (own[at, :] + back).astype(BF16)

        rows16(slots, chunk)
        held["grad"] = fetch(yrecv, grad_out, 25)
        sums[...] = jnp.zeros_like(sums)
        for j in range(4):
            total = jnp.sum(vecs[8 + 8 * j : 16 + 8 * j, :], axis=0, keepdims=True)
            for s in range(n):
                sums[s, j : j + 1, :] = total[:, s * rows : (s + 1) * rows]
        for s in range(n):
            for j, part in ((4, 0), (5, 2), (6, 1)):
                row = part * pairs + s // 2
                sums[s, j : j + 1, 0:128] = headsums[row : row + 1, :] * halves[s % 2].astype(F32)

    steps = {
        "far2": far2, "near2": near2, "mlpf": mlpf, "mlpn": mlpn, "ln2": ln2, "pass": pass_on,
        "ldrl": ldrl, "ey2": ey2, "far1": far1, "act": act, "near1": near1, "sums": add_up,
    }
    for name in BACK_ORDER:
        if name in steps:
            steps[name]()
        elif name[:2] == "dh":
            feed_back(int(name[2]))
        elif name[:2] == "at":
            attend_back(int(name[2]))
        elif name[0] == "f":
            finish(name[1])
        elif name[0] == "h":
            hand_on(name[1])
        else:
            if name in ("g0", "u0"):
                need(c_a2)
            if name in ("x0", "y0"):
                need(c_a1)
            serve(name[0], int(name[1]))
    for name in PARTS:
        for c in opened[name]:
            c.wait_recv()
    held["grad"].wait()
    for c in kept:
        c.wait()
    rep.finish()
    for c in flying.values():
        c.wait_send()


def backward_call(n, lands, kept, tok, meta, tables):
    slots, width = tok.shape
    q_land, o_land, g_land, u_land, d_land, s_land = lands
    a1, qs, ks, vs, ps, attn_t, resid, a2, gate, up, hid, dyl = kept
    all_slots, units = gate.shape
    lanes = q_land.shape[2]
    pairs = lanes // 3 // 128
    half = n // 2
    rows = width // n
    S = jax.ShapeDtypeStruct
    block = {
        "d": (d_land.shape[1], width),
        "g": (rows, units),
        "u": (rows, units),
        "x": (rows, lanes // 2),
        "y": (rows, lanes // 2),
        "o": (o_land.shape[1], width // 2),
        "p": (o_land.shape[1], width // 2),
        "s": (8, rows),
    }
    kind = {name: F32 if name == "s" else BF16 for name in PARTS}
    out_shape = (
        [S((slots, width), BF16), S((slots, width), BF16)]
        + [S((REPS,) + block[name], kind[name]) for name in PARTS]
        + [S((2, half) + block[name], kind[name]) for name in PARTS]
        + [S((3, 2, slots, width), BF16), S((3, slots, width), BF16), S((REPS, slots, width), BF16)]
    )
    V = pltpu.VMEM
    scratch = [
        V((all_slots, width), BF16),
        V(hid.shape, BF16),
        V((units, width), BF16),
        V((all_slots, units), BF16),
        V((all_slots, units), BF16),
        V((all_slots, width), BF16),
        V((all_slots, width), BF16),
        V((2, 2, rows, lanes), BF16),
        V((lanes // 3, width), BF16),
        V((lanes // 3, all_slots), BF16),
        V((2, 3, pairs, slots, 128), BF16),
        V((2, 2 * pairs, slots, slots), BF16),
        V((all_slots, lanes), BF16),
        V((slots, lanes // 3), BF16),
        V((2, slots, width), BF16),
        V((2, slots, width), BF16),
        V((slots, width), BF16),
        V((slots, width), BF16),
        V((slots, width), BF16),
        V((slots, width), F32),
        V((slots, width), F32),
        V((slots, width), F32),
        V((2, 2, rows, width), BF16),
        V((2, rows, width), BF16),
        V((5, 8, rows), F32),
        V((n, 16, rows), BF16),
        V((40, width), F32),
        V((n, 8, rows), F32),
        V((16, 128), F32),
        V((3, slots, 128), F32),
        pltpu.SemaphoreType.DMA((len(PARTS), 2, half)),
        pltpu.SemaphoreType.DMA((len(PARTS), 2, half)),
        pltpu.SemaphoreType.DMA((32 + n,)),
        pltpu.SemaphoreType.DMA((3 * len(PARTS) + 9,)),
        pltpu.SemaphoreType.DMA((3 * len(PARTS) + 9,)),
        pltpu.SemaphoreType.DMA((2, 6)),
        pltpu.SemaphoreType.DMA((2,)),
        pltpu.SemaphoreType.DMA((len(PARTS),)),
    ]
    anywhere = pl.BlockSpec(memory_space=pltpu.HBM)
    inside = pl.BlockSpec(memory_space=pltpu.VMEM)
    out = pl.pallas_call(
        functools.partial(backward_kernel, n),
        out_shape=out_shape,
        in_specs=[anywhere] * 19 + [inside] * 2,
        out_specs=[anywhere] * len(out_shape),
        scratch_shapes=scratch,
        compiler_params=pltpu.CompilerParams(
            collective_id=2, has_side_effects=True, vmem_limit_bytes=VMEM_LIMIT
        ),
    )(q_land, o_land, g_land, u_land, d_land.reshape(units, width), s_land, a1, qs, ks, vs, ps, attn_t,
      resid, a2, gate, up, hid, dyl, tok, meta, tables)
    return out[:2], dict(zip(PARTS, out[2 : 2 + len(PARTS)]))


def weave_kernel(
    n,
    d_in, g_in, u_in, x_in, y_in, o_in, p_in, s_in, act_in, grad_in,
    out_act, out_grad, out_vectors, out_key, out_qkv, out_out, out_gu, out_down,
    dv, gv, uv, xv, yv, ov, pv, av, qkv, outs, gu, down, small, load_sem, save_sem,
):
    r = lax.axis_index("rep")
    rel = [(r // 2 + q // 2) % 2 + 2 * ((r + q) % 2) for q in range(REPS)]
    turns = 2 * REPS
    count = g_in.shape[1] // turns
    lane = lax.broadcasted_iota(jnp.int32, (count, 128), 1)
    units = g_in.shape[2]
    piece = units // n
    cut = ((g_in, gv), (u_in, uv), (x_in, xv), (y_in, yv))

    def lines(c):
        return pl.ds(pl.multiple_of(c * count, 16), count)

    def load(j, c):
        src, dst = cut[j]
        return pltpu.make_async_copy(src.at[:, lines(c)], dst.at[:, lines(c)], load_sem.at[j, c])

    def load_slab(j, q):
        src, dst = ((d_in, dv), (o_in, ov), (p_in, pv))[j]
        return pltpu.make_async_copy(src.at[rel[q]], dst.at[q], load_sem.at[4 + j, q])

    def save(j, c):
        src, dst = ((gu, out_gu), (qkv, out_qkv))[j]
        return pltpu.make_async_copy(src.at[lines(c)], dst.at[lines(c)], save_sem.at[j, c])

    def save_slab(j, q):
        src, dst = ((down, out_down), (outs, out_out))[j]
        high = src.shape[0] // REPS
        at = pl.ds(q * high, high)
        return pltpu.make_async_copy(src.at[at], dst.at[at], save_sem.at[2 + j, q])

    pair = ((act_in, out_act), (grad_in, out_grad))
    through = [pltpu.make_async_copy(pair[j][0], av.at[j], load_sem.at[7, j]) for j in (0, 1)]
    onward = [pltpu.make_async_copy(av.at[j], pair[j][1], save_sem.at[4, j]) for j in (0, 1)]
    for q in range(REPS):
        load_slab(0, q).start()
    for c in range(turns):
        for j in range(4):
            load(j, c).start()
    for q in range(REPS):
        load_slab(1, q).start()
        load_slab(2, q).start()
    for c in through:
        c.start()
    for q in range(REPS):
        load_slab(0, q).wait()
        high = dv.shape[1]
        down[q * high : (q + 1) * high, :] = dv[q].astype(F32)
        save_slab(0, q).start()

    def join(segments):
        whole = segments[0][1]
        for low, value in segments[1:]:
            whole = jnp.where(lane >= low, value, whole)
        return whole

    @pl.loop(0, turns)
    def _(c):
        for j in range(4):
            load(j, c).wait()

        def tile(ref, q, a):
            return ref[rel[q], lines(c), a * 128 : (a + 1) * 128].astype(F32)

        for side, ref in ((0, gv), (1, uv)):
            for j in range(REPS * units // 128):
                segments = []
                for k in range(128 * j // piece, (128 * j + 127) // piece + 1):
                    s, q = k // REPS, k % REPS
                    low, high = max(0, k * piece - 128 * j), min(128, (k + 1) * piece - 128 * j)
                    start = 128 * j - piece * (k - s)
                    a, m = start // 128, start % 128
                    if low < 128 - m:
                        value = tile(ref, q, a)
                        segments.append((low, pltpu.roll(value, 128 - m, 1) if m else value))
                    if high > 128 - m:
                        segments.append(
                            (max(low, 128 - m), pltpu.roll(tile(ref, q, a + 1), 128 - m, 1))
                        )
                first = side * REPS * units + j * 128
                gu[lines(c), first : first + 128] = join(segments)
        save(0, c).start()
        per = x_in.shape[2] // 64
        for t in range(qkv.shape[1] // 128):
            group = t // 2
            ref, at = (xv, group) if group < per else (yv, group - per)
            values = []
            for h in (0, 1):
                value = tile(ref, 2 * (t % 2) + h, at // 2)
                values.append((64 * h, pltpu.roll(value, 64, 1) if at % 2 != h else value))
            qkv[lines(c), t * 128 : (t + 1) * 128] = join(values)
        save(1, c).start()

    for c, d in zip(through, onward):
        c.wait()
        d.start()
    for q in range(REPS):
        load_slab(1, q).wait()
        load_slab(2, q).wait()
        high, half = ov.shape[1:]
        outs[q * high : (q + 1) * high, :half] = ov[q].astype(F32)
        outs[q * high : (q + 1) * high, half:] = pv[q].astype(F32)
        save_slab(1, q).start()
    small[...] = jnp.zeros_like(small)
    small[0:4, :] = s_in[0, 0:4, :] + s_in[1, 0:4, :] + s_in[2, 0:4, :] + s_in[3, 0:4, :]
    row = lax.broadcasted_iota(jnp.int32, (1, 128), 1)
    own = []
    for q in range(REPS):
        v = s_in[rel[q], 4:7, 0:128]
        own.append(v + pltpu.roll(v, 64, 1))
    for j in (0, 1):
        for p in (0, 1):
            small[4 + j : 5 + j, p * 128 : (p + 1) * 128] = jnp.where(
                row < 64, own[2 * p][j : j + 1], own[2 * p + 1][j : j + 1]
            )
    keys = own[0][2:3]
    for q in range(1, REPS):
        keys = jnp.where(row >= q * ROT, pltpu.roll(own[q][2:3], q * ROT, 1), keys)
    out_vectors[...] = small[0:6, :]
    out_key[...] = keys[:, : out_key.shape[1]]
    for c in onward:
        c.wait()
    for q in range(REPS):
        save_slab(0, q).wait()
        save_slab(1, q).wait()
    for c in range(turns):
        save(0, c).wait()
        save(1, c).wait()


def weave_call(n, act, grad, key_rows, parts):
    d, g, u, x, y, o, p, s = [parts[name] for name in PARTS]
    rows = g.shape[1]
    S = jax.ShapeDtypeStruct
    V = pltpu.VMEM
    big = [
        (rows, 2 * REPS * x.shape[2]),
        (REPS * o.shape[1], 2 * o.shape[2]),
        (rows, 2 * REPS * g.shape[2]),
        (REPS * d.shape[1], d.shape[2]),
    ]
    anywhere = pl.BlockSpec(memory_space=pltpu.HBM)
    inside = pl.BlockSpec(memory_space=pltpu.VMEM)
    out = pl.pallas_call(
        functools.partial(weave_kernel, n),
        out_shape=[S(act.shape, BF16), S(grad.shape, BF16), S((6, rows), F32), S((1, key_rows), F32)]
        + [S(shape, F32) for shape in big],
        in_specs=[anywhere] * 7 + [inside] + [anywhere] * 2,
        out_specs=[anywhere] * 2 + [inside] * 2 + [anywhere] * 4,
        scratch_shapes=[V(a.shape, BF16) for a in (d, g, u, x, y, o, p)]
        + [V((2,) + act.shape, BF16)]
        + [V(shape, F32) for shape in big]
        + [
            V(s.shape[1:], F32),
            pltpu.SemaphoreType.DMA((8, 2 * REPS)),
            pltpu.SemaphoreType.DMA((5, 2 * REPS)),
        ],
        compiler_params=pltpu.CompilerParams(vmem_limit_bytes=VMEM_LIMIT),
    )(d, g, u, x, y, o, p, s, act, grad)
    return (out[0], out[1], out[2].T, out[3].reshape(key_rows, 1)) + tuple(out[4:])


def core_swap(x):
    return lax.ppermute(x, "rep", [(0, 1), (1, 0), (2, 3), (3, 2)])


def y_swap(x):
    return lax.ppermute(x, "rep", [(0, 2), (1, 3), (2, 0), (3, 1)])


def rep_parts(x):
    across = y_swap(x)
    return [x, across, core_swap(x), core_swap(across)]


def rep_gather(x):
    return jnp.concatenate(rep_parts(x), axis=0)


def rep_reduce(a, w_dot, slots):
    far = core_swap(w_dot(a[2 * slots :]).astype(BF16))
    near = w_dot(a[: 2 * slots]) + far.astype(F32)
    return near[:slots] + y_swap(near[slots:].astype(BF16)).astype(F32)


def solution(mesh):
    n = mesh.shape["shard"]
    half_ring = n // 2
    order = list(range(0, n, 2)) + list(range(n - 1, 0, -2))
    place = [order.index(s) for s in range(n)]
    up_ring = [(order[i], order[(i + 1) % n]) for i in range(n)]
    down_ring = [(b, a) for a, b in up_ring]

    def hop(x, ring, sent):
        if len(sent) >= DEPTH:
            x, _ = lax.optimization_barrier((x, sent[-DEPTH]))
        x = lax.ppermute(x, "shard", ring)
        sent.append(x)
        return x

    def ring_ids():
        spot = jnp.array(place, jnp.int32)[lax.axis_index("shard")]
        table = jnp.array(order, jnp.int32)
        return {k: table[(spot + k) % n] for k in range(-half_ring, half_ring + 1)}

    def gather(x, ids, forward_extra, places, line):
        bufs = places(None, x, ids[0])
        up = down = x
        for k in range(1, half_ring + 1):
            go_up = k < half_ring or forward_extra
            go_down = k < half_ring or not forward_extra
            if go_up:
                up = hop(up, up_ring, line[0])
            if go_down:
                down = hop(down, down_ring, line[1])
            if go_up:
                bufs = places(bufs, up, ids[-k])
            if go_down:
                bufs = places(bufs, down, ids[k])
            yield
        return bufs

    def put(bufs, block, at):
        if bufs is None:
            bufs = jnp.zeros((n,) + block.shape, block.dtype)
        return lax.dynamic_update_index_in_dim(bufs, block, at, 0)

    def reduce(term, ids, forward_extra, line, kind=BF16):
        acc = {}
        for k in range(half_ring, 0, -1):
            for side, (ring, sign, extra) in enumerate(
                ((up_ring, 1, forward_extra), (down_ring, -1, not forward_extra))
            ):
                if k == half_ring and not extra:
                    continue
                part = term(ids[sign * k])
                if side in acc:
                    part = part + acc[side].astype(F32)
                acc[side] = hop(part.astype(kind), ring, line[side])
            yield
        return term(ids[0]) + acc[0].astype(F32) + acc[1].astype(F32)

    def run(chains, turns):
        done = {}
        for name in turns:
            for _ in range(n // 8):
                if name in done:
                    continue
                try:
                    next(chains[name])
                except StopIteration as stop:
                    done[name] = stop.value
        for name, chain in chains.items():
            while name not in done:
                try:
                    next(chain)
                except StopIteration as stop:
                    done[name] = stop.value
        return done

    def pick_columns(w, groups, width, r):
        chosen = [
            lax.select_n(
                r,
                *[
                    w[:, (g * REPS + q) * width : (g * REPS + q + 1) * width]
                    for q in range(REPS)
                ],
            )
            for g in range(groups)
        ]
        return jnp.concatenate(chosen, axis=1)

    def by_rep(parts, y, core):
        own, across, beside, both = parts
        low0 = lax.select(core == 0, own, beside)
        low1 = lax.select(core == 0, beside, own)
        high0 = lax.select(core == 0, across, both)
        high1 = lax.select(core == 0, both, across)
        return [
            lax.select(y == 0, low0, high0),
            lax.select(y == 0, low1, high1),
            lax.select(y == 0, high0, low0),
            lax.select(y == 0, high1, low1),
        ]

    def weave(parts, groups, width):
        pieces = [
            parts[q][:, g * width : (g + 1) * width]
            for g in range(groups)
            for q in range(REPS)
        ]
        return jnp.concatenate(pieces, axis=1).astype(F32)

    def on_device(
        tokens, cotangent, block_seq, block_len, vectors, key_bias, w_qkv, w_out, w_gate_up, w_down
    ):
        slots, features = tokens.shape
        blocks = block_seq.shape[0]
        block_size = slots // blocks
        head_dim = features // HEADS
        own_heads = HEADS // REPS
        own_width = own_heads * head_dim
        all_slots = REPS * slots
        scale = 1.0 / math.sqrt(head_dim)
        rows = features // n
        hidden_units = w_gate_up.shape[1] // 2
        own_hidden = hidden_units // REPS
        down_rows = w_down.shape[0] // REPS
        out_rows = w_out.shape[0] // REPS
        regroup = out_rows < head_dim
        r = lax.axis_index("rep")
        y, core = r // 2, r % 2
        ids = ring_ids()

        def mix_out(x):
            if not regroup:
                return x
            pairs = [
                (k * n + 4 * j + q, q * n + 4 * j + k)
                for k in range(REPS)
                for j in range(n // 4)
                for q in range(REPS)
            ]
            return lax.ppermute(x, BOTH, pairs)

        fast = blocks == 2 and down_rows % 16 == 0 and out_rows == head_dim and rows % 128 == 0
        own_valid = (
            jnp.arange(block_size, dtype=jnp.int32)[None, :] < block_len[:, None]
        ).reshape(-1)
        grad_output = cotangent.astype(F32) * own_valid[:, None].astype(F32)
        dyl_own = grad_output.astype(BF16)
        if fast:
            angles = np.arange(slots, dtype=np.float32)[:, None] * np.exp(
                np.arange(ROT // 2, dtype=np.float32) * np.float32(-2.0 * math.log(10000.0) / ROT)
            ).astype(np.float32)
            cosine, sine = np.cos(angles), np.sin(angles)
            rest = np.ones((slots, head_dim - ROT), np.float32)
            none = np.zeros((slots, ROT // 2), np.float32)
            tables = np.stack(
                [
                    np.concatenate([cosine, cosine, rest] * 2, axis=1),
                    np.concatenate([-sine, none, 0 * rest] * 2, axis=1),
                    np.concatenate([none, sine, 0 * rest] * 2, axis=1),
                ]
            ).astype(np.float32)
            weights = (w_qkv, w_out, w_gate_up, w_down)
            out = forward_call(
                n, weights, tokens, cotangent, vectors.T, key_bias.T, block_seq, block_len, jnp.asarray(tables)
            )
            a1, qs, ks, vs, ps, attn, resid, a2, gate, up, hid, dyl_all, metas = out[6:]
            whole = (all_slots, features)
            (activations, grad_input), parts = backward_call(
                n,
                out[:6],
                (a1, qs, ks, vs, ps, attn, resid, a2.reshape(whole), gate, up, hid, dyl_all.reshape(whole)),
                tokens,
                metas,
                tables,
            )

            return weave_call(n, activations, grad_input, key_bias.shape[0], parts)
        else:
            small = jnp.concatenate([vectors.T.reshape(-1), key_bias.reshape(-1)])
            lanes = 3 * own_width
            small_rows = -(-small.size // lanes)
            small_rows = -(-small_rows // 16) * 16
            small = jnp.pad(small, (0, small_rows * lanes - small.size)).reshape(small_rows, lanes)
            qkv_block = jnp.concatenate([pick_columns(w_qkv, 3 * own_heads, head_dim, r), small], axis=0)

            def put_qkv(bufs, block, at):
                a, b = (None, None) if bufs is None else bufs
                return put(a, block[:rows], at), put(b, block[rows:], at)

            out_block = mix_out(lax.dynamic_slice_in_dim(w_out, r * out_rows, out_rows, 0))
            gate_block = pick_columns(w_gate_up[:, :hidden_units], n, down_rows, r)
            up_block = pick_columns(w_gate_up[:, hidden_units:], n, down_rows, r)
            down_block = lax.dynamic_slice_in_dim(w_down, r * down_rows, down_rows, 0)
            line = ([], [])
            got = run(
                {
                    "q": gather(qkv_block, ids, True, put_qkv, line),
                    "o": gather(out_block, ids, False, put, line),
                    "g": gather(gate_block, ids, True, put, line),
                    "u": gather(up_block, ids, False, put, line),
                    "d": gather(down_block, ids, False, put, line),
                },
                "qoqoqoqoguguguguddddd",
            )
            wq, smalls = got["q"]
            wq = wq.reshape(features, lanes)
            smalls = smalls.reshape(n, -1).astype(F32)
            vec = smalls[:, : 6 * rows].reshape(n, 6, rows).transpose(1, 0, 2).reshape(6, features)
            key_full = smalls[:, 6 * rows : 6 * rows + HEADS * ROT // n].reshape(own_heads, REPS, ROT)
            key_own = lax.dynamic_index_in_dim(key_full, r, 1, keepdims=False)
            key_shift = jnp.pad(key_own, ((0, 0), (0, head_dim - ROT))).reshape(own_width)

            def own_heads_of(v):
                return lax.dynamic_index_in_dim(
                    v.reshape(own_heads, REPS, head_dim), r, 1, keepdims=False
                ).reshape(own_width)

            wo = got["o"].reshape(own_width, features)
            wg = got["g"].reshape(features, own_hidden)
            wu = got["u"].reshape(features, own_hidden)
            wd = got["d"].reshape(own_hidden, features)

            meta = jnp.concatenate([block_seq, block_len]).astype(F32)
            meta = jnp.pad(meta, (0, 128 - 2 * blocks)).reshape(1, 128)
            meta = jnp.concatenate(rep_parts(jnp.broadcast_to(meta, (8, 128))), axis=0)
            meta = meta.reshape(REPS, 8, 128)[:, 0, :]
            seqs = meta[:, :blocks].astype(jnp.int32)
            lens = meta[:, blocks : 2 * blocks].astype(jnp.int32)
            index = jnp.arange(blocks, dtype=jnp.int32)
            same = seqs[:, None, :] == seqs[:, :, None]
            earlier = jnp.sum(
                jnp.where((index[None, :] < index[:, None]) & same, 1, 0), axis=2
            ).astype(jnp.int32)
            offset = jnp.arange(block_size, dtype=jnp.int32)
            seq_slot = jnp.broadcast_to(seqs[:, :, None], (REPS, blocks, block_size)).reshape(REPS, slots)
            valid = (offset[None, None, :] < lens[:, :, None]).reshape(REPS, slots)
            positions = (earlier[:, :, None] * block_size + offset[None, None, :]).reshape(all_slots)
            slot_index = jnp.arange(slots, dtype=jnp.int32)
            allowed = (seq_slot[:, None, :] == seq_slot[:, :, None]) & (
                slot_index[None, :] <= slot_index[:, None]
            )[None]
            allowed = allowed & (valid[:, None, :] | (slot_index[None, :] == slot_index[:, None])[None])
            cosine, sine = turn_tables(positions)

            x_all = rep_gather(tokens)
            dyl = rep_gather(dyl_own)

            tokens_f = tokens.astype(F32)
            normal_one, inv_one = normalize(tokens_f)
            normal_all, _ = normalize(x_all.astype(F32))
            a1 = (normal_all * vec[0] + vec[1]).astype(BF16)
            projected = dot(a1, wq)
            head_shape = (all_slots, own_heads, head_dim)
            group_shape = (REPS, slots, own_heads, head_dim)
            q = rotate((projected[:, :own_width] + own_heads_of(vec[4])).reshape(head_shape), cosine, sine)
            k = rotate((projected[:, own_width : 2 * own_width] + key_shift).reshape(head_shape), cosine, sine)
            v = projected[:, 2 * own_width :] + own_heads_of(vec[5])
            q = q.astype(BF16).reshape(group_shape)
            k = k.astype(BF16).reshape(group_shape)
            v = v.astype(BF16).reshape(group_shape)
            scores = jnp.einsum("gshd,gthd->ghst", q, k, preferred_element_type=F32) * scale
            scores = jnp.where(allowed[:, None], scores, -1e30)
            exponent = jnp.exp(scores - jnp.max(scores, axis=-1, keepdims=True))
            probs = exponent / jnp.sum(exponent, axis=-1, keepdims=True)
            probs_low = probs.astype(BF16)
            attn = jnp.einsum("ghst,gthd->gshd", probs_low, v, preferred_element_type=F32)
            attn = attn.reshape(all_slots, own_width).astype(BF16)
            resid = tokens_f + rep_reduce(attn, lambda a: dot(a, wo), slots)
            normal_two, inv_two = normalize(resid)
            a2 = rep_gather((normal_two * vec[2] + vec[3]).astype(BF16))
            gate = dot(a2, wg)
            up = dot(a2, wu)
            sig = jax.nn.sigmoid(gate)
            hidden = (gate * sig * up).astype(BF16)

        def blocks_of(a):
            return a.reshape(all_slots, n, -1).transpose(1, 0, 2)

        hidden_b = blocks_of(hidden)
        activations = (resid + rep_reduce(hidden, lambda a: dot(a, wd), slots)).astype(BF16)
        grad_hidden = dot_rt(dyl, wd)
        grad_gate = (grad_hidden * up * sig * (1.0 + gate * (1.0 - sig))).astype(BF16)
        grad_up = (grad_hidden * gate * sig).astype(BF16)
        a2_b = blocks_of(a2)
        grad_gu = jnp.concatenate([grad_gate, grad_up], axis=1)
        wgu = jnp.concatenate([wg, wu], axis=1)
        grad_a2 = rep_reduce(grad_gu, lambda a: dot_rt(a, wgu), slots)
        grad_resid = grad_output + norm_back(grad_a2 * vec[2], normal_two, inv_two)
        drl = rep_gather(grad_resid.astype(BF16))
        attn_b = blocks_of(attn)
        d_attn = dot_rt(drl, wo).astype(BF16).reshape(group_shape)
        grad_v = jnp.einsum("ghst,gshd->gthd", probs_low, d_attn, preferred_element_type=F32)
        grad_p = jnp.einsum("gshd,gthd->ghst", d_attn, v, preferred_element_type=F32)
        delta = jnp.sum(grad_p * probs, axis=-1, keepdims=True)
        grad_s = (probs * (grad_p - delta)).astype(BF16)
        grad_q = jnp.einsum("ghst,gthd->gshd", grad_s, k, preferred_element_type=F32) * scale
        grad_k = jnp.einsum("ghst,gshd->gthd", grad_s, q, preferred_element_type=F32) * scale
        grad_q = rotate(grad_q.reshape(head_shape), cosine, -sine)
        grad_k = rotate(grad_k.reshape(head_shape), cosine, -sine)
        grad_v = grad_v.reshape(head_shape)
        key_sum = jnp.sum(grad_k[:, :, :ROT], axis=0)
        d_qkv = jnp.concatenate(
            [g.reshape(all_slots, own_width) for g in (grad_q, grad_k, grad_v)], axis=1
        ).astype(BF16)
        a1_b = blocks_of(a1)
        grad_a1 = rep_reduce(d_qkv, lambda a: dot_rt(a, wq), slots)
        grad_input = (grad_resid + norm_back(grad_a1 * vec[0], normal_one, inv_one)).astype(BF16)

        def spread(sums):
            zero = jnp.zeros((own_heads, REPS, sums.shape[1]), F32)
            return lax.dynamic_update_index_in_dim(zero, sums, r, 1)

        vec_sums = jnp.stack(
            [
                jnp.sum(grad_a1 * normal_one, axis=0),
                jnp.sum(grad_a1, axis=0),
                jnp.sum(grad_a2 * normal_two, axis=0),
                jnp.sum(grad_a2, axis=0),
                spread(jnp.sum(grad_q, axis=0)).reshape(features),
                spread(jnp.sum(grad_v, axis=0)).reshape(features),
            ],
            axis=0,
        )
        key_rows = HEADS * ROT // n
        packed = jnp.concatenate(
            [
                vec_sums.reshape(6, n, rows).transpose(1, 0, 2).reshape(n, 6 * rows),
                spread(key_sum).reshape(n, key_rows),
            ],
            axis=1,
        )
        width = -(-packed.shape[1] // 1024) * 1024
        packed = jnp.pad(packed, ((0, 0), (0, width - packed.shape[1]))).reshape(n, width // 128, 128)
        line = ([], [])
        sums = run(
            {
                "d": reduce(lambda i: dot_lt(hidden_b[i], dyl), ids, False, line),
                "g": reduce(lambda i: dot_lt(a2_b[i], grad_gate), ids, True, line),
                "u": reduce(lambda i: dot_lt(a2_b[i], grad_up), ids, False, line),
                "q": reduce(lambda i: dot_lt(a1_b[i], d_qkv), ids, True, line),
                "o": reduce(lambda i: dot_lt(attn_b[i], drl), ids, False, line),
                "s": reduce(lambda i: packed[i], ids, True, line, F32),
            },
            "dgdgdudugugugqoqoqosoqsoss",
        )
        grad_down, grad_wg, grad_wu = sums["d"], sums["g"], sums["u"]
        grad_wq, grad_wo, packed = sums["q"], sums["o"], sums["s"]
        packed = packed + core_swap(packed)
        packed = (packed + y_swap(packed)).reshape(-1)
        out_vectors = packed[: 6 * rows].reshape(6, rows).T
        out_key = packed[6 * rows : 6 * rows + key_rows].reshape(key_rows, 1)

        def everywhere(g):
            return by_rep(rep_parts(g.astype(BF16)), y, core)

        out_down = jnp.concatenate(everywhere(grad_down), axis=0).astype(F32)
        out_gate_up = jnp.concatenate(
            [weave(everywhere(g), n, down_rows) for g in (grad_wg, grad_wu)], axis=1
        )
        out_qkv = weave(everywhere(grad_wq), 3 * own_heads, head_dim)
        out_out = jnp.concatenate(everywhere(mix_out(grad_wo.astype(BF16))), axis=0).astype(F32)
        return activations, grad_input, out_vectors, out_key, out_qkv, out_out, out_gate_up, out_down

    tok, row = P(BOTH, None), P("shard", None)
    return jax.shard_map(
        on_device,
        mesh=mesh,
        in_specs=(tok, tok, P(BOTH), P(BOTH)) + (row,) * 6,
        out_specs=(tok, tok) + (row,) * 6,
        check_vma=False,
    )
```
